32 devices in a mesh: expert: 8 (over z, x), shard: 4 (over y, core).
Axes of the slice: x: 2, y: 2, z: 4, core: 2. Of those that a mesh axis runs over, the one named last changes fastest.
Arguments:
- tokens: bfloat16 [2, 4096, 768], P(None, ('expert', 'shard')), may hold values from -6 to 6
- cotangent: bfloat16 [2, 4096, 768], P(None, ('expert', 'shard')), may hold values from -6 to 6
- routes: int32 [2, 4096, 2], P(None, ('expert', 'shard')), may hold values from 0 to 15, all different within a row; in each aligned block of 128 rows (0 to 127, 128 to 255, ..., all dimensions but the last counted through in order) at most 18 rows name the same one
- prompt_rows: int32 [2, 8, 4], P(None, 'expert'), may hold values from 1 to 96, 256 in all within a row
- w_query: bfloat16 [768, 768], P('shard'), may hold values from -0.21875 to 0.21875
- w_key: bfloat16 [768, 768], P('shard'), may hold values from -0.21875 to 0.21875
- w_value: bfloat16 [768, 768], P('shard'), may hold values from -0.21875 to 0.21875
- w_output: bfloat16 [768, 768], P('shard'), may hold values from -3.5 to 3.5
- w_router: bfloat16 [768, 16], P('shard'), may hold values from -0.15625 to 0.15625
- gain_attn: bfloat16 [768], P('shard'), may hold values from 0.099609375 to 1.8984375
- gain_ffn: bfloat16 [768], P('shard'), may hold values from 0.099609375 to 1.8984375
- pos_table: bfloat16 [384], P('shard'), may hold values from -4 to 4
- w_in: bfloat16 [16, 768, 3072], P('expert', None, 'shard'), may hold values from -0.21875 to 0.21875
- w_out: bfloat16 [16, 3072, 768], P('expert', 'shard'), may hold values from -0.109375 to 0.109375
Outputs:
- mixed: bfloat16 [2, 4096, 768], P(None, ('expert', 'shard'))
- d_tokens: float32 [2, 4096, 768], P(None, ('expert', 'shard'))
- d_query: float32 [768, 768], P('shard')
- d_key: float32 [768, 768], P('shard')
- d_value: float32 [768, 768], P('shard')
- d_output: float32 [768, 768], P('shard')
- d_router: float32 [768, 16], P('shard')
- d_gain_attn: float32 [768], P('shard')
- d_gain_ffn: float32 [768], P('shard')
- d_table: float32 [384], P('shard')
- d_in: float32 [16, 768, 3072], P('expert', None, 'shard')
- d_out: float32 [16, 3072, 768], P('expert', 'shard')
The draws below stay inside these ranges and needn't reach their ends.
Inputs may be any that keep to these rules, and one draw needn't show every extreme that they name: `routes`: each row names two different experts. In each micro-batch, the 128 rows of one device name no expert more than 18 times, a bound that some block reaches. `prompt_rows`: the 4 counts of a group sum to 256; the largest is exactly 96.
All inputs are finite; a program needn't handle non-finite values.
Results may differ from the reference program's by a relative error of at most 0.02.
Values may be sent and summed in bfloat16 or wider, within the bound.
A program may use at most 192 MiB of HBM per device.

```python
import math
from functools import reduce
import jax
import jax.numpy as jnp
import numpy as np
from jax import lax

D = 768
HEADS = 12
HEAD_DIM = 64
FF = 3072
BUCKETS = 32
MICRO = 2
TOK_DEV = 128
EXPERTS = 16
ROWS = 4096
PROMPT = 256
PROMPT_MOST = 96
CAP = 18
N_EXPERT = 8
N_SHARD = 4


def block_scale(own_key, dims, cuts, low, high):
    level, own = 1.0, jax.random.fold_in(own_key, 6)
    for dim, parts in cuts:
        heights = jnp.exp(jax.random.uniform(jax.random.fold_in(own, dim), (parts,), jnp.float32, low / len(cuts), high / len(cuts)))
        level = level * jnp.repeat(heights, dims[dim] // parts).reshape([-1 if axis == dim else 1 for axis in range(len(dims))])
    return level


def split_up(count, total, reach, skew):
    loads = [(1 << 20) // math.isqrt(grade ** skew) + 1 for grade in range(2, count + 1)]
    rest, given = total - reach - (count - 1), [1] * (count - 1)
    while rest > 0:
        candidates = [i for i in range(count - 1) if given[i] < reach]
        whole, left = sum([loads[i] for i in candidates]), rest
        for i in candidates:
            more = min(reach - given[i], max(1, left * loads[i] // whole), rest)
            given[i] = given[i] + more
            rest = rest - more
    return np.array([reach] + given)


def uneven_parts(stream_key, count, total, most, slope):
    if count == 2:
        one = jax.random.randint(stream_key, (), max(1, total - most), min(most, total - 1) + 1)
        return jnp.stack([one, total - one])
    lengths = jnp.asarray(split_up(count, total, most, slope), jnp.int32)
    twos = (count - 1) // 2
    source_of, taker = lengths[1:1 + 2 * twos:2], lengths[2:2 + 2 * twos:2]
    room = jnp.minimum(source_of - 1, most - taker)
    moved = jax.random.randint(jax.random.fold_in(stream_key, 1), (twos,), 0, 1 << 20) % (room + 1)
    lengths = lengths.at[1:1 + 2 * twos:2].set(source_of - moved).at[2:2 + 2 * twos:2].set(taker + moved)
    return lengths[jax.random.permutation(jax.random.fold_in(stream_key, 2), count)]


def shared_out(rng, own, number, rows, number_of, top, bound, lean):
    sequence = jax.random.permutation(rng, number_of)
    crowded, ordinary = load_shares(number_of, rows * top, bound, lean, True), load_shares(number_of, rows * top, bound, lean, False)
    places = jnp.arange(number_of)

    def named(lengths, rotation):
        used = int((lengths > 0).sum())
        fixed = max(1, used // 4)
        passed = fixed + (places - fixed + rotation * (used - fixed)) % max(1, number_of - fixed)
        return jnp.zeros((number_of,), jnp.int32).at[sequence[jnp.where(places < fixed, places, passed)]].set(jnp.asarray(lengths, jnp.int32))

    lengths = jnp.where(number % 4 == 0, named(crowded, number // 4), named(ordinary, number - number // 4 - 1))
    mixed = jax.random.permutation(jax.random.fold_in(own, 3), number_of)
    donor, receiver = mixed[0:number_of // 2 * 2:2], mixed[1:number_of // 2 * 2:2]
    room = jnp.minimum(lengths[donor] - 1, bound - lengths[receiver]) // 2
    room = jnp.where((donor == sequence[0]) | (receiver == sequence[0]) | (lengths[receiver] == 0), 0, jnp.maximum(room, 0))
    passed = jax.random.randint(jax.random.fold_in(own, 4), (number_of // 2,), 0, 1 << 20) % (room + 1)
    lengths = lengths.at[donor].add(-passed).at[receiver].add(passed)
    labels = jnp.searchsorted(jnp.cumsum(lengths), jnp.arange(rows * top), side="right").astype(jnp.int32)
    listing = labels.reshape(top, rows).T
    listing = listing[jax.random.permutation(jax.random.fold_in(own, 1), rows)]
    rotation = jax.random.randint(jax.random.fold_in(own, 2), (rows, 1), 0, top)
    return jnp.take_along_axis(listing, (jnp.arange(top)[None, :] + rotation) % top, axis=1)


def load_shares(amount, total, bound, lean, full):
    loads = [(1 << 20) // math.isqrt(grade ** lean) + 1 for grade in range(1, amount + 1)]
    largest = bound if full else min(bound, max(-(-total // amount), total * loads[0] // sum(loads)))
    least = 1 if total - largest >= amount - 1 else 0
    given, surplus = [largest] + [least] * (amount - 1), total - largest - least * (amount - 1)
    while surplus > 0:
        candidates = [i for i in range(1, amount) if given[i] < largest] or [i for i in range(1, amount) if given[i] < bound]
        whole, remaining = sum([loads[i] for i in candidates]), surplus
        for i in candidates:
            extra = min(bound - given[i], max(1, remaining * loads[i] // whole), surplus)
            given[i] = given[i] + extra
            surplus = surplus - extra
    return np.array(given)


def noise(own_key, extent, deviation, reach, shards=(), kind=jnp.bfloat16):
    level = block_scale(own_key, extent, shards, -0.22, 0.18) if shards else 1.0
    values = jax.random.normal(own_key, extent, jnp.float32) * deviation * level
    return jnp.minimum(jnp.maximum(values, -reach), reach).astype(kind)


def setup_inputs(seed: int = 0) -> dict:
    arg_keys = jax.random.split(jax.random.key(seed), 15)
    tokens = noise(arg_keys[0], (MICRO, ROWS, D), 1.0, 6.0, ((1, 32),))
    cotangent = noise(arg_keys[1], (MICRO, ROWS, D), 1.0, 6.0, ((1, 32),))
    routes_keys = jax.random.split(jax.random.fold_in(arg_keys[2], 1), MICRO * ROWS // TOK_DEV)
    routes_turns = jax.random.permutation(jax.random.fold_in(arg_keys[2], 3), MICRO * ROWS // TOK_DEV)
    routes = jax.vmap(lambda own, number: shared_out(jax.random.fold_in(arg_keys[2], 2), own, number, TOK_DEV, EXPERTS, 2, CAP, 1))(routes_keys, routes_turns).reshape((MICRO, ROWS, 2))
    prompt_rows = jax.vmap(lambda own: uneven_parts(own, N_SHARD, PROMPT, PROMPT_MOST, 1))(jax.random.split(arg_keys[3], MICRO * N_EXPERT)).reshape((MICRO, N_EXPERT, N_SHARD)).astype(jnp.int32)
    w_query = noise(arg_keys[4], (D, D), D ** -0.5, 0.21875, ((0, 4),))
    w_key = noise(arg_keys[5], (D, D), D ** -0.5, 0.21875, ((0, 4),))
    w_value = noise(arg_keys[6], (D, D), D ** -0.5, 0.21875, ((0, 4),))
    w_output = noise(arg_keys[7], (D, D), (max(1, D // 256)) ** -0.5, 3.5, ((0, 4),))
    w_router = noise(arg_keys[8], (D, EXPERTS), (2 * D) ** -0.5, 0.15625, ((0, 4),))
    gain_attn = jnp.clip(1.0 + 0.18 * jax.random.normal(arg_keys[9], (D,), jnp.float32), 0.099609375, 1.8984375).astype(jnp.bfloat16)
    gain_ffn = jnp.clip(1.0 + 0.18 * jax.random.normal(arg_keys[10], (D,), jnp.float32), 0.099609375, 1.8984375).astype(jnp.bfloat16)
    pos_table = noise(arg_keys[11], (HEADS * BUCKETS,), 1.0, 4.0, ((0, 4),))
    w_in = noise(arg_keys[12], (EXPERTS, D, FF), D ** -0.5, 0.21875, ((0, 8), (2, 4)))
    w_out = noise(arg_keys[13], (EXPERTS, FF, D), FF ** -0.5, 0.109375, ((0, 8), (1, 4)))
    return dict(tokens=tokens, cotangent=cotangent, routes=routes, prompt_rows=prompt_rows, w_query=w_query, w_key=w_key, w_value=w_value, w_output=w_output, w_router=w_router, gain_attn=gain_attn, gain_ffn=gain_ffn, pos_table=pos_table, w_in=w_in, w_out=w_out)


EPS = 1e-06
MASKED = -1e+30
BUCKET_EDGES = (24, 32, 48, 64, 96, 128, 192, 256, 384, 512, 768, 1024, 1536, 2048, 3072)
HIGHEST = lax.Precision.HIGHEST

@jax.custom_vjp
def low(v):
    return lax.optimization_barrier(v.astype(jnp.bfloat16)).astype(jnp.float32)

@jax.custom_vjp
def low_back(v):
    return v

def low_keep(v):
    return (low(v), None)

def low_pass(kept, grad):
    return (grad,)

def back_keep(v):
    return (v, None)

def back_low(kept, grad):
    return (low(grad),)
low.defvjp(low_keep, low_pass)
low_back.defvjp(back_keep, back_low)

def distance_bucket(distance):
    coarse = reduce(lambda running, border: running + (distance >= border).astype(jnp.int32), BUCKET_EDGES, jnp.full(distance.shape, 16, jnp.int32))
    return jnp.where(distance < 16, distance, coarse)

def layout(counts, block_rows):
    shard_count = counts.shape[0]
    offsets = jnp.cumsum(counts, dtype=jnp.int32) - counts
    row_index = jnp.arange(shard_count * block_rows, dtype=jnp.int32)
    device = row_index // block_rows
    local_row = row_index - device * block_rows
    own_count = counts[device]
    is_prompt = local_row < own_count
    prompt_total = jnp.sum(counts, dtype=jnp.int32)
    position = jnp.where(is_prompt, offsets[device] + local_row, prompt_total + local_row - own_count)
    return (position, is_prompt, device)

def rms_norm(values, gain):
    return values * lax.rsqrt(lax.optimization_barrier(jnp.mean(values * values, axis=-1, keepdims=True)) + EPS) * gain

def dense(left, right):
    return jnp.dot(left, right, precision=HIGHEST, preferred_element_type=jnp.float32)

def group_forward(weights_all, inputs, routes, counts):
    w_query, w_key, w_value, w_output, w_router, gain_attn, gain_ffn, pos_table, w_in, w_out = weights_all
    group_rows = inputs.shape[0]
    shard_count = counts.shape[0]
    position, is_prompt, device = layout(counts, TOK_DEV)
    hidden = low(rms_norm(inputs, gain_attn))
    query = low(low_back(dense(hidden, w_query)))
    key = low(low_back(dense(hidden, w_key)))
    value = low(low_back(dense(hidden, w_value)))
    table = pos_table.reshape(HEADS, BUCKETS)
    key_heads = key.reshape(group_rows, HEADS, HEAD_DIM)
    value_heads = value.reshape(group_rows, HEADS, HEAD_DIM)
    query_block = math.gcd(group_rows, 512)
    blocks = group_rows // query_block

    def attend(block_item):
        query_piece, query_pos, query_dev = block_item
        raw = low_back(jnp.einsum('qhd,khd->hqk', query_piece, key_heads, precision=HIGHEST))
        distance = query_pos[:, None] - position[None, :]
        visible = (distance >= 0) & (is_prompt[None, :] | (device[None, :] == query_dev[:, None]))
        bias = table[:, distance_bucket(jnp.maximum(distance, 0))]
        scores = jnp.where(visible[None], raw * HEAD_DIM ** (-0.5) + bias, MASKED)
        return jnp.einsum('hqk,khd->qhd', low(jax.nn.softmax(scores, axis=-1)), value_heads, precision=HIGHEST)
    context = lax.map(jax.checkpoint(attend), (query.reshape(blocks, query_block, HEADS, HEAD_DIM), position.reshape(blocks, query_block), device.reshape(blocks, query_block)))
    context = low(low_back(context.reshape(group_rows, D)))
    middle = inputs + low_back(dense(context, w_output))
    normed = low(rms_norm(middle, gain_ffn))
    logits = low_back(dense(normed, w_router))
    gate_weights = jax.nn.softmax(jnp.take_along_axis(logits, routes, axis=1), axis=-1)
    flat_routes = routes.reshape(shard_count, 2 * TOK_DEV)
    expert_hits = (flat_routes[:, :, None] == jnp.arange(EXPERTS, dtype=jnp.int32)).astype(jnp.int32)
    expert_rank = lax.optimization_barrier(jnp.sum(jnp.cumsum(expert_hits, axis=1, dtype=jnp.int32) * expert_hits, axis=2, dtype=jnp.int32)) - 1
    slot_width = shard_count * CAP
    slot_index = (flat_routes * slot_width + jnp.arange(shard_count, dtype=jnp.int32)[:, None] * CAP + expert_rank).reshape(-1)
    slot_owner = jnp.full((EXPERTS * slot_width,), 2 * group_rows, jnp.int32).at[slot_index].set(jnp.arange(2 * group_rows, dtype=jnp.int32))
    padded = jnp.concatenate([normed, jnp.zeros((1, D), normed.dtype)], axis=0)
    taken = low_back(padded[slot_owner // 2]).reshape(EXPERTS, slot_width, D)
    pre_act = low_back(jnp.einsum('erd,edf->erf', taken, w_in, precision=HIGHEST))
    activation = low(jax.nn.gelu(pre_act))
    expert_result = low_back(low(jnp.einsum('erf,efd->erd', activation, w_out, precision=HIGHEST)))
    picked_rows = expert_result.reshape(EXPERTS * slot_width, D)[slot_index].reshape(group_rows, 2, D)
    return middle + lax.optimization_barrier(jnp.sum(gate_weights[:, :, None] * picked_rows, axis=1))

def reference(tokens, cotangent, routes, prompt_rows, w_query, w_key, w_value, w_output, w_router, gain_attn, gain_ffn, pos_table, w_in, w_out):
    weights_all = tuple((weight.astype(jnp.float32) for weight in (w_query, w_key, w_value, w_output, w_router, gain_attn, gain_ffn, pos_table, w_in, w_out)))
    group_count = MICRO * N_EXPERT
    group_rows = N_SHARD * TOK_DEV
    route_groups = routes.reshape(group_count, group_rows, 2)
    count_groups = prompt_rows.reshape(group_count, N_SHARD)
    stepper = jax.checkpoint(group_forward)

    def forward(weight_set, inputs):

        def scan_step(unused, block_item):
            return (unused, stepper(weight_set, block_item[0], block_item[1], block_item[2]))
        _, outputs = lax.scan(scan_step, jnp.zeros((), jnp.float32), (inputs.reshape(group_count, group_rows, D), route_groups, count_groups))
        return outputs.reshape(inputs.shape)
    result, pullback = jax.vjp(forward, weights_all, tokens.astype(jnp.float32))
    weight_grads, input_grads = pullback(cotangent.astype(jnp.float32))
    return (result.astype(jnp.bfloat16), input_grads, weight_grads[0], weight_grads[1], weight_grads[2], weight_grads[3], weight_grads[4], weight_grads[5], weight_grads[6], weight_grads[7], weight_grads[8], weight_grads[9])
```

```python
import functools
from functools import reduce
import math

import jax
import jax.numpy as jnp
import numpy as np
from jax import lax
from jax.experimental import pallas as pl
from jax.experimental.pallas import tpu as pltpu
from jax.sharding import PartitionSpec as P

HEADS = 12
BUCKETS = 32
EPS = 1e-06
MASKED = -1e30
BUCKET_EDGES = (24, 32, 48, 64, 96, 128, 192, 256, 384, 512, 768, 1024, 1536, 2048, 3072)
MESH = pl.DeviceIdType.MESH
BF = jnp.bfloat16
F32 = jnp.float32
I32 = jnp.int32
LANES = 128


class Sizes:
    def __init__(self, ne, ns, micro, rows, width, experts, local_experts, ff):
        self.ne, self.ns, self.ny = ne, ns, ns // 2
        self.m, self.t, self.d = micro, rows, width
        self.e, self.el, self.ff = experts, local_experts, ff
        self.g = ns * rows
        self.mt = micro * rows
        self.r = width // ns
        self.cap = (9 * rows + 4 * experts - 1) // (4 * experts)
        self.per = micro * self.cap
        self.sp = -(-(local_experts * self.per + 2) // 16) * 16
        self.slots = ne * self.sp
        self.nz = ne // 2
        self.hn = ne // 2
        self.cr = self.hn * self.per
        self.cb = local_experts * self.cr
        self.blk = 2 * self.cb
        self.hs = self.hn * self.sp
        self.n16 = -(-ne // 16) * 16
        self.pairs = HEADS // 2
        self.small = experts + 16
        self.far = self.g // 2 + rows

    def fits(self):
        return (
            self.ns % 2 == 0
            and self.t == LANES
            and self.d == HEADS * 64
            and self.cr % 16 == 0
            and self.ne % 4 == 0
            and self.e % 16 == 0
            and self.r % (16 * self.nz) == 0
            and self.slots % LANES == 0
            and self.el * self.per <= LANES
            and self.d % 256 == 0
        )


def layout_constants(z):
    perm = np.zeros((z.cb, z.hs), np.float32)
    rows_of = np.zeros((2 * z.n16, z.slots), np.float32)
    dest = np.zeros((2 * z.n16, z.slots), np.float32)
    place = np.zeros((z.slots, LANES), np.float32)
    gate_of = np.zeros((2 * z.n16, z.hs), np.float32)
    source = np.zeros((z.cb, 2 * z.n16), np.float32)
    pick = np.zeros((z.cb, LANES), np.float32)
    used = z.el * z.per
    for src in range(z.ne):
        rows_of[src, src * z.sp + used] = 1
        rows_of[z.n16 + src, src * z.sp + used + 1] = 1
        dest[src, src * z.sp : (src + 1) * z.sp] = 1
        dest[z.n16 + src, src * z.sp : (src + 1) * z.sp] = 1
        for q in range(used):
            place[src * z.sp + q, q] = 1
    for src in range(z.hn):
        gate_of[src, src * z.sp + used] = 1
        gate_of[z.n16 + src, src * z.sp + used + 1] = 1
        for q in range(used):
            row = (q // z.per) * z.cr + src * z.per + q % z.per
            perm[row, src * z.sp + q] = 1
            source[row, src] = 1
            source[row, z.n16 + src] = 1
            pick[row, q] = 1
    return [jnp.asarray(a, BF) for a in (perm, rows_of, dest, place, gate_of, source, pick)]


def dot(a, b):
    return jnp.dot(a, b, preferred_element_type=F32)


def dot_t(a, b):
    return lax.dot_general(a, b, (((1,), (1,)), ((), ())), preferred_element_type=F32)


def tdot(a, b):
    return lax.dot_general(a, b, (((0,), (0,)), ((), ())), preferred_element_type=F32)


def iota(shape, dim):
    return lax.broadcasted_iota(I32, shape, dim)


def aligned(start, size, multiple):
    return pl.ds(pl.multiple_of(start, multiple), size)


def offsets(z, chunk=None):
    every = [(kz, kx) for kz in range(z.nz) for kx in range(2)][1:]
    return [k for k in every if chunk is None or k[0] % 2 == chunk]


def position(z, k):
    return (k[0] % 2) * z.hn + (k[0] // 2) * 2 + k[1]


class Place:
    def __init__(self, z):
        self.z = z
        self.e = lax.axis_index("expert")
        self.s = lax.axis_index("shard")
        self.y, self.c = lax.div(self.s, 2), lax.rem(self.s, 2)

    def shard(self, k, other):
        y = lax.rem(self.y + k, self.z.ny)
        return y * 2 + (1 - self.c if other else self.c)

    def expert(self, kz, kx):
        high = lax.rem(lax.div(self.e, 2) + kz, self.z.nz)
        return high * 2 + lax.rem(lax.rem(self.e, 2) + kx, 2)

    def barrier(self, with_experts=True):
        sem = pltpu.get_barrier_semaphore()
        others = [(self.e, self.shard(0, True))]
        others += [(self.e, self.shard(k, False)) for k in range(1, self.z.ny)]
        if with_experts:
            others += [(self.expert(*k), self.s) for k in offsets(self.z)]
        for other in others:
            pl.semaphore_signal(sem, inc=1, device_id=other, device_id_type=MESH)
        pl.semaphore_wait(sem, len(others))


def rcopy(src, dst, send, recv, to):
    return pltpu.make_async_remote_copy(
        src_ref=src, dst_ref=dst, send_sem=send, recv_sem=recv, device_id=to, device_id_type=MESH
    )


class Gather:
    def __init__(self, place, own, full, send, recv, item):
        self.p, self.own, self.full = place, own, full
        self.send, self.recv, self.item = send, recv, item

    def copy(self, origin, src, slot, to):
        return rcopy(
            src, self.full(origin), self.send.at[self.item, slot], self.recv.at[self.item, origin], to
        )

    def partner(self):
        return (self.p.e, self.p.shard(0, True))

    def start(self):
        p, ny = self.p, self.p.z.ny
        for k in range(1, ny):
            self.copy(p.s, self.own, k, (p.e, p.shard(k, False))).start()
        self.copy(p.s, self.own, 0, self.partner()).start()

    def forward(self):
        p, ny = self.p, self.p.z.ny
        for k in range(1, ny):
            origin = p.shard(k, False)
            self.copy(origin, self.full(origin), ny + k - 1, self.partner()).wait_recv()
            self.copy(origin, self.full(origin), ny + k - 1, self.partner()).start()

    def arrive(self):
        p, ny = self.p, self.p.z.ny
        for k in range(ny):
            origin = p.shard(k, True)
            self.copy(origin, self.full(origin), 0, self.partner()).wait_recv()

    def finish(self):
        p, ny = self.p, self.p.z.ny
        for slot in range(2 * ny - 1):
            self.copy(p.s, self.own, slot, self.partner()).wait_send()


class Exchange:
    def __init__(self, place, src, dst, send, recv, item):
        self.p, self.src, self.dst = place, src, dst
        self.send, self.recv, self.item = send, recv, item

    def copy(self, k):
        z = self.p.z
        back = (-k[0] % z.nz, k[1])
        at = position(z, back)
        to = self.p.expert(*k)
        return rcopy(
            self.src(to),
            self.dst(at),
            self.send.at[self.item, position(z, k)],
            self.recv.at[self.item, at],
            (to, self.p.s),
        )

    def start(self, chunk=None):
        for k in offsets(self.p.z, chunk):
            self.copy(k).start()

    def arrive(self, chunk=None):
        z = self.p.z
        for k in offsets(z, chunk):
            self.copy((-k[0] % z.nz, k[1])).wait_recv()

    def finish(self):
        for k in offsets(self.p.z):
            self.copy(k).wait_send()


def slot_ids(z, routes):
    lane = iota((z.t, LANES), 1)
    lower = (iota((z.t, z.t), 0) > iota((z.t, z.t), 1)).astype(F32).astype(BF)
    base = lane * z.per
    for d in range(1, z.ne):
        base = base + jnp.where(lane >= d * z.el, z.sp - z.el * z.per, 0)
    firsts, seconds = [], []
    for m in range(z.m):
        r0 = routes[m * z.t : (m + 1) * z.t, 0:1]
        r1 = routes[m * z.t : (m + 1) * z.t, 1:2]
        hit0, hit1 = lane == r0, lane == r1
        hits = jnp.where(hit0 | hit1, 1.0, 0.0).astype(BF)
        spot = dot(lower, hits) + (base + m * z.cap).astype(F32)
        firsts.append(jnp.sum(jnp.where(hit0, spot, 0.0), axis=1, keepdims=True))
        seconds.append(jnp.sum(jnp.where(hit1, spot, 0.0), axis=1, keepdims=True))
    return jnp.concatenate(firsts, 0), jnp.concatenate(seconds, 0)


def one_hot(z, slot):
    return (iota((z.mt, z.slots), 1) == slot.astype(I32)).astype(F32)


def key_layout(z, counts, m, shape, dim):
    row = iota(shape, dim)
    total = counts[m, 0]
    for b in range(1, z.ns):
        total = total + counts[m, b]
    position = jnp.zeros(shape, I32)
    prompt = jnp.zeros(shape, I32)
    offset = 0
    for b in range(z.ns):
        own = counts[m, b]
        local = row - b * z.t
        inside = (local >= 0) & (local < z.t)
        first = local < own
        position = jnp.where(inside, jnp.where(first, offset + local, total + local - own), position)
        prompt = jnp.where(inside & first, 1, prompt)
        offset = offset + own
    return position, prompt


def query_position(z, counts, m, s):
    total, offset, own = 0, 0, 0
    for b in range(z.ns):
        count = counts[m, b]
        total = total + count
        offset = offset + jnp.where(b < s, count, 0)
        own = own + jnp.where(b == s, count, 0)
    local = iota((z.t, 1), 0)
    return jnp.where(local < own, offset + local, total + local - own)


def bucket_of(z, distance):
    coarse = jnp.full(distance.shape, 16, I32)
    for edge in BUCKET_EDGES:
        if edge < z.far:
            coarse = coarse + jnp.where(distance >= edge, 1, 0)
    return jnp.where(distance < 16, distance, coarse)


def front_kernel(
    z,
    tokens, dy, routes, counts, wk, wv, wq, wo, small, perm, rows_of, dest, place_m,
    toks, hid, kk, vv, qq, pp, ctx, mid, nrm, sd, xs, dyg, fk, fv, fq, fo, smallg,
    dys, dyr, table, bias_id, bias_mask,
    gsend, grecv, xsend, xrecv,
):
    p = Place(z)
    p.barrier()
    mt, t, d, r = z.mt, z.t, z.d, z.r

    def rows(ref, size):
        return lambda origin: ref.at[aligned(origin * size, size, 16)]

    items = [Gather(p, small, lambda o: smallg.at[o], gsend, grecv, 0)]
    for m in range(z.m):
        items.append(
            Gather(
                p,
                tokens.at[m],
                lambda o, m=m: toks.at[m, aligned(o * t, t, 16)],
                gsend,
                grecv,
                1 + m,
            )
        )
    base = 1 + z.m
    for i, (own, full) in enumerate(((wk, fk), (wv, fv), (wq, fq), (wo, fo))):
        items.append(Gather(p, own, rows(full, r), gsend, grecv, base + i))
    for item in items:
        item.start()
    g_dy = Gather(p, dyg.at[p.s], lambda o: dyg.at[o], gsend, grecv, base + 4)
    x_dy = Exchange(
        p,
        lambda to: dys.at[aligned(to * z.sp, z.sp, 16)],
        lambda at: dyr.at[pl.ds(at * z.sp, z.sp)],
        xsend,
        xrecv,
        0,
    )
    smallg[p.s] = small[...]
    for m in range(z.m):
        toks[m, aligned(p.s * t, t, 16), :] = tokens[m]
    for own, full in ((wk, fk), (wv, fv), (wq, fq), (wo, fo)):
        full[aligned(p.s * r, r, 16), :] = own[...]

    slot0, slot1 = slot_ids(z, routes)
    hot = (one_hot(z, slot0) + one_hot(z, slot1)).astype(BF)

    def send_dy(i, carry):
        cols = aligned(i * 256, 256, 256)
        dys[:, cols] = tdot(hot, dy[:, cols]).astype(BF)
        return carry

    lax.fori_loop(0, d // 256, send_dy, 0)
    x_dy.start()
    mine = aligned(p.e * z.sp, z.sp, 16)
    dyr[0 : z.sp, :] = dys[mine, :]

    for m in range(z.m):
        key_pos, prompt = key_layout(z, counts, m, (1, z.g), 1)
        distance = query_position(z, counts, m, p.s) - key_pos
        lane = iota((1, z.g), 1)
        own_block = (lane >= p.s * t) & (lane < (p.s + 1) * t)
        visible = (distance >= 0) & (own_block | (prompt == 1))
        bias_id[m] = jnp.where(visible, bucket_of(z, distance), 0)
        bias_mask[m] = jnp.where(visible, 0.0, MASKED)

    for item in items[: 1 + z.m]:
        item.forward()
    for item in items[: 1 + z.m]:
        item.arrive()
    sums = smallg[0].astype(F32)
    for b in range(1, z.ns):
        sums = sums + smallg[b].astype(F32)
    gain_one = sums[z.e : z.e + 1, :]
    gain_two = sums[z.e + 1 : z.e + 2, :]
    router = sums.astype(BF)
    for i in range(HEADS * BUCKETS // LANES):
        table[:, i * LANES : (i + 1) * LANES] = jnp.broadcast_to(
            sums[z.e + 2 : z.e + 3, i * LANES : (i + 1) * LANES], (8, LANES)
        )
    for m in range(z.m):
        def norm(i, carry, m=m):
            at = aligned(i * t, t, 16)
            x = toks[m, at, :].astype(F32)
            scale = lax.rsqrt(jnp.mean(x * x, axis=1, keepdims=True) + EPS)
            hid[m, at, :] = (x * scale * gain_one).astype(BF)
            return carry

        lax.fori_loop(0, z.ns, norm, 0)

    for item, full, out in ((items[base], fk, kk), (items[base + 1], fv, vv)):
        item.forward()
        item.arrive()

        def project(i, carry, full=full, out=out):
            m, cols = lax.div(i, d // 256), aligned(lax.rem(i, d // 256) * 256, 256, 256)
            out[m, :, cols] = dot(hid[m], full[:, cols]).astype(BF)
            return carry

        lax.fori_loop(0, z.m * (d // 256), project, 0)
    items[base + 2].forward()
    items[base + 2].arrive()
    items[base + 3].forward()

    def project_query(i, carry):
        m, cols = lax.div(i, d // 256), aligned(lax.rem(i, d // 256) * 256, 256, 256)
        own = hid[m, aligned(p.s * t, t, 16), :]
        qq[aligned(m * t, t, 16), cols] = (dot(own, fq[:, cols]).astype(BF).astype(F32) * 0.125).astype(BF)
        return carry

    lax.fori_loop(0, z.m * (d // 256), project_query, 0)

    x_dy.arrive()

    def order_dy(i, carry):
        cols = aligned(i * 256, 256, 256)
        for h in range(2):
            rows_h = slice(h * z.hs, (h + 1) * z.hs)
            dyg[p.s, h * z.cb : (h + 1) * z.cb, cols] = dot(perm[...], dyr[rows_h, cols]).astype(BF)
        return carry

    lax.fori_loop(0, d // 256, order_dy, 0)
    g_dy.start()

    low = iota((t, LANES), 1) < 64

    def attend(i, carry):
        m, pair = lax.div(i, z.pairs), lax.rem(i, z.pairs)
        cols = aligned(pair * LANES, LANES, LANES)
        q = qq[aligned(m * t, t, 16), cols]
        zero = jnp.zeros_like(q)
        q_two = jnp.concatenate([jnp.where(low, q, zero), jnp.where(low, zero, q)], 0)
        scores = dot_t(q_two, kk[m, :, cols])
        part = table[0:1, aligned(lax.div(pair, 2) * LANES, LANES, LANES)]
        part = jnp.broadcast_to(part, (t, LANES))
        shift = lax.rem(pair, 2) * 64
        for half in range(2):
            halves = []
            for b in range(z.ns):
                idx = bias_id[m, :, b * LANES : (b + 1) * LANES] + (shift + 32 * half)
                bias = jnp.take_along_axis(part, idx, axis=1)
                halves.append(
                    scores[half * t : (half + 1) * t, b * LANES : (b + 1) * LANES]
                    + (bias + bias_mask[m, :, b * LANES : (b + 1) * LANES])
                )
            s = jnp.concatenate(halves, 1)
            top = jnp.max(s, axis=1, keepdims=True)
            e = jnp.exp(s - top)
            total = jnp.sum(e, axis=1, keepdims=True)
            pp[i, half * t : (half + 1) * t, :] = (e * (1.0 / total)).astype(BF)
        two = dot(pp[i], vv[m, :, cols])
        ctx[aligned(m * t, t, 16), cols] = jnp.where(low, two[:t], two[t:]).astype(BF)
        return carry

    lax.fori_loop(0, z.m * z.pairs, attend, 0)
    g_dy.forward()
    items[base + 3].arrive()

    def output(i, carry):
        cols = aligned(i * 256, 256, 256)
        mid[:, cols] = dot(ctx[...], fo[:, cols])
        return carry

    lax.fori_loop(0, d // 256, output, 0)
    for m in range(z.m):
        at = slice(m * t, (m + 1) * t)
        x = mid[at, :] + tokens[m].astype(F32)
        mid[at, :] = x
        scale = lax.rsqrt(jnp.mean(x * x, axis=1, keepdims=True) + EPS)
        nrm[at, :] = (x * scale * gain_two).astype(BF)
    logits = dot_t(nrm[...], router)
    lane = iota((mt, z.small), 1)
    pick0 = jnp.sum(jnp.where(lane == routes[:, 0:1], logits, 0.0), axis=1, keepdims=True)
    pick1 = jnp.sum(jnp.where(lane == routes[:, 1:2], logits, 0.0), axis=1, keepdims=True)
    top = jnp.maximum(pick0, pick1)
    e0, e1 = jnp.exp(pick0 - top), jnp.exp(pick1 - top)
    gate0, gate1 = e0 / (e0 + e1), e1 / (e0 + e1)
    lane = iota((mt, LANES), 1)
    sd[...] = jnp.where(
        lane == 0, slot0, jnp.where(lane == 1, slot1, jnp.where(lane == 2, gate0, jnp.where(lane == 3, gate1, 0.0)))
    )
    hot0, hot1 = one_hot(z, slot0), one_hot(z, slot1)
    gate_row = jnp.sum(hot0 * gate0 + hot1 * gate1, axis=0, keepdims=True)
    high = gate_row.astype(BF).astype(F32)
    is_high = iota((2 * z.n16, 1), 0) < z.n16
    gates = (dest[...].astype(F32) * jnp.where(is_high, high, gate_row - high)).astype(BF)
    gates = dot(gates, place_m[...]).astype(BF)
    hot = (hot0 + hot1).astype(BF)

    def dispatch(i, carry):
        cols = aligned(i * 256, 256, 256)
        xs[:, cols] = tdot(hot, nrm[:, cols]).astype(BF)
        return carry

    lax.fori_loop(0, d // 256, dispatch, 0)
    xs[:, :LANES] = (xs[:, :LANES].astype(F32) + tdot(rows_of[...], gates)).astype(BF)
    g_dy.arrive()
    for item in items + [g_dy]:
        item.finish()
    x_dy.finish()


VMEM = pl.BlockSpec(memory_space=pltpu.VMEM)
SMEM = pl.BlockSpec(memory_space=pltpu.SMEM)


def front(z, tokens, dy, routes, counts, wk, wv, wq, wo, small, perm, rows_of, dest, place_m):
    def bf(*shape):
        return jax.ShapeDtypeStruct(shape, BF)

    def f32(*shape):
        return jax.ShapeDtypeStruct(shape, F32)

    outs = (
        bf(z.m, z.g, z.d), bf(z.m, z.g, z.d), bf(z.m, z.g, z.d), bf(z.m, z.g, z.d), bf(z.mt, z.d),
        bf(z.m * z.pairs, 2 * z.t, z.g), bf(z.mt, z.d), f32(z.mt, z.d), bf(z.mt, z.d), f32(z.mt, LANES),
        bf(z.slots, z.d), bf(z.ns, z.blk, z.d), bf(z.d, z.d), bf(z.d, z.d), bf(z.d, z.d), bf(z.d, z.d),
        bf(z.ns, z.small, z.d),
    )
    n_items = 1 + z.m + 5
    return pl.pallas_call(
        functools.partial(front_kernel, z),
        out_shape=outs,
        in_specs=[VMEM] * 3 + [SMEM] + [VMEM] * 9,
        out_specs=[VMEM] * len(outs),
        scratch_shapes=[
            pltpu.VMEM((z.slots, z.d), BF),
            pltpu.VMEM((z.slots, z.d), BF),
            pltpu.VMEM((8, HEADS * BUCKETS), F32),
            pltpu.VMEM((z.m, z.t, z.g), I32),
            pltpu.VMEM((z.m, z.t, z.g), F32),
            pltpu.SemaphoreType.DMA((n_items, z.ns)),
            pltpu.SemaphoreType.DMA((n_items, z.ns)),
            pltpu.SemaphoreType.DMA((1, z.ne)),
            pltpu.SemaphoreType.DMA((1, z.ne)),
        ],
        compiler_params=pltpu.CompilerParams(
            collective_id=0, has_side_effects=True, vmem_limit_bytes=60 * 2**20
        ),
        name="front",
    )(tokens, dy, routes, counts, wk, wv, wq, wo, small, perm, rows_of, dest, place_m)


def small_block(z, own, w_router, gain_attn, gain_ffn, pos_table):
    share = jnp.concatenate(
        [w_router.T, gain_attn[None], gain_ffn[None], jnp.zeros((14, z.r), BF)], 0
    )
    col = jnp.arange(z.d)
    wide = jnp.where(col[None] // z.r == own, jnp.tile(share, (1, z.ns)), 0)
    n = pos_table.shape[0]
    table = jnp.where(col // n == own, jnp.tile(pos_table, z.d // n), 0)
    return jnp.where(jnp.arange(z.small)[:, None] == z.e + 2, table[None], wide)


GELU_A = math.sqrt(2.0 / math.pi)
GELU_B = 0.044715


def expert_kernel(
    z,
    xs, dyg_in, w_in, w_out, perm, gate_of, source, pick,
    ret, din, dout,
    xr, xg, gwg, gwc, act, gp, dyg, part, rp, ysum, ry, fin,
    csem, gsend, grecv, xsend, xrecv, psend, precv, ysend, yrecv, rsend, rrecv,
):
    p = Place(z)
    load = pltpu.make_async_copy(dyg_in, dyg, csem.at[0])
    load.start()
    p.barrier()
    t, d = z.t, z.d
    half = d // 2
    x_move = Exchange(
        p,
        lambda to: xs.at[aligned(to * z.sp, z.sp, 16)],
        lambda at: xr.at[pl.ds(at * z.sp, z.sp)],
        xsend,
        xrecv,
        0,
    )
    x_move.start(0)
    x_move.start(1)
    xr[0 : z.sp, :] = xs[aligned(p.e * z.sp, z.sp, 16), :]
    load.wait()

    tiles = z.ff // 256

    def expert_rows(ref, h, l, cols):
        return ref[:, aligned(h * z.cb + l * z.cr, z.cr, 16), cols].reshape(z.ns * z.cr, -1)

    def gradient(i, carry):
        h = lax.div(i, z.el * tiles)
        l = lax.div(lax.rem(i, z.el * tiles), tiles)
        at = aligned(lax.rem(i, tiles) * 256, 256, 256)
        g = dot_t(expert_rows(dyg, h, l, slice(None)), w_out[l, at, :])
        gp[:, aligned(h * z.cb + l * z.cr, z.cr, 16), at] = g.astype(BF).reshape(z.ns, z.cr, 256)
        return carry

    lax.fori_loop(0, 2 * z.el * tiles, gradient, 0)

    def gather_of(h):
        at = pl.ds(h * z.cb, z.cb)
        return (
            Gather(p, gwg.at[p.s, h], lambda o: gwg.at[o, h], gsend, grecv, 2 * h),
            Gather(p, xg.at[p.s, at], lambda o: xg.at[o, at], gsend, grecv, 2 * h + 1),
        )

    gathers = [gather_of(h) for h in range(2)]

    def distribute(h):
        x_move.arrive(h)
        rows_h = slice(h * z.hs, (h + 1) * z.hs)
        gwg[p.s, h] = dot(gate_of[...], xr[rows_h, :LANES]).astype(BF)
        gathers[h][0].start()

        def order(i, carry):
            cols = aligned(i * 256, 256, 256)
            xg[p.s, h * z.cb : (h + 1) * z.cb, cols] = dot(perm[...], xr[rows_h, cols]).astype(BF)
            return carry

        lax.fori_loop(0, d // 256, order, 0)
        gathers[h][1].start()

    def collect(h, forward):
        for item in gathers[h]:
            if forward:
                item.forward()
            else:
                item.arrive()

    def gate_columns(h):
        for b in range(z.ns):
            wide = dot(source[...], gwg[b, h]) * pick[...].astype(F32)
            gwc[b, h * z.cb : (h + 1) * z.cb, :] = jnp.sum(wide, axis=1, keepdims=True)

    def activate(h):
        gate_columns(h)

        def step(i, carry):
            l = lax.div(i, tiles)
            at = aligned(lax.rem(i, tiles) * 256, 256, 256)
            rows = aligned(h * z.cb + l * z.cr, z.cr, 16)
            x = dot(expert_rows(xg, h, l, slice(None)), w_in[l, :, at])
            g = expert_rows(gp, h, l, at).astype(F32)
            gate = gwc[:, rows, :].reshape(z.ns * z.cr, 1)
            x2 = x * x
            th = jnp.tanh(x * (GELU_A + (GELU_A * GELU_B) * x2))
            hx = 0.5 * x
            up = 1.0 + th
            act[:, rows, at] = (hx * up).astype(BF).reshape(z.ns, z.cr, 256)
            slope = 0.5 * up + hx * (1.0 - th * th) * (GELU_A + (3.0 * GELU_A * GELU_B) * x2)
            gp[:, rows, at] = (g * gate * slope).astype(BF).reshape(z.ns, z.cr, 256)
            return carry

        lax.fori_loop(0, z.el * tiles, step, 0)

    def unit(kind, h, half_id):
        return (kind * 2 + h) * 2 + half_id

    partner = (p.e, p.shard(0, True))

    def to_partner(u):
        return rcopy(part.at[u, 1 - p.c], rp.at[u], psend.at[u], precv.at[u], partner)

    def to_y(u, k):
        return rcopy(
            ysum.at[u, k - 1], ry.at[u, k - 1], ysend.at[u, k - 1], yrecv.at[u, k - 1], (p.e, p.shard(k, False))
        )

    def stage_a(kind, h, half_id):
        u = unit(kind, h, half_id)
        cols = slice(half_id * half, (half_id + 1) * half)

        def step(l, carry):
            if kind == 0:
                out = dot_t(expert_rows(gp, h, l, slice(None)), w_in[l, cols, :])
            else:
                out = dot(expert_rows(act, h, l, slice(None)), w_out[l, :, cols])
            out = out.astype(BF)
            for b in range(z.ns):
                part[u, b % 2, b // 2, aligned(l * z.cr, z.cr, 16), :] = out[b * z.cr : (b + 1) * z.cr]
            return carry

        lax.fori_loop(0, z.el, step, 0)
        to_partner(u).start()

    def stage_b(kind, h, half_id):
        u = unit(kind, h, half_id)
        to_partner(u).wait_recv()
        for k in range(1, z.ny):
            yy = lax.rem(p.y + k, z.ny)
            ysum[u, k - 1] = (part[u, p.c, yy].astype(F32) + rp[u, yy].astype(F32)).astype(BF)
            to_y(u, k).start()

    def back(u, h, half_id, kind):
        def copy(k):
            cols = pl.ds(half_id * half, half)
            away = (-k[0] % z.nz, k[1])
            return rcopy(
                fin.at[u, pl.ds((position(z, k) - h * z.hn) * z.sp, z.sp)],
                ret.at[kind, aligned(p.e * z.sp, z.sp, 16), cols],
                rsend.at[u, position(z, k) - h * z.hn],
                rrecv.at[u, position(z, away) - h * z.hn],
                (p.expert(*k), p.s),
            )

        def landing(k):
            cols = pl.ds(half_id * half, half)
            return rcopy(
                fin.at[u, pl.ds((position(z, k) - h * z.hn) * z.sp, z.sp)],
                ret.at[kind, aligned(p.expert(*k) * z.sp, z.sp, 16), cols],
                rsend.at[u, position(z, k) - h * z.hn],
                rrecv.at[u, position(z, k) - h * z.hn],
                (p.expert(*k), p.s),
            )

        return copy, landing

    def stage_c(kind, h, half_id):
        u = unit(kind, h, half_id)
        total = part[u, p.c, p.y].astype(F32) + rp[u, p.y].astype(F32)
        for k in range(1, z.ny):
            to_y(u, k).wait_recv()
            total = total + ry[u, k - 1].astype(F32)
        fin[u] = tdot(perm[...], total.astype(BF)).astype(BF)
        copy, _ = back(u, h, half_id, kind)
        for k in offsets(z, h):
            copy(k).start()
        if h == 0:
            cols = slice(half_id * half, (half_id + 1) * half)
            ret[kind, aligned(p.e * z.sp, z.sp, 16), cols] = fin[u, 0 : z.sp, :]

    def stage_d(kind, h, half_id):
        u = unit(kind, h, half_id)
        copy, landing = back(u, h, half_id, kind)
        for k in offsets(z, h):
            landing(k).wait_recv()
        for k in offsets(z, h):
            copy(k).wait_send()
        to_partner(u).wait_send()
        for k in range(1, z.ny):
            to_y(u, k).wait_send()

    def weights(l):
        def gate_dy(i, carry):
            rows = aligned(lax.div(i, 2) * z.cb + l * z.cr, z.cr, 16)
            cols = aligned(lax.rem(i, 2) * half, half, LANES)
            dyg[:, rows, cols] = (dyg[:, rows, cols].astype(F32) * gwc[:, rows, :]).astype(BF)
            return carry

        lax.fori_loop(0, 4, gate_dy, 0)

        def both(ref, cols):
            return jnp.concatenate([expert_rows(ref, h, l, cols) for h in range(2)], 0)

        def step(i, carry):
            at = aligned(i * 256, 256, 256)
            dout[l, :, at] = tdot(both(act, slice(None)), both(dyg, at)).astype(BF)
            return carry

        lax.fori_loop(0, d // 256, step, 0)

        def step_in(i, carry):
            at = aligned(i * 256, 256, 256)
            din[l, :, at] = tdot(both(xg, slice(None)), both(gp, at)).astype(BF)
            return carry

        lax.fori_loop(0, tiles, step_in, 0)

    distribute(0)
    distribute(1)
    collect(0, True)
    collect(0, False)
    activate(0)
    stage_a(0, 0, 0)
    stage_a(0, 0, 1)
    stage_b(0, 0, 0)
    stage_b(0, 0, 1)
    collect(1, True)
    collect(1, False)
    activate(1)
    stage_a(0, 1, 0)
    stage_c(0, 0, 0)
    stage_b(0, 1, 0)
    stage_a(0, 1, 1)
    stage_c(0, 0, 1)
    stage_b(0, 1, 1)
    stage_a(1, 0, 0)
    stage_a(1, 0, 1)
    stage_b(1, 0, 0)
    stage_b(1, 0, 1)
    stage_a(1, 1, 0)
    stage_a(1, 1, 1)
    stage_c(0, 1, 0)
    stage_b(1, 1, 0)
    stage_b(1, 1, 1)
    stage_c(0, 1, 1)
    weights(0)
    stage_c(1, 0, 0)
    stage_c(1, 0, 1)
    weights(1)
    stage_c(1, 1, 0)
    stage_c(1, 1, 1)
    for kind in range(2):
        for h in range(2):
            for half_id in range(2):
                stage_d(kind, h, half_id)
    x_move.finish()
    for pair in gathers:
        for item in pair:
            item.finish()


def experts(z, xs, dyg, w_in, w_out, perm, gate_of, source, pick):
    def bf(*shape):
        return jax.ShapeDtypeStruct(shape, BF)

    dma = pltpu.SemaphoreType.DMA
    half = z.d // 2
    return pl.pallas_call(
        functools.partial(expert_kernel, z),
        out_shape=(bf(2, z.slots, z.d), bf(z.el, z.d, z.ff), bf(z.el, z.ff, z.d)),
        in_specs=[VMEM, pl.BlockSpec(memory_space=pl.ANY)] + [VMEM] * 6,
        out_specs=[VMEM] * 3,
        scratch_shapes=[
            pltpu.VMEM((z.slots, z.d), BF),
            pltpu.VMEM((z.ns, z.blk, z.d), BF),
            pltpu.VMEM((z.ns, 2, 2 * z.n16, LANES), BF),
            pltpu.VMEM((z.ns, z.blk, 1), F32),
            pltpu.VMEM((z.ns, z.blk, z.ff), BF),
            pltpu.VMEM((z.ns, z.blk, z.ff), BF),
            pltpu.VMEM((z.ns, z.blk, z.d), BF),
            pltpu.VMEM((8, 2, z.ny, z.cb, half), BF),
            pltpu.VMEM((8, z.ny, z.cb, half), BF),
            pltpu.VMEM((8, z.ny - 1, z.cb, half), BF),
            pltpu.VMEM((8, z.ny - 1, z.cb, half), BF),
            pltpu.VMEM((8, z.hs, half), BF),
            dma((1,)),
            dma((4, z.ns)), dma((4, z.ns)),
            dma((1, z.ne)), dma((1, z.ne)),
            dma((8,)), dma((8,)),
            dma((8, z.ny)), dma((8, z.ny)),
            dma((8, z.hn)), dma((8, z.hn)),
        ],
        compiler_params=pltpu.CompilerParams(
            collective_id=1, has_side_effects=True, vmem_limit_bytes=60 * 2**20
        ),
        name="experts",
    )(xs, dyg, w_in, w_out, perm, gate_of, source, pick)


class Scatter:
    def __init__(self, place, part, from_core, to_y, from_y, psend, precv, ysend, yrecv):
        self.p, self.part, self.from_core = place, part, from_core
        self.to_y, self.from_y = to_y, from_y
        self.psend, self.precv, self.ysend, self.yrecv = psend, precv, ysend, yrecv

    def core_copy(self):
        p = self.p
        return rcopy(
            self.part.at[1 - p.c], self.from_core, self.psend, self.precv, (p.e, p.shard(0, True))
        )

    def y_copy(self, k):
        p = self.p
        return rcopy(
            self.to_y.at[k - 1], self.from_y.at[k - 1], self.ysend.at[k - 1], self.yrecv.at[k - 1],
            (p.e, p.shard(k, False)),
        )

    def send(self):
        self.core_copy().start()

    def middle(self):
        p = self.p
        self.core_copy().wait_recv()
        for k in range(1, p.z.ny):
            yy = lax.rem(p.y + k, p.z.ny)
            both = self.part[p.c, yy].astype(F32) + self.from_core[yy].astype(F32)
            self.to_y[k - 1] = both.astype(BF)
            self.y_copy(k).start()

    def total(self):
        p = self.p
        out = self.part[p.c, p.y].astype(F32) + self.from_core[p.y].astype(F32)
        for k in range(1, p.z.ny):
            self.y_copy(k).wait_recv()
            out = out + self.from_y[k - 1].astype(F32)
        return out

    def finish(self):
        self.core_copy().wait_send()
        for k in range(1, self.p.z.ny):
            self.y_copy(k).wait_send()


class Sum:
    def __init__(self, place, own, xin, xsum, zin, done, sems):
        self.p, self.own, self.xin, self.xsum, self.zin, self.done = place, own, xin, xsum, zin, done
        self.sx, self.rx, self.sz, self.rz, self.sg, self.rg, self.sh, self.rh = sems
        self.rows, self.cols = own.shape
        self.nz = place.z.nz
        self.x, self.zz = lax.rem(place.e, 2), lax.div(place.e, 2)

    def half(self, x):
        return aligned(x * (self.cols // 2), self.cols // 2, LANES)

    def piece(self, zz):
        return aligned(zz * (self.rows // self.nz), self.rows // self.nz, 16)

    def other_x(self):
        return (self.p.expert(0, 1), self.p.s)

    def other_z(self, k):
        return (self.p.expert(k, 0), self.p.s)

    def z_at(self, k):
        return lax.rem(self.zz + k, self.nz)

    def copy_x(self):
        return rcopy(self.own.at[:, self.half(1 - self.x)], self.xin, self.sx, self.rx, self.other_x())

    def copy_z(self, k):
        return rcopy(
            self.xsum.at[self.piece(self.z_at(k))], self.zin.at[k - 1], self.sz.at[k - 1], self.rz.at[k - 1],
            self.other_z(k),
        )

    def copy_g(self, k, origin):
        block = self.done.at[self.piece(origin), self.half(self.x)]
        return rcopy(block, block, self.sg.at[k - 1], self.rg.at[k - 1], self.other_z(k))

    def copy_h(self, x):
        block = self.done.at[:, self.half(x)]
        return rcopy(block, block, self.sh, self.rh, self.other_x())

    def one(self):
        self.copy_x().start()

    def two(self):
        self.copy_x().wait_recv()
        self.xsum[...] = (self.own[:, self.half(self.x)].astype(F32) + self.xin[...].astype(F32)).astype(BF)
        for k in range(1, self.nz):
            self.copy_z(k).start()

    def three(self):
        out = self.xsum[self.piece(self.zz), :].astype(F32)
        for k in range(1, self.nz):
            self.copy_z(k).wait_recv()
            out = out + self.zin[k - 1].astype(F32)
        self.done[self.piece(self.zz), self.half(self.x)] = out.astype(BF)
        for k in range(1, self.nz):
            self.copy_g(k, self.zz).start()

    def four(self):
        for k in range(1, self.nz):
            self.copy_g(k, self.z_at(self.nz - k)).wait_recv()
        self.copy_h(self.x).start()

    def five(self):
        self.copy_h(1 - self.x).wait_recv()

    def finish(self):
        self.copy_x().wait_send()
        for k in range(1, self.nz):
            self.copy_z(k).wait_send()
            self.copy_g(k, self.zz).wait_send()
        self.copy_h(self.x).wait_send()


def back_kernel(
    z,
    dy, routes, counts, toks, hid, kk, vv, qq, pp, ctx, mid, nrm, sd, smallg, fk, fv, fq, fo, ret,
    mixed, dtok, dq, dk, dv, do, dsmall,
    gctx, gqb, gkb, gvb, gmid, lower, edge_id, edge_ok, tab, gain_rows,
    wpart, wrp, wys, wyr, wsum, wxin, wxs, wzin, wdone,
    gpart, grp, gys, gyr, sbuf, sone, stwo, sthree, sfour,
    wp1, wp2, wy1, wy2, ux1, ux2, uz1, uz2, ug1, ug2, uh1, uh2, gp1, gp2, gy1, gy2, ss1, ss2,
):
    p = Place(z)
    p.barrier()
    t, d, mt = z.t, z.d, z.mt
    sums = smallg[0].astype(F32)
    for b in range(1, z.ns):
        sums = sums + smallg[b].astype(F32)
    gain_one = sums[z.e : z.e + 1, :]
    gain_two = sums[z.e + 1 : z.e + 2, :]
    router = sums.astype(BF)

    slot0, slot1 = sd[:, 0:1], sd[:, 1:2]
    gate0, gate1 = sd[:, 2:3], sd[:, 3:4]
    hot0, hot1 = one_hot(z, slot0).astype(BF), one_hot(z, slot1).astype(BF)
    grad = dy[...].astype(F32)
    first, second = dot(hot0, ret[1]), dot(hot1, ret[1])
    mixed[...] = (mid[...] + gate0 * first + gate1 * second).astype(BF)
    toward0 = jnp.sum(grad * first, axis=1, keepdims=True)
    toward1 = jnp.sum(grad * second, axis=1, keepdims=True)
    mean = gate0 * toward0 + gate1 * toward1
    lane = iota((mt, z.small), 1)
    glog = jnp.where(lane == routes[:, 0:1], gate0 * (toward0 - mean), 0.0)
    glog = (glog + jnp.where(lane == routes[:, 1:2], gate1 * (toward1 - mean), 0.0)).astype(BF)
    gnorm = dot(glog, router) + dot(hot0, ret[0]) + dot(hot1, ret[0])
    x = mid[...]
    scale = lax.rsqrt(jnp.mean(x * x, axis=1, keepdims=True) + EPS)
    xh = x * scale
    gain_rows[1:2, :] = jnp.sum(gnorm * xh, axis=0, keepdims=True)
    gy = gnorm * gain_two
    gm = grad + scale * (gy - xh * jnp.mean(gy * xh, axis=1, keepdims=True))
    gmid[...] = gm
    gattn = gm.astype(BF)
    sbuf[...] = tdot(glog, nrm[...])

    def reduction(u):
        shard_sum = Scatter(
            p, wpart.at[u], wrp.at[u], wys.at[u], wyr.at[u], wp1.at[u], wp2.at[u], wy1.at[u], wy2.at[u]
        )
        expert_sum = Sum(
            p, wsum.at[u], wxin.at[u], wxs.at[u], wzin.at[u], wdone.at[u],
            (ux1.at[u], ux2.at[u], uz1.at[u], uz2.at[u], ug1.at[u], ug2.at[u], uh1.at[u], uh2.at[u]),
        )
        return shard_sum, expert_sum

    pairs = [reduction(u) for u in range(4)]

    def stage(u, n):
        shard_sum, expert_sum = pairs[u]
        if n == 0:
            shard_sum.send()
        elif n == 1:
            shard_sum.middle()
        elif n == 2:
            wsum[u] = shard_sum.total().astype(BF)
            expert_sum.one()
        elif n == 3:
            expert_sum.two()
        elif n == 4:
            expert_sum.three()
        elif n == 5:
            expert_sum.four()
        else:
            expert_sum.five()

    def put(u, cols, value):
        value = value.astype(BF)
        for b in range(z.ns):
            wpart[u, b % 2, b // 2, :, cols] = value[b * z.r : (b + 1) * z.r]

    for i in range(d // 256):
        cols = slice(i * 256, (i + 1) * 256)
        put(3, cols, tdot(ctx[...], gattn[:, cols]))
    stage(3, 0)
    for i in range(d // 256):
        cols = slice(i * 256, (i + 1) * 256)
        gctx[:, cols] = dot_t(gattn, fo[cols, :]).astype(BF)

    tab[...] = jnp.zeros_like(tab)
    lane = iota((1, LANES), 1)
    starts = jnp.where(lane <= 16, lane, 0)
    for i, edge in enumerate(BUCKET_EDGES):
        starts = jnp.where(lane == 17 + i, edge, starts)
    for m in range(z.m):
        key_pos, _ = key_layout(z, counts, m, (z.g, 1), 0)
        lower[m] = jnp.where(key_pos <= iota((z.g, z.far), 1), 1.0, 0.0).astype(BF)
        at = query_position(z, counts, m, p.s) - starts
        ok = (at >= 0) & (lane < BUCKETS)
        edge_id[m] = jnp.where(ok, at, 0)
        edge_ok[m] = jnp.where(ok, 1.0, 0.0)
    low = iota((t, LANES), 1) < 64

    def attend_back(i, unit):
        m = lax.rem(i, z.m)
        pair = unit * 2 + lax.div(i, z.m)
        cols = aligned(pair * LANES, LANES, LANES)
        rows = aligned(m * t, t, 16)
        q, g = qq[rows, cols], gctx[rows, cols]
        zero = jnp.zeros_like(q)
        q_two = jnp.concatenate([jnp.where(low, q, zero), jnp.where(low, zero, q)], 0)
        g_two = jnp.concatenate([jnp.where(low, g, zero), jnp.where(low, zero, g)], 0)
        probs = pp[m * z.pairs + pair]
        pf = probs.astype(F32)
        gp = dot_t(g_two, vv[m, :, cols])
        gs = (pf * (gp - jnp.sum(pf * gp, axis=1, keepdims=True))).astype(BF)
        two = dot(gs, kk[m, :, cols])
        gqb[rows, cols] = (jnp.where(low, two[:t], two[t:]) * 0.125).astype(BF)
        gkb[m, :, cols] = tdot(gs, q_two).astype(BF)
        gvb[m, :, cols] = tdot(probs, g_two).astype(BF)
        total = dot(gs, lower[m])
        for half in range(2):
            found = jnp.zeros((t, LANES), F32)
            for b in range(z.far // LANES):
                at = edge_id[m] - b * LANES
                inside = (at >= 0) & (at < LANES)
                got = jnp.take_along_axis(
                    total[half * t : (half + 1) * t, b * LANES : (b + 1) * LANES], jnp.where(inside, at, 0), axis=1
                )
                found = jnp.where(inside, got, found)
            found = jnp.sum(found * edge_ok[m], axis=0, keepdims=True)
            row = pl.ds(pair * 2 + half, 1)
            tab[row, :] = tab[row, :] + found
        return unit

    def attention(unit):
        lax.fori_loop(0, z.m * 2, attend_back, unit)

    def own_hidden():
        return jnp.concatenate([hid[m, aligned(p.s * t, t, 16), :] for m in range(z.m)], 0)

    def weight_grads(u):
        cols = slice(u * 256, (u + 1) * 256)
        put(u, slice(0, 256), tdot(own_hidden(), gqb[:, cols]))
        every = hid[...].reshape(z.m * z.g, d)
        put(u, slice(256, 512), tdot(every, gkb[:, :, cols].reshape(z.m * z.g, 256)))
        put(u, slice(512, 768), tdot(every, gvb[:, :, cols].reshape(z.m * z.g, 256)))

    grads = [
        Scatter(p, gpart.at[m], grp.at[m], gys.at[m], gyr.at[m], gp1.at[m], gp2.at[m], gy1.at[m], gy2.at[m])
        for m in range(z.m)
    ]

    def hidden_grads(m):
        for b in range(z.ns):
            rows = slice(b * t, (b + 1) * t)
            gh = dot_t(gkb[m, rows, :], fk[...]) + dot_t(gvb[m, rows, :], fv[...])
            mine = jnp.where(p.s == b, 1.0, 0.0)
            gh = gh + mine * dot_t(gqb[m * t : (m + 1) * t, :], fq[...])
            gpart[m, b % 2, b // 2] = gh.astype(BF)
            x = toks[m, rows, :].astype(F32)
            scale = lax.rsqrt(jnp.mean(x * x, axis=1, keepdims=True) + EPS)
            row = jnp.sum(gh * x * scale, axis=0, keepdims=True)
            if m == 0 and b == 0:
                gain_rows[0:1, :] = row
            else:
                gain_rows[0:1, :] = gain_rows[0:1, :] + row

    def token_grads(m):
        gh = grads[m].total()
        rows = slice(m * t, (m + 1) * t)
        x = toks[m, aligned(p.s * t, t, 16), :].astype(F32)
        scale = lax.rsqrt(jnp.mean(x * x, axis=1, keepdims=True) + EPS)
        xh = x * scale
        gy = gh * gain_one
        dtok[rows, :] = gmid[rows, :] + scale * (gy - xh * jnp.mean(gy * xh, axis=1, keepdims=True))

    nz = z.nz

    def small_copy(n, k=0):
        if n == 0:
            return rcopy(sone.at[0], sone.at[1], ss1.at[0], ss2.at[0], (p.e, p.shard(0, True)))
        if n == 1:
            return rcopy(stwo.at[0], stwo.at[k], ss1.at[k], ss2.at[k], (p.e, p.shard(k, False)))
        if n == 2:
            return rcopy(sthree.at[0], sthree.at[1], ss1.at[z.ny], ss2.at[z.ny], (p.expert(0, 1), p.s))
        zz = lax.div(p.e, 2)
        return rcopy(sfour.at[zz], sfour.at[zz], ss1.at[z.ny + k], ss2.at[z.ny + k], (p.expert(k, 0), p.s))

    def small_pack():
        tabs = tab[...]
        tabs = tabs - pltpu.roll(tabs, LANES - 1, 1)
        lane16 = iota(tabs.shape, 1)
        tabs = jnp.where(lane16 < BUCKETS, tabs, 0.0)
        row = iota(sbuf.shape, 0)
        out = sbuf[...]
        out = jnp.where(row == z.e, gain_rows[0:1, :], out)
        out = jnp.where(row == z.e + 1, gain_rows[1:2, :], out)
        sbuf[...] = out
        line = []
        per = LANES // BUCKETS
        for c in range(HEADS // per):
            piece = tabs[c * per : c * per + 1, :]
            for j in range(1, per):
                piece = piece + pltpu.roll(tabs[c * per + j : c * per + j + 1, :], j * BUCKETS, 1)
            line.append(piece)
        for c, piece in enumerate(line):
            sbuf[z.e + 2 : z.e + 3, c * LANES : (c + 1) * LANES] = piece
        sone[0] = sbuf[...].astype(BF)
        small_copy(0).start()

    def small_step(n):
        if n == 1:
            small_copy(0).wait_recv()
            stwo[0] = (sone[0].astype(F32) + sone[1].astype(F32)).astype(BF)
            for k in range(1, z.ny):
                small_copy(1, k).start()
        elif n == 2:
            out = stwo[0].astype(F32)
            for k in range(1, z.ny):
                small_copy(1, k).wait_recv()
                out = out + stwo[k].astype(F32)
            sthree[0] = out.astype(BF)
            small_copy(2).start()
        elif n == 3:
            small_copy(2).wait_recv()
            sfour[lax.div(p.e, 2)] = (sthree[0].astype(F32) + sthree[1].astype(F32)).astype(BF)
            for k in range(1, nz):
                small_copy(3, k).start()
        else:
            for k in range(1, nz):
                small_copy(3, k).wait_recv()
            out = sfour[0].astype(F32)
            for k in range(1, nz):
                out = out + sfour[k].astype(F32)
            dsmall[...] = out

    attention(0)
    stage(3, 1)
    weight_grads(0)
    stage(0, 0)
    stage(3, 2)
    attention(1)
    stage(0, 1)
    stage(3, 3)
    weight_grads(1)
    stage(1, 0)
    stage(0, 2)
    stage(3, 4)
    attention(2)
    stage(1, 1)
    stage(0, 3)
    stage(3, 5)
    weight_grads(2)
    stage(2, 0)
    stage(1, 2)
    stage(0, 4)
    hidden_grads(0)
    grads[0].send()
    stage(2, 1)
    stage(1, 3)
    stage(0, 5)
    hidden_grads(1)
    grads[1].send()
    grads[0].middle()
    small_pack()
    stage(2, 2)
    stage(1, 4)
    grads[1].middle()
    small_step(1)
    token_grads(0)
    stage(2, 3)
    stage(1, 5)
    small_step(2)
    token_grads(1)
    small_step(3)
    stage(2, 4)
    small_step(4)
    stage(2, 5)
    for u in (3, 0, 1, 2):
        stage(u, 6)
        if u == 3:
            do[...] = wdone[3].astype(F32)
        else:
            cols = slice(u * 256, (u + 1) * 256)
            dq[:, cols] = wdone[u, :, 0:256].astype(F32)
            dk[:, cols] = wdone[u, :, 256:512].astype(F32)
            dv[:, cols] = wdone[u, :, 512:768].astype(F32)
    for shard_sum, expert_sum in pairs:
        shard_sum.finish()
        expert_sum.finish()
    for item in grads:
        item.finish()
    small_copy(0).wait_send()
    for k in range(1, z.ny):
        small_copy(1, k).wait_send()
    small_copy(2).wait_send()
    for k in range(1, nz):
        small_copy(3, k).wait_send()


def back(z, *inputs):
    def bf(*shape):
        return pltpu.VMEM(shape, BF)

    def f32(*shape):
        return jax.ShapeDtypeStruct(shape, F32)

    dma = pltpu.SemaphoreType.DMA
    d, r, ny, nz = z.d, z.r, z.ny, z.nz
    n_small = z.ny + z.nz
    outs = (
        jax.ShapeDtypeStruct((z.mt, d), BF), f32(z.mt, d),
        f32(r, d), f32(r, d), f32(r, d), f32(r, d), f32(z.small, d),
    )
    return pl.pallas_call(
        functools.partial(back_kernel, z),
        out_shape=outs,
        in_specs=[VMEM] * 2 + [SMEM] + [VMEM] * 16,
        out_specs=[VMEM] * len(outs),
        scratch_shapes=[
            bf(z.mt, d), bf(z.mt, d), bf(z.m, z.g, d), bf(z.m, z.g, d), pltpu.VMEM((z.mt, d), F32),
            bf(z.m, z.g, z.far), pltpu.VMEM((z.m, z.t, LANES), I32), pltpu.VMEM((z.m, z.t, LANES), F32),
            pltpu.VMEM((16, LANES), F32), pltpu.VMEM((8, d), F32),
            bf(4, 2, ny, r, d), bf(4, ny, r, d), bf(4, ny - 1, r, d), bf(4, ny - 1, r, d),
            bf(4, r, d), bf(4, r, d // 2), bf(4, r, d // 2), bf(4, nz - 1, r // nz, d // 2), bf(4, r, d),
            bf(z.m, 2, ny, z.t, d), bf(z.m, ny, z.t, d), bf(z.m, ny - 1, z.t, d), bf(z.m, ny - 1, z.t, d),
            pltpu.VMEM((z.small, d), F32), bf(2, z.small, d), bf(ny, z.small, d), bf(2, z.small, d),
            bf(nz, z.small, d),
            dma((4,)), dma((4,)), dma((4, ny)), dma((4, ny)),
            dma((4,)), dma((4,)), dma((4, nz)), dma((4, nz)), dma((4, nz)), dma((4, nz)), dma((4,)), dma((4,)),
            dma((z.m,)), dma((z.m,)), dma((z.m, ny)), dma((z.m, ny)),
            dma((n_small,)), dma((n_small,)),
        ],
        compiler_params=pltpu.CompilerParams(
            collective_id=2, has_side_effects=True, vmem_limit_bytes=60 * 2**20
        ),
        name="back",
    )(*inputs)


def fused_device(
    z, tokens, cotangent, routes, prompt_rows, w_query, w_key, w_value, w_output, w_router, gain_attn, gain_ffn,
    pos_table, w_in, w_out,
):
    own = lax.axis_index("shard")
    perm, rows_of, dest, place, gate_of, source, pick = layout_constants(z)
    small = small_block(z, own, w_router, gain_attn, gain_ffn, pos_table)
    dy = cotangent.reshape(z.mt, z.d)
    routes = routes.reshape(z.mt, 2)
    counts = prompt_rows[:, 0]
    toks, hid, kk, vv, qq, pp, ctx, mid, nrm, sd, xs, dyg, fk, fv, fq, fo, smallg = front(
        z, tokens, dy, routes, counts, w_key, w_value, w_query, w_output, small, perm, rows_of, dest, place
    )
    ret, din, dout = experts(z, xs, dyg, w_in, w_out, perm, gate_of, source, pick)
    mixed, dtok, dq, dk, dv, do, dsmall = back(
        z, dy, routes, counts, toks, hid, kk, vv, qq, pp, ctx, mid, nrm, sd, smallg, fk, fv, fq, fo, ret
    )
    share = lax.dynamic_slice_in_dim(dsmall, own * z.r, z.r, axis=1)
    n = pos_table.shape[0]
    return (
        mixed.reshape(tokens.shape),
        dtok.reshape(tokens.shape),
        dq,
        dk,
        dv,
        do,
        share[: z.e].T,
        share[z.e],
        share[z.e + 1],
        lax.dynamic_slice_in_dim(dsmall[z.e + 2], own * n, n),
        din.astype(F32),
        dout.astype(F32),
    )


HIGHEST = lax.Precision.HIGHEST


def distance_bucket(distance):
    coarse = reduce(
        lambda running, border: running + (distance >= border).astype(jnp.int32),
        BUCKET_EDGES,
        jnp.full(distance.shape, 16, jnp.int32),
    )
    return jnp.where(distance < 16, distance, coarse)


def layout(counts, block_rows):
    shard_count = counts.shape[0]
    offsets = jnp.cumsum(counts, dtype=jnp.int32) - counts
    row_index = jnp.arange(shard_count * block_rows, dtype=jnp.int32)
    device = row_index // block_rows
    local_row = row_index - device * block_rows
    own_count = counts[device]
    is_prompt = local_row < own_count
    prompt_total = jnp.sum(counts, dtype=jnp.int32)
    position = jnp.where(
        is_prompt, offsets[device] + local_row, prompt_total + local_row - own_count
    )
    return (position, is_prompt, device)


def rms_norm(values, gain):
    return values * lax.rsqrt(jnp.mean(values * values, axis=-1, keepdims=True) + EPS) * gain


def matmul(left, right):
    return jnp.dot(left, right, preferred_element_type=jnp.float32)


def matmul_left(left, right):
    return lax.dot_general(
        left, right, (((0,), (0,)), ((), ())), preferred_element_type=jnp.float32
    )


def matmul_right(left, right):
    return lax.dot_general(
        left, right, (((1,), (1,)), ((), ())), preferred_element_type=jnp.float32
    )


def per_device(
    tokens,
    cotangent,
    routes,
    prompt_rows,
    w_query,
    w_key,
    w_value,
    w_output,
    w_router,
    gain_attn,
    gain_ffn,
    pos_table,
    w_in,
    w_out,
):
    shard_count = lax.axis_size("shard")
    expert_ranks = lax.axis_size("expert")
    own_index = lax.axis_index("shard")
    micro_count, tok_rows, model_width = tokens.shape
    local_experts = w_in.shape[0]
    expert_count = w_router.shape[1]
    capacity = (9 * tok_rows + 4 * expert_count - 1) // (4 * expert_count)
    head_count = HEADS
    head_size = model_width // head_count
    bucket_count = BUCKETS
    score_scale = head_size ** (-0.5)
    group_rows = shard_count * tok_rows
    slot_count = expert_ranks * capacity * local_experts
    recv_rows = expert_ranks * capacity
    bucket_ids = jnp.arange(bucket_count, dtype=jnp.int32)
    expert_ids = jnp.arange(expert_count, dtype=jnp.int32)
    gathered = (
        lax.all_gather(w_query, "shard", axis=0, tiled=True),
        lax.all_gather(w_key, "shard", axis=0, tiled=True),
        lax.all_gather(w_value, "shard", axis=0, tiled=True),
        lax.all_gather(w_output, "shard", axis=0, tiled=True),
        lax.all_gather(w_router, "shard", axis=0, tiled=True),
        lax.all_gather(gain_attn, "shard", axis=0, tiled=True),
        lax.all_gather(gain_ffn, "shard", axis=0, tiled=True),
        lax.all_gather(pos_table, "shard", axis=0, tiled=True),
    )
    full_query, full_key, full_value, full_output, full_router, gain_one, gain_two, table_flat = (
        gathered
    )
    gain_first = gain_one.astype(jnp.float32)
    gain_second = gain_two.astype(jnp.float32)
    table = table_flat.astype(jnp.float32).reshape(head_count, bucket_count)
    expert_in, expert_out = (
        lax.all_gather(w_in, "shard", axis=2, tiled=True),
        lax.all_gather(w_out, "shard", axis=1, tiled=True),
    )
    sum_query = jnp.zeros(full_query.shape, jnp.float32)
    sum_key = jnp.zeros(full_key.shape, jnp.float32)
    sum_value = jnp.zeros(full_value.shape, jnp.float32)
    sum_output = jnp.zeros(full_output.shape, jnp.float32)
    sum_router = jnp.zeros(full_router.shape, jnp.float32)
    sum_gain_one = jnp.zeros((model_width,), jnp.float32)
    sum_gain_two = jnp.zeros((model_width,), jnp.float32)
    sum_table = jnp.zeros((head_count, bucket_count), jnp.float32)
    sum_expert_in = jnp.zeros(expert_in.shape, jnp.float32)
    sum_expert_out = jnp.zeros(expert_out.shape, jnp.float32)
    mixed_parts = []
    grad_parts = []
    for micro_index in range(micro_count):
        inputs = tokens[micro_index].astype(jnp.float32)
        counts = prompt_rows[micro_index, 0]
        pos_all, prompt_all, device_all = layout(counts, tok_rows)
        query_pos = lax.dynamic_slice_in_dim(pos_all, own_index * tok_rows, tok_rows)
        hidden = rms_norm(inputs, gain_first).astype(jnp.bfloat16)
        query = matmul(hidden, full_query).astype(jnp.bfloat16)
        key = matmul(hidden, full_key).astype(jnp.bfloat16)
        value = matmul(hidden, full_value).astype(jnp.bfloat16)
        keys_all, values_all = (
            lax.all_gather(key, "shard", axis=0, tiled=True),
            lax.all_gather(value, "shard", axis=0, tiled=True),
        )
        key_index = jnp.arange(group_rows, dtype=jnp.int32)
        key_far = jnp.zeros((group_rows,), jnp.bool_)
        key_total = keys_all.shape[0]
        key_block = math.gcd(key_total, 512)
        block_count = key_total // key_block
        key_pos = pos_all[key_index]
        key_prompt = prompt_all[key_index]
        key_device = device_all[key_index]
        key_mine = key_device == own_index
        distance = query_pos[:, None] - key_pos[None, :]
        visible = (
            (distance >= 0)
            & (key_prompt | key_mine)[None, :]
            & jnp.logical_not(key_far & key_mine)[None, :]
        )
        bucket_all = distance_bucket(jnp.maximum(distance, 0))
        bucket_blocks = bucket_all.reshape(tok_rows, block_count, key_block).transpose(1, 0, 2)
        visible_blocks = visible.reshape(tok_rows, block_count, key_block).transpose(1, 0, 2)
        query_heads = query.reshape(tok_rows, head_count, head_size)
        key_blocks = keys_all.reshape(block_count, key_block, head_count, head_size)
        value_blocks = values_all.reshape(block_count, key_block, head_count, head_size)

        def make_bias(unused, block_item):
            bucket_piece, visible_piece = block_item
            bucket_hits = (bucket_piece[:, :, None] == bucket_ids).astype(jnp.float32)
            bias = jnp.einsum("qkb,hb->hqk", bucket_hits, table, precision=HIGHEST)
            return (unused, jnp.where(visible_piece[None], bias, MASKED))

        _, bias_blocks = lax.scan(
            make_bias, jnp.zeros((), jnp.float32), (bucket_blocks, visible_blocks)
        )

        def score_piece(key_piece, bias_piece):
            raw = jnp.einsum(
                "qhd,khd->hqk", query_heads, key_piece, preferred_element_type=jnp.float32
            )
            return raw * score_scale + bias_piece

        def running(state_pair, block_item):
            running_max, running_sum = state_pair
            key_piece, bias_piece = block_item
            scores = score_piece(key_piece, bias_piece)
            new_max = jnp.maximum(running_max, jnp.max(scores, axis=-1))
            running_sum = running_sum * jnp.exp(running_max - new_max) + jnp.sum(
                jnp.exp(scores - new_max[:, :, None]), axis=-1
            )
            return ((new_max, running_sum), None)

        start_pair = (
            jnp.full((head_count, tok_rows), MASKED, jnp.float32),
            jnp.zeros((head_count, tok_rows), jnp.float32),
        )
        (running_max, running_sum), _ = lax.scan(running, start_pair, (key_blocks, bias_blocks))
        log_total = running_max + jnp.log(running_sum)

        def gather_context(context_sum, block_item):
            key_piece, value_piece, bias_piece = block_item
            weights_low = jnp.exp(
                score_piece(key_piece, bias_piece) - log_total[:, :, None]
            ).astype(jnp.bfloat16)
            return (
                context_sum
                + jnp.einsum(
                    "hqk,khd->qhd", weights_low, value_piece, preferred_element_type=jnp.float32
                ),
                None,
            )

        context, _ = lax.scan(
            gather_context,
            jnp.zeros((tok_rows, head_count, head_size), jnp.float32),
            (key_blocks, value_blocks, bias_blocks),
        )
        context_low = context.reshape(tok_rows, model_width).astype(jnp.bfloat16)
        middle = inputs + matmul(context_low, full_output)
        normed = rms_norm(middle, gain_second).astype(jnp.bfloat16)
        logits = matmul(normed, full_router)
        chosen = routes[micro_index]
        pick_table = (chosen[:, :, None] == expert_ids).astype(jnp.float32)
        picked = jnp.sum(pick_table * logits[:, None, :], axis=-1)
        gate_weights = jax.nn.softmax(picked, axis=-1)
        flat_routes = chosen.reshape(-1)
        expert_hits = (flat_routes[:, None] == expert_ids).astype(jnp.int32)
        expert_rank = (
            jnp.sum(
                jnp.cumsum(expert_hits, axis=0, dtype=jnp.int32) * expert_hits,
                axis=1,
                dtype=jnp.int32,
            )
            - 1
        )
        slot_index = (
            flat_routes // local_experts * (capacity * local_experts)
            + expert_rank * local_experts
            + flat_routes % local_experts
        )
        slot_owner = (
            jnp.full((slot_count,), 2 * tok_rows, jnp.int32)
            .at[slot_index]
            .set(jnp.arange(2 * tok_rows, dtype=jnp.int32))
        )
        padded = jnp.concatenate([normed, jnp.zeros((1, model_width), jnp.bfloat16)], axis=0)
        outgoing = padded[slot_owner // 2].reshape(
            expert_ranks, capacity, local_experts, model_width
        )
        received = lax.all_to_all(
            outgoing, "expert", split_axis=0, concat_axis=0, tiled=True
        ).reshape(recv_rows, local_experts, model_width)
        pre_act = jnp.einsum(
            "red,edf->ref", received, expert_in, preferred_element_type=jnp.float32
        )
        activation = jax.nn.gelu(pre_act).astype(jnp.bfloat16)
        expert_result = jnp.einsum(
            "ref,efd->red", activation, expert_out, preferred_element_type=jnp.float32
        )
        result_low = expert_result.astype(jnp.bfloat16).reshape(
            expert_ranks, capacity, local_experts, model_width
        )
        returned = lax.all_to_all(
            result_low, "expert", split_axis=0, concat_axis=0, tiled=True
        ).reshape(slot_count, model_width)
        picked_rows = returned[slot_index].astype(jnp.float32).reshape(tok_rows, 2, model_width)
        output_rows = middle + jnp.sum(gate_weights[:, :, None] * picked_rows, axis=1)
        mixed_parts.append(output_rows.astype(jnp.bfloat16))
        grad_output = cotangent[micro_index].astype(jnp.float32)
        grad_gate = jnp.sum(grad_output[:, None, :] * picked_rows, axis=-1)
        grad_pick = gate_weights * (
            grad_gate - jnp.sum(gate_weights * grad_gate, axis=-1, keepdims=True)
        )
        grad_logits = jnp.sum(pick_table * grad_pick[:, :, None], axis=1).astype(jnp.bfloat16)
        sum_router = sum_router + matmul_left(normed, grad_logits)
        grad_normed = matmul_right(grad_logits, full_router)
        branch_grad = (gate_weights[:, :, None] * grad_output[:, None, :]).reshape(
            2 * tok_rows, model_width
        )
        padded_grad = jnp.concatenate(
            [branch_grad, jnp.zeros((1, model_width), jnp.float32)], axis=0
        )
        grad_send = (
            padded_grad[slot_owner]
            .astype(jnp.bfloat16)
            .reshape(expert_ranks, capacity, local_experts, model_width)
        )
        grad_recv = lax.all_to_all(
            grad_send, "expert", split_axis=0, concat_axis=0, tiled=True
        ).reshape(recv_rows, local_experts, model_width)
        grad_act = jnp.einsum(
            "red,efd->ref", grad_recv, expert_out, preferred_element_type=jnp.float32
        )
        sum_expert_out = sum_expert_out + jnp.einsum(
            "ref,red->efd", activation, grad_recv, preferred_element_type=jnp.float32
        )
        _, gelu_pull = jax.vjp(jax.nn.gelu, pre_act)
        grad_pre = gelu_pull(grad_act)[0].astype(jnp.bfloat16)
        sum_expert_in = sum_expert_in + jnp.einsum(
            "red,ref->edf", received, grad_pre, preferred_element_type=jnp.float32
        )
        grad_in_rows = jnp.einsum(
            "ref,edf->red", grad_pre, expert_in, preferred_element_type=jnp.float32
        )
        grad_in_low = grad_in_rows.astype(jnp.bfloat16).reshape(
            expert_ranks, capacity, local_experts, model_width
        )
        grad_back = lax.all_to_all(
            grad_in_low, "expert", split_axis=0, concat_axis=0, tiled=True
        ).reshape(slot_count, model_width)
        grad_normed = grad_normed + jnp.sum(
            grad_back[slot_index].astype(jnp.float32).reshape(tok_rows, 2, model_width), axis=1
        )
        _, norm_pull = jax.vjp(rms_norm, middle, gain_second)
        grad_middle, grad_gain_second = norm_pull(grad_normed)
        grad_middle = grad_middle + grad_output
        sum_gain_two = sum_gain_two + grad_gain_second
        grad_attn = grad_middle.astype(jnp.bfloat16)
        sum_output = sum_output + matmul_left(context_low, grad_attn)
        grad_context = (
            matmul_right(grad_attn, full_output)
            .astype(jnp.bfloat16)
            .reshape(tok_rows, head_count, head_size)
        )
        row_delta = jnp.einsum("qhd,qhd->hq", grad_context.astype(jnp.float32), context)

        def attend_back(state_pair, block_item):
            grad_query_sum, grad_table_sum = state_pair
            key_piece, value_piece, bias_piece, bucket_piece = block_item
            probs = jnp.exp(score_piece(key_piece, bias_piece) - log_total[:, :, None])
            grad_probs = jnp.einsum(
                "qhd,khd->hqk", grad_context, value_piece, preferred_element_type=jnp.float32
            )
            grad_scores = probs * (grad_probs - row_delta[:, :, None])
            bucket_hits = (bucket_piece[:, :, None] == bucket_ids).astype(jnp.float32)
            grad_table_sum = grad_table_sum + jnp.einsum(
                "hqk,qkb->hb", grad_scores, bucket_hits, precision=HIGHEST
            )
            grad_raw = (grad_scores * score_scale).astype(jnp.bfloat16)
            grad_query_sum = grad_query_sum + jnp.einsum(
                "hqk,khd->qhd", grad_raw, key_piece, preferred_element_type=jnp.float32
            )
            grad_key_piece = jnp.einsum(
                "hqk,qhd->khd", grad_raw, query_heads, preferred_element_type=jnp.float32
            )
            grad_value_piece = jnp.einsum(
                "hqk,qhd->khd",
                probs.astype(jnp.bfloat16),
                grad_context,
                preferred_element_type=jnp.float32,
            )
            return ((grad_query_sum, grad_table_sum), (grad_key_piece, grad_value_piece))

        back_start = (
            jnp.zeros((tok_rows, head_count, head_size), jnp.float32),
            jnp.zeros((head_count, bucket_count), jnp.float32),
        )
        (grad_query_all, grad_table_all), (grad_key_blocks, grad_value_blocks) = lax.scan(
            attend_back, back_start, (key_blocks, value_blocks, bias_blocks, bucket_blocks)
        )
        sum_table = sum_table + grad_table_all
        key_grad_rows = grad_key_blocks.reshape(key_total, model_width)
        value_grad_rows = grad_value_blocks.reshape(key_total, model_width)
        own_key_grad, own_value_grad = (
            lax.psum_scatter(
                key_grad_rows.astype(jnp.bfloat16), "shard", scatter_dimension=0, tiled=True
            ).astype(jnp.float32),
            lax.psum_scatter(
                value_grad_rows.astype(jnp.bfloat16), "shard", scatter_dimension=0, tiled=True
            ).astype(jnp.float32),
        )
        grad_query_low = grad_query_all.reshape(tok_rows, model_width).astype(jnp.bfloat16)
        grad_key_low = own_key_grad.astype(jnp.bfloat16)
        grad_value_low = own_value_grad.astype(jnp.bfloat16)
        sum_query = sum_query + matmul_left(hidden, grad_query_low)
        sum_key = sum_key + matmul_left(hidden, grad_key_low)
        sum_value = sum_value + matmul_left(hidden, grad_value_low)
        grad_hidden = (
            matmul_right(grad_query_low, full_query)
            + matmul_right(grad_key_low, full_key)
            + matmul_right(grad_value_low, full_value)
        )
        _, first_pull = jax.vjp(rms_norm, inputs, gain_first)
        grad_inputs, grad_gain_first = first_pull(grad_hidden)
        sum_gain_one = sum_gain_one + grad_gain_first
        grad_parts.append(grad_inputs + grad_middle)
    shares = (
        lax.psum_scatter(
            sum_query.astype(jnp.bfloat16), "shard", scatter_dimension=0, tiled=True
        ).astype(jnp.float32),
        lax.psum_scatter(
            sum_key.astype(jnp.bfloat16), "shard", scatter_dimension=0, tiled=True
        ).astype(jnp.float32),
        lax.psum_scatter(
            sum_value.astype(jnp.bfloat16), "shard", scatter_dimension=0, tiled=True
        ).astype(jnp.float32),
        lax.psum_scatter(
            sum_output.astype(jnp.bfloat16), "shard", scatter_dimension=0, tiled=True
        ).astype(jnp.float32),
        lax.psum_scatter(
            sum_router.astype(jnp.bfloat16), "shard", scatter_dimension=0, tiled=True
        ).astype(jnp.float32),
        lax.psum_scatter(
            sum_gain_one.astype(jnp.bfloat16), "shard", scatter_dimension=0, tiled=True
        ).astype(jnp.float32),
        lax.psum_scatter(
            sum_gain_two.astype(jnp.bfloat16), "shard", scatter_dimension=0, tiled=True
        ).astype(jnp.float32),
        lax.psum_scatter(
            sum_table.reshape(-1).astype(jnp.bfloat16), "shard", scatter_dimension=0, tiled=True
        ).astype(jnp.float32),
    )
    own_grads = (
        lax.psum(shares[0].astype(jnp.bfloat16), "expert").astype(jnp.float32),
        lax.psum(shares[1].astype(jnp.bfloat16), "expert").astype(jnp.float32),
        lax.psum(shares[2].astype(jnp.bfloat16), "expert").astype(jnp.float32),
        lax.psum(shares[3].astype(jnp.bfloat16), "expert").astype(jnp.float32),
        lax.psum(shares[4].astype(jnp.bfloat16), "expert").astype(jnp.float32),
        lax.psum(shares[5].astype(jnp.bfloat16), "expert").astype(jnp.float32),
        lax.psum(shares[6].astype(jnp.bfloat16), "expert").astype(jnp.float32),
        lax.psum(shares[7].astype(jnp.bfloat16), "expert").astype(jnp.float32),
    )
    grad_expert_in, grad_expert_out = (
        lax.psum_scatter(
            sum_expert_in.astype(jnp.bfloat16), "shard", scatter_dimension=2, tiled=True
        ).astype(jnp.float32),
        lax.psum_scatter(
            sum_expert_out.astype(jnp.bfloat16), "shard", scatter_dimension=1, tiled=True
        ).astype(jnp.float32),
    )
    return (
        jnp.stack(mixed_parts),
        jnp.stack(grad_parts),
        own_grads[0],
        own_grads[1],
        own_grads[2],
        own_grads[3],
        own_grads[4],
        own_grads[5],
        own_grads[6],
        own_grads[7],
        grad_expert_in,
        grad_expert_out,
    )


def solution(mesh):
    in_specs = (
        P(None, ("expert", "shard"), None),
        P(None, ("expert", "shard"), None),
        P(None, ("expert", "shard"), None),
        P(None, "expert", None),
        P("shard", None),
        P("shard", None),
        P("shard", None),
        P("shard", None),
        P("shard", None),
        P("shard"),
        P("shard"),
        P("shard"),
        P("expert", None, "shard"),
        P("expert", "shard", None),
    )
    out_specs = (
        P(None, ("expert", "shard"), None),
        P(None, ("expert", "shard"), None),
        P("shard", None),
        P("shard", None),
        P("shard", None),
        P("shard", None),
        P("shard", None),
        P("shard"),
        P("shard"),
        P("shard"),
        P("expert", None, "shard"),
        P("expert", "shard", None),
    )
    ne, ns = mesh.shape["expert"], mesh.shape["shard"]

    def device(*args):
        tokens, w_router, w_in = args[0], args[8], args[12]
        z = Sizes(
            ne, ns, tokens.shape[0], tokens.shape[1], tokens.shape[2], w_router.shape[1], w_in.shape[0], w_in.shape[2]
        )
        return fused_device(z, *args) if z.fits() else per_device(*args)

    return jax.shard_map(
        device, mesh=mesh, in_specs=in_specs, out_specs=out_specs, check_vma=False
    )
```

```python
import functools
from functools import reduce
import math

import jax
import jax.numpy as jnp
import numpy as np
from jax import lax
from jax.experimental import pallas as pl
from jax.experimental.pallas import tpu as pltpu
from jax.sharding import PartitionSpec as P

HEADS = 12
BUCKETS = 32
EPS = 1e-06
MASKED = -1e30
BUCKET_EDGES = (24, 32, 48, 64, 96, 128, 192, 256, 384, 512, 768, 1024, 1536, 2048, 3072)
MESH = pl.DeviceIdType.MESH
BF = jnp.bfloat16
F32 = jnp.float32
I32 = jnp.int32
LANES = 128


class Sizes:
    def __init__(self, ne, ns, micro, rows, width, experts, local_experts, ff):
        self.ne, self.ns, self.ny = ne, ns, ns // 2
        self.m, self.t, self.d = micro, rows, width
        self.e, self.el, self.ff = experts, local_experts, ff
        self.g = ns * rows
        self.mt = micro * rows
        self.r = width // ns
        self.cap = (9 * rows + 4 * experts - 1) // (4 * experts)
        self.per = micro * self.cap
        self.sp = -(-(local_experts * self.per + 2) // 16) * 16
        self.slots = ne * self.sp
        self.nz = ne // 2
        self.hn = ne // 2
        self.cr = self.hn * self.per
        self.cb = local_experts * self.cr
        self.blk = 2 * self.cb
        self.hs = self.hn * self.sp
        self.n16 = -(-ne // 16) * 16
        self.pairs = HEADS // 2
        self.small = experts + 16
        self.far = self.g // 2 + rows

    def fits(self):
        return (
            self.ns % 2 == 0
            and self.t == LANES
            and self.d == HEADS * 64
            and self.cr % 16 == 0
            and self.ne % 4 == 0
            and self.e % 16 == 0
            and self.r % (16 * self.nz) == 0
            and self.slots % LANES == 0
            and self.el * self.per <= LANES
            and self.d == self.ff
            and self.ns >= 2 * self.m
            and self.blk >= self.g
            and self.d % 256 == 0
        )


def layout_constants(z):
    perm = np.zeros((z.cb, z.hs), np.float32)
    rows_of = np.zeros((2 * z.n16, z.slots), np.float32)
    dest = np.zeros((2 * z.n16, z.slots), np.float32)
    place = np.zeros((z.slots, LANES), np.float32)
    gate_of = np.zeros((2 * z.n16, z.hs), np.float32)
    source = np.zeros((z.cb, 2 * z.n16), np.float32)
    pick = np.zeros((z.cb, LANES), np.float32)
    used = z.el * z.per
    for src in range(z.ne):
        rows_of[src, src * z.sp + used] = 1
        rows_of[z.n16 + src, src * z.sp + used + 1] = 1
        dest[src, src * z.sp : (src + 1) * z.sp] = 1
        dest[z.n16 + src, src * z.sp : (src + 1) * z.sp] = 1
        for q in range(used):
            place[src * z.sp + q, q] = 1
    for src in range(z.hn):
        gate_of[src, src * z.sp + used] = 1
        gate_of[z.n16 + src, src * z.sp + used + 1] = 1
        for q in range(used):
            row = (q // z.per) * z.cr + src * z.per + q % z.per
            perm[row, src * z.sp + q] = 1
            source[row, src] = 1
            source[row, z.n16 + src] = 1
            pick[row, q] = 1
    return [jnp.asarray(a, BF) for a in (perm, rows_of, dest, place, gate_of, source, pick)]


def dot(a, b):
    return jnp.dot(a, b, preferred_element_type=F32)


def dot_t(a, b):
    return lax.dot_general(a, b, (((1,), (1,)), ((), ())), preferred_element_type=F32)


def tdot(a, b):
    return lax.dot_general(a, b, (((0,), (0,)), ((), ())), preferred_element_type=F32)


def iota(shape, dim):
    return lax.broadcasted_iota(I32, shape, dim)


def aligned(start, size, multiple):
    return pl.ds(pl.multiple_of(start, multiple), size)


def offsets(z, chunk=None):
    every = [(kz, kx) for kz in range(z.nz) for kx in range(2)][1:]
    return [k for k in every if chunk is None or k[0] % 2 == chunk]


def position(z, k):
    return (k[0] % 2) * z.hn + (k[0] // 2) * 2 + k[1]


class Place:
    def __init__(self, z):
        self.z = z
        self.e = lax.axis_index("expert")
        self.s = lax.axis_index("shard")
        self.y, self.c = lax.div(self.s, 2), lax.rem(self.s, 2)

    def shard(self, k, other):
        y = lax.rem(self.y + k, self.z.ny)
        return y * 2 + (1 - self.c if other else self.c)

    def expert(self, kz, kx):
        high = lax.rem(lax.div(self.e, 2) + kz, self.z.nz)
        return high * 2 + lax.rem(lax.rem(self.e, 2) + kx, 2)

    def barrier(self, with_experts=True):
        sem = pltpu.get_barrier_semaphore()
        others = [(self.e, self.shard(0, True))]
        others += [(self.e, self.shard(k, False)) for k in range(1, self.z.ny)]
        if with_experts:
            others += [(self.expert(*k), self.s) for k in offsets(self.z)]
        for other in others:
            pl.semaphore_signal(sem, inc=1, device_id=other, device_id_type=MESH)
        pl.semaphore_wait(sem, len(others))


def rcopy(src, dst, send, recv, to):
    return pltpu.make_async_remote_copy(
        src_ref=src, dst_ref=dst, send_sem=send, recv_sem=recv, device_id=to, device_id_type=MESH
    )


class Gather:
    def __init__(self, place, own, full, send, recv, item):
        self.p, self.own, self.full = place, own, full
        self.send, self.recv, self.item = send, recv, item

    def copy(self, origin, src, slot, to):
        return rcopy(
            src, self.full(origin), self.send.at[self.item, slot], self.recv.at[self.item, origin], to
        )

    def partner(self):
        return (self.p.e, self.p.shard(0, True))

    def start(self):
        p, ny = self.p, self.p.z.ny
        for k in range(1, ny):
            self.copy(p.s, self.own, k, (p.e, p.shard(k, False))).start()
        self.copy(p.s, self.own, 0, self.partner()).start()

    def forward(self):
        p, ny = self.p, self.p.z.ny
        for k in range(1, ny):
            origin = p.shard(k, False)
            self.copy(origin, self.full(origin), ny + k - 1, self.partner()).wait_recv()
            self.copy(origin, self.full(origin), ny + k - 1, self.partner()).start()

    def arrive(self):
        p, ny = self.p, self.p.z.ny
        for k in range(ny):
            origin = p.shard(k, True)
            self.copy(origin, self.full(origin), 0, self.partner()).wait_recv()

    def finish(self):
        p, ny = self.p, self.p.z.ny
        for slot in range(2 * ny - 1):
            self.copy(p.s, self.own, slot, self.partner()).wait_send()


class Exchange:
    def __init__(self, place, src, dst, send, recv, item):
        self.p, self.src, self.dst = place, src, dst
        self.send, self.recv, self.item = send, recv, item

    def copy(self, k):
        z = self.p.z
        back = (-k[0] % z.nz, k[1])
        at = position(z, back)
        to = self.p.expert(*k)
        return rcopy(
            self.src(to),
            self.dst(at),
            self.send.at[self.item, position(z, k)],
            self.recv.at[self.item, at],
            (to, self.p.s),
        )

    def start(self, chunk=None):
        for k in offsets(self.p.z, chunk):
            self.copy(k).start()

    def arrive(self, chunk=None):
        z = self.p.z
        for k in offsets(z, chunk):
            self.copy((-k[0] % z.nz, k[1])).wait_recv()

    def finish(self):
        for k in offsets(self.p.z):
            self.copy(k).wait_send()


def slot_ids(z, route0, route1):
    lane = iota((z.t, LANES), 1)
    lower = (iota((z.t, z.t), 0) > iota((z.t, z.t), 1)).astype(F32).astype(BF)
    base = lane * z.per
    for d in range(1, z.ne):
        base = base + jnp.where(lane >= d * z.el, z.sp - z.el * z.per, 0)
    firsts, seconds = [], []
    for m in range(z.m):
        rows = slice(m * z.t, (m + 1) * z.t)
        hit0, hit1 = lane == route0[rows], lane == route1[rows]
        hits = jnp.where(hit0 | hit1, 1.0, 0.0).astype(BF)
        spot = dot(lower, hits) + (base + m * z.cap).astype(F32)
        firsts.append(jnp.sum(jnp.where(hit0, spot, 0.0), axis=1, keepdims=True))
        seconds.append(jnp.sum(jnp.where(hit1, spot, 0.0), axis=1, keepdims=True))
    return jnp.concatenate(firsts, 0), jnp.concatenate(seconds, 0)


def one_hot(z, slot):
    return (iota((z.mt, z.slots), 1) == slot.astype(I32)).astype(F32)


def key_layout(z, counts, m, shape, dim):
    row = iota(shape, dim)
    total = counts[m, 0]
    for b in range(1, z.ns):
        total = total + counts[m, b]
    position = jnp.zeros(shape, I32)
    prompt = jnp.zeros(shape, I32)
    offset = 0
    for b in range(z.ns):
        own = counts[m, b]
        local = row - b * z.t
        inside = (local >= 0) & (local < z.t)
        first = local < own
        position = jnp.where(inside, jnp.where(first, offset + local, total + local - own), position)
        prompt = jnp.where(inside & first, 1, prompt)
        offset = offset + own
    return position, prompt


def query_position(z, counts, m, s):
    total, offset, own = 0, 0, 0
    for b in range(z.ns):
        count = counts[m, b]
        total = total + count
        offset = offset + jnp.where(b < s, count, 0)
        own = own + jnp.where(b == s, count, 0)
    local = iota((z.t, 1), 0)
    return jnp.where(local < own, offset + local, total + local - own)


def bucket_of(z, distance):
    coarse = jnp.full(distance.shape, 16, I32)
    for edge in BUCKET_EDGES:
        if edge < z.far:
            coarse = coarse + jnp.where(distance >= edge, 1, 0)
    return jnp.where(distance < 16, distance, coarse)


VMEM = pl.BlockSpec(memory_space=pltpu.VMEM)
SMEM = pl.BlockSpec(memory_space=pltpu.SMEM)


GELU_A = math.sqrt(2.0 / math.pi)
GELU_B = 0.044715


class Scatter:
    def __init__(self, place, mine, other, from_core, to_y, from_y, psend, precv, ysend, yrecv):
        self.p, self.mine, self.other, self.from_core = place, mine, other, from_core
        self.to_y, self.from_y = to_y, from_y
        self.psend, self.precv, self.ysend, self.yrecv = psend, precv, ysend, yrecv

    def core_copy(self):
        p = self.p
        return rcopy(self.other, self.from_core, self.psend, self.precv, (p.e, p.shard(0, True)))

    def y_copy(self, k):
        p = self.p
        return rcopy(
            self.to_y.at[k - 1], self.from_y.at[k - 1], self.ysend.at[k - 1], self.yrecv.at[k - 1],
            (p.e, p.shard(k, False)),
        )

    def send(self):
        self.core_copy().start()

    def middle(self):
        p = self.p
        self.core_copy().wait_recv()
        for k in range(1, p.z.ny):
            yy = lax.rem(p.y + k, p.z.ny)
            both = self.mine[yy].astype(F32) + self.from_core[yy].astype(F32)
            self.to_y[k - 1] = both.astype(BF)
            self.y_copy(k).start()

    def total(self):
        p = self.p
        out = self.mine[p.y].astype(F32) + self.from_core[p.y].astype(F32)
        for k in range(1, p.z.ny):
            self.y_copy(k).wait_recv()
            out = out + self.from_y[k - 1].astype(F32)
        return out

    def finish(self):
        self.core_copy().wait_send()
        for k in range(1, self.p.z.ny):
            self.y_copy(k).wait_send()


class Return:
    def __init__(self, place, rows, ret, chunk, cols, send, recv):
        self.p, self.rows, self.ret, self.chunk, self.cols = place, rows, ret, chunk, cols
        self.sems = send, recv

    def copy(self, k, at, away):
        z = self.p.z
        first = self.chunk * z.hn
        return rcopy(
            self.rows.at[pl.ds((position(z, k) - first) * z.sp, z.sp)],
            self.ret.at[aligned(at * z.sp, z.sp, 16), self.cols],
            self.sems[0].at[position(z, k) - first],
            self.sems[1].at[position(z, away) - first],
            (self.p.expert(*k), self.p.s),
        )

    def start_remote(self):
        z = self.p.z
        for k in offsets(z, self.chunk):
            self.copy(k, self.p.e, (-k[0] % z.nz, k[1])).start()

    def start(self):
        z = self.p.z
        self.start_remote()
        if self.chunk == 0:
            self.ret[aligned(self.p.e * z.sp, z.sp, 16), self.cols] = self.rows[0 : z.sp, :]

    def arrive(self):
        for k in offsets(self.p.z, self.chunk):
            self.copy(k, self.p.expert(*k), k).wait_recv()

    def finish(self):
        z = self.p.z
        for k in offsets(z, self.chunk):
            self.copy(k, self.p.e, (-k[0] % z.nz, k[1])).wait_send()


def column_of(row):
    n = row.shape[1]
    return jnp.sum(jnp.where(iota((n, n), 0) == iota((n, n), 1), row, 0.0), axis=1, keepdims=True)


def route_columns(z, routes):
    out = []
    for j in range(2):
        parts = [column_of(routes[m, j : j + 1, :].astype(F32)) for m in range(z.m)]
        out.append(jnp.concatenate(parts, 0).astype(I32))
    return out


def spread(z, s, n):
    row, lane = iota((z.r, z.d), 0), iota((z.r, z.d), 1)
    return jnp.where((lane - s * n == row) & (row < n), 1.0, 0.0).astype(BF)


def split_high(x):
    high = x.astype(BF)
    return high, (x - high.astype(F32)).astype(BF)


def forward_kernel(
    z,
    tokens, dy, routes, counts, wk, wv, wq, wo, wr, vecs, w_in_hbm, w_out_hbm,
    perm, rows_of, dest, place_m, gate_of, source, pick,
    o_toks, o_hid, o_kk, o_vv, o_qq, o_pp, o_ctx, o_mid, o_nrm, o_sd, o_fk, o_fv, o_fq, o_fo, o_small,
    o_ret, o_rfin, ggrows, din, dout,
    qq, pp, ctx, mid, nrm, sd, fk, fv, fq, fo, small, smallg,
    xs, dyr, xr, dyg, xg, act, gp, w_in, w_out, table, bias_id, bias_mask, gwg, gwc, ggc,
    part, rp, ys, yr, fin, ret, rpart, rrp, rys, ryr, wstage, gpart, grp, gys, gyr, gout, gret,
    csem, ssem, gsend, grecv, xsend, xrecv, psend, precv, ysend, yrecv, rsend, rrecv, gsem,
):
    p = Place(z)
    mt, t, d, r, ff = z.mt, z.t, z.d, z.r, z.ff
    half = d // 2
    tiles = ff // 256
    load_in = pltpu.make_async_copy(w_in_hbm, w_in, csem.at[0])
    load_out = pltpu.make_async_copy(w_out_hbm, w_out, csem.at[1])
    spills, waiting = [], {}

    def spill(src, dst, before=None):
        copy = pltpu.make_async_copy(src, dst, ssem.at[len(spills)])
        copy.start()
        spills.append(copy)
        waiting.setdefault(before, []).append(copy)

    toks, hid = gp.at[pl.ds(0, z.m), pl.ds(0, z.g)], gp.at[pl.ds(z.m, z.m), pl.ds(0, z.g)]
    kk, vv = act.at[pl.ds(0, z.m), pl.ds(0, z.g)], act.at[pl.ds(z.m, z.m), pl.ds(0, z.g)]

    whole = spread(z, p.s, r)
    line = iota((16, d), 0)
    tail = dot(vecs[...], whole)
    bias_row = dot(vecs[...], spread(z, p.s, HEADS * BUCKETS // z.ns))
    tail = jnp.where(line < 2, tail, jnp.where(line == 2, bias_row, 0.0))
    small[0 : z.e, :] = dot(wr[...], whole).astype(BF)
    small[z.e : z.small, :] = tail.astype(BF)
    p.barrier()

    def rows(ref, size):
        return lambda origin: ref.at[aligned(origin * size, size, 16)]

    g_small = Gather(p, small, lambda o: smallg.at[o], gsend, grecv, 0)
    g_tok = [
        Gather(p, tokens.at[m], lambda o, m=m: toks.at[m, aligned(o * t, t, 16)], gsend, grecv, 1 + m)
        for m in range(z.m)
    ]
    base = 1 + z.m
    groups = d // 256

    def columns_item(own, full, g, item):
        cols = pl.ds(g * 256, 256)
        return Gather(
            p, own.at[:, cols], lambda o: full.at[aligned(o * r, r, 16), cols], gsend, grecv, item
        )

    g_w = [
        [columns_item(own, full, g, base + 3 * g + i) for i, (own, full) in enumerate(((wk, fk), (wv, fv), (wq, fq)))]
        for g in range(groups)
    ]
    base = base + 3 * groups
    g_o = Gather(p, wo, rows(fo, r), gsend, grecv, base)
    base = base + 1
    for item in [g_small] + g_tok + sum(g_w, []) + [g_o]:
        item.start()
    load_out.start()
    load_in.start()
    g_dy = Gather(p, dyg.at[p.s], lambda o: dyg.at[o], gsend, grecv, base)

    def exchange(dst, item):
        return Exchange(
            p,
            lambda to: xs.at[aligned(to * z.sp, z.sp, 16)],
            lambda at: dst.at[pl.ds(at * z.sp, z.sp)],
            xsend,
            xrecv,
            item,
        )

    x_dy, x_move = exchange(dyr, 0), exchange(xr, 1)
    smallg[p.s] = small[...]
    for m in range(z.m):
        toks[m, aligned(p.s * t, t, 16), :] = tokens[m]
    own_weights = []
    for i, (own, full) in enumerate(((wk, fk), (wv, fv), (wq, fq), (wo, fo))):
        own_weights.append(pltpu.make_async_copy(own, full.at[aligned(p.s * r, r, 16)], csem.at[6 + i]))
        own_weights[i].start()

    route0, route1 = route_columns(z, routes)
    slot0, slot1 = slot_ids(z, route0, route1)
    hot = (one_hot(z, slot0) + one_hot(z, slot1)).astype(BF)
    mine = aligned(p.e * z.sp, z.sp, 16)

    def to_slots(ref):
        def step(i, carry):
            cols = aligned(i * 256, 256, 256)
            xs[:, cols] = tdot(hot, ref[:, cols]).astype(BF)
            return carry

        lax.fori_loop(0, d // 256, step, 0)

    to_slots(dy)
    x_dy.start()
    dyr[0 : z.sp, :] = xs[mine, :]

    for m in range(z.m):
        key_pos, prompt = key_layout(z, counts, m, (1, z.g), 1)
        distance = query_position(z, counts, m, p.s) - key_pos
        lane = iota((1, z.g), 1)
        own_block = (lane >= p.s * t) & (lane < (p.s + 1) * t)
        visible = (distance >= 0) & (own_block | (prompt == 1))
        bias_id[m] = jnp.where(visible, bucket_of(z, distance), 0)
        bias_mask[m] = jnp.where(visible, 0.0, MASKED)

    for item in [g_small] + g_tok:
        item.forward()
    for item in [g_small] + g_tok:
        item.arrive()
    spill(smallg, o_small)
    spill(toks, o_toks, "gp")
    sums = smallg[0].astype(F32)
    for b in range(1, z.ns):
        sums = sums + smallg[b].astype(F32)
    gain_one = sums[z.e : z.e + 1, :]
    gain_two = sums[z.e + 1 : z.e + 2, :]
    router = sums.astype(BF)
    table[...] = jnp.broadcast_to(sums[z.e + 2 : z.e + 3, : HEADS * BUCKETS], table.shape)

    def norm(i, carry):
        m, at = lax.div(i, z.ns), aligned(lax.rem(i, z.ns) * t, t, 16)
        x = toks[m, at, :].astype(F32)
        scale = lax.rsqrt(jnp.mean(x * x, axis=1, keepdims=True) + EPS)
        hid[m, at, :] = (x * scale * gain_one).astype(BF)
        return carry

    lax.fori_loop(0, z.m * z.ns, norm, 0)
    spill(hid, o_hid, "gp")

    for copy in own_weights:
        copy.wait()

    def project(g):
        for item in g_w[g]:
            item.forward()
        cols = slice(g * 256, (g + 1) * 256)
        for item, full, out in zip(g_w[g][:2], (fk, fv), (kk, vv)):
            item.arrive()
            out[:, :, cols] = dot(hid[...].reshape(z.m * z.g, d), full[:, cols]).astype(BF).reshape(z.m, z.g, 256)
        g_w[g][2].arrive()
        own = jnp.concatenate([hid[m, aligned(p.s * t, t, 16), :] for m in range(z.m)], 0)
        qq[:, cols] = (dot(own, fq[:, cols]).astype(BF).astype(F32) * 0.125).astype(BF)


    def in_order(src, dst, h):
        def step(i, carry):
            cols = aligned(i * 256, 256, 256)
            moved = dot(perm[...], src[h * z.hs : (h + 1) * z.hs, cols])
            dst[p.s, h * z.cb : (h + 1) * z.cb, cols] = moved.astype(BF)
            return carry

        lax.fori_loop(0, d // 256, step, 0)

    def send_dy_rows():
        x_dy.arrive()
        in_order(dyr, dyg, 0)
        in_order(dyr, dyg, 1)
        g_dy.start()

    low = iota((t, LANES), 1) < 64

    def attend(i, g):
        m, pair = lax.rem(i, z.m), g * 2 + lax.div(i, z.m)
        spot = m * z.pairs + pair
        cols = aligned(pair * LANES, LANES, LANES)
        q = qq[aligned(m * t, t, 16), cols]
        zero = jnp.zeros_like(q)
        q_two = jnp.concatenate([jnp.where(low, q, zero), jnp.where(low, zero, q)], 0)
        scores = dot_t(q_two, kk[m, :, cols])
        biases = table[0:1, aligned(lax.div(pair, 2) * LANES, LANES, LANES)]
        biases = jnp.broadcast_to(biases, (t, LANES))
        shift = lax.rem(pair, 2) * 64
        for side in range(2):
            pieces = []
            for b in range(z.ns):
                at = slice(b * LANES, (b + 1) * LANES)
                bias = jnp.take_along_axis(biases, bias_id[m, :, at] + (shift + 32 * side), axis=1)
                pieces.append(scores[side * t : (side + 1) * t, at] + (bias + bias_mask[m, :, at]))
            s = jnp.concatenate(pieces, 1)
            top = jnp.max(s, axis=1, keepdims=True)
            e = jnp.exp(s - top)
            total = jnp.sum(e, axis=1, keepdims=True)
            pp[spot, side * t : (side + 1) * t, :] = (e * (1.0 / total)).astype(BF)
        two = dot(pp[spot], vv[m, :, cols])
        ctx[aligned(m * t, t, 16), cols] = jnp.where(low, two[:t], two[t:]).astype(BF)
        return g

    for g in range(groups):
        project(g)
        if g == groups - 1:
            for full, dst in ((fk, o_fk), (fv, o_fv), (fq, o_fq), (qq, o_qq)):
                spill(full, dst)
            spill(kk, o_kk, "act")
            spill(vv, o_vv, "act")
            g_o.forward()
        lax.fori_loop(0, 2 * z.m, attend, g, unroll=2)
        if g == groups - 2:
            send_dy_rows()
    spill(pp, o_pp)
    spill(ctx, o_ctx)
    g_o.arrive()
    spill(fo, o_fo)

    def output(i, carry):
        cols = aligned(i * 256, 256, 256)
        mid[:, cols] = dot(ctx[...], fo[:, cols])
        return carry

    lax.fori_loop(0, d // 256, output, 0)
    for m in range(z.m):
        at = slice(m * t, (m + 1) * t)
        x = mid[at, :] + tokens[m].astype(F32)
        mid[at, :] = x
        scale = lax.rsqrt(jnp.mean(x * x, axis=1, keepdims=True) + EPS)
        nrm[at, :] = (x * scale * gain_two).astype(BF)
    spill(mid, o_mid)
    spill(nrm, o_nrm)
    logits = dot_t(nrm[...], router)
    lane = iota((mt, z.small), 1)
    pick0 = jnp.sum(jnp.where(lane == route0, logits, 0.0), axis=1, keepdims=True)
    pick1 = jnp.sum(jnp.where(lane == route1, logits, 0.0), axis=1, keepdims=True)
    top = jnp.maximum(pick0, pick1)
    e0, e1 = jnp.exp(pick0 - top), jnp.exp(pick1 - top)
    gate0, gate1 = e0 / (e0 + e1), e1 / (e0 + e1)
    lane = iota((mt, LANES), 1)
    sd[...] = jnp.where(
        lane == 0, slot0, jnp.where(lane == 1, slot1, jnp.where(lane == 2, gate0, jnp.where(lane == 3, gate1, 0.0)))
    )
    spill(sd, o_sd)
    gate_row = jnp.sum(one_hot(z, slot0) * gate0 + one_hot(z, slot1) * gate1, axis=0, keepdims=True)
    high = gate_row.astype(BF).astype(F32)
    is_high = iota((2 * z.n16, 1), 0) < z.n16
    gates = (dest[...].astype(F32) * jnp.where(is_high, high, gate_row - high)).astype(BF)
    gates = dot(gates, place_m[...]).astype(BF)
    x_dy.finish()
    to_slots(nrm)
    xs[:, :LANES] = (xs[:, :LANES].astype(F32) + tdot(rows_of[...], gates)).astype(BF)
    x_move.start(0)
    x_move.start(1)
    xr[0 : z.sp, :] = xs[mine, :]

    g_dy.forward()
    g_dy.arrive()
    load_out.wait()

    def expert_rows(ref, h, l, cols):
        return ref[:, aligned(h * z.cb + l * z.cr, z.cr, 16), cols].reshape(z.ns * z.cr, -1)

    def gradient(h):
        def step(i, carry):
            l, at = lax.div(i, tiles), aligned(lax.rem(i, tiles) * 256, 256, 256)
            g = dot_t(expert_rows(dyg, h, l, slice(None)), w_out[l, at, :])
            gp[:, aligned(h * z.cb + l * z.cr, z.cr, 16), at] = g.astype(BF).reshape(z.ns, z.cr, 256)
            return carry

        lax.fori_loop(0, z.el * tiles, step, 0)

    def gather_of(h):
        at = pl.ds(h * z.cb, z.cb)
        return (
            Gather(p, gwg.at[p.s, h], lambda o: gwg.at[o, h], gsend, grecv, base + 1 + 2 * h),
            Gather(p, xg.at[p.s, at], lambda o: xg.at[o, at], gsend, grecv, base + 2 + 2 * h),
        )

    gathers = [gather_of(h) for h in range(2)]

    def distribute(h):
        x_move.arrive(h)
        gwg[p.s, h] = dot(gate_of[...], xr[h * z.hs : (h + 1) * z.hs, :LANES]).astype(BF)
        gathers[h][0].start()
        in_order(xr, xg, h)
        gathers[h][1].start()

    def collect(h):
        for item in gathers[h]:
            item.forward()
        for item in gathers[h]:
            item.arrive()
        for b in range(z.ns):
            wide = dot(source[...], gwg[b, h]) * pick[...].astype(F32)
            gwc[b] = jnp.sum(wide, axis=1, keepdims=True)

    def activate(h):
        def step(i, carry):
            l, tile = lax.div(i, tiles), lax.rem(i, tiles)
            at = aligned(tile * 256, 256, 256)
            local = aligned(l * z.cr, z.cr, 16)
            at_rows = aligned(h * z.cb + l * z.cr, z.cr, 16)
            x = dot(expert_rows(xg, h, l, slice(None)), w_in[l, :, at])
            g = expert_rows(gp, h, l, at).astype(F32)
            gate = gwc[:, local, :].reshape(z.ns * z.cr, 1)
            x2 = x * x
            th = jnp.tanh(x * (GELU_A + (GELU_A * GELU_B) * x2))
            hx = 0.5 * x
            up = 1.0 + th
            a = hx * up
            act[:, at_rows, at] = a.astype(BF).reshape(z.ns, z.cr, 256)
            slope = 0.5 * up + hx * (1.0 - th * th) * (GELU_A + (3.0 * GELU_A * GELU_B) * x2)
            gp[:, at_rows, at] = (g * gate * slope).astype(BF).reshape(z.ns, z.cr, 256)
            toward = jnp.sum(a * g, axis=1, keepdims=True).reshape(z.ns, z.cr, 1)
            ggc[:, at_rows, :] = toward + jnp.where(tile == 0, 0.0, ggc[:, at_rows, :])
            return carry

        lax.fori_loop(0, z.el * tiles, step, 0)

        def gate_dy(l, carry):
            at_rows = aligned(h * z.cb + l * z.cr, z.cr, 16)
            gate = gwc[:, aligned(l * z.cr, z.cr, 16), :]
            dyg[:, at_rows, :] = (dyg[:, at_rows, :].astype(F32) * gate).astype(BF)
            return carry

        lax.fori_loop(0, z.el, gate_dy, 0)

    def unit(u):
        h, cols = u // 2, pl.ds((u % 2) * half, half)
        return (
            Scatter(
                p, part.at[u, p.c], part.at[u, 1 - p.c], rp.at[u], ys.at[u], yr.at[u],
                psend.at[u], precv.at[u], ysend.at[u], yrecv.at[u],
            ),
            Return(p, fin.at[u], ret, h, cols, rsend.at[u], rrecv.at[u]),
        )

    units = [unit(u) for u in range(4)]
    results = [
        Scatter(
            p, rpart.at[u, p.c], rpart.at[u, 1 - p.c], rrp.at[u], rys.at[u], ryr.at[u],
            psend.at[4 + u], precv.at[4 + u], ysend.at[4 + u], yrecv.at[4 + u],
        )
        for u in range(4)
    ]

    def products(ref, weight, transposed, dst, u):
        h, cols = u // 2, slice((u % 2) * half, (u % 2 + 1) * half)

        def step(l, carry):
            if transposed:
                out = dot_t(expert_rows(ref, h, l, slice(None)), weight[l, cols, :])
            else:
                out = dot(expert_rows(ref, h, l, slice(None)), weight[l, :, cols])
            out = out.astype(BF)
            for b in range(z.ns):
                dst[u, b % 2, b // 2, aligned(l * z.cr, z.cr, 16), :] = out[b * z.cr : (b + 1) * z.cr]
            return carry

        lax.fori_loop(0, z.el, step, 0)

    def stage_a(u):
        products(gp, w_in, True, part, u)
        units[u][0].send()

    def stage_b(u):
        units[u][0].middle()

    def stage_c(u):
        fin[u] = tdot(perm[...], units[u][0].total().astype(BF)).astype(BF)
        units[u][1].start()

    g_scatter = Scatter(
        p, gpart.at[p.c], gpart.at[1 - p.c], grp, gys, gyr, gsem.at[0, 0], gsem.at[1, 0], gsem.at[2], gsem.at[3]
    )

    def toward_a():
        for b in range(z.ns):
            for h in range(2):
                col = ggc[b, h * z.cb : (h + 1) * z.cb, :]
                high = col.astype(BF).astype(F32)
                put = pick[...].astype(F32)
                top = tdot(source[...], (high * put).astype(BF))
                rest = tdot(source[...], ((col - high) * put).astype(BF))
                both = jnp.where(iota(top.shape, 0) < z.n16, top, rest)
                gpart[b % 2, b // 2, h * 2 * z.n16 : (h + 1) * 2 * z.n16, :] = both.astype(BF)
        g_scatter.send()

    def toward_copy(k):
        back = (-k[0] % z.nz, k[1])
        return rcopy(
            gout.at[k[0] % 2], gret.at[position(z, back)], gsem.at[4, position(z, k)], gsem.at[5, position(z, back)],
            (p.expert(*k), p.s),
        )

    def toward_c():
        total = g_scatter.total()
        for h in range(2):
            first = total[h * 2 * z.n16 : h * 2 * z.n16 + z.n16]
            value = first + total[h * 2 * z.n16 + z.n16 : (h + 1) * 2 * z.n16]
            high, rest = split_high(value)
            gout[h, 0 : z.n16, :] = high
            gout[h, z.n16 : 2 * z.n16, :] = rest
        for k in offsets(z):
            toward_copy(k).start()
        gret[0] = gout[0]

    def toward_d():
        for k in offsets(z):
            toward_copy((-k[0] % z.nz, k[1])).wait_recv()
        line = iota((2 * z.n16, LANES), 0)
        out = jnp.zeros((2 * z.n16, LANES), F32)
        for k in [(0, 0)] + offsets(z):
            back = (-k[0] % z.nz, k[1])
            at = position(z, back) - (k[0] % 2) * z.hn
            got = gret[position(z, k)].astype(F32)
            rank = p.expert(*k)
            out = jnp.where(line == rank, got[at : at + 1, :], out)
            out = jnp.where(line == z.n16 + rank, got[z.n16 + at : z.n16 + at + 1, :], out)
        ggrows[...] = out.astype(BF)
        for k in offsets(z):
            toward_copy(k).wait_send()

    def both(ref, l, cols):
        return jnp.concatenate([expert_rows(ref, h, l, cols) for h in range(2)], 0)

    stores = []

    def weight_grad(n, left, right, out, l):
        if n >= 2:
            stores[n - 2].wait()

        def step(i, carry):
            at = aligned(i * 256, 256, 256)
            wstage[n % 2, :, at] = tdot(both(left, l, slice(None)), both(right, l, at)).astype(BF)
            return carry

        lax.fori_loop(0, d // 256, step, 0)
        copy = pltpu.make_async_copy(wstage.at[n % 2], out.at[l], csem.at[2 + n])
        copy.start()
        stores.append(copy)

    def result_a(u):
        products(act, w_out, False, rpart, u)
        results[u].send()

    def result_c(u):
        units[u][1].finish()
        fin[u] = tdot(perm[...], results[u].total().astype(BF)).astype(BF)
        spill(fin.at[u], o_rfin.at[u])

    for copy in waiting["gp"]:
        copy.wait()
    for item in g_tok:
        item.finish()
    gradient(0)
    distribute(0)
    gradient(1)
    distribute(1)
    load_in.wait()
    for copy in waiting["act"]:
        copy.wait()
    g_dy.finish()
    collect(0)
    activate(0)
    stage_a(0)
    stage_a(1)
    stage_b(0)
    stage_b(1)
    collect(1)
    activate(1)
    toward_a()
    stage_a(2)
    stage_c(0)
    stage_b(2)
    stage_a(3)
    stage_c(1)
    g_scatter.middle()
    stage_b(3)
    result_a(0)
    result_a(1)
    toward_c()
    results[0].middle()
    results[1].middle()
    result_a(2)
    stage_c(2)
    results[2].middle()
    result_a(3)
    stage_c(3)
    results[3].middle()
    weight_grad(0, act, dyg, dout, 0)
    weight_grad(1, act, dyg, dout, 1)
    result_c(0)
    weight_grad(2, xg, gp, din, 0)
    result_c(1)
    weight_grad(3, xg, gp, din, 1)
    result_c(2)
    result_c(3)
    toward_d()
    for u in range(4):
        units[u][1].arrive()
    spill(ret, o_ret)
    for item in [g_small] + sum(g_w, []) + [g_o] + list(gathers[0]) + list(gathers[1]):
        item.finish()
    x_move.finish()
    g_scatter.finish()
    for scatter, _ in units:
        scatter.finish()
    for scatter in results:
        scatter.finish()
    for copy in waiting[None] + stores[2:]:
        copy.wait()


ANY = pl.BlockSpec(memory_space=pl.ANY)


def forward(z, *inputs):
    def bf(*shape):
        return jax.ShapeDtypeStruct(shape, BF)

    def f32(*shape):
        return jax.ShapeDtypeStruct(shape, F32)

    def vm(x):
        return pltpu.VMEM(x.shape, x.dtype)

    dma = pltpu.SemaphoreType.DMA
    half, ny, nb = z.d // 2, z.ny, 2 * z.n16
    kept = (
        bf(z.m, z.g, z.d), bf(z.m, z.g, z.d), bf(z.m, z.g, z.d), bf(z.m, z.g, z.d), bf(z.mt, z.d),
        bf(z.m * z.pairs, 2 * z.t, z.g), bf(z.mt, z.d), f32(z.mt, z.d), bf(z.mt, z.d), f32(z.mt, LANES),
        bf(z.d, z.d), bf(z.d, z.d), bf(z.d, z.d), bf(z.d, z.d),
    )
    smallg = bf(z.ns, z.small, z.d)
    ret, rpart, rfin = bf(z.slots, z.d), bf(4, 2, ny, z.cb, half), bf(4, z.hs, half)
    outs = kept + (smallg, ret, rfin, bf(nb, LANES), bf(z.el, z.d, z.ff), bf(z.el, z.ff, z.d))
    rows = bf(z.ns, z.blk, z.d)
    scratch = [vm(x) for x in kept[4:]]
    scratch += [vm(bf(z.small, z.d)), vm(smallg)]
    scratch += [vm(ret)] * 3 + [vm(rows)] * 2 + [vm(bf(z.ns, z.blk, z.ff))] * 2
    scratch += [vm(bf(z.el, z.d, z.ff)), vm(bf(z.el, z.ff, z.d))]
    scratch += [pltpu.VMEM((8, HEADS * BUCKETS), F32), pltpu.VMEM((z.m, z.t, z.g), I32), pltpu.VMEM((z.m, z.t, z.g), F32)]
    scratch += [vm(bf(z.ns, 2, nb, LANES)), vm(f32(z.ns, z.cb, 1)), vm(f32(z.ns, z.blk, 1))]
    shares = [vm(rpart), vm(bf(4, ny, z.cb, half)), vm(bf(4, ny - 1, z.cb, half)), vm(bf(4, ny - 1, z.cb, half))]
    scratch += shares + [vm(rfin), vm(ret)] + shares + [vm(bf(2, z.d, z.d))]
    scratch += [vm(bf(2, ny, 2 * nb, LANES)), vm(bf(ny, 2 * nb, LANES))]
    scratch += [vm(bf(ny - 1, 2 * nb, LANES))] * 2 + [vm(bf(2, nb, LANES)), vm(bf(z.ne, nb, LANES))]
    n_items = 1 + z.m + 3 * (z.d // 256) + 1 + 5
    scratch += [dma((10,)), dma((24,)), dma((n_items, z.ns)), dma((n_items, z.ns)), dma((2, z.ne)), dma((2, z.ne))]
    scratch += [dma((8,))] * 2 + [dma((8, ny))] * 2 + [dma((4, z.hn))] * 2 + [dma((6, z.ne))]
    return pl.pallas_call(
        functools.partial(forward_kernel, z),
        out_shape=outs,
        in_specs=[VMEM] * 3 + [SMEM] + [ANY] * 4 + [VMEM] * 2 + [ANY] * 2 + [VMEM] * 7,
        out_specs=[ANY] * 17 + [VMEM] + [ANY] * 2,
        scratch_shapes=scratch,
        compiler_params=pltpu.CompilerParams(
            collective_id=0, has_side_effects=True, vmem_limit_bytes=63 * 2**20
        ),
        name="forward",
    )(*inputs)


class Sum:
    def __init__(self, place, own, xin, xsum, zin, done, sems):
        self.p, self.own, self.xin, self.xsum, self.zin, self.done = place, own, xin, xsum, zin, done
        self.sx, self.rx, self.sz, self.rz, self.sg, self.rg, self.sh, self.rh = sems
        self.rows, self.nz = own.shape[1], place.z.nz
        self.x, self.zz = lax.rem(place.e, 2), lax.div(place.e, 2)

    def piece(self, zz):
        return aligned(zz * (self.rows // self.nz), self.rows // self.nz, 16)

    def other_x(self):
        return (self.p.expert(0, 1), self.p.s)

    def other_z(self, k):
        return (self.p.expert(k, 0), self.p.s)

    def z_at(self, k):
        return lax.rem(self.zz + k, self.nz)

    def copy_x(self):
        return rcopy(self.own.at[1 - self.x], self.xin, self.sx, self.rx, self.other_x())

    def copy_z(self, k):
        return rcopy(
            self.xsum.at[self.piece(self.z_at(k))], self.zin.at[k - 1], self.sz.at[k - 1], self.rz.at[k - 1],
            self.other_z(k),
        )

    def copy_g(self, k, origin):
        block = self.done.at[self.x, self.piece(origin)]
        return rcopy(block, block, self.sg.at[k - 1], self.rg.at[k - 1], self.other_z(k))

    def copy_h(self, x):
        block = self.done.at[x]
        return rcopy(block, block, self.sh, self.rh, self.other_x())

    def one(self):
        self.copy_x().start()

    def two(self):
        self.copy_x().wait_recv()
        self.xsum[...] = (self.own[self.x].astype(F32) + self.xin[...].astype(F32)).astype(BF)
        for k in range(1, self.nz):
            self.copy_z(k).start()

    def three(self):
        out = self.xsum[self.piece(self.zz), :].astype(F32)
        for k in range(1, self.nz):
            self.copy_z(k).wait_recv()
            out = out + self.zin[k - 1].astype(F32)
        self.done[self.x, self.piece(self.zz), :] = out.astype(BF)
        for k in range(1, self.nz):
            self.copy_g(k, self.zz).start()

    def four(self):
        for k in range(1, self.nz):
            self.copy_g(k, self.z_at(self.nz - k)).wait_recv()
        self.copy_h(self.x).start()

    def five(self):
        self.copy_h(1 - self.x).wait_recv()

    def finish(self):
        self.copy_x().wait_send()
        for k in range(1, self.nz):
            self.copy_z(k).wait_send()
            self.copy_g(k, self.zz).wait_send()
        self.copy_h(self.x).wait_send()


def backward_kernel(
    z,
    dy, counts, routes, dest, place_m, ggrows,
    i_toks, i_hid, i_kk, i_vv, i_qq, i_pp, i_ctx, i_mid, i_nrm, i_sd, i_fk, i_fv, i_fq, i_fo, i_small, i_ret, i_rfin,
    mixed, dtok, wdone, drouter, dvecs,
    toks, hid, kk, vv, qq, pp, ctx, mid, nrm, sd, fk, fv, fq, fo, smallg, ret, retr,
    gctx, gqb, gkb, gvb, gmid, lower, edge_id, edge_ok, tab, gain_rows,
    wpart, wrp, wys, wyr, wsum, wxin, wxs, wzin,
    gpart, grp, gys, gyr, sbuf, sone, stwo, sthree, sfour,
    csem, rr1, rr2,
    wp1, wp2, wy1, wy2, ux1, ux2, uz1, uz2, ug1, ug2, uh1, uh2, gp1, gp2, gy1, gy2, ss1, ss2,
):
    p = Place(z)
    t, d, mt = z.t, z.d, z.mt
    half = d // 2
    loads = {}

    def load(src, dst, name):
        loads[name] = pltpu.make_async_copy(src, dst, csem.at[len(loads)])
        loads[name].start()

    load(i_sd, sd, "sd")
    load(i_ret, ret, "ret")
    load(i_small, smallg, "small")
    load(i_mid, mid, "mid")
    load(i_nrm, nrm, "nrm")
    load(i_ctx, ctx, "ctx")
    load(i_fo, fo, "fo")
    load(i_qq, qq, "qq")
    load(i_vv, vv, "vv")
    load(i_kk, kk, "kk")
    load(i_pp, pp, "pp")
    load(i_hid, hid, "hid")
    load(i_fk, fk, "fk")
    load(i_fv, fv, "fv")
    load(i_fq, fq, "fq")
    load(i_toks, toks, "toks")
    p.barrier()

    returns = []
    for u in range(4):
        h, cols = u // 2, pl.ds((u % 2) * half, half)
        returns.append(Return(p, i_rfin.at[u], retr, h, cols, rr1.at[u], rr2.at[u]))
        returns[u].start_remote()
        if h == 0:
            load(i_rfin.at[u, pl.ds(0, z.sp)], retr.at[aligned(p.e * z.sp, z.sp, 16), cols], ("r", u))

    route0, route1 = route_columns(z, routes)
    loads["sd"].wait()
    slot0, slot1 = sd[:, 0:1], sd[:, 1:2]
    gate0, gate1 = sd[:, 2:3], sd[:, 3:4]
    hot0, hot1 = one_hot(z, slot0).astype(BF), one_hot(z, slot1).astype(BF)
    hot = hot0 + hot1

    def toward(hots):
        wide = dot(dot_t(hots, dest[...]).astype(BF), ggrows[...]) * dot(hots, place_m[...])
        return jnp.sum(wide, axis=1, keepdims=True)

    toward0, toward1 = toward(hot0), toward(hot1)
    mean = gate0 * toward0 + gate1 * toward1
    lane = iota((mt, z.small), 1)
    glog = jnp.where(lane == route0, gate0 * (toward0 - mean), 0.0)
    glog = (glog + jnp.where(lane == route1, gate1 * (toward1 - mean), 0.0)).astype(BF)
    loads["small"].wait()
    sums = smallg[0].astype(F32)
    for b in range(1, z.ns):
        sums = sums + smallg[b].astype(F32)
    gain_one = sums[z.e : z.e + 1, :]
    gain_two = sums[z.e + 1 : z.e + 2, :]
    router = sums.astype(BF)
    loads["ret"].wait()
    gnorm = dot(glog, router) + dot(hot, ret[...])
    loads["mid"].wait()
    x = mid[...]
    scale = lax.rsqrt(jnp.mean(x * x, axis=1, keepdims=True) + EPS)
    xh = x * scale
    gain_rows[1:2, :] = jnp.sum(gnorm * xh, axis=0, keepdims=True)
    gy = gnorm * gain_two
    gm = dy[...].astype(F32) + scale * (gy - xh * jnp.mean(gy * xh, axis=1, keepdims=True))
    gmid[...] = gm
    gattn = gm.astype(BF)
    loads["nrm"].wait()
    sbuf[...] = tdot(glog, nrm[...])

    def reduction(u):
        shard_sum = Scatter(
            p, wpart.at[u, p.c], wpart.at[u, 1 - p.c], wrp.at[u], wys.at[u], wyr.at[u],
            wp1.at[u], wp2.at[u], wy1.at[u], wy2.at[u],
        )
        expert_sum = Sum(
            p, wsum.at[u], wxin.at[u], wxs.at[u], wzin.at[u], wdone.at[u],
            (ux1.at[u], ux2.at[u], uz1.at[u], uz2.at[u], ug1.at[u], ug2.at[u], uh1.at[u], uh2.at[u]),
        )
        return shard_sum, expert_sum

    pairs = [reduction(u) for u in range(4)]

    def stage(u, n):
        shard_sum, expert_sum = pairs[u]
        if n == 0:
            shard_sum.send()
        elif n == 1:
            shard_sum.middle()
        elif n == 2:
            wsum[u] = shard_sum.total().astype(BF)
            expert_sum.one()
        elif n == 3:
            expert_sum.two()
        elif n == 4:
            expert_sum.three()
        elif n == 5:
            expert_sum.four()
        else:
            expert_sum.five()

    def put(u, first, value):
        value = value.astype(BF)
        for b in range(z.ns):
            rows = value[b * z.r : (b + 1) * z.r]
            for c in range(2):
                at = first + c * LANES
                wpart[u, b % 2, b // 2, at // half, :, at % half : at % half + LANES] = rows[:, c * LANES : (c + 1) * LANES]

    loads["ctx"].wait()
    for i in range(d // 256):
        put(3, i * 256, tdot(ctx[...], gattn[:, i * 256 : (i + 1) * 256]))
    stage(3, 0)
    loads["fo"].wait()
    for i in range(d // 256):
        cols = slice(i * 256, (i + 1) * 256)
        gctx[:, cols] = dot_t(gattn, fo[cols, :]).astype(BF)

    tab[...] = jnp.zeros_like(tab)
    lane = iota((1, LANES), 1)
    starts = jnp.where(lane <= 16, lane, 0)
    for i, edge in enumerate(BUCKET_EDGES):
        starts = jnp.where(lane == 17 + i, edge, starts)
    for m in range(z.m):
        key_pos, _ = key_layout(z, counts, m, (z.g, 1), 0)
        lower[m] = jnp.where(key_pos <= iota((z.g, z.far), 1), 1.0, 0.0).astype(BF)
        at = query_position(z, counts, m, p.s) - starts
        ok = (at >= 0) & (lane < BUCKETS)
        edge_id[m] = jnp.where(ok, at, 0)
        edge_ok[m] = jnp.where(ok, 1.0, 0.0)
    low = iota((t, LANES), 1) < 64

    def attend_back(i, unit):
        m = lax.rem(i, z.m)
        pair = unit * 2 + lax.div(i, z.m)
        cols = aligned(pair * LANES, LANES, LANES)
        rows = aligned(m * t, t, 16)
        q, g = qq[rows, cols], gctx[rows, cols]
        zero = jnp.zeros_like(q)
        q_two = jnp.concatenate([jnp.where(low, q, zero), jnp.where(low, zero, q)], 0)
        g_two = jnp.concatenate([jnp.where(low, g, zero), jnp.where(low, zero, g)], 0)
        probs = pp[m * z.pairs + pair]
        pf = probs.astype(F32)
        gp = dot_t(g_two, vv[m, :, cols])
        gs = (pf * (gp - jnp.sum(pf * gp, axis=1, keepdims=True))).astype(BF)
        two = dot(gs, kk[m, :, cols])
        gqb[rows, cols] = (jnp.where(low, two[:t], two[t:]) * 0.125).astype(BF)
        gkb[m, :, cols] = tdot(gs, q_two).astype(BF)
        gvb[m, :, cols] = tdot(probs, g_two).astype(BF)
        total = dot(gs, lower[m])
        for side in range(2):
            found = jnp.zeros((t, LANES), F32)
            for b in range(z.far // LANES):
                at = edge_id[m] - b * LANES
                inside = (at >= 0) & (at < LANES)
                got = jnp.take_along_axis(
                    total[side * t : (side + 1) * t, b * LANES : (b + 1) * LANES], jnp.where(inside, at, 0), axis=1
                )
                found = jnp.where(inside, got, found)
            found = jnp.sum(found * edge_ok[m], axis=0, keepdims=True)
            row = pl.ds(pair * 2 + side, 1)
            tab[row, :] = tab[row, :] + found
        return unit

    def attention(unit):
        lax.fori_loop(0, z.m * 2, attend_back, unit, unroll=2)

    def own_hidden():
        return jnp.concatenate([hid[m, aligned(p.s * t, t, 16), :] for m in range(z.m)], 0)

    def weight_grads(u):
        cols = slice(u * 256, (u + 1) * 256)
        put(u, 0, tdot(own_hidden(), gqb[:, cols]))
        every = hid[...].reshape(z.m * z.g, d)
        put(u, 256, tdot(every, gkb[:, :, cols].reshape(z.m * z.g, 256)))
        put(u, 512, tdot(every, gvb[:, :, cols].reshape(z.m * z.g, 256)))

    grads = [
        Scatter(
            p, gpart.at[m, p.c], gpart.at[m, 1 - p.c], grp.at[m], gys.at[m], gyr.at[m],
            gp1.at[m], gp2.at[m], gy1.at[m], gy2.at[m],
        )
        for m in range(z.m)
    ]

    def hidden_grads(m):
        x = toks[m].astype(F32)
        scale = lax.rsqrt(jnp.mean(x * x, axis=1, keepdims=True) + EPS)
        for i in range(d // 256):
            cols = slice(i * 256, (i + 1) * 256)
            gh = dot_t(gkb[m], fk[cols, :]) + dot_t(gvb[m], fv[cols, :])
            own = dot_t(gqb[m * t : (m + 1) * t, :], fq[cols, :])
            for b in range(z.ns):
                rows = slice(b * t, (b + 1) * t)
                part = gh[rows] + jnp.where(p.s == b, 1.0, 0.0) * own
                gpart[m, b % 2, b // 2, :, cols] = part.astype(BF)
                row = jnp.sum(part * (toks[m, rows, cols].astype(F32) * scale[rows]), axis=0, keepdims=True)
                if m == 0 and b == 0:
                    gain_rows[0:1, cols] = row
                else:
                    gain_rows[0:1, cols] = gain_rows[0:1, cols] + row

    def token_grads(m):
        gh = grads[m].total()
        rows = slice(m * t, (m + 1) * t)
        x = toks[m, aligned(p.s * t, t, 16), :].astype(F32)
        scale = lax.rsqrt(jnp.mean(x * x, axis=1, keepdims=True) + EPS)
        xh = x * scale
        gy = gh * gain_one
        dtok[rows, :] = gmid[rows, :] + scale * (gy - xh * jnp.mean(gy * xh, axis=1, keepdims=True))

    nz = z.nz

    def small_copy(n, k=0):
        if n == 0:
            return rcopy(sone.at[0], sone.at[1], ss1.at[0], ss2.at[0], (p.e, p.shard(0, True)))
        if n == 1:
            return rcopy(stwo.at[0], stwo.at[k], ss1.at[k], ss2.at[k], (p.e, p.shard(k, False)))
        if n == 2:
            return rcopy(sthree.at[0], sthree.at[1], ss1.at[z.ny], ss2.at[z.ny], (p.expert(0, 1), p.s))
        zz = lax.div(p.e, 2)
        return rcopy(sfour.at[zz], sfour.at[zz], ss1.at[z.ny + k], ss2.at[z.ny + k], (p.expert(k, 0), p.s))

    def small_pack():
        tabs = tab[...]
        tabs = tabs - pltpu.roll(tabs, LANES - 1, 1)
        tabs = jnp.where(iota(tabs.shape, 1) < BUCKETS, tabs, 0.0)
        row = iota(sbuf.shape, 0)
        out = sbuf[...]
        out = jnp.where(row == z.e, gain_rows[0:1, :], out)
        out = jnp.where(row == z.e + 1, gain_rows[1:2, :], out)
        sbuf[...] = out
        per = LANES // BUCKETS
        for c in range(HEADS // per):
            piece = tabs[c * per : c * per + 1, :]
            for j in range(1, per):
                piece = piece + pltpu.roll(tabs[c * per + j : c * per + j + 1, :], j * BUCKETS, 1)
            sbuf[z.e + 2 : z.e + 3, c * LANES : (c + 1) * LANES] = piece
        sone[0] = sbuf[...].astype(BF)
        small_copy(0).start()

    def small_step(n):
        if n == 1:
            small_copy(0).wait_recv()
            stwo[0] = (sone[0].astype(F32) + sone[1].astype(F32)).astype(BF)
            for k in range(1, z.ny):
                small_copy(1, k).start()
        elif n == 2:
            out = stwo[0].astype(F32)
            for k in range(1, z.ny):
                small_copy(1, k).wait_recv()
                out = out + stwo[k].astype(F32)
            sthree[0] = out.astype(BF)
            small_copy(2).start()
        elif n == 3:
            small_copy(2).wait_recv()
            sfour[lax.div(p.e, 2)] = (sthree[0].astype(F32) + sthree[1].astype(F32)).astype(BF)
            for k in range(1, nz):
                small_copy(3, k).start()
        else:
            for k in range(1, nz):
                small_copy(3, k).wait_recv()
            out = sfour[0].astype(F32)
            for k in range(1, nz):
                out = out + sfour[k].astype(F32)
            high, rest = split_high(out)
            whole = spread(z, p.s, z.r)
            own = dot_t(high, whole) + dot_t(rest, whole)
            drouter[...] = own[0 : z.e, :]
            tail, tail_rest = high[z.e : z.small, :], rest[z.e : z.small, :]
            biases = spread(z, p.s, HEADS * BUCKETS // z.ns)
            own_bias = dot_t(tail, biases) + dot_t(tail_rest, biases)
            dvecs[...] = jnp.where(iota(own_bias.shape, 0) == 2, own_bias, own[z.e : z.small, :])

    def finish_mixed():
        for u in range(4):
            returns[u].arrive()
        for u in range(2):
            loads["r", u].wait()
        for m in range(z.m):
            rows = slice(m * t, (m + 1) * t)
            first, second = dot(hot0[rows], retr[...]), dot(hot1[rows], retr[...])
            mixed[rows, :] = (mid[rows, :] + gate0[rows] * first + gate1[rows] * second).astype(BF)

    for name in ("qq", "vv", "kk", "pp"):
        loads[name].wait()
    attention(0)
    stage(3, 1)
    loads["hid"].wait()
    weight_grads(0)
    stage(0, 0)
    attention(1)
    stage(0, 1)
    stage(3, 2)
    weight_grads(1)
    stage(1, 0)
    stage(3, 3)
    attention(2)
    stage(0, 2)
    stage(1, 1)
    stage(3, 4)
    weight_grads(2)
    stage(2, 0)
    stage(0, 3)
    for name in ("fk", "fv", "fq", "toks"):
        loads[name].wait()
    hidden_grads(0)
    grads[0].send()
    stage(2, 1)
    stage(1, 2)
    stage(0, 4)
    stage(3, 5)
    hidden_grads(1)
    grads[1].send()
    grads[0].middle()
    small_pack()
    stage(1, 3)
    stage(0, 5)
    grads[1].middle()
    small_step(1)
    stage(2, 2)
    finish_mixed()
    stage(1, 4)
    token_grads(0)
    stage(2, 3)
    small_step(2)
    token_grads(1)
    stage(1, 5)
    small_step(3)
    stage(2, 4)
    small_step(4)
    stage(2, 5)
    for u in (3, 0, 1, 2):
        stage(u, 6)
    for shard_sum, expert_sum in pairs:
        shard_sum.finish()
        expert_sum.finish()
    for item in returns:
        item.finish()
    for item in grads:
        item.finish()
    small_copy(0).wait_send()
    for k in range(1, z.ny):
        small_copy(1, k).wait_send()
    small_copy(2).wait_send()
    for k in range(1, nz):
        small_copy(3, k).wait_send()


def backward(z, *inputs):
    def bf(*shape):
        return pltpu.VMEM(shape, BF)

    def f32(*shape):
        return jax.ShapeDtypeStruct(shape, F32)

    dma = pltpu.SemaphoreType.DMA
    d, r, ny, nz, half = z.d, z.r, z.ny, z.nz, z.d // 2
    n_small = z.ny + z.nz
    outs = (
        jax.ShapeDtypeStruct((z.mt, d), BF), f32(z.mt, d), jax.ShapeDtypeStruct((4, 2, r, half), BF),
        f32(z.e, r), f32(z.small - z.e, r),
    )
    kept = [pltpu.VMEM(x.shape, x.dtype) for x in inputs[6:-1]]
    return pl.pallas_call(
        functools.partial(backward_kernel, z),
        out_shape=outs,
        in_specs=[VMEM, SMEM] + [VMEM] * 4 + [ANY] * 17,
        out_specs=[VMEM] * len(outs),
        scratch_shapes=kept + [
            bf(z.slots, d),
            bf(z.mt, d), bf(z.mt, d), bf(z.m, z.g, d), bf(z.m, z.g, d), pltpu.VMEM((z.mt, d), F32),
            bf(z.m, z.g, z.far), pltpu.VMEM((z.m, z.t, LANES), I32), pltpu.VMEM((z.m, z.t, LANES), F32),
            pltpu.VMEM((16, LANES), F32), pltpu.VMEM((8, d), F32),
            bf(4, 2, ny, 2, r, half), bf(4, ny, 2, r, half), bf(4, ny - 1, 2, r, half), bf(4, ny - 1, 2, r, half),
            bf(4, 2, r, half), bf(4, r, half), bf(4, r, half), bf(4, nz - 1, r // nz, half),
            bf(z.m, 2, ny, z.t, d), bf(z.m, ny, z.t, d), bf(z.m, ny - 1, z.t, d), bf(z.m, ny - 1, z.t, d),
            pltpu.VMEM((z.small, d), F32), bf(2, z.small, d), bf(ny, z.small, d), bf(2, z.small, d),
            bf(nz, z.small, d),
            dma((24,)), dma((4, z.hn)), dma((4, z.hn)),
            dma((4,)), dma((4,)), dma((4, ny)), dma((4, ny)),
            dma((4,)), dma((4,)), dma((4, nz)), dma((4, nz)), dma((4, nz)), dma((4, nz)), dma((4,)), dma((4,)),
            dma((z.m,)), dma((z.m,)), dma((z.m, ny)), dma((z.m, ny)),
            dma((n_small,)), dma((n_small,)),
        ],
        compiler_params=pltpu.CompilerParams(
            collective_id=1, has_side_effects=True, vmem_limit_bytes=63 * 2**20
        ),
        name="backward",
    )(*inputs)


def finish_kernel(z, wdone, din, dout, mixed, dtok, o_mixed, o_dtok, o_q, o_k, o_v, o_o, o_in, o_out):
    i = pl.program_id(0)
    o_in[...] = din[...].astype(F32)
    o_out[...] = dout[...].astype(F32)
    o_mixed[...] = mixed[...]
    o_dtok[...] = dtok[...]
    left, right = wdone[0, 0].astype(F32), wdone[0, 1].astype(F32)

    @pl.when(i < 3)
    def _():
        o_q[...] = left[:, :256]
        o_k[:, :LANES] = left[:, 256:]
        o_k[:, LANES:] = right[:, :LANES]
        o_v[...] = right[:, LANES:]

    @pl.when(i == 3)
    def _():
        o_o[:, : z.d // 2] = left
        o_o[:, z.d // 2 :] = right


def finish(z, wdone, din, dout, mixed, dtok):
    d, r, rows = z.d, z.r, z.el * z.d // 4

    def f32(*shape):
        return jax.ShapeDtypeStruct(shape, F32)

    by_row = lambda n: pl.BlockSpec((n, d), lambda i: (i, 0))
    third = pl.BlockSpec((r, 256), lambda i: (0, jnp.minimum(i, 2)))
    return pl.pallas_call(
        functools.partial(finish_kernel, z),
        grid=(4,),
        out_shape=(
            jax.ShapeDtypeStruct((z.mt, d), BF), f32(z.mt, d), f32(r, d), f32(r, d), f32(r, d), f32(r, d),
            f32(4 * rows, d), f32(4 * rows, d),
        ),
        in_specs=[
            pl.BlockSpec((1, 2, r, d // 2), lambda i: (i, 0, 0, 0)), by_row(rows), by_row(rows),
            by_row(z.mt // 4), by_row(z.mt // 4),
        ],
        out_specs=[
            by_row(z.mt // 4), by_row(z.mt // 4), third, third, third,
            pl.BlockSpec((r, d), lambda i: (0, 0)), by_row(rows), by_row(rows),
        ],
        name="finish",
    )(wdone, din.reshape(4 * rows, d), dout.reshape(4 * rows, d), mixed, dtok)


def fused_device(
    z, tokens, cotangent, routes, prompt_rows, w_query, w_key, w_value, w_output, w_router, gain_attn, gain_ffn,
    pos_table, w_in, w_out,
):
    perm, rows_of, dest, place, gate_of, source, pick = layout_constants(z)
    n = pos_table.shape[0]
    vecs = jnp.zeros((16, z.r), BF)
    vecs = vecs.at[0].set(gain_attn).at[1].set(gain_ffn).at[2, :n].set(pos_table)
    dy = cotangent.reshape(z.mt, z.d)
    routes = routes.transpose(0, 2, 1)
    counts = prompt_rows[:, 0]
    kept = forward(
        z, tokens, dy, routes, counts, w_key, w_value, w_query, w_output, w_router.T, vecs, w_in, w_out,
        perm, rows_of, dest, place, gate_of, source, pick,
    )
    kept, (ggrows, din, dout) = kept[:17], kept[17:]
    mixed, dtok, wdone, drouter, dvecs = backward(z, dy, counts, routes, dest, place, ggrows, *kept)
    mixed, dtok, dq, dk, dv, do, din, dout = finish(z, wdone, din, dout, mixed, dtok)
    return (
        mixed.reshape(tokens.shape),
        dtok.reshape(tokens.shape),
        dq,
        dk,
        dv,
        do,
        drouter.T,
        dvecs[0],
        dvecs[1],
        dvecs[2, :n],
        din.reshape(w_in.shape),
        dout.reshape(w_out.shape),
    )


HIGHEST = lax.Precision.HIGHEST


def distance_bucket(distance):
    coarse = reduce(
        lambda running, border: running + (distance >= border).astype(jnp.int32),
        BUCKET_EDGES,
        jnp.full(distance.shape, 16, jnp.int32),
    )
    return jnp.where(distance < 16, distance, coarse)


def layout(counts, block_rows):
    shard_count = counts.shape[0]
    offsets = jnp.cumsum(counts, dtype=jnp.int32) - counts
    row_index = jnp.arange(shard_count * block_rows, dtype=jnp.int32)
    device = row_index // block_rows
    local_row = row_index - device * block_rows
    own_count = counts[device]
    is_prompt = local_row < own_count
    prompt_total = jnp.sum(counts, dtype=jnp.int32)
    position = jnp.where(
        is_prompt, offsets[device] + local_row, prompt_total + local_row - own_count
    )
    return (position, is_prompt, device)


def rms_norm(values, gain):
    return values * lax.rsqrt(jnp.mean(values * values, axis=-1, keepdims=True) + EPS) * gain


def matmul(left, right):
    return jnp.dot(left, right, preferred_element_type=jnp.float32)


def matmul_left(left, right):
    return lax.dot_general(
        left, right, (((0,), (0,)), ((), ())), preferred_element_type=jnp.float32
    )


def matmul_right(left, right):
    return lax.dot_general(
        left, right, (((1,), (1,)), ((), ())), preferred_element_type=jnp.float32
    )


def per_device(
    tokens,
    cotangent,
    routes,
    prompt_rows,
    w_query,
    w_key,
    w_value,
    w_output,
    w_router,
    gain_attn,
    gain_ffn,
    pos_table,
    w_in,
    w_out,
):
    shard_count = lax.axis_size("shard")
    expert_ranks = lax.axis_size("expert")
    own_index = lax.axis_index("shard")
    micro_count, tok_rows, model_width = tokens.shape
    local_experts = w_in.shape[0]
    expert_count = w_router.shape[1]
    capacity = (9 * tok_rows + 4 * expert_count - 1) // (4 * expert_count)
    head_count = HEADS
    head_size = model_width // head_count
    bucket_count = BUCKETS
    score_scale = head_size ** (-0.5)
    group_rows = shard_count * tok_rows
    slot_count = expert_ranks * capacity * local_experts
    recv_rows = expert_ranks * capacity
    bucket_ids = jnp.arange(bucket_count, dtype=jnp.int32)
    expert_ids = jnp.arange(expert_count, dtype=jnp.int32)
    gathered = (
        lax.all_gather(w_query, "shard", axis=0, tiled=True),
        lax.all_gather(w_key, "shard", axis=0, tiled=True),
        lax.all_gather(w_value, "shard", axis=0, tiled=True),
        lax.all_gather(w_output, "shard", axis=0, tiled=True),
        lax.all_gather(w_router, "shard", axis=0, tiled=True),
        lax.all_gather(gain_attn, "shard", axis=0, tiled=True),
        lax.all_gather(gain_ffn, "shard", axis=0, tiled=True),
        lax.all_gather(pos_table, "shard", axis=0, tiled=True),
    )
    full_query, full_key, full_value, full_output, full_router, gain_one, gain_two, table_flat = (
        gathered
    )
    gain_first = gain_one.astype(jnp.float32)
    gain_second = gain_two.astype(jnp.float32)
    table = table_flat.astype(jnp.float32).reshape(head_count, bucket_count)
    expert_in, expert_out = (
        lax.all_gather(w_in, "shard", axis=2, tiled=True),
        lax.all_gather(w_out, "shard", axis=1, tiled=True),
    )
    sum_query = jnp.zeros(full_query.shape, jnp.float32)
    sum_key = jnp.zeros(full_key.shape, jnp.float32)
    sum_value = jnp.zeros(full_value.shape, jnp.float32)
    sum_output = jnp.zeros(full_output.shape, jnp.float32)
    sum_router = jnp.zeros(full_router.shape, jnp.float32)
    sum_gain_one = jnp.zeros((model_width,), jnp.float32)
    sum_gain_two = jnp.zeros((model_width,), jnp.float32)
    sum_table = jnp.zeros((head_count, bucket_count), jnp.float32)
    sum_expert_in = jnp.zeros(expert_in.shape, jnp.float32)
    sum_expert_out = jnp.zeros(expert_out.shape, jnp.float32)
    mixed_parts = []
    grad_parts = []
    for micro_index in range(micro_count):
        inputs = tokens[micro_index].astype(jnp.float32)
        counts = prompt_rows[micro_index, 0]
        pos_all, prompt_all, device_all = layout(counts, tok_rows)
        query_pos = lax.dynamic_slice_in_dim(pos_all, own_index * tok_rows, tok_rows)
        hidden = rms_norm(inputs, gain_first).astype(jnp.bfloat16)
        query = matmul(hidden, full_query).astype(jnp.bfloat16)
        key = matmul(hidden, full_key).astype(jnp.bfloat16)
        value = matmul(hidden, full_value).astype(jnp.bfloat16)
        keys_all, values_all = (
            lax.all_gather(key, "shard", axis=0, tiled=True),
            lax.all_gather(value, "shard", axis=0, tiled=True),
        )
        key_index = jnp.arange(group_rows, dtype=jnp.int32)
        key_far = jnp.zeros((group_rows,), jnp.bool_)
        key_total = keys_all.shape[0]
        key_block = math.gcd(key_total, 512)
        block_count = key_total // key_block
        key_pos = pos_all[key_index]
        key_prompt = prompt_all[key_index]
        key_device = device_all[key_index]
        key_mine = key_device == own_index
        distance = query_pos[:, None] - key_pos[None, :]
        visible = (
            (distance >= 0)
            & (key_prompt | key_mine)[None, :]
            & jnp.logical_not(key_far & key_mine)[None, :]
        )
        bucket_all = distance_bucket(jnp.maximum(distance, 0))
        bucket_blocks = bucket_all.reshape(tok_rows, block_count, key_block).transpose(1, 0, 2)
        visible_blocks = visible.reshape(tok_rows, block_count, key_block).transpose(1, 0, 2)
        query_heads = query.reshape(tok_rows, head_count, head_size)
        key_blocks = keys_all.reshape(block_count, key_block, head_count, head_size)
        value_blocks = values_all.reshape(block_count, key_block, head_count, head_size)

        def make_bias(unused, block_item):
            bucket_piece, visible_piece = block_item
            bucket_hits = (bucket_piece[:, :, None] == bucket_ids).astype(jnp.float32)
            bias = jnp.einsum("qkb,hb->hqk", bucket_hits, table, precision=HIGHEST)
            return (unused, jnp.where(visible_piece[None], bias, MASKED))

        _, bias_blocks = lax.scan(
            make_bias, jnp.zeros((), jnp.float32), (bucket_blocks, visible_blocks)
        )

        def score_piece(key_piece, bias_piece):
            raw = jnp.einsum(
                "qhd,khd->hqk", query_heads, key_piece, preferred_element_type=jnp.float32
            )
            return raw * score_scale + bias_piece

        def running(state_pair, block_item):
            running_max, running_sum = state_pair
            key_piece, bias_piece = block_item
            scores = score_piece(key_piece, bias_piece)
            new_max = jnp.maximum(running_max, jnp.max(scores, axis=-1))
            running_sum = running_sum * jnp.exp(running_max - new_max) + jnp.sum(
                jnp.exp(scores - new_max[:, :, None]), axis=-1
            )
            return ((new_max, running_sum), None)

        start_pair = (
            jnp.full((head_count, tok_rows), MASKED, jnp.float32),
            jnp.zeros((head_count, tok_rows), jnp.float32),
        )
        (running_max, running_sum), _ = lax.scan(running, start_pair, (key_blocks, bias_blocks))
        log_total = running_max + jnp.log(running_sum)

        def gather_context(context_sum, block_item):
            key_piece, value_piece, bias_piece = block_item
            weights_low = jnp.exp(
                score_piece(key_piece, bias_piece) - log_total[:, :, None]
            ).astype(jnp.bfloat16)
            return (
                context_sum
                + jnp.einsum(
                    "hqk,khd->qhd", weights_low, value_piece, preferred_element_type=jnp.float32
                ),
                None,
            )

        context, _ = lax.scan(
            gather_context,
            jnp.zeros((tok_rows, head_count, head_size), jnp.float32),
            (key_blocks, value_blocks, bias_blocks),
        )
        context_low = context.reshape(tok_rows, model_width).astype(jnp.bfloat16)
        middle = inputs + matmul(context_low, full_output)
        normed = rms_norm(middle, gain_second).astype(jnp.bfloat16)
        logits = matmul(normed, full_router)
        chosen = routes[micro_index]
        pick_table = (chosen[:, :, None] == expert_ids).astype(jnp.float32)
        picked = jnp.sum(pick_table * logits[:, None, :], axis=-1)
        gate_weights = jax.nn.softmax(picked, axis=-1)
        flat_routes = chosen.reshape(-1)
        expert_hits = (flat_routes[:, None] == expert_ids).astype(jnp.int32)
        expert_rank = (
            jnp.sum(
                jnp.cumsum(expert_hits, axis=0, dtype=jnp.int32) * expert_hits,
                axis=1,
                dtype=jnp.int32,
            )
            - 1
        )
        slot_index = (
            flat_routes // local_experts * (capacity * local_experts)
            + expert_rank * local_experts
            + flat_routes % local_experts
        )
        slot_owner = (
            jnp.full((slot_count,), 2 * tok_rows, jnp.int32)
            .at[slot_index]
            .set(jnp.arange(2 * tok_rows, dtype=jnp.int32))
        )
        padded = jnp.concatenate([normed, jnp.zeros((1, model_width), jnp.bfloat16)], axis=0)
        outgoing = padded[slot_owner // 2].reshape(
            expert_ranks, capacity, local_experts, model_width
        )
        received = lax.all_to_all(
            outgoing, "expert", split_axis=0, concat_axis=0, tiled=True
        ).reshape(recv_rows, local_experts, model_width)
        pre_act = jnp.einsum(
            "red,edf->ref", received, expert_in, preferred_element_type=jnp.float32
        )
        activation = jax.nn.gelu(pre_act).astype(jnp.bfloat16)
        expert_result = jnp.einsum(
            "ref,efd->red", activation, expert_out, preferred_element_type=jnp.float32
        )
        result_low = expert_result.astype(jnp.bfloat16).reshape(
            expert_ranks, capacity, local_experts, model_width
        )
        returned = lax.all_to_all(
            result_low, "expert", split_axis=0, concat_axis=0, tiled=True
        ).reshape(slot_count, model_width)
        picked_rows = returned[slot_index].astype(jnp.float32).reshape(tok_rows, 2, model_width)
        output_rows = middle + jnp.sum(gate_weights[:, :, None] * picked_rows, axis=1)
        mixed_parts.append(output_rows.astype(jnp.bfloat16))
        grad_output = cotangent[micro_index].astype(jnp.float32)
        grad_gate = jnp.sum(grad_output[:, None, :] * picked_rows, axis=-1)
        grad_pick = gate_weights * (
            grad_gate - jnp.sum(gate_weights * grad_gate, axis=-1, keepdims=True)
        )
        grad_logits = jnp.sum(pick_table * grad_pick[:, :, None], axis=1).astype(jnp.bfloat16)
        sum_router = sum_router + matmul_left(normed, grad_logits)
        grad_normed = matmul_right(grad_logits, full_router)
        branch_grad = (gate_weights[:, :, None] * grad_output[:, None, :]).reshape(
            2 * tok_rows, model_width
        )
        padded_grad = jnp.concatenate(
            [branch_grad, jnp.zeros((1, model_width), jnp.float32)], axis=0
        )
        grad_send = (
            padded_grad[slot_owner]
            .astype(jnp.bfloat16)
            .reshape(expert_ranks, capacity, local_experts, model_width)
        )
        grad_recv = lax.all_to_all(
            grad_send, "expert", split_axis=0, concat_axis=0, tiled=True
        ).reshape(recv_rows, local_experts, model_width)
        grad_act = jnp.einsum(
            "red,efd->ref", grad_recv, expert_out, preferred_element_type=jnp.float32
        )
        sum_expert_out = sum_expert_out + jnp.einsum(
            "ref,red->efd", activation, grad_recv, preferred_element_type=jnp.float32
        )
        _, gelu_pull = jax.vjp(jax.nn.gelu, pre_act)
        grad_pre = gelu_pull(grad_act)[0].astype(jnp.bfloat16)
        sum_expert_in = sum_expert_in + jnp.einsum(
            "red,ref->edf", received, grad_pre, preferred_element_type=jnp.float32
        )
        grad_in_rows = jnp.einsum(
            "ref,edf->red", grad_pre, expert_in, preferred_element_type=jnp.float32
        )
        grad_in_low = grad_in_rows.astype(jnp.bfloat16).reshape(
            expert_ranks, capacity, local_experts, model_width
        )
        grad_back = lax.all_to_all(
            grad_in_low, "expert", split_axis=0, concat_axis=0, tiled=True
        ).reshape(slot_count, model_width)
        grad_normed = grad_normed + jnp.sum(
            grad_back[slot_index].astype(jnp.float32).reshape(tok_rows, 2, model_width), axis=1
        )
        _, norm_pull = jax.vjp(rms_norm, middle, gain_second)
        grad_middle, grad_gain_second = norm_pull(grad_normed)
        grad_middle = grad_middle + grad_output
        sum_gain_two = sum_gain_two + grad_gain_second
        grad_attn = grad_middle.astype(jnp.bfloat16)
        sum_output = sum_output + matmul_left(context_low, grad_attn)
        grad_context = (
            matmul_right(grad_attn, full_output)
            .astype(jnp.bfloat16)
            .reshape(tok_rows, head_count, head_size)
        )
        row_delta = jnp.einsum("qhd,qhd->hq", grad_context.astype(jnp.float32), context)

        def attend_back(state_pair, block_item):
            grad_query_sum, grad_table_sum = state_pair
            key_piece, value_piece, bias_piece, bucket_piece = block_item
            probs = jnp.exp(score_piece(key_piece, bias_piece) - log_total[:, :, None])
            grad_probs = jnp.einsum(
                "qhd,khd->hqk", grad_context, value_piece, preferred_element_type=jnp.float32
            )
            grad_scores = probs * (grad_probs - row_delta[:, :, None])
            bucket_hits = (bucket_piece[:, :, None] == bucket_ids).astype(jnp.float32)
            grad_table_sum = grad_table_sum + jnp.einsum(
                "hqk,qkb->hb", grad_scores, bucket_hits, precision=HIGHEST
            )
            grad_raw = (grad_scores * score_scale).astype(jnp.bfloat16)
            grad_query_sum = grad_query_sum + jnp.einsum(
                "hqk,khd->qhd", grad_raw, key_piece, preferred_element_type=jnp.float32
            )
            grad_key_piece = jnp.einsum(
                "hqk,qhd->khd", grad_raw, query_heads, preferred_element_type=jnp.float32
            )
            grad_value_piece = jnp.einsum(
                "hqk,qhd->khd",
                probs.astype(jnp.bfloat16),
                grad_context,
                preferred_element_type=jnp.float32,
            )
            return ((grad_query_sum, grad_table_sum), (grad_key_piece, grad_value_piece))

        back_start = (
            jnp.zeros((tok_rows, head_count, head_size), jnp.float32),
            jnp.zeros((head_count, bucket_count), jnp.float32),
        )
        (grad_query_all, grad_table_all), (grad_key_blocks, grad_value_blocks) = lax.scan(
            attend_back, back_start, (key_blocks, value_blocks, bias_blocks, bucket_blocks)
        )
        sum_table = sum_table + grad_table_all
        key_grad_rows = grad_key_blocks.reshape(key_total, model_width)
        value_grad_rows = grad_value_blocks.reshape(key_total, model_width)
        own_key_grad, own_value_grad = (
            lax.psum_scatter(
                key_grad_rows.astype(jnp.bfloat16), "shard", scatter_dimension=0, tiled=True
            ).astype(jnp.float32),
            lax.psum_scatter(
                value_grad_rows.astype(jnp.bfloat16), "shard", scatter_dimension=0, tiled=True
            ).astype(jnp.float32),
        )
        grad_query_low = grad_query_all.reshape(tok_rows, model_width).astype(jnp.bfloat16)
        grad_key_low = own_key_grad.astype(jnp.bfloat16)
        grad_value_low = own_value_grad.astype(jnp.bfloat16)
        sum_query = sum_query + matmul_left(hidden, grad_query_low)
        sum_key = sum_key + matmul_left(hidden, grad_key_low)
        sum_value = sum_value + matmul_left(hidden, grad_value_low)
        grad_hidden = (
            matmul_right(grad_query_low, full_query)
            + matmul_right(grad_key_low, full_key)
            + matmul_right(grad_value_low, full_value)
        )
        _, first_pull = jax.vjp(rms_norm, inputs, gain_first)
        grad_inputs, grad_gain_first = first_pull(grad_hidden)
        sum_gain_one = sum_gain_one + grad_gain_first
        grad_parts.append(grad_inputs + grad_middle)
    shares = (
        lax.psum_scatter(
            sum_query.astype(jnp.bfloat16), "shard", scatter_dimension=0, tiled=True
        ).astype(jnp.float32),
        lax.psum_scatter(
            sum_key.astype(jnp.bfloat16), "shard", scatter_dimension=0, tiled=True
        ).astype(jnp.float32),
        lax.psum_scatter(
            sum_value.astype(jnp.bfloat16), "shard", scatter_dimension=0, tiled=True
        ).astype(jnp.float32),
        lax.psum_scatter(
            sum_output.astype(jnp.bfloat16), "shard", scatter_dimension=0, tiled=True
        ).astype(jnp.float32),
        lax.psum_scatter(
            sum_router.astype(jnp.bfloat16), "shard", scatter_dimension=0, tiled=True
        ).astype(jnp.float32),
        lax.psum_scatter(
            sum_gain_one.astype(jnp.bfloat16), "shard", scatter_dimension=0, tiled=True
        ).astype(jnp.float32),
        lax.psum_scatter(
            sum_gain_two.astype(jnp.bfloat16), "shard", scatter_dimension=0, tiled=True
        ).astype(jnp.float32),
        lax.psum_scatter(
            sum_table.reshape(-1).astype(jnp.bfloat16), "shard", scatter_dimension=0, tiled=True
        ).astype(jnp.float32),
    )
    own_grads = (
        lax.psum(shares[0].astype(jnp.bfloat16), "expert").astype(jnp.float32),
        lax.psum(shares[1].astype(jnp.bfloat16), "expert").astype(jnp.float32),
        lax.psum(shares[2].astype(jnp.bfloat16), "expert").astype(jnp.float32),
        lax.psum(shares[3].astype(jnp.bfloat16), "expert").astype(jnp.float32),
        lax.psum(shares[4].astype(jnp.bfloat16), "expert").astype(jnp.float32),
        lax.psum(shares[5].astype(jnp.bfloat16), "expert").astype(jnp.float32),
        lax.psum(shares[6].astype(jnp.bfloat16), "expert").astype(jnp.float32),
        lax.psum(shares[7].astype(jnp.bfloat16), "expert").astype(jnp.float32),
    )
    grad_expert_in, grad_expert_out = (
        lax.psum_scatter(
            sum_expert_in.astype(jnp.bfloat16), "shard", scatter_dimension=2, tiled=True
        ).astype(jnp.float32),
        lax.psum_scatter(
            sum_expert_out.astype(jnp.bfloat16), "shard", scatter_dimension=1, tiled=True
        ).astype(jnp.float32),
    )
    return (
        jnp.stack(mixed_parts),
        jnp.stack(grad_parts),
        own_grads[0],
        own_grads[1],
        own_grads[2],
        own_grads[3],
        own_grads[4],
        own_grads[5],
        own_grads[6],
        own_grads[7],
        grad_expert_in,
        grad_expert_out,
    )


def solution(mesh):
    in_specs = (
        P(None, ("expert", "shard"), None),
        P(None, ("expert", "shard"), None),
        P(None, ("expert", "shard"), None),
        P(None, "expert", None),
        P("shard", None),
        P("shard", None),
        P("shard", None),
        P("shard", None),
        P("shard", None),
        P("shard"),
        P("shard"),
        P("shard"),
        P("expert", None, "shard"),
        P("expert", "shard", None),
    )
    out_specs = (
        P(None, ("expert", "shard"), None),
        P(None, ("expert", "shard"), None),
        P("shard", None),
        P("shard", None),
        P("shard", None),
        P("shard", None),
        P("shard", None),
        P("shard"),
        P("shard"),
        P("shard"),
        P("expert", None, "shard"),
        P("expert", "shard", None),
    )
    ne, ns = mesh.shape["expert"], mesh.shape["shard"]

    def device(*args):
        tokens, w_router, w_in = args[0], args[8], args[12]
        z = Sizes(
            ne, ns, tokens.shape[0], tokens.shape[1], tokens.shape[2], w_router.shape[1], w_in.shape[0], w_in.shape[2]
        )
        return fused_device(z, *args) if z.fits() else per_device(*args)

    return jax.shard_map(
        device, mesh=mesh, in_specs=in_specs, out_specs=out_specs, check_vma=False
    )
```

```python
import functools
from functools import reduce
import math

import jax
import jax.numpy as jnp
import numpy as np
from jax import lax
from jax.experimental import pallas as pl
from jax.experimental.pallas import tpu as pltpu
from jax.sharding import PartitionSpec as P

HEADS = 12
BUCKETS = 32
EPS = 1e-06
MASKED = -1e30
BUCKET_EDGES = (24, 32, 48, 64, 96, 128, 192, 256, 384, 512, 768, 1024, 1536, 2048, 3072)
MESH = pl.DeviceIdType.MESH
BF = jnp.bfloat16
F32 = jnp.float32
I32 = jnp.int32
LANES = 128


class Sizes:
    def __init__(self, ne, ns, micro, rows, width, experts, local_experts, ff):
        self.ne, self.ns, self.ny = ne, ns, ns // 2
        self.m, self.t, self.d = micro, rows, width
        self.e, self.el, self.ff = experts, local_experts, ff
        self.g = ns * rows
        self.mt = micro * rows
        self.r = width // ns
        self.cap = (9 * rows + 4 * experts - 1) // (4 * experts)
        self.per = micro * self.cap
        self.sp = -(-(local_experts * self.per + 2) // 16) * 16
        self.slots = ne * self.sp
        self.nz = ne // 2
        self.hn = ne // 2
        self.cr = self.hn * self.per
        self.cb = local_experts * self.cr
        self.blk = 2 * self.cb
        self.hs = self.hn * self.sp
        self.n16 = -(-ne // 16) * 16
        self.pairs = HEADS // 2
        self.small = experts + 16
        self.far = self.g // 2 + rows

    def fits(self):
        return (
            self.ns % 2 == 0
            and self.t == LANES
            and self.d == HEADS * 64
            and self.cr % 16 == 0
            and self.nz == 4
            and self.e % 16 == 0
            and self.r % (16 * self.nz) == 0
            and self.slots % LANES == 0
            and self.el * self.per <= LANES
            and self.d == self.ff
            and self.ns >= 2 * self.m
            and self.blk >= self.g
            and self.d % 256 == 0
        )


def layout_constants(z):
    perm = np.zeros((z.cb, z.hs), np.float32)
    rows_of = np.zeros((2 * z.n16, z.slots), np.float32)
    dest = np.zeros((2 * z.n16, z.slots), np.float32)
    place = np.zeros((z.slots, LANES), np.float32)
    gate_of = np.zeros((2 * z.n16, z.hs), np.float32)
    source = np.zeros((z.cb, 2 * z.n16), np.float32)
    pick = np.zeros((z.cb, LANES), np.float32)
    used = z.el * z.per
    for src in range(z.ne):
        rows_of[src, src * z.sp + used] = 1
        rows_of[z.n16 + src, src * z.sp + used + 1] = 1
        dest[src, src * z.sp : (src + 1) * z.sp] = 1
        dest[z.n16 + src, src * z.sp : (src + 1) * z.sp] = 1
        for q in range(used):
            place[src * z.sp + q, q] = 1
    for src in range(z.hn):
        gate_of[src, src * z.sp + used] = 1
        gate_of[z.n16 + src, src * z.sp + used + 1] = 1
        for q in range(used):
            row = (q // z.per) * z.cr + src * z.per + q % z.per
            perm[row, src * z.sp + q] = 1
            source[row, src] = 1
            source[row, z.n16 + src] = 1
            pick[row, q] = 1
    return [jnp.asarray(a, BF) for a in (perm, rows_of, dest, place, gate_of, source, pick)]


def dot(a, b):
    return jnp.dot(a, b, preferred_element_type=F32)


def dot_t(a, b):
    return lax.dot_general(a, b, (((1,), (1,)), ((), ())), preferred_element_type=F32)


def tdot(a, b):
    return lax.dot_general(a, b, (((0,), (0,)), ((), ())), preferred_element_type=F32)


def iota(shape, dim):
    return lax.broadcasted_iota(I32, shape, dim)


def aligned(start, size, multiple):
    return pl.ds(pl.multiple_of(start, multiple), size)


def offsets(z, chunk=None):
    every = [(kz, kx) for kz in range(z.nz) for kx in range(2)][1:]
    return [k for k in every if chunk is None or k[0] % 2 == chunk]


def position(z, k):
    return (k[0] % 2) * z.hn + (k[0] // 2) * 2 + k[1]


class Place:
    def __init__(self, z):
        self.z = z
        self.e = lax.axis_index("expert")
        self.s = lax.axis_index("shard")
        self.y, self.c = lax.div(self.s, 2), lax.rem(self.s, 2)

    def shard(self, k, other):
        y = lax.rem(self.y + k, self.z.ny)
        return y * 2 + (1 - self.c if other else self.c)

    def expert(self, kz, kx):
        high = lax.rem(lax.div(self.e, 2) + kz, self.z.nz)
        return high * 2 + lax.rem(lax.rem(self.e, 2) + kx, 2)

    def barrier(self, with_experts=True):
        sem = pltpu.get_barrier_semaphore()
        others = [(self.e, self.shard(0, True))]
        others += [(self.e, self.shard(k, False)) for k in range(1, self.z.ny)]
        if with_experts:
            others += [(self.expert(*k), self.s) for k in offsets(self.z)]
        for other in others:
            pl.semaphore_signal(sem, inc=1, device_id=other, device_id_type=MESH)
        pl.semaphore_wait(sem, len(others))


def rcopy(src, dst, send, recv, to):
    return pltpu.make_async_remote_copy(
        src_ref=src, dst_ref=dst, send_sem=send, recv_sem=recv, device_id=to, device_id_type=MESH
    )


class Gather:
    def __init__(self, place, own, full, send, recv, item):
        self.p, self.own, self.full = place, own, full
        self.send, self.recv, self.item = send, recv, item

    def copy(self, origin, src, slot, to):
        return rcopy(
            src, self.full(origin), self.send.at[self.item, slot], self.recv.at[self.item, origin], to
        )

    def partner(self):
        return (self.p.e, self.p.shard(0, True))

    def start(self):
        p, ny = self.p, self.p.z.ny
        for k in range(1, ny):
            self.copy(p.s, self.own, k, (p.e, p.shard(k, False))).start()
        self.copy(p.s, self.own, 0, self.partner()).start()

    def forward(self):
        p, ny = self.p, self.p.z.ny
        for k in range(1, ny):
            origin = p.shard(k, False)
            self.copy(origin, self.full(origin), ny + k - 1, self.partner()).wait_recv()
            self.copy(origin, self.full(origin), ny + k - 1, self.partner()).start()

    def arrive(self):
        p, ny = self.p, self.p.z.ny
        for k in range(ny):
            origin = p.shard(k, True)
            self.copy(origin, self.full(origin), 0, self.partner()).wait_recv()

    def finish(self):
        p, ny = self.p, self.p.z.ny
        for slot in range(2 * ny - 1):
            self.copy(p.s, self.own, slot, self.partner()).wait_send()


class Exchange:
    def __init__(self, place, src, dst, send, recv, item):
        self.p, self.src, self.dst = place, src, dst
        self.send, self.recv, self.item = send, recv, item

    def copy(self, k):
        z = self.p.z
        back = (-k[0] % z.nz, k[1])
        at = position(z, back)
        to = self.p.expert(*k)
        return rcopy(
            self.src(to),
            self.dst(at),
            self.send.at[self.item, position(z, k)],
            self.recv.at[self.item, at],
            (to, self.p.s),
        )

    def start(self, some=None):
        for k in filter(some, offsets(self.p.z)):
            self.copy(k).start()

    def arrive(self, some=None):
        z = self.p.z
        for k in filter(some, offsets(z)):
            self.copy((-k[0] % z.nz, k[1])).wait_recv()

    def finish(self, some=None):
        for k in filter(some, offsets(self.p.z)):
            self.copy(k).wait_send()


def slot_ids(z, route0, route1):
    lane = iota((z.t, LANES), 1)
    lower = (iota((z.t, z.t), 0) > iota((z.t, z.t), 1)).astype(F32).astype(BF)
    base = lane * z.per
    for d in range(1, z.ne):
        base = base + jnp.where(lane >= d * z.el, z.sp - z.el * z.per, 0)
    firsts, seconds = [], []
    for m in range(z.m):
        rows = slice(m * z.t, (m + 1) * z.t)
        hit0, hit1 = lane == route0[rows], lane == route1[rows]
        hits = jnp.where(hit0 | hit1, 1.0, 0.0).astype(BF)
        spot = dot(lower, hits) + (base + m * z.cap).astype(F32)
        firsts.append(jnp.sum(jnp.where(hit0, spot, 0.0), axis=1, keepdims=True))
        seconds.append(jnp.sum(jnp.where(hit1, spot, 0.0), axis=1, keepdims=True))
    return jnp.concatenate(firsts, 0), jnp.concatenate(seconds, 0)


def one_hot(z, slot):
    return (iota((z.mt, z.slots), 1) == slot.astype(I32)).astype(F32)


def key_layout(z, counts, m, shape, dim):
    row = iota(shape, dim)
    total = counts[m, 0]
    for b in range(1, z.ns):
        total = total + counts[m, b]
    position = jnp.zeros(shape, I32)
    prompt = jnp.zeros(shape, I32)
    offset = 0
    for b in range(z.ns):
        own = counts[m, b]
        local = row - b * z.t
        inside = (local >= 0) & (local < z.t)
        first = local < own
        position = jnp.where(inside, jnp.where(first, offset + local, total + local - own), position)
        prompt = jnp.where(inside & first, 1, prompt)
        offset = offset + own
    return position, prompt


def query_position(z, counts, m, s):
    total, offset, own = 0, 0, 0
    for b in range(z.ns):
        count = counts[m, b]
        total = total + count
        offset = offset + jnp.where(b < s, count, 0)
        own = own + jnp.where(b == s, count, 0)
    local = iota((z.t, 1), 0)
    return jnp.where(local < own, offset + local, total + local - own)


def bucket_of(z, distance):
    coarse = jnp.full(distance.shape, 16, I32)
    for edge in BUCKET_EDGES:
        if edge < z.far:
            coarse = coarse + jnp.where(distance >= edge, 1, 0)
    return jnp.where(distance < 16, distance, coarse)


VMEM = pl.BlockSpec(memory_space=pltpu.VMEM)
SMEM = pl.BlockSpec(memory_space=pltpu.SMEM)


GELU_A = math.sqrt(2.0 / math.pi)
GELU_B = 0.044715


class SharedGather:
    def __init__(self, place, own, full, send, recv, item):
        self.p, self.own, self.full = place, own, full
        self.send, self.recv, self.item = send, recv, item
        self.x = lax.rem(place.e, 2)

    def half(self, ref, x):
        n = ref.shape[1] // 2
        return ref.at[:, aligned(x * n, n, LANES)]

    def copy(self, src, dst, slot, origin, x, to):
        return rcopy(src, dst, self.send.at[self.item, slot], self.recv.at[self.item, origin, x], to)

    def partner(self):
        return (self.p.e, self.p.shard(0, True))

    def own_copy(self, origin):
        return self.copy(self.own, self.full(origin), 0, origin, 0, self.partner())

    def y_copy(self, k, origin):
        return self.copy(
            self.half(self.own, self.x), self.half(self.full(origin), self.x), k, origin, self.x,
            (self.p.e, self.p.shard(k, False)),
        )

    def on_copy(self, k, kind, origin, x, to):
        block = self.half(self.full(origin), x)
        return self.copy(block, block, self.p.z.ny + 3 * (k - 1) + kind, origin, x, to)

    def start(self):
        p = self.p
        for k in range(1, p.z.ny):
            self.y_copy(k, p.s).start()
        self.own_copy(p.s).start()

    def forward(self):
        p = self.p
        for k in range(1, p.z.ny):
            origin = p.shard(k, False)
            self.y_copy(k, origin).wait_recv()
            self.on_copy(k, 0, origin, self.x, (p.expert(0, 1), p.s)).start()
            self.on_copy(k, 1, origin, self.x, self.partner()).start()

    def forward_rest(self):
        p = self.p
        for k in range(1, p.z.ny):
            origin = p.shard(k, False)
            self.on_copy(k, 0, origin, 1 - self.x, (p.expert(0, 1), p.s)).wait_recv()
            self.on_copy(k, 2, origin, 1 - self.x, self.partner()).start()

    def arrive(self):
        p = self.p
        self.own_copy(p.shard(0, True)).wait_recv()
        for k in range(1, p.z.ny):
            origin = p.shard(k, True)
            for x in range(2):
                self.on_copy(k, 1, origin, x, self.partner()).wait_recv()

    def finish(self):
        p = self.p
        self.own_copy(p.s).wait_send()
        for k in range(1, p.z.ny):
            self.y_copy(k, p.s).wait_send()
            for kind in range(3):
                self.on_copy(k, kind, p.s, 0, self.partner()).wait_send()


class Scatter:
    def __init__(self, place, mine, other, from_core, to_y, from_y, psend, precv, ysend, yrecv):
        self.p, self.mine, self.other, self.from_core = place, mine, other, from_core
        self.to_y, self.from_y = to_y, from_y
        self.psend, self.precv, self.ysend, self.yrecv = psend, precv, ysend, yrecv

    def core_copy(self):
        p = self.p
        return rcopy(self.other, self.from_core, self.psend, self.precv, (p.e, p.shard(0, True)))

    def y_copy(self, k):
        p = self.p
        return rcopy(
            self.to_y.at[k - 1], self.from_y.at[k - 1], self.ysend.at[k - 1], self.yrecv.at[k - 1],
            (p.e, p.shard(k, False)),
        )

    def send(self):
        self.core_copy().start()

    def middle(self):
        p = self.p
        self.core_copy().wait_recv()
        for k in range(1, p.z.ny):
            yy = lax.rem(p.y + k, p.z.ny)
            both = self.mine[yy].astype(F32) + self.from_core[yy].astype(F32)
            self.to_y[k - 1] = both.astype(BF)
            self.y_copy(k).start()

    def total(self):
        p = self.p
        out = self.mine[p.y].astype(F32) + self.from_core[p.y].astype(F32)
        for k in range(1, p.z.ny):
            self.y_copy(k).wait_recv()
            out = out + self.from_y[k - 1].astype(F32)
        return out

    def finish(self):
        self.core_copy().wait_send()
        for k in range(1, self.p.z.ny):
            self.y_copy(k).wait_send()


class Return:
    def __init__(self, place, rows, ret, chunk, cols, send, recv):
        self.p, self.rows, self.ret, self.chunk, self.cols = place, rows, ret, chunk, cols
        self.sems = send, recv

    def copy(self, k, at, away):
        z = self.p.z
        first = self.chunk * z.hn
        return rcopy(
            self.rows.at[pl.ds((position(z, k) - first) * z.sp, z.sp)],
            self.ret.at[aligned(at * z.sp, z.sp, 16), self.cols],
            self.sems[0].at[position(z, k) - first],
            self.sems[1].at[position(z, away) - first],
            (self.p.expert(*k), self.p.s),
        )

    def start_remote(self):
        z = self.p.z
        for k in offsets(z, self.chunk):
            self.copy(k, self.p.e, (-k[0] % z.nz, k[1])).start()

    def start(self):
        z = self.p.z
        self.start_remote()
        if self.chunk == 0:
            self.ret[aligned(self.p.e * z.sp, z.sp, 16), self.cols] = self.rows[0 : z.sp, :]

    def arrive(self):
        for k in offsets(self.p.z, self.chunk):
            self.copy(k, self.p.expert(*k), k).wait_recv()

    def finish(self):
        z = self.p.z
        for k in offsets(z, self.chunk):
            self.copy(k, self.p.e, (-k[0] % z.nz, k[1])).wait_send()


def column_of(row):
    n = row.shape[1]
    return jnp.sum(jnp.where(iota((n, n), 0) == iota((n, n), 1), row, 0.0), axis=1, keepdims=True)


def route_columns(z, routes):
    out = []
    for j in range(2):
        parts = [column_of(routes[m, j : j + 1, :].astype(F32)) for m in range(z.m)]
        out.append(jnp.concatenate(parts, 0).astype(I32))
    return out


def spread(z, s, n):
    row, lane = iota((z.r, z.d), 0), iota((z.r, z.d), 1)
    return jnp.where((lane - s * n == row) & (row < n), 1.0, 0.0).astype(BF)


def split_high(x):
    high = x.astype(BF)
    return high, (x - high.astype(F32)).astype(BF)


def forward_kernel(
    z,
    tokens, dy, routes, counts, wk, wv, wq, wo, wr, vecs, w_in_hbm, w_out_hbm,
    perm, rows_of, dest, place_m, gate_of, source, pick,
    o_toks, o_hid, o_kk, o_vv, o_qq, o_pp, o_ctx, o_mid, o_nrm, o_sd, o_fk, o_fv, o_fq, o_fo, o_small,
    o_ret, o_rfin, o_rpart, ggrows, din, dout,
    qq, pp, ctx, mid, nrm, sd, fk, fv, fq, fo, small, smallg,
    xs, dyr, xr, dyg, xg, act, gp, w_in, w_out, table, bias_id, gwg, gwc, ggc,
    part, rp, ys, yr, fin, ret, rpart, rrp, rys, ryr, wstage, gpart, grp, gys, gyr, gout, gret,
    csem, ssem, gsend, grecv, wsend, wrecv, xsend, xrecv, psend, precv, ysend, yrecv, rsend, rrecv, gsem,
):
    p = Place(z)
    mt, t, d, r, ff = z.mt, z.t, z.d, z.r, z.ff
    half = d // 2
    tiles = ff // 256
    load_in = pltpu.make_async_copy(w_in_hbm, w_in, csem.at[0])
    load_out = pltpu.make_async_copy(w_out_hbm, w_out, csem.at[1])
    spills, waiting = [], {}

    def spill(src, dst, before=None):
        copy = pltpu.make_async_copy(src, dst, ssem.at[len(spills)])
        copy.start()
        spills.append(copy)
        waiting.setdefault(before, []).append(copy)

    toks, hid = gp.at[pl.ds(0, z.m), pl.ds(0, z.g)], gp.at[pl.ds(z.m, z.m), pl.ds(0, z.g)]
    kk, vv = act.at[pl.ds(0, z.m), pl.ds(0, z.g)], act.at[pl.ds(z.m, z.m), pl.ds(0, z.g)]

    whole = spread(z, p.s, r)
    line = iota((16, d), 0)
    n_bias = HEADS * BUCKETS // z.ns
    row = vecs[...].astype(F32)
    first = jnp.broadcast_to(row[:, 0:r], (16, r))
    gains = jnp.where(iota((16, r), 0) == 0, first, jnp.broadcast_to(row[:, r : 2 * r], (16, r)))
    biases = jnp.broadcast_to(row[:, 2 * r : 2 * r + n_bias], (16, n_bias))
    tail = dot(gains.astype(BF), whole)
    bias_row = dot(biases.astype(BF), spread(z, p.s, n_bias)[0:n_bias, :])
    tail = jnp.where(line < 2, tail, jnp.where(line == 2, bias_row, 0.0))
    small[0 : z.e, :] = dot(wr[...], whole).astype(BF)
    small[z.e : z.small, :] = tail.astype(BF)
    p.barrier()

    def rows(ref, size):
        return lambda origin: ref.at[aligned(origin * size, size, 16)]

    g_small = Gather(p, small, lambda o: smallg.at[o], gsend, grecv, 0)
    g_tok = [
        Gather(p, tokens.at[m], lambda o, m=m: toks.at[m, aligned(o * t, t, 16)], gsend, grecv, 1 + m)
        for m in range(z.m)
    ]
    base = 1 + z.m
    groups = d // 256

    def columns_item(own, full, g, item):
        cols = pl.ds(g * 256, 256)
        return SharedGather(
            p, own.at[:, cols], lambda o: full.at[aligned(o * r, r, 16), cols], wsend, wrecv, item
        )

    g_w = [
        [columns_item(own, full, g, 3 * g + i) for i, (own, full) in enumerate(((wk, fk), (wv, fv), (wq, fq)))]
        for g in range(groups)
    ]
    g_o = SharedGather(p, wo, rows(fo, r), wsend, wrecv, 3 * groups)
    for item in [g_small, g_tok[0]] + g_w[0] + g_tok[1:] + sum(g_w[1:], []) + [g_o]:
        item.start()
    load_out.start()
    load_in.start()
    g_dy = Gather(p, dyg.at[p.s], lambda o: dyg.at[o], gsend, grecv, base)

    def exchange(dst, item):
        return Exchange(
            p,
            lambda to: xs.at[aligned(to * z.sp, z.sp, 16)],
            lambda at: dst.at[pl.ds(at * z.sp, z.sp)],
            xsend,
            xrecv,
            item,
        )

    x_dy, x_move = exchange(dyr, 0), exchange(xr, 1)
    smallg[p.s] = small[...]
    for m in range(z.m):
        toks[m, aligned(p.s * t, t, 16), :] = tokens[m]
    own_weights = []
    for i, (own, full) in enumerate(((wk, fk), (wv, fv), (wq, fq), (wo, fo))):
        own_weights.append(pltpu.make_async_copy(own, full.at[aligned(p.s * r, r, 16)], csem.at[6 + i]))
        own_weights[i].start()

    route0, route1 = route_columns(z, routes)
    slot0, slot1 = slot_ids(z, route0, route1)
    hot = (one_hot(z, slot0) + one_hot(z, slot1)).astype(BF)
    mine = aligned(p.e * z.sp, z.sp, 16)

    def to_slots(ref):
        def step(i, carry):
            cols = aligned(i * 256, 256, 256)
            xs[:, cols] = tdot(hot, ref[:, cols]).astype(BF)
            return carry

        lax.fori_loop(0, d // 256, step, 0)

    across, along = lambda k: k[1] == 1, lambda k: k[1] == 0
    even, odd = lambda k: k[0] % 2 == 0, lambda k: k[0] % 2 == 1
    to_slots(dy)
    x_dy.start(across)
    dyr[0 : z.sp, :] = xs[mine, :]

    for m in range(z.m):
        key_pos, prompt = key_layout(z, counts, m, (1, z.g), 1)
        distance = query_position(z, counts, m, p.s) - key_pos
        lane = iota((1, z.g), 1)
        own_block = (lane >= p.s * t) & (lane < (p.s + 1) * t)
        visible = (distance >= 0) & (own_block | (prompt == 1))
        bias_id[m] = jnp.where(visible, bucket_of(z, distance), 2 * BUCKETS)

    for item in (g_small, g_tok[0]):
        item.forward()
    for item in (g_small, g_tok[0]):
        item.arrive()
    x_dy.start(along)
    spill(smallg, o_small)
    sums = smallg[0].astype(F32)
    for b in range(1, z.ns):
        sums = sums + smallg[b].astype(F32)
    gain_one = sums[z.e : z.e + 1, :]
    gain_two = sums[z.e + 1 : z.e + 2, :]
    router = sums.astype(BF)
    for pair in range(z.pairs):
        lanes = slice(pair // 2 * LANES, (pair // 2 + 1) * LANES)
        row = sums[z.e + 2 : z.e + 3, lanes]
        if pair % 2:
            row = pltpu.roll(row, 2 * BUCKETS, 1)
        table[pair : pair + 1, :] = jnp.where(iota((1, LANES), 1) < 2 * BUCKETS, row, MASKED)

    def normalize(m):
        def step(i, carry):
            at = aligned(i * t, t, 16)
            x = toks[m, at, :].astype(F32)
            scale = lax.rsqrt(jnp.mean(x * x, axis=1, keepdims=True) + EPS)
            hid[m, at, :] = (x * scale * gain_one).astype(BF)
            return carry

        lax.fori_loop(0, z.ns, step, 0)

    for copy in own_weights:
        copy.wait()

    def project(g, m):
        cols = slice(g * 256, (g + 1) * 256)
        for item, full, out in zip(g_w[g][:2], (fk, fv), (kk, vv)):
            if m == 0:
                item.arrive()
            out[m, :, cols] = dot(hid[m], full[:, cols]).astype(BF)
        if m == 0:
            g_w[g][2].arrive()
        own = hid[m, aligned(p.s * t, t, 16), :]
        qq[m * t : (m + 1) * t, cols] = (dot(own, fq[:, cols]).astype(BF).astype(F32) * 0.125).astype(BF)


    def in_order(src, dst, h):
        def step(i, carry):
            cols = aligned(i * 256, 256, 256)
            moved = dot(perm[...], src[h * z.hs : (h + 1) * z.hs, cols])
            dst[p.s, h * z.cb : (h + 1) * z.cb, cols] = moved.astype(BF)
            return carry

        lax.fori_loop(0, d // 256, step, 0)

    def send_dy_rows():
        x_dy.arrive()
        in_order(dyr, dyg, 0)
        in_order(dyr, dyg, 1)
        g_dy.start()

    low = iota((t, LANES), 1) < 64

    def attend(m, pair):
        spot = m * z.pairs + pair
        cols = aligned(pair * LANES, LANES, LANES)
        q = qq[aligned(m * t, t, 16), cols]
        zero = jnp.zeros_like(q)
        q_two = jnp.concatenate([jnp.where(low, q, zero), jnp.where(low, zero, q)], 0)
        scores = dot_t(q_two, kk[m, :, cols])
        biases = jnp.broadcast_to(table[pl.ds(pair, 1), :], (t, LANES))
        for side in range(2):
            pieces = []
            for b in range(z.ns):
                at = slice(b * LANES, (b + 1) * LANES)
                bias = jnp.take_along_axis(biases, bias_id[m, :, at] + BUCKETS * side, axis=1)
                pieces.append(scores[side * t : (side + 1) * t, at] + bias)
            s = jnp.concatenate(pieces, 1)
            top = jnp.max(s, axis=1, keepdims=True)
            e = jnp.exp(s - top)
            total = jnp.sum(e, axis=1, keepdims=True)
            pp[spot, side * t : (side + 1) * t, :] = (e * (1.0 / total)).astype(BF)
        two = dot(pp[spot], vv[m, :, cols])
        ctx[aligned(m * t, t, 16), cols] = jnp.where(low, two[:t], two[t:]).astype(BF)

    chain = g_w + [[g_o]]

    def attention(g, m):
        def step(i, carry):
            attend(m, g * 2 + i)
            return carry

        lax.fori_loop(0, 2, step, 0, unroll=2)

    for item in chain[0]:
        item.forward()
    normalize(0)
    for item in chain[0]:
        item.forward_rest()
    for item in g_tok[1:]:
        item.forward()
    for g in range(groups):
        for m in range(z.m):
            if g == 0 and m > 0:
                g_tok[m].arrive()
                normalize(m)
                spill(toks, o_toks, "gp")
                spill(hid, o_hid, "gp")
            project(g, m)
            if m == 0 and g > 0 or m == 1 and g == 0:
                for item in chain[g + 1]:
                    item.forward()
            if g == 1 and m == 0:
                send_dy_rows()
            attention(g, m)
            if m == z.m - 1:
                for item in chain[g + 1]:
                    item.forward_rest()
    g_o.arrive()

    def output(i, carry):
        cols = aligned(i * 256, 256, 256)
        mid[:, cols] = dot(ctx[...], fo[:, cols])
        return carry

    lax.fori_loop(0, d // 256, output, 0)
    for m in range(z.m):
        at = slice(m * t, (m + 1) * t)
        x = mid[at, :] + tokens[m].astype(F32)
        mid[at, :] = x
        scale = lax.rsqrt(jnp.mean(x * x, axis=1, keepdims=True) + EPS)
        nrm[at, :] = (x * scale * gain_two).astype(BF)
    logits = dot_t(nrm[...], router)
    lane = iota((mt, z.small), 1)
    pick0 = jnp.sum(jnp.where(lane == route0, logits, 0.0), axis=1, keepdims=True)
    pick1 = jnp.sum(jnp.where(lane == route1, logits, 0.0), axis=1, keepdims=True)
    top = jnp.maximum(pick0, pick1)
    e0, e1 = jnp.exp(pick0 - top), jnp.exp(pick1 - top)
    gate0, gate1 = e0 / (e0 + e1), e1 / (e0 + e1)
    lane = iota((mt, LANES), 1)
    sd[...] = jnp.where(
        lane == 0, slot0, jnp.where(lane == 1, slot1, jnp.where(lane == 2, gate0, jnp.where(lane == 3, gate1, 0.0)))
    )
    gate_row = jnp.sum(one_hot(z, slot0) * gate0 + one_hot(z, slot1) * gate1, axis=0, keepdims=True)
    high = gate_row.astype(BF).astype(F32)
    is_high = iota((2 * z.n16, 1), 0) < z.n16
    gates = (dest[...].astype(F32) * jnp.where(is_high, high, gate_row - high)).astype(BF)
    gates = dot(gates, place_m[...]).astype(BF)
    x_dy.finish()
    to_slots(nrm)
    xs[:, :LANES] = (xs[:, :LANES].astype(F32) + tdot(rows_of[...], gates)).astype(BF)
    x_move.start(even)
    xr[0 : z.sp, :] = xs[mine, :]

    load_out.wait()

    def expert_rows(ref, h, l, cols):
        return ref[:, aligned(h * z.cb + l * z.cr, z.cr, 16), cols].reshape(z.ns * z.cr, -1)

    def gradient(h):
        def step(l, carry):
            g = dot_t(expert_rows(dyg, h, l, slice(None)), w_out[l])
            gp[:, aligned(h * z.cb + l * z.cr, z.cr, 16), :] = g.astype(BF).reshape(z.ns, z.cr, ff)
            return carry

        lax.fori_loop(0, z.el, step, 0)

    def gather_of(h):
        at = pl.ds(h * z.cb, z.cb)
        return (
            Gather(p, gwg.at[p.s, h], lambda o: gwg.at[o, h], gsend, grecv, base + 1 + 2 * h),
            Gather(p, xg.at[p.s, at], lambda o: xg.at[o, at], gsend, grecv, base + 2 + 2 * h),
        )

    gathers = [gather_of(h) for h in range(2)]

    def distribute(h):
        x_move.arrive((even, odd)[h])
        if h == 0:
            x_move.start(odd)
        gwg[p.s, h] = dot(gate_of[...], xr[h * z.hs : (h + 1) * z.hs, :LANES]).astype(BF)
        gathers[h][0].start()
        in_order(xr, xg, h)
        gathers[h][1].start()

    def hand_on(h):
        for item in gathers[h]:
            item.forward()

    def collect(h):
        for item in gathers[h]:
            item.arrive()
        for b in range(z.ns):
            wide = dot(source[...], gwg[b, h]) * pick[...].astype(F32)
            gwc[b] = jnp.sum(wide, axis=1, keepdims=True)

    def activate(h):
        def step(i, carry):
            l, tile = lax.div(i, tiles), lax.rem(i, tiles)
            at = aligned(tile * 256, 256, 256)
            local = aligned(l * z.cr, z.cr, 16)
            at_rows = aligned(h * z.cb + l * z.cr, z.cr, 16)
            x = dot(expert_rows(xg, h, l, slice(None)), w_in[l, :, at])
            g = expert_rows(gp, h, l, at).astype(F32)
            gate = gwc[:, local, :].reshape(z.ns * z.cr, 1)
            x2 = x * x
            th = jnp.tanh(x * (GELU_A + (GELU_A * GELU_B) * x2))
            hx = 0.5 * x
            up = 1.0 + th
            a = hx * up
            act[:, at_rows, at] = a.astype(BF).reshape(z.ns, z.cr, 256)
            slope = 0.5 * up + hx * (1.0 - th * th) * (GELU_A + (3.0 * GELU_A * GELU_B) * x2)
            gp[:, at_rows, at] = (g * gate * slope).astype(BF).reshape(z.ns, z.cr, 256)
            toward = jnp.sum(a * g, axis=1, keepdims=True).reshape(z.ns, z.cr, 1)
            ggc[:, at_rows, :] = toward + jnp.where(tile == 0, 0.0, ggc[:, at_rows, :])
            return carry

        lax.fori_loop(0, z.el * tiles, step, 0, unroll=z.el * tiles)

        def gate_dy(l, carry):
            at_rows = aligned(h * z.cb + l * z.cr, z.cr, 16)
            gate = gwc[:, aligned(l * z.cr, z.cr, 16), :]
            dyg[:, at_rows, :] = (dyg[:, at_rows, :].astype(F32) * gate).astype(BF)
            return carry

        lax.fori_loop(0, z.el, gate_dy, 0)

    def unit(u):
        h, cols = u // 2, pl.ds((u % 2) * half, half)
        return (
            Scatter(
                p, part.at[u, p.c], part.at[u, 1 - p.c], rp.at[u], ys.at[u], yr.at[u],
                psend.at[u], precv.at[u], ysend.at[u], yrecv.at[u],
            ),
            Return(p, fin.at[u], ret, h, cols, rsend.at[u], rrecv.at[u]),
        )

    units = [unit(u) for u in range(4)]
    results = [
        Scatter(
            p, rpart.at[u, p.c], rpart.at[u, 1 - p.c], rrp.at[u], rys.at[u], ryr.at[u],
            psend.at[4 + u], precv.at[4 + u], ysend.at[4 + u], yrecv.at[4 + u],
        )
        for u in range(2)
    ]

    def products(ref, weight, transposed, dst, h):
        def step(l, carry):
            rows = expert_rows(ref, h, l, slice(None))
            out = (dot_t(rows, weight[l]) if transposed else dot(rows, weight[l])).astype(BF)
            for b in range(z.ns):
                for c in range(2):
                    block = out[b * z.cr : (b + 1) * z.cr, c * half : (c + 1) * half]
                    dst[2 * h + c, b % 2, b // 2, aligned(l * z.cr, z.cr, 16), :] = block
            return carry

        lax.fori_loop(0, z.el, step, 0)

    def stage_a(h):
        products(gp, w_in, True, part, h)
        units[2 * h][0].send()
        units[2 * h + 1][0].send()

    def stage_b(u):
        units[u][0].middle()

    def stage_c(u):
        fin[u] = tdot(perm[...], units[u][0].total().astype(BF)).astype(BF)
        units[u][1].start()

    g_scatter = Scatter(
        p, gpart.at[p.c], gpart.at[1 - p.c], grp, gys, gyr, gsem.at[0, 0], gsem.at[1, 0], gsem.at[2], gsem.at[3]
    )

    def toward_a():
        for b in range(z.ns):
            for h in range(2):
                col = ggc[b, h * z.cb : (h + 1) * z.cb, :]
                high = col.astype(BF).astype(F32)
                put = pick[...].astype(F32)
                top = tdot(source[...], (high * put).astype(BF))
                rest = tdot(source[...], ((col - high) * put).astype(BF))
                both = jnp.where(iota(top.shape, 0) < z.n16, top, rest)
                gpart[b % 2, b // 2, h * 2 * z.n16 : (h + 1) * 2 * z.n16, :] = both.astype(BF)
        g_scatter.send()

    def toward_copy(k):
        back = (-k[0] % z.nz, k[1])
        return rcopy(
            gout.at[k[0] % 2], gret.at[position(z, back)], gsem.at[4, position(z, k)], gsem.at[5, position(z, back)],
            (p.expert(*k), p.s),
        )

    def toward_c():
        total = g_scatter.total()
        for h in range(2):
            first = total[h * 2 * z.n16 : h * 2 * z.n16 + z.n16]
            value = first + total[h * 2 * z.n16 + z.n16 : (h + 1) * 2 * z.n16]
            high, rest = split_high(value)
            gout[h, 0 : z.n16, :] = high
            gout[h, z.n16 : 2 * z.n16, :] = rest
        for k in offsets(z):
            toward_copy(k).start()
        gret[0] = gout[0]

    def toward_d():
        for k in offsets(z):
            toward_copy((-k[0] % z.nz, k[1])).wait_recv()
        line = iota((2 * z.n16, LANES), 0)
        out = jnp.zeros((2 * z.n16, LANES), F32)
        for k in [(0, 0)] + offsets(z):
            back = (-k[0] % z.nz, k[1])
            at = position(z, back) - (k[0] % 2) * z.hn
            got = gret[position(z, k)].astype(F32)
            rank = p.expert(*k)
            out = jnp.where(line == rank, got[at : at + 1, :], out)
            out = jnp.where(line == z.n16 + rank, got[z.n16 + at : z.n16 + at + 1, :], out)
        ggrows[...] = out.astype(BF)
        for k in offsets(z):
            toward_copy(k).wait_send()

    def both(ref, l, cols):
        return jnp.concatenate([expert_rows(ref, h, l, cols) for h in range(2)], 0)

    stores = []

    def weight_grad(n, left, right, out, l):
        if n >= 2:
            stores[n - 2].wait()

        def step(i, carry):
            at = aligned(i * 256, 256, 256)
            wstage[n % 2, :, at] = tdot(both(left, l, slice(None)), both(right, l, at)).astype(BF)
            return carry

        lax.fori_loop(0, d // 256, step, 0)
        copy = pltpu.make_async_copy(wstage.at[n % 2], out.at[l], csem.at[2 + n])
        copy.start()
        stores.append(copy)

    def result_a(h):
        products(act, w_out, False, rpart, h)
        for u in (2 * h, 2 * h + 1):
            if h == 0:
                results[u].send()
            else:
                spill(rpart.at[u], o_rpart.at[u - 2])

    def result_c(u):
        units[u][1].finish()
        fin[u] = tdot(perm[...], results[u].total().astype(BF)).astype(BF)
        spill(fin.at[u], o_rfin.at[u])

    spill(kk, o_kk, "act")
    spill(vv, o_vv, "act")
    g_dy.forward()
    distribute(0)
    g_dy.arrive()
    for copy in waiting["gp"]:
        copy.wait()
    for item in g_tok:
        item.finish()
    gradient(0)
    gradient(1)
    hand_on(0)
    distribute(1)
    load_in.wait()
    for copy in waiting["act"]:
        copy.wait()
    g_dy.finish()
    collect(0)
    activate(0)
    stage_a(0)
    stage_b(0)
    stage_b(1)
    hand_on(1)
    result_a(0)
    collect(1)
    activate(1)
    stage_a(1)
    toward_a()
    stage_b(2)
    stage_b(3)
    g_scatter.middle()
    stage_c(0)
    stage_c(1)
    results[0].middle()
    results[1].middle()
    result_a(1)
    for src, dst in (
        (sd, o_sd), (mid, o_mid), (nrm, o_nrm), (ctx, o_ctx), (fo, o_fo), (qq, o_qq), (pp, o_pp), (fk, o_fk), (fv, o_fv),
        (fq, o_fq),
    ):
        spill(src, dst)
    weight_grad(0, act, dyg, dout, 0)
    stage_c(2)
    weight_grad(1, act, dyg, dout, 1)
    stage_c(3)
    toward_c()
    weight_grad(2, xg, gp, din, 0)
    result_c(0)
    weight_grad(3, xg, gp, din, 1)
    result_c(1)
    toward_d()
    for u in range(4):
        units[u][1].arrive()
    spill(ret, o_ret)
    for item in [g_small] + sum(g_w, []) + [g_o] + list(gathers[0]) + list(gathers[1]):
        item.finish()
    x_move.finish()
    g_scatter.finish()
    for u in (2, 3):
        units[u][1].finish()
    for scatter, _ in units:
        scatter.finish()
    for scatter in results:
        scatter.finish()
    for copy in waiting[None] + stores[2:]:
        copy.wait()


ANY = pl.BlockSpec(memory_space=pl.ANY)


def forward(z, *inputs):
    def bf(*shape):
        return jax.ShapeDtypeStruct(shape, BF)

    def f32(*shape):
        return jax.ShapeDtypeStruct(shape, F32)

    def vm(x):
        return pltpu.VMEM(x.shape, x.dtype)

    dma = pltpu.SemaphoreType.DMA
    half, ny, nb = z.d // 2, z.ny, 2 * z.n16
    kept = (
        bf(z.m, z.g, z.d), bf(z.m, z.g, z.d), bf(z.m, z.g, z.d), bf(z.m, z.g, z.d), bf(z.mt, z.d),
        bf(z.m * z.pairs, 2 * z.t, z.g), bf(z.mt, z.d), f32(z.mt, z.d), bf(z.mt, z.d), f32(z.mt, LANES),
        bf(z.d, z.d), bf(z.d, z.d), bf(z.d, z.d), bf(z.d, z.d),
    )
    smallg = bf(z.ns, z.small, z.d)
    ret, rpart, rfin = bf(z.slots, z.d), bf(4, 2, ny, z.cb, half), bf(4, z.hs, half)
    outs = kept + (smallg, ret, bf(2, z.hs, half), bf(2, 2, ny, z.cb, half), bf(nb, LANES), bf(z.el, z.d, z.ff), bf(z.el, z.ff, z.d))
    rows = bf(z.ns, z.blk, z.d)
    scratch = [vm(x) for x in kept[4:]]
    scratch += [vm(bf(z.small, z.d)), vm(smallg)]
    scratch += [vm(ret)] * 3 + [vm(rows)] * 2 + [vm(bf(z.ns, z.blk, z.ff))] * 2
    scratch += [vm(bf(z.el, z.d, z.ff)), vm(bf(z.el, z.ff, z.d))]
    scratch += [pltpu.VMEM((8, LANES), F32), pltpu.VMEM((z.m, z.t, z.g), I32)]
    scratch += [vm(bf(z.ns, 2, nb, LANES)), vm(f32(z.ns, z.cb, 1)), vm(f32(z.ns, z.blk, 1))]
    shares = [vm(rpart), vm(bf(4, ny, z.cb, half)), vm(bf(4, ny - 1, z.cb, half)), vm(bf(4, ny - 1, z.cb, half))]
    scratch += shares + [vm(rfin), vm(ret)] + [vm(rpart), vm(bf(2, ny, z.cb, half)), vm(bf(2, ny - 1, z.cb, half)), vm(bf(2, ny - 1, z.cb, half))]
    scratch += [vm(bf(2, z.d, z.d))]
    scratch += [vm(bf(2, ny, 2 * nb, LANES)), vm(bf(ny, 2 * nb, LANES))]
    scratch += [vm(bf(ny - 1, 2 * nb, LANES))] * 2 + [vm(bf(2, nb, LANES)), vm(bf(z.ne, nb, LANES))]
    n_items, n_weights = 1 + z.m + 5, 3 * (z.d // 256) + 1
    scratch += [dma((10,)), dma((24,)), dma((n_items, z.ns)), dma((n_items, z.ns)),
        dma((n_weights, 4 * ny)), dma((n_weights, z.ns, 2)), dma((2, z.ne)), dma((2, z.ne))]
    scratch += [dma((8,))] * 2 + [dma((8, ny))] * 2 + [dma((4, z.hn))] * 2 + [dma((6, z.ne))]
    return pl.pallas_call(
        functools.partial(forward_kernel, z),
        out_shape=outs,
        in_specs=[VMEM] * 3 + [SMEM] + [ANY] * 4 + [VMEM] * 2 + [ANY] * 2 + [VMEM] * 7,
        out_specs=[ANY] * 18 + [VMEM] + [ANY] * 2,
        scratch_shapes=scratch,
        compiler_params=pltpu.CompilerParams(
            collective_id=0, has_side_effects=True, vmem_limit_bytes=63 * 2**20
        ),
        name="forward",
    )(*inputs)


class Reduce:
    def __init__(self, place, part, from_core, to_y, from_y, to_x, from_x, summed, near_in, mid, mid_in, done, sems):
        self.p, self.part, self.from_core, self.done, self.sems = place, part, from_core, done, sems
        self.to_y, self.from_y, self.to_x, self.from_x = to_y, from_y, to_x, from_x
        self.summed, self.near_in, self.mid, self.mid_in = summed, near_in, mid, mid_in
        self.rows = done.shape[0] // 4
        self.x, zz = lax.rem(place.e, 2), lax.div(place.e, 2)
        self.side = lax.rem(zz, 2)
        self.near_at = ((zz + 1 - 2 * self.side) * 2 + self.x, place.s)

    def x_rows(self, x):
        return aligned(x * (2 * self.rows), 2 * self.rows, 16)

    def side_rows(self, side):
        return aligned(side * self.rows, self.rows, 16)

    def done_rows(self, side):
        return aligned((self.x * 2 + side) * self.rows, self.rows, 16)

    def hop(self, n, src, dst, to):
        return rcopy(src, dst, self.sems.at[0, n], self.sems.at[1, n], to)

    def copy(self, n, out=True):
        p = self.p
        if n == 0:
            return self.hop(0, self.part.at[1 - p.c], self.from_core, (p.e, p.shard(0, True)))
        if n == 2:
            return self.hop(2, self.to_x, self.from_x, (p.expert(0, 1), p.s))
        if n == 3:
            return self.hop(3, self.summed.at[self.side_rows(1 - self.side)], self.near_in, self.near_at)
        if n == 4:
            return self.hop(4, self.mid, self.mid_in, (p.expert(2, 0), p.s))
        if n == 5:
            block = self.done.at[self.done_rows(self.side if out else 1 - self.side)]
            return self.hop(5, block, block, self.near_at)
        block = self.done.at[self.x_rows(self.x if out else 1 - self.x)]
        return self.hop(6, block, block, (p.expert(0, 1), p.s))

    def copy_y(self, k):
        p = self.p
        return self.hop(6 + k, self.to_y.at[k - 1], self.from_y.at[k - 1], (p.e, p.shard(k, False)))

    def chip(self, y, rows=slice(None)):
        return self.part[self.p.c, y, rows, :].astype(F32) + self.from_core[y, rows, :].astype(F32)

    def step(self, n):
        p, ny = self.p, self.p.z.ny
        if n == 2:
            for k in range(1, ny):
                self.copy_y(k).wait_recv()
        elif n > 0:
            self.copy(n - 1, False).wait_recv()
        if n == 1:
            for k in range(1, ny):
                self.to_y[k - 1] = self.chip(lax.rem(p.y + k, ny)).astype(BF)
                self.copy_y(k).start()
        elif n == 2:
            def whole(x):
                out = self.chip(p.y, self.x_rows(x))
                for k in range(1, ny):
                    out = out + self.from_y[k - 1, self.x_rows(x), :].astype(F32)
                return out.astype(BF)

            self.to_x[...] = whole(1 - self.x)
            self.summed[...] = whole(self.x)
        elif n == 3:
            self.summed[...] = (self.summed[...].astype(F32) + self.from_x[...].astype(F32)).astype(BF)
        elif n == 4:
            own = self.summed[self.side_rows(self.side), :].astype(F32)
            self.mid[...] = (own + self.near_in[...].astype(F32)).astype(BF)
        elif n == 5:
            out = self.mid[...].astype(F32) + self.mid_in[...].astype(F32)
            self.done[self.done_rows(self.side), :] = out.astype(BF)
        if n != 1 and n < 7:
            self.copy(n).start()

    def finish(self):
        for n in (0, 2, 3, 4, 5, 6):
            self.copy(n).wait_send()
        for k in range(1, self.p.z.ny):
            self.copy_y(k).wait_send()


class SmallReduce:
    def __init__(self, place, part, from_core, to_y, from_y, own, other, sems):
        self.p, self.part, self.from_core = place, part, from_core
        self.to_y, self.from_y, self.own, self.other, self.sems = to_y, from_y, own, other, sems
        zz = lax.div(place.e, 2)
        near = ((zz + 1 - 2 * lax.rem(zz, 2)) * 2 + lax.rem(place.e, 2), place.s)
        self.partners = [(place.expert(0, 1), place.s), near, (place.expert(2, 0), place.s)]

    def copy(self, n):
        p = self.p
        sems = self.sems.at[0, n], self.sems.at[1, n]
        if n == 0:
            return rcopy(self.part.at[1 - p.c], self.from_core, *sems, (p.e, p.shard(0, True)))
        return rcopy(self.own.at[n - 2], self.other.at[n - 2], *sems, self.partners[n - 2])

    def copy_y(self, k):
        p = self.p
        return rcopy(
            self.to_y.at[k - 1], self.from_y.at[k - 1], self.sems.at[0, 4 + k], self.sems.at[1, 4 + k],
            (p.e, p.shard(k, False)),
        )

    def step(self, n):
        p, ny = self.p, self.p.z.ny
        if n == 0:
            self.copy(0).start()
        elif n == 1:
            self.copy(0).wait_recv()
            for k in range(1, ny):
                y = lax.rem(p.y + k, ny)
                self.to_y[k - 1] = (self.part[p.c, y].astype(F32) + self.from_core[y].astype(F32)).astype(BF)
                self.copy_y(k).start()
        elif n == 2:
            out = self.part[p.c, p.y].astype(F32) + self.from_core[p.y].astype(F32)
            for k in range(1, ny):
                self.copy_y(k).wait_recv()
                out = out + self.from_y[k - 1].astype(F32)
            self.own[0] = out.astype(BF)
            self.copy(2).start()
        else:
            self.copy(n - 1).wait_recv()
            out = self.own[n - 3].astype(F32) + self.other[n - 3].astype(F32)
            if n == 5:
                return out
            self.own[n - 2] = out.astype(BF)
            self.copy(n).start()

    def finish(self):
        for n in (0, 2, 3, 4):
            self.copy(n).wait_send()
        for k in range(1, self.p.z.ny):
            self.copy_y(k).wait_send()


GROUPS = ((0, 1), (2, 3), (4,), (5,))


def backward_kernel(
    z,
    dy, counts, routes, dest, place_m, perm, ggrows,
    i_toks, i_hid, i_kk, i_vv, i_qq, i_pp, i_ctx, i_mid, i_nrm, i_sd, i_fk, i_fv, i_fq, i_fo, i_small, i_ret, i_rfin, i_rpart,
    mixed, dtok, done_o, done_0, done_1, done_2, done_3, drouter, dvecs,
    toks, hid, kk, vv, qq, pp, ctx, mid, nrm, sd, fk, fv, fq, fo, smallg, ret, retr,
    fin, rmine, rp, rys, ryr, gctx, gqb, gkb, gvb, gmid, lower, edge_id, edge_ok, tab, gain_rows,
    red_o, red_0, red_1, red_2, red_3,
    gpart, grp, gys, gyr, sbuf, small_refs,
    csem, rr1, rr2, rs1, rs2, rs3, rs4,
    gp1, gp2, gy1, gy2,
):
    p = Place(z)
    t, d, mt = z.t, z.d, z.mt
    half = d // 2
    loads = {}

    def load(src, dst, name):
        loads[name] = pltpu.make_async_copy(src, dst, csem.at[len(loads)])
        loads[name].start()

    load(i_sd, sd, "sd")
    load(i_ret, ret, "ret")
    load(i_small, smallg, "small")
    load(i_mid, mid, "mid")
    load(i_nrm, nrm, "nrm")
    load(i_ctx, ctx, "ctx")
    load(i_fo, fo, "fo")
    for u in range(2):
        load(i_rpart.at[u, p.c], rmine.at[u], ("part", u))
    load(i_qq, qq, "qq")
    load(i_vv, vv, "vv")
    load(i_kk, kk, "kk")
    load(i_pp, pp, "pp")
    load(i_hid, hid, "hid")
    load(i_fk, fk, "fk")
    load(i_fv, fv, "fv")
    load(i_fq, fq, "fq")
    load(i_toks, toks, "toks")
    p.barrier()

    returns, halves = [], []
    for u in range(4):
        h, cols = u // 2, pl.ds((u % 2) * half, half)
        src = i_rfin.at[u] if h == 0 else fin.at[u - 2]
        returns.append(Return(p, src, retr, h, cols, rr1.at[u], rr2.at[u]))
        if h == 0:
            returns[u].start_remote()
            load(i_rfin.at[u, pl.ds(0, z.sp)], retr.at[aligned(p.e * z.sp, z.sp, 16), cols], ("r", u))
    for u in range(2):
        halves.append(
            Scatter(
                p, rmine.at[u], i_rpart.at[u, 1 - p.c], rp.at[u], rys.at[u], ryr.at[u],
                rs1.at[u], rs2.at[u], rs3.at[u], rs4.at[u],
            )
        )
        halves[u].send()

    def result_b(u):
        loads["part", u].wait()
        halves[u].middle()

    def result_c(u):
        fin[u] = tdot(perm[...], halves[u].total().astype(BF)).astype(BF)
        returns[2 + u].start_remote()

    route0, route1 = route_columns(z, routes)
    loads["sd"].wait()
    slot0, slot1 = sd[:, 0:1], sd[:, 1:2]
    gate0, gate1 = sd[:, 2:3], sd[:, 3:4]
    hot0, hot1 = one_hot(z, slot0).astype(BF), one_hot(z, slot1).astype(BF)
    hot = hot0 + hot1

    def toward(hots):
        wide = dot(dot_t(hots, dest[...]).astype(BF), ggrows[...]) * dot(hots, place_m[...])
        return jnp.sum(wide, axis=1, keepdims=True)

    toward0, toward1 = toward(hot0), toward(hot1)
    mean = gate0 * toward0 + gate1 * toward1
    lane = iota((mt, z.small), 1)
    glog = jnp.where(lane == route0, gate0 * (toward0 - mean), 0.0)
    glog = (glog + jnp.where(lane == route1, gate1 * (toward1 - mean), 0.0)).astype(BF)
    result_b(0)
    loads["small"].wait()
    sums = smallg[0].astype(F32)
    for b in range(1, z.ns):
        sums = sums + smallg[b].astype(F32)
    gain_one = sums[z.e : z.e + 1, :]
    gain_two = sums[z.e + 1 : z.e + 2, :]
    router = sums.astype(BF)
    loads["ret"].wait()
    gnorm = dot(glog, router) + dot(hot, ret[...])
    loads["mid"].wait()
    x = mid[...]
    scale = lax.rsqrt(jnp.mean(x * x, axis=1, keepdims=True) + EPS)
    xh = x * scale
    gain_rows[1:2, :] = jnp.sum(gnorm * xh, axis=0, keepdims=True)
    gy = gnorm * gain_two
    gm = dy[...].astype(F32) + scale * (gy - xh * jnp.mean(gy * xh, axis=1, keepdims=True))
    gmid[...] = gm
    gattn = gm.astype(BF)
    loads["nrm"].wait()
    sbuf[...] = tdot(glog, nrm[...])

    reductions = [
        Reduce(p, *refs[:-1], done, refs[-1])
        for refs, done in ((red_0, done_0), (red_1, done_1), (red_2, done_2), (red_3, done_3), (red_o, done_o))
    ]
    parts = [red_0[0], red_1[0], red_2[0], red_3[0], red_o[0]]

    def stage(u, n):
        reductions[u].step(n)

    def put(u, first, value):
        value = value.astype(BF)
        for b in range(z.ns):
            parts[u][b % 2, b // 2, :, first : first + value.shape[1]] = value[b * z.r : (b + 1) * z.r]

    loads["ctx"].wait()
    for i in range(d // 256):
        put(4, i * 256, tdot(ctx[...], gattn[:, i * 256 : (i + 1) * 256]))
    stage(4, 0)
    loads["fo"].wait()
    for i in range(d // 256):
        cols = slice(i * 256, (i + 1) * 256)
        gctx[:, cols] = dot_t(gattn, fo[cols, :]).astype(BF)

    tab[...] = jnp.zeros_like(tab)
    lane = iota((1, LANES), 1)
    starts = jnp.where(lane <= 16, lane, 0)
    for i, edge in enumerate(BUCKET_EDGES):
        starts = jnp.where(lane == 17 + i, edge, starts)
    for m in range(z.m):
        key_pos, _ = key_layout(z, counts, m, (z.g, 1), 0)
        lower[m] = jnp.where(key_pos <= iota((z.g, z.far), 1), 1.0, 0.0).astype(BF)
        at = query_position(z, counts, m, p.s) - starts
        ok = (at >= 0) & (lane < BUCKETS)
        edge_id[m] = jnp.where(ok, at, 0)
        edge_ok[m] = jnp.where(ok, 1.0, 0.0)
    low = iota((t, LANES), 1) < 64

    def attend_back(i, unit):
        m = lax.rem(i, z.m)
        pair = unit
        cols = aligned(pair * LANES, LANES, LANES)
        rows = aligned(m * t, t, 16)
        q, g = qq[rows, cols], gctx[rows, cols]
        zero = jnp.zeros_like(q)
        q_two = jnp.concatenate([jnp.where(low, q, zero), jnp.where(low, zero, q)], 0)
        g_two = jnp.concatenate([jnp.where(low, g, zero), jnp.where(low, zero, g)], 0)
        probs = pp[m * z.pairs + pair]
        pf = probs.astype(F32)
        gp = dot_t(g_two, vv[m, :, cols])
        gs = (pf * (gp - jnp.sum(pf * gp, axis=1, keepdims=True))).astype(BF)
        two = dot(gs, kk[m, :, cols])
        gqb[rows, cols] = (jnp.where(low, two[:t], two[t:]) * 0.125).astype(BF)
        gkb[m, :, cols] = tdot(gs, q_two).astype(BF)
        gvb[m, :, cols] = tdot(probs, g_two).astype(BF)
        total = dot(gs, lower[m])
        for side in range(2):
            found = jnp.zeros((t, LANES), F32)
            for b in range(z.far // LANES):
                at = edge_id[m] - b * LANES
                inside = (at >= 0) & (at < LANES)
                got = jnp.take_along_axis(
                    total[side * t : (side + 1) * t, b * LANES : (b + 1) * LANES], jnp.where(inside, at, 0), axis=1
                )
                found = jnp.where(inside, got, found)
            found = jnp.sum(found * edge_ok[m], axis=0, keepdims=True)
            row = pl.ds(pair * 2 + side, 1)
            tab[row, :] = tab[row, :] + found
        return unit

    def attention(pair):
        lax.fori_loop(0, z.m, attend_back, pair, unroll=2)

    def own_hidden():
        return jnp.concatenate([hid[m, aligned(p.s * t, t, 16), :] for m in range(z.m)], 0)

    def weight_grads(u):
        n = len(GROUPS[u]) * LANES
        cols = slice(GROUPS[u][0] * LANES, GROUPS[u][0] * LANES + n)
        put(u, 0, tdot(own_hidden(), gqb[:, cols]))
        every = hid[...].reshape(z.m * z.g, d)
        put(u, n, tdot(every, gkb[:, :, cols].reshape(z.m * z.g, n)))
        put(u, 2 * n, tdot(every, gvb[:, :, cols].reshape(z.m * z.g, n)))

    grads = [
        Scatter(
            p, gpart.at[m, p.c], gpart.at[m, 1 - p.c], grp.at[m], gys.at[m], gyr.at[m],
            gp1.at[m], gp2.at[m], gy1.at[m], gy2.at[m],
        )
        for m in range(z.m)
    ]

    def hidden_grads(m):
        x = toks[m].astype(F32)
        scale = lax.rsqrt(jnp.mean(x * x, axis=1, keepdims=True) + EPS)
        for i in range(d // 256):
            cols = slice(i * 256, (i + 1) * 256)
            gh = dot_t(gkb[m], fk[cols, :]) + dot_t(gvb[m], fv[cols, :])
            own = dot_t(gqb[m * t : (m + 1) * t, :], fq[cols, :])
            for b in range(z.ns):
                rows = slice(b * t, (b + 1) * t)
                part = gh[rows] + jnp.where(p.s == b, 1.0, 0.0) * own
                gpart[m, b % 2, b // 2, :, cols] = part.astype(BF)
                row = jnp.sum(part * (toks[m, rows, cols].astype(F32) * scale[rows]), axis=0, keepdims=True)
                if m == 0 and b == 0:
                    gain_rows[0:1, cols] = row
                else:
                    gain_rows[0:1, cols] = gain_rows[0:1, cols] + row

    def token_grads(m):
        gh = grads[m].total()
        rows = slice(m * t, (m + 1) * t)
        x = toks[m, aligned(p.s * t, t, 16), :].astype(F32)
        scale = lax.rsqrt(jnp.mean(x * x, axis=1, keepdims=True) + EPS)
        xh = x * scale
        gy = gh * gain_one
        dtok[rows, :] = gmid[rows, :] + scale * (gy - xh * jnp.mean(gy * xh, axis=1, keepdims=True))

    small_sum = SmallReduce(p, *small_refs)

    def small_step(n):
        if n:
            return small_sum.step(n)
        tabs = tab[...]
        tabs = tabs - pltpu.roll(tabs, LANES - 1, 1)
        tabs = jnp.where(iota(tabs.shape, 1) < BUCKETS, tabs, 0.0)
        row = iota(sbuf.shape, 0)
        out = sbuf[...]
        out = jnp.where(row == z.e, gain_rows[0:1, :], out)
        out = jnp.where(row == z.e + 1, gain_rows[1:2, :], out)
        sbuf[...] = out
        per = LANES // BUCKETS
        for c in range(HEADS // per):
            piece = tabs[c * per : c * per + 1, :]
            for j in range(1, per):
                piece = piece + pltpu.roll(tabs[c * per + j : c * per + j + 1, :], j * BUCKETS, 1)
            sbuf[z.e + 2 : z.e + 3, c * LANES : (c + 1) * LANES] = piece
        every = sbuf[...].astype(BF)
        tail = every[z.e : z.small, :]
        for b in range(z.ns):
            block = dot_t(every, spread(z, b, z.r))
            biases = dot_t(tail, spread(z, b, HEADS * BUCKETS // z.ns))
            low_rows = jnp.where(iota(biases.shape, 0) == 2, biases, block[z.e : z.small])
            small_refs[0][b % 2, b // 2, 0 : z.e, :] = block[0 : z.e].astype(BF)
            small_refs[0][b % 2, b // 2, z.e : z.small, :] = low_rows.astype(BF)
        small_sum.step(0)

    def finish_mixed():
        for u in range(4):
            returns[u].arrive()
        for u in range(2):
            loads["r", u].wait()
        for m in range(z.m):
            rows = slice(m * t, (m + 1) * t)
            first, second = dot(hot0[rows], retr[...]), dot(hot1[rows], retr[...])
            mixed[rows, :] = (mid[rows, :] + gate0[rows] * first + gate1[rows] * second).astype(BF)

    for name in ("qq", "vv", "kk", "pp"):
        loads[name].wait()
    attention(0)
    stage(4, 1)
    attention(1)
    loads["hid"].wait()
    weight_grads(0)
    stage(0, 0)
    result_c(0)
    attention(2)
    stage(0, 1)
    attention(3)
    stage(4, 2)
    weight_grads(1)
    stage(1, 0)
    attention(4)
    stage(1, 1)
    weight_grads(2)
    stage(2, 0)
    stage(4, 3)
    attention(5)
    stage(2, 1)
    weight_grads(3)
    stage(3, 0)
    stage(0, 2)
    stage(4, 4)
    for name in ("fk", "fv", "fq", "toks"):
        loads[name].wait()
    hidden_grads(0)
    grads[0].send()
    stage(3, 1)
    stage(4, 5)
    stage(0, 3)
    hidden_grads(1)
    grads[1].send()
    small_step(0)
    stage(1, 2)
    stage(4, 6)
    stage(0, 4)
    small_step(1)
    result_b(1)
    grads[0].middle()
    grads[1].middle()
    stage(2, 2)
    stage(1, 3)
    stage(0, 5)
    stage(3, 2)
    small_step(2)
    stage(2, 3)
    stage(1, 4)
    stage(3, 3)
    stage(0, 6)
    small_step(3)
    stage(2, 4)
    stage(1, 5)
    stage(3, 4)
    result_c(1)
    small_step(4)
    stage(2, 5)
    stage(1, 6)
    stage(3, 5)
    token_grads(0)
    out = small_step(5)
    drouter[...] = out[0 : z.e, :]
    dvecs[...] = out[z.e : z.small, :]
    stage(2, 6)
    stage(3, 6)
    token_grads(1)
    finish_mixed()
    for u in (4, 0, 1, 2, 3):
        stage(u, 7)
    for item in reductions + returns + halves + grads + [small_sum]:
        item.finish()


def backward(z, *inputs):
    def bf(*shape):
        return pltpu.VMEM(shape, BF)

    def f32(*shape):
        return jax.ShapeDtypeStruct(shape, F32)

    dma = pltpu.SemaphoreType.DMA
    d, r, ny, nz, half = z.d, z.r, z.ny, z.nz, z.d // 2
    widths = [d] + [3 * LANES * len(g) for g in GROUPS]
    blocks = [jax.ShapeDtypeStruct((r, w), BF) for w in widths]
    outs = (jax.ShapeDtypeStruct((z.mt, d), BF), f32(z.mt, d), *blocks, f32(z.e, r), f32(z.small - z.e, r))

    def reduction(w):
        half, piece = bf(r // 2, w), bf(r // 4, w)
        return (
            bf(2, ny, r, w), bf(ny, r, w), bf(ny - 1, r, w), bf(ny - 1, r, w), half, half, half, piece, piece, piece,
            dma((2, 6 + ny)),
        )

    small = (
        bf(2, ny, z.small, r), bf(ny, z.small, r), bf(ny - 1, z.small, r), bf(ny - 1, z.small, r),
        bf(3, z.small, r), bf(3, z.small, r), dma((2, 4 + ny)),
    )
    kept = [pltpu.VMEM(x.shape, x.dtype) for x in inputs[7:-2]]
    return pl.pallas_call(
        functools.partial(backward_kernel, z),
        out_shape=outs,
        in_specs=[VMEM, SMEM] + [VMEM] * 5 + [ANY] * 18,
        out_specs=[VMEM] * len(outs),
        scratch_shapes=kept + [
            bf(z.slots, d),
            bf(2, z.hs, half), bf(2, ny, z.cb, half), bf(2, ny, z.cb, half), bf(2, ny - 1, z.cb, half), bf(2, ny - 1, z.cb, half),
            bf(z.mt, d), bf(z.mt, d), bf(z.m, z.g, d), bf(z.m, z.g, d), pltpu.VMEM((z.mt, d), F32),
            bf(z.m, z.g, z.far), pltpu.VMEM((z.m, z.t, LANES), I32), pltpu.VMEM((z.m, z.t, LANES), F32),
            pltpu.VMEM((16, LANES), F32), pltpu.VMEM((8, d), F32),
            *[reduction(w) for w in widths],
            bf(z.m, 2, ny, z.t, d), bf(z.m, ny, z.t, d), bf(z.m, ny - 1, z.t, d), bf(z.m, ny - 1, z.t, d),
            pltpu.VMEM((z.small, d), F32), small,
            dma((24,)), dma((4, z.hn)), dma((4, z.hn)), dma((2,)), dma((2,)), dma((2, ny)), dma((2, ny)),
            dma((z.m,)), dma((z.m,)), dma((z.m, ny)), dma((z.m, ny)),
        ],
        compiler_params=pltpu.CompilerParams(
            collective_id=1, has_side_effects=True, vmem_limit_bytes=63 * 2**20
        ),
        name="backward",
    )(*inputs)


def finish_kernel(
    d_o, d_0, d_1, d_2, d_3, din, dout, mixed, dtok, vecs, o_mixed, o_dtok, o_q, o_k, o_v, o_o, o_in, o_out, o_one, o_two, o_bias
):
    o_in[...] = din[...].astype(F32)
    o_out[...] = dout[...].astype(F32)
    o_mixed[...] = mixed[...]
    o_dtok[...] = dtok[...]
    o_o[...] = d_o[...].astype(F32)
    o_one[...] = vecs[0:1, :]
    o_two[...] = vecs[1:2, :]
    o_bias[...] = vecs[2:3, : o_bias.shape[1]]
    for pairs, block in zip(GROUPS, (d_0, d_1, d_2, d_3)):
        n, first = len(pairs) * LANES, pairs[0] * LANES
        for i, out in enumerate((o_q, o_k, o_v)):
            out[:, first : first + n] = block[:, i * n : (i + 1) * n].astype(F32)


def finish(z, n_bias, blocks, din, dout, mixed, dtok, vecs):
    d, r, n = z.d, z.r, 4
    rows = z.el * d // n

    def f32(*shape):
        return jax.ShapeDtypeStruct(shape, F32)

    def by_row(size, width=d):
        return pl.BlockSpec((size, width), lambda i: (i, 0))

    def once(*shape):
        return pl.BlockSpec(shape, lambda i: (0, 0))

    return pl.pallas_call(
        finish_kernel,
        grid=(n,),
        out_shape=(
            jax.ShapeDtypeStruct((z.mt, d), BF), f32(z.mt, d), *[f32(r, d)] * 4, *[f32(n * rows, d)] * 2,
            f32(1, r), f32(1, r), f32(1, n_bias),
        ),
        in_specs=[by_row(r // n, b.shape[1]) for b in blocks] + [by_row(rows)] * 2 + [by_row(z.mt // n)] * 2
        + [once(*vecs.shape)],
        out_specs=[by_row(z.mt // n)] * 2 + [by_row(r // n)] * 4 + [by_row(rows)] * 2
        + [once(1, r), once(1, r), once(1, n_bias)],
        name="finish",
    )(*blocks, din.reshape(n * rows, d), dout.reshape(n * rows, d), mixed, dtok, vecs)


def fused_device(
    z, tokens, cotangent, routes, prompt_rows, w_query, w_key, w_value, w_output, w_router, gain_attn, gain_ffn,
    pos_table, w_in, w_out,
):
    perm, rows_of, dest, place, gate_of, source, pick = layout_constants(z)
    n = pos_table.shape[0]
    vecs = jnp.concatenate([gain_attn, gain_ffn, pos_table])[None]
    dy = cotangent.reshape(z.mt, z.d)
    routes = routes.transpose(0, 2, 1)
    counts = prompt_rows[:, 0]
    kept = forward(
        z, tokens, dy, routes, counts, w_key, w_value, w_query, w_output, w_router.T, vecs, w_in, w_out,
        perm, rows_of, dest, place, gate_of, source, pick,
    )
    kept, (ggrows, din, dout) = kept[:18], kept[18:]
    mixed, dtok, *blocks, drouter, dvecs = backward(z, dy, counts, routes, dest, place, perm, ggrows, *kept)
    mixed, dtok, dq, dk, dv, do, din, dout, one, two, bias = finish(z, n, blocks, din, dout, mixed, dtok, dvecs)
    return (
        mixed.reshape(tokens.shape),
        dtok.reshape(tokens.shape),
        dq,
        dk,
        dv,
        do,
        drouter.T,
        one.reshape(-1),
        two.reshape(-1),
        bias.reshape(-1),
        din.reshape(w_in.shape),
        dout.reshape(w_out.shape),
    )


HIGHEST = lax.Precision.HIGHEST


def distance_bucket(distance):
    coarse = reduce(
        lambda running, border: running + (distance >= border).astype(jnp.int32),
        BUCKET_EDGES,
        jnp.full(distance.shape, 16, jnp.int32),
    )
    return jnp.where(distance < 16, distance, coarse)


def layout(counts, block_rows):
    shard_count = counts.shape[0]
    offsets = jnp.cumsum(counts, dtype=jnp.int32) - counts
    row_index = jnp.arange(shard_count * block_rows, dtype=jnp.int32)
    device = row_index // block_rows
    local_row = row_index - device * block_rows
    own_count = counts[device]
    is_prompt = local_row < own_count
    prompt_total = jnp.sum(counts, dtype=jnp.int32)
    position = jnp.where(
        is_prompt, offsets[device] + local_row, prompt_total + local_row - own_count
    )
    return (position, is_prompt, device)


def rms_norm(values, gain):
    return values * lax.rsqrt(jnp.mean(values * values, axis=-1, keepdims=True) + EPS) * gain


def matmul(left, right):
    return jnp.dot(left, right, preferred_element_type=jnp.float32)


def matmul_left(left, right):
    return lax.dot_general(
        left, right, (((0,), (0,)), ((), ())), preferred_element_type=jnp.float32
    )


def matmul_right(left, right):
    return lax.dot_general(
        left, right, (((1,), (1,)), ((), ())), preferred_element_type=jnp.float32
    )


def per_device(
    tokens,
    cotangent,
    routes,
    prompt_rows,
    w_query,
    w_key,
    w_value,
    w_output,
    w_router,
    gain_attn,
    gain_ffn,
    pos_table,
    w_in,
    w_out,
):
    shard_count = lax.axis_size("shard")
    expert_ranks = lax.axis_size("expert")
    own_index = lax.axis_index("shard")
    micro_count, tok_rows, model_width = tokens.shape
    local_experts = w_in.shape[0]
    expert_count = w_router.shape[1]
    capacity = (9 * tok_rows + 4 * expert_count - 1) // (4 * expert_count)
    head_count = HEADS
    head_size = model_width // head_count
    bucket_count = BUCKETS
    score_scale = head_size ** (-0.5)
    group_rows = shard_count * tok_rows
    slot_count = expert_ranks * capacity * local_experts
    recv_rows = expert_ranks * capacity
    bucket_ids = jnp.arange(bucket_count, dtype=jnp.int32)
    expert_ids = jnp.arange(expert_count, dtype=jnp.int32)
    gathered = (
        lax.all_gather(w_query, "shard", axis=0, tiled=True),
        lax.all_gather(w_key, "shard", axis=0, tiled=True),
        lax.all_gather(w_value, "shard", axis=0, tiled=True),
        lax.all_gather(w_output, "shard", axis=0, tiled=True),
        lax.all_gather(w_router, "shard", axis=0, tiled=True),
        lax.all_gather(gain_attn, "shard", axis=0, tiled=True),
        lax.all_gather(gain_ffn, "shard", axis=0, tiled=True),
        lax.all_gather(pos_table, "shard", axis=0, tiled=True),
    )
    full_query, full_key, full_value, full_output, full_router, gain_one, gain_two, table_flat = (
        gathered
    )
    gain_first = gain_one.astype(jnp.float32)
    gain_second = gain_two.astype(jnp.float32)
    table = table_flat.astype(jnp.float32).reshape(head_count, bucket_count)
    expert_in, expert_out = (
        lax.all_gather(w_in, "shard", axis=2, tiled=True),
        lax.all_gather(w_out, "shard", axis=1, tiled=True),
    )
    sum_query = jnp.zeros(full_query.shape, jnp.float32)
    sum_key = jnp.zeros(full_key.shape, jnp.float32)
    sum_value = jnp.zeros(full_value.shape, jnp.float32)
    sum_output = jnp.zeros(full_output.shape, jnp.float32)
    sum_router = jnp.zeros(full_router.shape, jnp.float32)
    sum_gain_one = jnp.zeros((model_width,), jnp.float32)
    sum_gain_two = jnp.zeros((model_width,), jnp.float32)
    sum_table = jnp.zeros((head_count, bucket_count), jnp.float32)
    sum_expert_in = jnp.zeros(expert_in.shape, jnp.float32)
    sum_expert_out = jnp.zeros(expert_out.shape, jnp.float32)
    mixed_parts = []
    grad_parts = []
    for micro_index in range(micro_count):
        inputs = tokens[micro_index].astype(jnp.float32)
        counts = prompt_rows[micro_index, 0]
        pos_all, prompt_all, device_all = layout(counts, tok_rows)
        query_pos = lax.dynamic_slice_in_dim(pos_all, own_index * tok_rows, tok_rows)
        hidden = rms_norm(inputs, gain_first).astype(jnp.bfloat16)
        query = matmul(hidden, full_query).astype(jnp.bfloat16)
        key = matmul(hidden, full_key).astype(jnp.bfloat16)
        value = matmul(hidden, full_value).astype(jnp.bfloat16)
        keys_all, values_all = (
            lax.all_gather(key, "shard", axis=0, tiled=True),
            lax.all_gather(value, "shard", axis=0, tiled=True),
        )
        key_index = jnp.arange(group_rows, dtype=jnp.int32)
        key_far = jnp.zeros((group_rows,), jnp.bool_)
        key_total = keys_all.shape[0]
        key_block = math.gcd(key_total, 512)
        block_count = key_total // key_block
        key_pos = pos_all[key_index]
        key_prompt = prompt_all[key_index]
        key_device = device_all[key_index]
        key_mine = key_device == own_index
        distance = query_pos[:, None] - key_pos[None, :]
        visible = (
            (distance >= 0)
            & (key_prompt | key_mine)[None, :]
            & jnp.logical_not(key_far & key_mine)[None, :]
        )
        bucket_all = distance_bucket(jnp.maximum(distance, 0))
        bucket_blocks = bucket_all.reshape(tok_rows, block_count, key_block).transpose(1, 0, 2)
        visible_blocks = visible.reshape(tok_rows, block_count, key_block).transpose(1, 0, 2)
        query_heads = query.reshape(tok_rows, head_count, head_size)
        key_blocks = keys_all.reshape(block_count, key_block, head_count, head_size)
        value_blocks = values_all.reshape(block_count, key_block, head_count, head_size)

        def make_bias(unused, block_item):
            bucket_piece, visible_piece = block_item
            bucket_hits = (bucket_piece[:, :, None] == bucket_ids).astype(jnp.float32)
            bias = jnp.einsum("qkb,hb->hqk", bucket_hits, table, precision=HIGHEST)
            return (unused, jnp.where(visible_piece[None], bias, MASKED))

        _, bias_blocks = lax.scan(
            make_bias, jnp.zeros((), jnp.float32), (bucket_blocks, visible_blocks)
        )

        def score_piece(key_piece, bias_piece):
            raw = jnp.einsum(
                "qhd,khd->hqk", query_heads, key_piece, preferred_element_type=jnp.float32
            )
            return raw * score_scale + bias_piece

        def running(state_pair, block_item):
            running_max, running_sum = state_pair
            key_piece, bias_piece = block_item
            scores = score_piece(key_piece, bias_piece)
            new_max = jnp.maximum(running_max, jnp.max(scores, axis=-1))
            running_sum = running_sum * jnp.exp(running_max - new_max) + jnp.sum(
                jnp.exp(scores - new_max[:, :, None]), axis=-1
            )
            return ((new_max, running_sum), None)

        start_pair = (
            jnp.full((head_count, tok_rows), MASKED, jnp.float32),
            jnp.zeros((head_count, tok_rows), jnp.float32),
        )
        (running_max, running_sum), _ = lax.scan(running, start_pair, (key_blocks, bias_blocks))
        log_total = running_max + jnp.log(running_sum)

        def gather_context(context_sum, block_item):
            key_piece, value_piece, bias_piece = block_item
            weights_low = jnp.exp(
                score_piece(key_piece, bias_piece) - log_total[:, :, None]
            ).astype(jnp.bfloat16)
            return (
                context_sum
                + jnp.einsum(
                    "hqk,khd->qhd", weights_low, value_piece, preferred_element_type=jnp.float32
                ),
                None,
            )

        context, _ = lax.scan(
            gather_context,
            jnp.zeros((tok_rows, head_count, head_size), jnp.float32),
            (key_blocks, value_blocks, bias_blocks),
        )
        context_low = context.reshape(tok_rows, model_width).astype(jnp.bfloat16)
        middle = inputs + matmul(context_low, full_output)
        normed = rms_norm(middle, gain_second).astype(jnp.bfloat16)
        logits = matmul(normed, full_router)
        chosen = routes[micro_index]
        pick_table = (chosen[:, :, None] == expert_ids).astype(jnp.float32)
        picked = jnp.sum(pick_table * logits[:, None, :], axis=-1)
        gate_weights = jax.nn.softmax(picked, axis=-1)
        flat_routes = chosen.reshape(-1)
        expert_hits = (flat_routes[:, None] == expert_ids).astype(jnp.int32)
        expert_rank = (
            jnp.sum(
                jnp.cumsum(expert_hits, axis=0, dtype=jnp.int32) * expert_hits,
                axis=1,
                dtype=jnp.int32,
            )
            - 1
        )
        slot_index = (
            flat_routes // local_experts * (capacity * local_experts)
            + expert_rank * local_experts
            + flat_routes % local_experts
        )
        slot_owner = (
            jnp.full((slot_count,), 2 * tok_rows, jnp.int32)
            .at[slot_index]
            .set(jnp.arange(2 * tok_rows, dtype=jnp.int32))
        )
        padded = jnp.concatenate([normed, jnp.zeros((1, model_width), jnp.bfloat16)], axis=0)
        outgoing = padded[slot_owner // 2].reshape(
            expert_ranks, capacity, local_experts, model_width
        )
        received = lax.all_to_all(
            outgoing, "expert", split_axis=0, concat_axis=0, tiled=True
        ).reshape(recv_rows, local_experts, model_width)
        pre_act = jnp.einsum(
            "red,edf->ref", received, expert_in, preferred_element_type=jnp.float32
        )
        activation = jax.nn.gelu(pre_act).astype(jnp.bfloat16)
        expert_result = jnp.einsum(
            "ref,efd->red", activation, expert_out, preferred_element_type=jnp.float32
        )
        result_low = expert_result.astype(jnp.bfloat16).reshape(
            expert_ranks, capacity, local_experts, model_width
        )
        returned = lax.all_to_all(
            result_low, "expert", split_axis=0, concat_axis=0, tiled=True
        ).reshape(slot_count, model_width)
        picked_rows = returned[slot_index].astype(jnp.float32).reshape(tok_rows, 2, model_width)
        output_rows = middle + jnp.sum(gate_weights[:, :, None] * picked_rows, axis=1)
        mixed_parts.append(output_rows.astype(jnp.bfloat16))
        grad_output = cotangent[micro_index].astype(jnp.float32)
        grad_gate = jnp.sum(grad_output[:, None, :] * picked_rows, axis=-1)
        grad_pick = gate_weights * (
            grad_gate - jnp.sum(gate_weights * grad_gate, axis=-1, keepdims=True)
        )
        grad_logits = jnp.sum(pick_table * grad_pick[:, :, None], axis=1).astype(jnp.bfloat16)
        sum_router = sum_router + matmul_left(normed, grad_logits)
        grad_normed = matmul_right(grad_logits, full_router)
        branch_grad = (gate_weights[:, :, None] * grad_output[:, None, :]).reshape(
            2 * tok_rows, model_width
        )
        padded_grad = jnp.concatenate(
            [branch_grad, jnp.zeros((1, model_width), jnp.float32)], axis=0
        )
        grad_send = (
            padded_grad[slot_owner]
            .astype(jnp.bfloat16)
            .reshape(expert_ranks, capacity, local_experts, model_width)
        )
        grad_recv = lax.all_to_all(
            grad_send, "expert", split_axis=0, concat_axis=0, tiled=True
        ).reshape(recv_rows, local_experts, model_width)
        grad_act = jnp.einsum(
            "red,efd->ref", grad_recv, expert_out, preferred_element_type=jnp.float32
        )
        sum_expert_out = sum_expert_out + jnp.einsum(
            "ref,red->efd", activation, grad_recv, preferred_element_type=jnp.float32
        )
        _, gelu_pull = jax.vjp(jax.nn.gelu, pre_act)
        grad_pre = gelu_pull(grad_act)[0].astype(jnp.bfloat16)
        sum_expert_in = sum_expert_in + jnp.einsum(
            "red,ref->edf", received, grad_pre, preferred_element_type=jnp.float32
        )
        grad_in_rows = jnp.einsum(
            "ref,edf->red", grad_pre, expert_in, preferred_element_type=jnp.float32
        )
        grad_in_low = grad_in_rows.astype(jnp.bfloat16).reshape(
            expert_ranks, capacity, local_experts, model_width
        )
        grad_back = lax.all_to_all(
            grad_in_low, "expert", split_axis=0, concat_axis=0, tiled=True
        ).reshape(slot_count, model_width)
        grad_normed = grad_normed + jnp.sum(
            grad_back[slot_index].astype(jnp.float32).reshape(tok_rows, 2, model_width), axis=1
        )
        _, norm_pull = jax.vjp(rms_norm, middle, gain_second)
        grad_middle, grad_gain_second = norm_pull(grad_normed)
        grad_middle = grad_middle + grad_output
        sum_gain_two = sum_gain_two + grad_gain_second
        grad_attn = grad_middle.astype(jnp.bfloat16)
        sum_output = sum_output + matmul_left(context_low, grad_attn)
        grad_context = (
            matmul_right(grad_attn, full_output)
            .astype(jnp.bfloat16)
            .reshape(tok_rows, head_count, head_size)
        )
        row_delta = jnp.einsum("qhd,qhd->hq", grad_context.astype(jnp.float32), context)

        def attend_back(state_pair, block_item):
            grad_query_sum, grad_table_sum = state_pair
            key_piece, value_piece, bias_piece, bucket_piece = block_item
            probs = jnp.exp(score_piece(key_piece, bias_piece) - log_total[:, :, None])
            grad_probs = jnp.einsum(
                "qhd,khd->hqk", grad_context, value_piece, preferred_element_type=jnp.float32
            )
            grad_scores = probs * (grad_probs - row_delta[:, :, None])
            bucket_hits = (bucket_piece[:, :, None] == bucket_ids).astype(jnp.float32)
            grad_table_sum = grad_table_sum + jnp.einsum(
                "hqk,qkb->hb", grad_scores, bucket_hits, precision=HIGHEST
            )
            grad_raw = (grad_scores * score_scale).astype(jnp.bfloat16)
            grad_query_sum = grad_query_sum + jnp.einsum(
                "hqk,khd->qhd", grad_raw, key_piece, preferred_element_type=jnp.float32
            )
            grad_key_piece = jnp.einsum(
                "hqk,qhd->khd", grad_raw, query_heads, preferred_element_type=jnp.float32
            )
            grad_value_piece = jnp.einsum(
                "hqk,qhd->khd",
                probs.astype(jnp.bfloat16),
                grad_context,
                preferred_element_type=jnp.float32,
            )
            return ((grad_query_sum, grad_table_sum), (grad_key_piece, grad_value_piece))

        back_start = (
            jnp.zeros((tok_rows, head_count, head_size), jnp.float32),
            jnp.zeros((head_count, bucket_count), jnp.float32),
        )
        (grad_query_all, grad_table_all), (grad_key_blocks, grad_value_blocks) = lax.scan(
            attend_back, back_start, (key_blocks, value_blocks, bias_blocks, bucket_blocks)
        )
        sum_table = sum_table + grad_table_all
        key_grad_rows = grad_key_blocks.reshape(key_total, model_width)
        value_grad_rows = grad_value_blocks.reshape(key_total, model_width)
        own_key_grad, own_value_grad = (
            lax.psum_scatter(
                key_grad_rows.astype(jnp.bfloat16), "shard", scatter_dimension=0, tiled=True
            ).astype(jnp.float32),
            lax.psum_scatter(
                value_grad_rows.astype(jnp.bfloat16), "shard", scatter_dimension=0, tiled=True
            ).astype(jnp.float32),
        )
        grad_query_low = grad_query_all.reshape(tok_rows, model_width).astype(jnp.bfloat16)
        grad_key_low = own_key_grad.astype(jnp.bfloat16)
        grad_value_low = own_value_grad.astype(jnp.bfloat16)
        sum_query = sum_query + matmul_left(hidden, grad_query_low)
        sum_key = sum_key + matmul_left(hidden, grad_key_low)
        sum_value = sum_value + matmul_left(hidden, grad_value_low)
        grad_hidden = (
            matmul_right(grad_query_low, full_query)
            + matmul_right(grad_key_low, full_key)
            + matmul_right(grad_value_low, full_value)
        )
        _, first_pull = jax.vjp(rms_norm, inputs, gain_first)
        grad_inputs, grad_gain_first = first_pull(grad_hidden)
        sum_gain_one = sum_gain_one + grad_gain_first
        grad_parts.append(grad_inputs + grad_middle)
    shares = (
        lax.psum_scatter(
            sum_query.astype(jnp.bfloat16), "shard", scatter_dimension=0, tiled=True
        ).astype(jnp.float32),
        lax.psum_scatter(
            sum_key.astype(jnp.bfloat16), "shard", scatter_dimension=0, tiled=True
        ).astype(jnp.float32),
        lax.psum_scatter(
            sum_value.astype(jnp.bfloat16), "shard", scatter_dimension=0, tiled=True
        ).astype(jnp.float32),
        lax.psum_scatter(
            sum_output.astype(jnp.bfloat16), "shard", scatter_dimension=0, tiled=True
        ).astype(jnp.float32),
        lax.psum_scatter(
            sum_router.astype(jnp.bfloat16), "shard", scatter_dimension=0, tiled=True
        ).astype(jnp.float32),
        lax.psum_scatter(
            sum_gain_one.astype(jnp.bfloat16), "shard", scatter_dimension=0, tiled=True
        ).astype(jnp.float32),
        lax.psum_scatter(
            sum_gain_two.astype(jnp.bfloat16), "shard", scatter_dimension=0, tiled=True
        ).astype(jnp.float32),
        lax.psum_scatter(
            sum_table.reshape(-1).astype(jnp.bfloat16), "shard", scatter_dimension=0, tiled=True
        ).astype(jnp.float32),
    )
    own_grads = (
        lax.psum(shares[0].astype(jnp.bfloat16), "expert").astype(jnp.float32),
        lax.psum(shares[1].astype(jnp.bfloat16), "expert").astype(jnp.float32),
        lax.psum(shares[2].astype(jnp.bfloat16), "expert").astype(jnp.float32),
        lax.psum(shares[3].astype(jnp.bfloat16), "expert").astype(jnp.float32),
        lax.psum(shares[4].astype(jnp.bfloat16), "expert").astype(jnp.float32),
        lax.psum(shares[5].astype(jnp.bfloat16), "expert").astype(jnp.float32),
        lax.psum(shares[6].astype(jnp.bfloat16), "expert").astype(jnp.float32),
        lax.psum(shares[7].astype(jnp.bfloat16), "expert").astype(jnp.float32),
    )
    grad_expert_in, grad_expert_out = (
        lax.psum_scatter(
            sum_expert_in.astype(jnp.bfloat16), "shard", scatter_dimension=2, tiled=True
        ).astype(jnp.float32),
        lax.psum_scatter(
            sum_expert_out.astype(jnp.bfloat16), "shard", scatter_dimension=1, tiled=True
        ).astype(jnp.float32),
    )
    return (
        jnp.stack(mixed_parts),
        jnp.stack(grad_parts),
        own_grads[0],
        own_grads[1],
        own_grads[2],
        own_grads[3],
        own_grads[4],
        own_grads[5],
        own_grads[6],
        own_grads[7],
        grad_expert_in,
        grad_expert_out,
    )


def solution(mesh):
    in_specs = (
        P(None, ("expert", "shard"), None),
        P(None, ("expert", "shard"), None),
        P(None, ("expert", "shard"), None),
        P(None, "expert", None),
        P("shard", None),
        P("shard", None),
        P("shard", None),
        P("shard", None),
        P("shard", None),
        P("shard"),
        P("shard"),
        P("shard"),
        P("expert", None, "shard"),
        P("expert", "shard", None),
    )
    out_specs = (
        P(None, ("expert", "shard"), None),
        P(None, ("expert", "shard"), None),
        P("shard", None),
        P("shard", None),
        P("shard", None),
        P("shard", None),
        P("shard", None),
        P("shard"),
        P("shard"),
        P("shard"),
        P("expert", None, "shard"),
        P("expert", "shard", None),
    )
    ne, ns = mesh.shape["expert"], mesh.shape["shard"]

    def device(*args):
        tokens, w_router, w_in = args[0], args[8], args[12]
        z = Sizes(
            ne, ns, tokens.shape[0], tokens.shape[1], tokens.shape[2], w_router.shape[1], w_in.shape[0], w_in.shape[2]
        )
        return fused_device(z, *args) if z.fits() else per_device(*args)

    return jax.shard_map(
        device, mesh=mesh, in_specs=in_specs, out_specs=out_specs, check_vma=False
    )
```

```python
import functools
from functools import reduce
import math

import jax
import jax.numpy as jnp
import numpy as np
from jax import lax
from jax.experimental import pallas as pl
from jax.experimental.pallas import tpu as pltpu
from jax.sharding import PartitionSpec as P

HEADS = 12
BUCKETS = 32
EPS = 1e-06
MASKED = -1e30
BUCKET_EDGES = (24, 32, 48, 64, 96, 128, 192, 256, 384, 512, 768, 1024, 1536, 2048, 3072)
MESH = pl.DeviceIdType.MESH
BF = jnp.bfloat16
F32 = jnp.float32
I32 = jnp.int32
LANES = 128


class Sizes:
    def __init__(self, ne, ns, micro, rows, width, experts, local_experts, ff):
        self.ne, self.ns, self.ny = ne, ns, ns // 2
        self.m, self.t, self.d = micro, rows, width
        self.e, self.el, self.ff = experts, local_experts, ff
        self.g = ns * rows
        self.mt = micro * rows
        self.r = width // ns
        self.cap = (9 * rows + 4 * experts - 1) // (4 * experts)
        self.per = micro * self.cap
        self.sp = -(-(local_experts * self.per + 2) // 16) * 16
        self.slots = ne * self.sp
        self.nz = ne // 2
        self.hn = ne // 2
        self.cr = self.hn * self.per
        self.cb = local_experts * self.cr
        self.blk = 2 * self.cb
        self.hs = self.hn * self.sp
        self.n16 = -(-ne // 16) * 16
        self.pairs = HEADS // 2
        self.small = experts + 16
        self.far = self.g // 2 + rows

    def fits(self):
        return (
            self.ns % 2 == 0
            and self.t == LANES
            and self.d == HEADS * 64
            and self.cr % 16 == 0
            and self.nz == 4
            and self.e % 16 == 0
            and self.r % (16 * self.nz) == 0
            and self.slots % LANES == 0
            and self.el * self.per <= LANES
            and self.d == self.ff
            and self.ns >= 2 * self.m
            and self.blk >= self.g
            and self.d % 256 == 0
        )


def layout_constants(z):
    perm = np.zeros((z.cb, z.hs), np.float32)
    rows_of = np.zeros((2 * z.n16, z.slots), np.float32)
    dest = np.zeros((2 * z.n16, z.slots), np.float32)
    place = np.zeros((z.slots, LANES), np.float32)
    gate_of = np.zeros((2 * z.n16, z.hs), np.float32)
    source = np.zeros((z.cb, 2 * z.n16), np.float32)
    pick = np.zeros((z.cb, LANES), np.float32)
    used = z.el * z.per
    for src in range(z.ne):
        rows_of[src, src * z.sp + used] = 1
        rows_of[z.n16 + src, src * z.sp + used + 1] = 1
        dest[src, src * z.sp : (src + 1) * z.sp] = 1
        dest[z.n16 + src, src * z.sp : (src + 1) * z.sp] = 1
        for q in range(used):
            place[src * z.sp + q, q] = 1
    for src in range(z.hn):
        gate_of[src, src * z.sp + used] = 1
        gate_of[z.n16 + src, src * z.sp + used + 1] = 1
        for q in range(used):
            row = (q // z.per) * z.cr + src * z.per + q % z.per
            perm[row, src * z.sp + q] = 1
            source[row, src] = 1
            source[row, z.n16 + src] = 1
            pick[row, q] = 1
    return [jnp.asarray(a, BF) for a in (perm, rows_of, dest, place, gate_of, source, pick)]


def dot(a, b):
    return jnp.dot(a, b, preferred_element_type=F32)


def dot_t(a, b):
    return lax.dot_general(a, b, (((1,), (1,)), ((), ())), preferred_element_type=F32)


def tdot(a, b):
    return lax.dot_general(a, b, (((0,), (0,)), ((), ())), preferred_element_type=F32)


def iota(shape, dim):
    return lax.broadcasted_iota(I32, shape, dim)


def aligned(start, size, multiple):
    return pl.ds(pl.multiple_of(start, multiple), size)


def offsets(z, chunk=None):
    every = [(kz, kx) for kz in range(z.nz) for kx in range(2)][1:]
    return [k for k in every if chunk is None or k[0] % 2 == chunk]


def position(z, k):
    return (k[0] % 2) * z.hn + (k[0] // 2) * 2 + k[1]


class Place:
    def __init__(self, z):
        self.z = z
        self.e = lax.axis_index("expert")
        self.s = lax.axis_index("shard")
        self.y, self.c = lax.div(self.s, 2), lax.rem(self.s, 2)

    def shard(self, k, other):
        y = lax.rem(self.y + k, self.z.ny)
        return y * 2 + (1 - self.c if other else self.c)

    def expert(self, kz, kx):
        high = lax.rem(lax.div(self.e, 2) + kz, self.z.nz)
        return high * 2 + lax.rem(lax.rem(self.e, 2) + kx, 2)

    def barrier(self, with_experts=True):
        sem = pltpu.get_barrier_semaphore()
        others = [(self.e, self.shard(0, True))]
        others += [(self.e, self.shard(k, False)) for k in range(1, self.z.ny)]
        if with_experts:
            others += [(self.expert(*k), self.s) for k in offsets(self.z)]
        for other in others:
            pl.semaphore_signal(sem, inc=1, device_id=other, device_id_type=MESH)
        pl.semaphore_wait(sem, len(others))


def rcopy(src, dst, send, recv, to):
    return pltpu.make_async_remote_copy(
        src_ref=src, dst_ref=dst, send_sem=send, recv_sem=recv, device_id=to, device_id_type=MESH
    )


class Gather:
    def __init__(self, place, own, full, send, recv, item):
        self.p, self.own, self.full = place, own, full
        self.send, self.recv, self.item = send, recv, item

    def copy(self, origin, src, slot, to):
        return rcopy(src, self.full(origin), self.send.at[self.item, slot], self.recv.at[self.item, slot], to)

    def partner(self):
        return (self.p.e, self.p.shard(0, True))

    def start(self):
        p, ny = self.p, self.p.z.ny
        for k in range(1, ny):
            self.copy(p.s, self.own, k, (p.e, p.shard(k, False))).start()
        self.copy(p.s, self.own, 0, self.partner()).start()

    def forward(self):
        p, ny = self.p, self.p.z.ny
        for k in range(1, ny):
            origin = p.shard(k, False)
            self.copy(origin, self.full(origin), ny - k, self.partner()).wait_recv()
            self.copy(origin, self.full(origin), ny + k - 1, self.partner()).start()

    def arrive(self):
        p, ny = self.p, self.p.z.ny
        for k in range(ny):
            origin = p.shard(k, True)
            self.copy(origin, self.full(origin), ny + k - 1 if k else 0, self.partner()).wait_recv()

    def finish(self):
        p, ny = self.p, self.p.z.ny
        for slot in range(2 * ny - 1):
            self.copy(p.s, self.own, slot, self.partner()).wait_send()


class Exchange:
    def __init__(self, place, src, dst, send, recv, item):
        self.p, self.src, self.dst = place, src, dst
        self.send, self.recv, self.item = send, recv, item

    def copy(self, k):
        z = self.p.z
        back = (-k[0] % z.nz, k[1])
        at = position(z, back)
        to = self.p.expert(*k)
        return rcopy(
            self.src(to),
            self.dst(at),
            self.send.at[self.item, position(z, k) - 1],
            self.recv.at[self.item, at - 1],
            (to, self.p.s),
        )

    def start(self, some=None):
        for k in filter(some, offsets(self.p.z)):
            self.copy(k).start()

    def arrive(self, some=None):
        z = self.p.z
        for k in filter(some, offsets(z)):
            self.copy((-k[0] % z.nz, k[1])).wait_recv()

    def finish(self, some=None):
        for k in filter(some, offsets(self.p.z)):
            self.copy(k).wait_send()


def slot_ids(z, route0, route1):
    lane = iota((z.t, LANES), 1)
    lower = (iota((z.t, z.t), 0) > iota((z.t, z.t), 1)).astype(F32).astype(BF)
    base = lane * z.per
    for d in range(1, z.ne):
        base = base + jnp.where(lane >= d * z.el, z.sp - z.el * z.per, 0)
    firsts, seconds = [], []
    for m in range(z.m):
        rows = slice(m * z.t, (m + 1) * z.t)
        hit0, hit1 = lane == route0[rows], lane == route1[rows]
        hits = jnp.where(hit0 | hit1, 1.0, 0.0).astype(BF)
        spot = dot(lower, hits) + (base + m * z.cap).astype(F32)
        firsts.append(jnp.sum(jnp.where(hit0, spot, 0.0), axis=1, keepdims=True))
        seconds.append(jnp.sum(jnp.where(hit1, spot, 0.0), axis=1, keepdims=True))
    return jnp.concatenate(firsts, 0), jnp.concatenate(seconds, 0)


def one_hot(z, slot):
    return (iota((z.mt, z.slots), 1) == slot.astype(I32)).astype(F32)


def key_layout(z, counts, m, shape, dim):
    row = iota(shape, dim)
    total = counts[m, 0]
    for b in range(1, z.ns):
        total = total + counts[m, b]
    position = jnp.zeros(shape, I32)
    prompt = jnp.zeros(shape, I32)
    offset = 0
    for b in range(z.ns):
        own = counts[m, b]
        local = row - b * z.t
        inside = (local >= 0) & (local < z.t)
        first = local < own
        position = jnp.where(inside, jnp.where(first, offset + local, total + local - own), position)
        prompt = jnp.where(inside & first, 1, prompt)
        offset = offset + own
    return position, prompt


def query_position(z, counts, m, s):
    total, offset, own = 0, 0, 0
    for b in range(z.ns):
        count = counts[m, b]
        total = total + count
        offset = offset + jnp.where(b < s, count, 0)
        own = own + jnp.where(b == s, count, 0)
    local = iota((z.t, 1), 0)
    return jnp.where(local < own, offset + local, total + local - own)


def bucket_of(z, distance):
    coarse = jnp.full(distance.shape, 16, I32)
    for edge in BUCKET_EDGES:
        if edge < z.far:
            coarse = coarse + jnp.where(distance >= edge, 1, 0)
    return jnp.where(distance < 16, distance, coarse)


VMEM = pl.BlockSpec(memory_space=pltpu.VMEM)
SMEM = pl.BlockSpec(memory_space=pltpu.SMEM)


GELU_A = math.sqrt(2.0 / math.pi)
GELU_B = 0.044715


class SharedGather:
    def __init__(self, place, own, full, send, recv, item):
        self.p, self.own, self.full = place, own, full
        self.send, self.recv, self.item = send, recv, item
        self.x = lax.rem(place.e, 2)

    def half(self, ref, x):
        n = ref.shape[1] // 2
        return ref.at[:, aligned(x * n, n, LANES)]

    def copy(self, src, dst, slot, arrival, to):
        return rcopy(src, dst, self.send.at[self.item, slot], self.recv.at[self.item, arrival], to)

    def partner(self):
        return (self.p.e, self.p.shard(0, True))

    def own_copy(self, origin):
        return self.copy(self.own, self.full(origin), 0, 0, self.partner())

    def y_copy(self, k, origin, arrival=None):
        return self.copy(
            self.half(self.own, self.x), self.half(self.full(origin), self.x), k, k if arrival is None else arrival,
            (self.p.e, self.p.shard(k, False)),
        )

    def on_copy(self, k, kind, origin, x, to):
        block = self.half(self.full(origin), x)
        slot = self.p.z.ny + 3 * (k - 1) + kind
        return self.copy(block, block, slot, slot, to)

    def start(self):
        p = self.p
        for k in range(1, p.z.ny):
            self.y_copy(k, p.s).start()
        self.own_copy(p.s).start()

    def forward(self):
        p = self.p
        for k in range(1, p.z.ny):
            origin = p.shard(k, False)
            self.y_copy(k, origin, self.p.z.ny - k).wait_recv()
            self.on_copy(k, 0, origin, self.x, (p.expert(0, 1), p.s)).start()
            self.on_copy(k, 1, origin, self.x, self.partner()).start()

    def forward_rest(self):
        p = self.p
        for k in range(1, p.z.ny):
            origin = p.shard(k, False)
            self.on_copy(k, 0, origin, 1 - self.x, (p.expert(0, 1), p.s)).wait_recv()
            self.on_copy(k, 2, origin, 1 - self.x, self.partner()).start()

    def arrive(self):
        p = self.p
        self.own_copy(p.shard(0, True)).wait_recv()
        for k in range(1, p.z.ny):
            origin = p.shard(k, True)
            self.on_copy(k, 1, origin, self.x, self.partner()).wait_recv()
            self.on_copy(k, 2, origin, 1 - self.x, self.partner()).wait_recv()

    def finish(self):
        p = self.p
        self.own_copy(p.s).wait_send()
        for k in range(1, p.z.ny):
            self.y_copy(k, p.s).wait_send()
            for kind in range(3):
                self.on_copy(k, kind, p.s, 0, self.partner()).wait_send()


class Scatter:
    def __init__(self, place, mine, other, from_core, to_y, from_y, psend, precv, ysend, yrecv):
        self.p, self.mine, self.other, self.from_core = place, mine, other, from_core
        self.to_y, self.from_y = to_y, from_y
        self.psend, self.precv, self.ysend, self.yrecv = psend, precv, ysend, yrecv

    def core_copy(self):
        p = self.p
        return rcopy(self.other, self.from_core, self.psend, self.precv, (p.e, p.shard(0, True)))

    def y_copy(self, k):
        p = self.p
        return rcopy(
            self.to_y.at[k - 1], self.from_y.at[k - 1], self.ysend.at[k - 1], self.yrecv.at[k - 1],
            (p.e, p.shard(k, False)),
        )

    def send(self):
        self.core_copy().start()

    def middle(self):
        p = self.p
        self.core_copy().wait_recv()
        for k in range(1, p.z.ny):
            yy = lax.rem(p.y + k, p.z.ny)
            both = self.mine[yy].astype(F32) + self.from_core[yy].astype(F32)
            self.to_y[k - 1] = both.astype(BF)
            self.y_copy(k).start()

    def total(self):
        p = self.p
        out = self.mine[p.y].astype(F32) + self.from_core[p.y].astype(F32)
        for k in range(1, p.z.ny):
            self.y_copy(k).wait_recv()
            out = out + self.from_y[k - 1].astype(F32)
        return out

    def finish(self):
        self.core_copy().wait_send()
        for k in range(1, self.p.z.ny):
            self.y_copy(k).wait_send()


class Return:
    def __init__(self, place, rows, ret, chunk, cols, send, recv):
        self.p, self.rows, self.ret, self.chunk, self.cols = place, rows, ret, chunk, cols
        self.sems = send, recv

    def copy(self, k, at, away):
        z = self.p.z
        first = self.chunk * z.hn
        return rcopy(
            self.rows.at[pl.ds((position(z, k) - first) * z.sp, z.sp)],
            self.ret.at[aligned(at * z.sp, z.sp, 16), self.cols],
            self.sems[0].at[position(z, k) - first],
            self.sems[1].at[position(z, away) - first],
            (self.p.expert(*k), self.p.s),
        )

    def start_remote(self):
        z = self.p.z
        for k in offsets(z, self.chunk):
            self.copy(k, self.p.e, (-k[0] % z.nz, k[1])).start()

    def start(self):
        z = self.p.z
        self.start_remote()
        if self.chunk == 0:
            self.ret[aligned(self.p.e * z.sp, z.sp, 16), self.cols] = self.rows[0 : z.sp, :]

    def arrive(self):
        for k in offsets(self.p.z, self.chunk):
            self.copy(k, self.p.expert(*k), k).wait_recv()

    def finish(self):
        z = self.p.z
        for k in offsets(z, self.chunk):
            self.copy(k, self.p.e, (-k[0] % z.nz, k[1])).wait_send()


def column_of(row):
    n = row.shape[1]
    return jnp.sum(jnp.where(iota((n, n), 0) == iota((n, n), 1), row, 0.0), axis=1, keepdims=True)


def route_columns(z, routes):
    out = []
    for j in range(2):
        parts = [column_of(routes[m, j : j + 1, :].astype(F32)) for m in range(z.m)]
        out.append(jnp.concatenate(parts, 0).astype(I32))
    return out


def spread(z, s, n):
    row, lane = iota((z.r, z.d), 0), iota((z.r, z.d), 1)
    return jnp.where((lane - s * n == row) & (row < n), 1.0, 0.0).astype(BF)


def split_high(x):
    high = x.astype(BF)
    return high, (x - high.astype(F32)).astype(BF)


def forward_kernel(
    z,
    tokens, dy, routes, counts, wk, wv, wq, wo, wr, vecs, w_in_hbm, w_out_hbm,
    perm, rows_of, dest, place_m, gate_of, source, pick,
    o_toks, o_hid, o_kk, o_vv, o_qq, o_pp, o_ctx, o_mid, o_nrm, o_sd, o_fk, o_fv, o_fq, o_fo, o_small,
    o_ret, o_rfin, o_rpart, ggrows, din, dout,
    qq, pp, ctx, mid, nrm, sd, fk, fv, fq, fo, small, smallg,
    xs, dyr, xr, dyg, xg, act, gp, w_in, w_out, table, bias_id, gwg, gwc, ggc,
    part, rp, ys, yr, fin, ret, rpart, rrp, rys, ryr, wstage, gpart, grp, gys, gyr, gout, gret,
    csem, ssem, gsend, grecv, wsend, wrecv, xsend, xrecv, psend, precv, ysend, yrecv, rsend, rrecv, gsem, gsy, gsx,
):
    p = Place(z)
    mt, t, d, r, ff = z.mt, z.t, z.d, z.r, z.ff
    half = d // 2
    tiles = ff // 256
    load_in = pltpu.make_async_copy(w_in_hbm, w_in, csem.at[0])
    load_out = pltpu.make_async_copy(w_out_hbm, w_out, csem.at[1])
    spills, waiting = [], {}

    def spill(src, dst, before=None):
        copy = pltpu.make_async_copy(src, dst, ssem.at[len(spills)])
        copy.start()
        spills.append(copy)
        waiting.setdefault(before, []).append(copy)

    toks, hid = gp.at[pl.ds(0, z.m), pl.ds(0, z.g)], gp.at[pl.ds(z.m, z.m), pl.ds(0, z.g)]
    kk, vv = act.at[pl.ds(0, z.m), pl.ds(0, z.g)], act.at[pl.ds(z.m, z.m), pl.ds(0, z.g)]

    whole = spread(z, p.s, r)
    line = iota((16, d), 0)
    n_bias = HEADS * BUCKETS // z.ns
    row = vecs[...].astype(F32)
    first = jnp.broadcast_to(row[:, 0:r], (16, r))
    gains = jnp.where(iota((16, r), 0) == 0, first, jnp.broadcast_to(row[:, r : 2 * r], (16, r)))
    biases = jnp.broadcast_to(row[:, 2 * r : 2 * r + n_bias], (16, n_bias))
    tail = dot(gains.astype(BF), whole)
    bias_row = dot(biases.astype(BF), spread(z, p.s, n_bias)[0:n_bias, :])
    tail = jnp.where(line < 2, tail, jnp.where(line == 2, bias_row, 0.0))
    small[0 : z.e, :] = dot(wr[...], whole).astype(BF)
    small[z.e : z.small, :] = tail.astype(BF)
    p.barrier()

    def rows(ref, size):
        return lambda origin: ref.at[aligned(origin * size, size, 16)]

    g_small = Gather(p, small, lambda o: smallg.at[o], gsend, grecv, 0)
    g_tok = [
        Gather(p, tokens.at[m], lambda o, m=m: toks.at[m, aligned(o * t, t, 16)], gsend, grecv, 1 + m)
        for m in range(z.m)
    ]
    base = 1 + z.m
    groups = d // 256

    def columns_item(own, full, g, item):
        cols = pl.ds(g * 256, 256)
        return SharedGather(
            p, own.at[:, cols], lambda o: full.at[aligned(o * r, r, 16), cols], wsend, wrecv, item
        )

    g_w = [
        [columns_item(own, full, g, 3 * g + i) for i, (own, full) in enumerate(((wk, fk), (wv, fv), (wq, fq)))]
        for g in range(groups)
    ]
    g_o = SharedGather(p, wo, rows(fo, r), wsend, wrecv, 3 * groups)
    for item in [g_small, g_tok[0]] + g_w[0] + g_tok[1:] + sum(g_w[1:], []) + [g_o]:
        item.start()
    load_out.start()
    load_in.start()
    g_dy = Gather(p, dyg.at[p.s], lambda o: dyg.at[o], gsend, grecv, base)

    def exchange(dst, item):
        return Exchange(
            p,
            lambda to: xs.at[aligned(to * z.sp, z.sp, 16)],
            lambda at: dst.at[pl.ds(at * z.sp, z.sp)],
            xsend,
            xrecv,
            item,
        )

    x_dy, x_move = exchange(dyr, 0), exchange(xr, 1)
    smallg[p.s] = small[...]
    for m in range(z.m):
        toks[m, aligned(p.s * t, t, 16), :] = tokens[m]
    own_weights = []
    for i, (own, full) in enumerate(((wk, fk), (wv, fv), (wq, fq), (wo, fo))):
        own_weights.append(pltpu.make_async_copy(own, full.at[aligned(p.s * r, r, 16)], csem.at[6 + i]))
        own_weights[i].start()

    route0, route1 = route_columns(z, routes)
    slot0, slot1 = slot_ids(z, route0, route1)
    hot = (one_hot(z, slot0) + one_hot(z, slot1)).astype(BF)
    mine = aligned(p.e * z.sp, z.sp, 16)

    def to_slots(ref):
        def step(i, carry):
            cols = aligned(i * 256, 256, 256)
            xs[:, cols] = tdot(hot, ref[:, cols]).astype(BF)
            return carry

        lax.fori_loop(0, d // 256, step, 0)

    across, along = lambda k: k[1] == 1, lambda k: k[1] == 0
    even, odd = lambda k: k[0] % 2 == 0, lambda k: k[0] % 2 == 1
    to_slots(dy)
    x_dy.start(across)
    dyr[0 : z.sp, :] = xs[mine, :]

    for m in range(z.m):
        key_pos, prompt = key_layout(z, counts, m, (1, z.g), 1)
        distance = query_position(z, counts, m, p.s) - key_pos
        lane = iota((1, z.g), 1)
        own_block = (lane >= p.s * t) & (lane < (p.s + 1) * t)
        visible = (distance >= 0) & (own_block | (prompt == 1))
        bias_id[m] = jnp.where(visible, bucket_of(z, distance), 2 * BUCKETS)

    for item in (g_small, g_tok[0]):
        item.forward()
    for item in (g_small, g_tok[0]):
        item.arrive()
    x_dy.start(along)
    spill(smallg, o_small)
    sums = smallg[0].astype(F32)
    for b in range(1, z.ns):
        sums = sums + smallg[b].astype(F32)
    gain_one = sums[z.e : z.e + 1, :]
    gain_two = sums[z.e + 1 : z.e + 2, :]
    router = sums.astype(BF)
    for pair in range(z.pairs):
        lanes = slice(pair // 2 * LANES, (pair // 2 + 1) * LANES)
        row = sums[z.e + 2 : z.e + 3, lanes]
        if pair % 2:
            row = pltpu.roll(row, 2 * BUCKETS, 1)
        table[pair : pair + 1, :] = jnp.where(iota((1, LANES), 1) < 2 * BUCKETS, row, MASKED)

    def normalize(m):
        def step(i, carry):
            at = aligned(i * t, t, 16)
            x = toks[m, at, :].astype(F32)
            scale = lax.rsqrt(jnp.mean(x * x, axis=1, keepdims=True) + EPS)
            hid[m, at, :] = (x * scale * gain_one).astype(BF)
            return carry

        lax.fori_loop(0, z.ns, step, 0)

    for copy in own_weights:
        copy.wait()

    def project(g, m):
        cols = slice(g * 256, (g + 1) * 256)
        for item, full, out in zip(g_w[g][:2], (fk, fv), (kk, vv)):
            if m == 0:
                item.arrive()
            out[m, :, cols] = dot(hid[m], full[:, cols]).astype(BF)
        if m == 0:
            g_w[g][2].arrive()
        own = hid[m, aligned(p.s * t, t, 16), :]
        qq[m * t : (m + 1) * t, cols] = (dot(own, fq[:, cols]).astype(BF).astype(F32) * 0.125).astype(BF)


    def in_order(src, dst, h):
        def step(i, carry):
            cols = aligned(i * 256, 256, 256)
            moved = dot(perm[...], src[h * z.hs : (h + 1) * z.hs, cols])
            dst[p.s, h * z.cb : (h + 1) * z.cb, cols] = moved.astype(BF)
            return carry

        lax.fori_loop(0, d // 256, step, 0)

    def send_dy_rows():
        x_dy.arrive()
        in_order(dyr, dyg, 0)
        in_order(dyr, dyg, 1)
        g_dy.start()

    low = iota((t, LANES), 1) < 64

    def attend(m, pair):
        spot = m * z.pairs + pair
        cols = aligned(pair * LANES, LANES, LANES)
        q = qq[aligned(m * t, t, 16), cols]
        zero = jnp.zeros_like(q)
        q_two = jnp.concatenate([jnp.where(low, q, zero), jnp.where(low, zero, q)], 0)
        scores = dot_t(q_two, kk[m, :, cols])
        biases = jnp.broadcast_to(table[pl.ds(pair, 1), :], (t, LANES))
        for side in range(2):
            pieces = []
            for b in range(z.ns):
                at = slice(b * LANES, (b + 1) * LANES)
                bias = jnp.take_along_axis(biases, bias_id[m, :, at] + BUCKETS * side, axis=1)
                pieces.append(scores[side * t : (side + 1) * t, at] + bias)
            s = jnp.concatenate(pieces, 1)
            top = jnp.max(s, axis=1, keepdims=True)
            e = jnp.exp(s - top)
            total = jnp.sum(e, axis=1, keepdims=True)
            pp[spot, side * t : (side + 1) * t, :] = (e * (1.0 / total)).astype(BF)
        two = dot(pp[spot], vv[m, :, cols])
        ctx[aligned(m * t, t, 16), cols] = jnp.where(low, two[:t], two[t:]).astype(BF)

    chain = g_w + [[g_o]]

    def attention(g, m):
        def step(i, carry):
            attend(m, g * 2 + i)
            return carry

        lax.fori_loop(0, 2, step, 0, unroll=2)

    for item in chain[0]:
        item.forward()
    normalize(0)
    for item in chain[0]:
        item.forward_rest()
    for item in g_tok[1:]:
        item.forward()
    for g in range(groups):
        for m in range(z.m):
            if g == 0 and m > 0:
                g_tok[m].arrive()
                normalize(m)
                spill(toks, o_toks, "gp")
                spill(hid, o_hid, "gp")
            project(g, m)
            if m == 0 and g > 0 or m == 1 and g == 0:
                for item in chain[g + 1]:
                    item.forward()
            if g == 1 and m == 0:
                send_dy_rows()
            attention(g, m)
            if m == z.m - 1:
                for item in chain[g + 1]:
                    item.forward_rest()
    g_o.arrive()

    def output(i, carry):
        cols = aligned(i * 256, 256, 256)
        mid[:, cols] = dot(ctx[...], fo[:, cols])
        return carry

    lax.fori_loop(0, d // 256, output, 0)
    for m in range(z.m):
        at = slice(m * t, (m + 1) * t)
        x = mid[at, :] + tokens[m].astype(F32)
        mid[at, :] = x
        scale = lax.rsqrt(jnp.mean(x * x, axis=1, keepdims=True) + EPS)
        nrm[at, :] = (x * scale * gain_two).astype(BF)
    logits = dot_t(nrm[...], router)
    lane = iota((mt, z.small), 1)
    pick0 = jnp.sum(jnp.where(lane == route0, logits, 0.0), axis=1, keepdims=True)
    pick1 = jnp.sum(jnp.where(lane == route1, logits, 0.0), axis=1, keepdims=True)
    top = jnp.maximum(pick0, pick1)
    e0, e1 = jnp.exp(pick0 - top), jnp.exp(pick1 - top)
    gate0, gate1 = e0 / (e0 + e1), e1 / (e0 + e1)
    lane = iota((mt, LANES), 1)
    sd[...] = jnp.where(
        lane == 0, slot0, jnp.where(lane == 1, slot1, jnp.where(lane == 2, gate0, jnp.where(lane == 3, gate1, 0.0)))
    )
    gate_row = jnp.sum(one_hot(z, slot0) * gate0 + one_hot(z, slot1) * gate1, axis=0, keepdims=True)
    high = gate_row.astype(BF).astype(F32)
    is_high = iota((2 * z.n16, 1), 0) < z.n16
    gates = (dest[...].astype(F32) * jnp.where(is_high, high, gate_row - high)).astype(BF)
    gates = dot(gates, place_m[...]).astype(BF)
    x_dy.finish()
    to_slots(nrm)
    xs[:, :LANES] = (xs[:, :LANES].astype(F32) + tdot(rows_of[...], gates)).astype(BF)
    x_move.start(even)
    xr[0 : z.sp, :] = xs[mine, :]

    load_out.wait()

    def expert_rows(ref, h, l, cols):
        return ref[:, aligned(h * z.cb + l * z.cr, z.cr, 16), cols].reshape(z.ns * z.cr, -1)

    def gradient(h):
        def step(l, carry):
            g = dot_t(expert_rows(dyg, h, l, slice(None)), w_out[l])
            gp[:, aligned(h * z.cb + l * z.cr, z.cr, 16), :] = g.astype(BF).reshape(z.ns, z.cr, ff)
            return carry

        lax.fori_loop(0, z.el, step, 0)

    def gather_of(h):
        item = base + 1 + (1 + z.el) * h
        out = [Gather(p, gwg.at[p.s, h], lambda o: gwg.at[o, h], gsend, grecv, item)]
        for l in range(z.el):
            at = pl.ds(h * z.cb + l * z.cr, z.cr)
            out.append(Gather(p, xg.at[p.s, at], lambda o, at=at: xg.at[o, at], gsend, grecv, item + 1 + l))
        return out

    gathers = [gather_of(h) for h in range(2)]

    def distribute(h):
        x_move.arrive((even, odd)[h])
        if h == 0:
            x_move.start(odd)
        gwg[p.s, h] = dot(gate_of[...], xr[h * z.hs : (h + 1) * z.hs, :LANES]).astype(BF)
        gathers[h][0].start()
        in_order(xr, xg, h)
        for item in gathers[h][1:]:
            item.start()

    def gates_of(h):
        gathers[h][0].arrive()
        for b in range(z.ns):
            wide = dot(source[...], gwg[b, h]) * pick[...].astype(F32)
            gwc[b] = jnp.sum(wide, axis=1, keepdims=True)

    def activate(h, l):
        at_rows = pl.ds(h * z.cb + l * z.cr, z.cr)
        gate = gwc[:, l * z.cr : (l + 1) * z.cr, :]
        gate_column = gate.reshape(z.ns * z.cr, 1)

        def step(tile, carry):
            at = aligned(tile * 256, 256, 256)
            x = dot(expert_rows(xg, h, l, slice(None)), w_in[l, :, at])
            g = expert_rows(gp, h, l, at).astype(F32)
            x2 = x * x
            th = jnp.tanh(x * (GELU_A + (GELU_A * GELU_B) * x2))
            hx = 0.5 * x
            up = 1.0 + th
            a = hx * up
            act[:, at_rows, at] = a.astype(BF).reshape(z.ns, z.cr, 256)
            slope = 0.5 * up + hx * (1.0 - th * th) * (GELU_A + (3.0 * GELU_A * GELU_B) * x2)
            gp[:, at_rows, at] = (g * gate_column * slope).astype(BF).reshape(z.ns, z.cr, 256)
            toward = jnp.sum(a * g, axis=1, keepdims=True).reshape(z.ns, z.cr, 1)
            ggc[:, at_rows, :] = toward + jnp.where(tile == 0, 0.0, ggc[:, at_rows, :])
            return carry

        lax.fori_loop(0, tiles, step, 0, unroll=tiles)
        dyg[:, at_rows, :] = (dyg[:, at_rows, :].astype(F32) * gate).astype(BF)

    def unit(u):
        h, cols = u // 2, pl.ds((u % 2) * half, half)
        return (
            Scatter(
                p, part.at[u, p.c], part.at[u, 1 - p.c], rp.at[u], ys.at[u], yr.at[u],
                psend.at[u], precv.at[u], ysend.at[u], yrecv.at[u],
            ),
            Return(p, fin.at[u], ret, h, cols, rsend.at[u], rrecv.at[u]),
        )

    units = [unit(u) for u in range(4)]
    results = [
        Scatter(
            p, rpart.at[u, p.c], rpart.at[u, 1 - p.c], rrp.at[u], rys.at[u], ryr.at[u],
            psend.at[4 + u], precv.at[4 + u], ysend.at[4 + u], yrecv.at[4 + u],
        )
        for u in range(2)
    ]

    def products(ref, weight, transposed, dst, h, l):
        rows = expert_rows(ref, h, l, slice(None))
        out = (dot_t(rows, weight[l]) if transposed else dot(rows, weight[l])).astype(BF)
        for b in range(z.ns):
            for c in range(2):
                block = out[b * z.cr : (b + 1) * z.cr, c * half : (c + 1) * half]
                dst[2 * h + c, b % 2, b // 2, l * z.cr : (l + 1) * z.cr, :] = block

    def stage_a(h, l):
        products(gp, w_in, True, part, h, l)
        if l == z.el - 1:
            units[2 * h][0].send()
            units[2 * h + 1][0].send()

    def stage_b(u):
        units[u][0].middle()

    def stage_c(u):
        fin[u] = tdot(perm[...], units[u][0].total().astype(BF)).astype(BF)
        units[u][1].start()

    g_scatter = Scatter(
        p, gpart.at[p.c], gpart.at[1 - p.c], grp, gys, gyr, gsem.at[0], gsem.at[1], gsy.at[0], gsy.at[1]
    )

    def toward_a():
        for b in range(z.ns):
            for h in range(2):
                col = ggc[b, h * z.cb : (h + 1) * z.cb, :]
                high = col.astype(BF).astype(F32)
                put = pick[...].astype(F32)
                top = tdot(source[...], (high * put).astype(BF))
                rest = tdot(source[...], ((col - high) * put).astype(BF))
                both = jnp.where(iota(top.shape, 0) < z.n16, top, rest)
                gpart[b % 2, b // 2, h * 2 * z.n16 : (h + 1) * 2 * z.n16, :] = both.astype(BF)
        g_scatter.send()

    def toward_copy(k):
        back = (-k[0] % z.nz, k[1])
        return rcopy(
            gout.at[k[0] % 2], gret.at[position(z, back)], gsx.at[0, position(z, k) - 1], gsx.at[1, position(z, back) - 1],
            (p.expert(*k), p.s),
        )

    def toward_c():
        total = g_scatter.total()
        for h in range(2):
            first = total[h * 2 * z.n16 : h * 2 * z.n16 + z.n16]
            value = first + total[h * 2 * z.n16 + z.n16 : (h + 1) * 2 * z.n16]
            high, rest = split_high(value)
            gout[h, 0 : z.n16, :] = high
            gout[h, z.n16 : 2 * z.n16, :] = rest
        for k in offsets(z):
            toward_copy(k).start()
        gret[0] = gout[0]

    def toward_d():
        for k in offsets(z):
            toward_copy((-k[0] % z.nz, k[1])).wait_recv()
        line = iota((2 * z.n16, LANES), 0)
        out = jnp.zeros((2 * z.n16, LANES), F32)
        for k in [(0, 0)] + offsets(z):
            back = (-k[0] % z.nz, k[1])
            at = position(z, back) - (k[0] % 2) * z.hn
            got = gret[position(z, k)].astype(F32)
            rank = p.expert(*k)
            out = jnp.where(line == rank, got[at : at + 1, :], out)
            out = jnp.where(line == z.n16 + rank, got[z.n16 + at : z.n16 + at + 1, :], out)
        ggrows[...] = out.astype(BF)
        for k in offsets(z):
            toward_copy(k).wait_send()

    def both(ref, l, cols):
        return jnp.concatenate([expert_rows(ref, h, l, cols) for h in range(2)], 0)

    stores = []

    def weight_grad(n, left, right, out, l):
        if n >= 2:
            stores[n - 2].wait()

        def step(i, carry):
            at = aligned(i * 256, 256, 256)
            wstage[n % 2, :, at] = tdot(both(left, l, slice(None)), both(right, l, at)).astype(BF)
            return carry

        lax.fori_loop(0, d // 256, step, 0)
        copy = pltpu.make_async_copy(wstage.at[n % 2], out.at[l], csem.at[2 + n])
        copy.start()
        stores.append(copy)

    def result_a(h):
        for l in range(z.el):
            products(act, w_out, False, rpart, h, l)
        for u in (2 * h, 2 * h + 1):
            if h == 0:
                results[u].send()
            else:
                spill(rpart.at[u], o_rpart.at[u - 2])

    def result_c(u):
        units[u][1].finish()
        fin[u] = tdot(perm[...], results[u].total().astype(BF)).astype(BF)
        spill(fin.at[u], o_rfin.at[u])

    spill(kk, o_kk, "act")
    spill(vv, o_vv, "act")
    g_dy.forward()
    g_dy.arrive()
    for copy in waiting["gp"]:
        copy.wait()
    for item in g_tok:
        item.finish()
    gradient(0)
    gradient(1)
    distribute(0)
    load_in.wait()
    for copy in waiting["act"]:
        copy.wait()
    g_dy.finish()
    gathers[0][0].forward()
    gathers[0][1].forward()
    gates_of(0)
    gathers[0][1].arrive()
    activate(0, 0)
    stage_a(0, 0)
    for l in range(1, z.el):
        gathers[0][1 + l].forward()
    distribute(1)
    for l in range(1, z.el):
        gathers[0][1 + l].arrive()
        activate(0, l)
        stage_a(0, l)
    gathers[1][0].forward()
    stage_b(0)
    stage_b(1)
    gathers[1][1].forward()
    gates_of(1)
    result_a(0)
    gathers[1][1].arrive()
    activate(1, 0)
    stage_a(1, 0)
    for l in range(1, z.el):
        gathers[1][1 + l].forward()
        gathers[1][1 + l].arrive()
        activate(1, l)
        stage_a(1, l)
    toward_a()
    stage_b(2)
    stage_b(3)
    g_scatter.middle()
    stage_c(0)
    stage_c(1)
    results[0].middle()
    results[1].middle()
    result_a(1)
    for src, dst in (
        (sd, o_sd), (mid, o_mid), (nrm, o_nrm), (ctx, o_ctx), (fo, o_fo), (qq, o_qq), (pp, o_pp), (fk, o_fk), (fv, o_fv),
        (fq, o_fq),
    ):
        spill(src, dst)
    weight_grad(0, act, dyg, dout, 0)
    stage_c(2)
    weight_grad(1, act, dyg, dout, 1)
    stage_c(3)
    toward_c()
    weight_grad(2, xg, gp, din, 0)
    result_c(0)
    weight_grad(3, xg, gp, din, 1)
    result_c(1)
    toward_d()
    for u in range(4):
        units[u][1].arrive()
    spill(ret, o_ret)
    for item in [g_small] + sum(g_w, []) + [g_o] + list(gathers[0]) + list(gathers[1]):
        item.finish()
    x_move.finish()
    g_scatter.finish()
    for u in (2, 3):
        units[u][1].finish()
    for scatter, _ in units:
        scatter.finish()
    for scatter in results:
        scatter.finish()
    for copy in waiting[None] + stores[2:]:
        copy.wait()


ANY = pl.BlockSpec(memory_space=pl.ANY)


def forward(z, *inputs):
    def bf(*shape):
        return jax.ShapeDtypeStruct(shape, BF)

    def f32(*shape):
        return jax.ShapeDtypeStruct(shape, F32)

    def vm(x):
        return pltpu.VMEM(x.shape, x.dtype)

    dma = pltpu.SemaphoreType.DMA
    half, ny, nb = z.d // 2, z.ny, 2 * z.n16
    kept = (
        bf(z.m, z.g, z.d), bf(z.m, z.g, z.d), bf(z.m, z.g, z.d), bf(z.m, z.g, z.d), bf(z.mt, z.d),
        bf(z.m * z.pairs, 2 * z.t, z.g), bf(z.mt, z.d), f32(z.mt, z.d), bf(z.mt, z.d), f32(z.mt, LANES),
        bf(z.d, z.d), bf(z.d, z.d), bf(z.d, z.d), bf(z.d, z.d),
    )
    smallg = bf(z.ns, z.small, z.d)
    ret, rpart, rfin = bf(z.slots, z.d), bf(4, 2, ny, z.cb, half), bf(4, z.hs, half)
    outs = kept + (smallg, ret, bf(2, z.hs, half), bf(2, 2, ny, z.cb, half), bf(nb, LANES), bf(z.el, z.d, z.ff), bf(z.el, z.ff, z.d))
    rows = bf(z.ns, z.blk, z.d)
    scratch = [vm(x) for x in kept[4:]]
    scratch += [vm(bf(z.small, z.d)), vm(smallg)]
    scratch += [vm(ret)] * 3 + [vm(rows)] * 2 + [vm(bf(z.ns, z.blk, z.ff))] * 2
    scratch += [vm(bf(z.el, z.d, z.ff)), vm(bf(z.el, z.ff, z.d))]
    scratch += [pltpu.VMEM((8, LANES), F32), pltpu.VMEM((z.m, z.t, z.g), I32)]
    scratch += [vm(bf(z.ns, 2, nb, LANES)), vm(f32(z.ns, z.cb, 1)), vm(f32(z.ns, z.blk, 1))]
    shares = [vm(rpart), vm(bf(4, ny, z.cb, half)), vm(bf(4, ny - 1, z.cb, half)), vm(bf(4, ny - 1, z.cb, half))]
    scratch += shares + [vm(rfin), vm(ret)] + [vm(rpart), vm(bf(2, ny, z.cb, half)), vm(bf(2, ny - 1, z.cb, half)), vm(bf(2, ny - 1, z.cb, half))]
    scratch += [vm(bf(2, z.d, z.d))]
    scratch += [vm(bf(2, ny, 2 * nb, LANES)), vm(bf(ny, 2 * nb, LANES))]
    scratch += [vm(bf(ny - 1, 2 * nb, LANES))] * 2 + [vm(bf(2, nb, LANES)), vm(bf(z.ne, nb, LANES))]
    n_items, n_weights = 1 + z.m + 3 + 2 * z.el, 3 * (z.d // 256) + 1
    scratch += [dma((10,)), dma((20,)), dma((n_items, 2 * ny - 1)), dma((n_items, 2 * ny - 1))]
    scratch += [dma((n_weights, 4 * ny - 3))] * 2 + [dma((2, z.ne - 1))] * 2
    scratch += [dma((6,))] * 2 + [dma((6, ny - 1))] * 2 + [dma((4, z.hn))] * 2
    scratch += [dma((2,)), dma((2, ny - 1)), dma((2, z.ne - 1))]
    return pl.pallas_call(
        functools.partial(forward_kernel, z),
        out_shape=outs,
        in_specs=[VMEM] * 3 + [SMEM] + [ANY] * 4 + [VMEM] * 2 + [ANY] * 2 + [VMEM] * 7,
        out_specs=[ANY] * 18 + [VMEM] + [ANY] * 2,
        scratch_shapes=scratch,
        compiler_params=pltpu.CompilerParams(
            collective_id=0, has_side_effects=True, vmem_limit_bytes=63 * 2**20
        ),
        name="forward",
    )(*inputs)


class Reduce:
    def __init__(self, place, part, from_core, to_y, from_y, to_x, from_x, summed, near_in, mid, mid_in, done, sems):
        self.p, self.part, self.from_core, self.done, self.sems = place, part, from_core, done, sems
        self.to_y, self.from_y, self.to_x, self.from_x = to_y, from_y, to_x, from_x
        self.summed, self.near_in, self.mid, self.mid_in = summed, near_in, mid, mid_in
        self.rows = done.shape[0] // 4
        self.x, zz = lax.rem(place.e, 2), lax.div(place.e, 2)
        self.side = lax.rem(zz, 2)
        self.near_at = ((zz + 1 - 2 * self.side) * 2 + self.x, place.s)

    def x_rows(self, x):
        return aligned(x * (2 * self.rows), 2 * self.rows, 16)

    def side_rows(self, side):
        return aligned(side * self.rows, self.rows, 16)

    def done_rows(self, side):
        return aligned((self.x * 2 + side) * self.rows, self.rows, 16)

    def hop(self, n, src, dst, to):
        return rcopy(src, dst, self.sems.at[0, n], self.sems.at[1, n], to)

    def copy(self, n, out=True):
        p = self.p
        if n == 0:
            return self.hop(0, self.part.at[1 - p.c], self.from_core, (p.e, p.shard(0, True)))
        if n == 2:
            return self.hop(2, self.to_x, self.from_x, (p.expert(0, 1), p.s))
        if n == 3:
            return self.hop(3, self.summed.at[self.side_rows(1 - self.side)], self.near_in, self.near_at)
        if n == 4:
            return self.hop(4, self.mid, self.mid_in, (p.expert(2, 0), p.s))
        if n == 5:
            block = self.done.at[self.done_rows(self.side if out else 1 - self.side)]
            return self.hop(5, block, block, self.near_at)
        block = self.done.at[self.x_rows(self.x if out else 1 - self.x)]
        return self.hop(6, block, block, (p.expert(0, 1), p.s))

    def copy_y(self, k):
        p = self.p
        return self.hop(6 + k if k > 1 else 1, self.to_y.at[k - 1], self.from_y.at[k - 1], (p.e, p.shard(k, False)))

    def chip(self, y, rows=slice(None)):
        return self.part[self.p.c, y, rows, :].astype(F32) + self.from_core[y, rows, :].astype(F32)

    def step(self, n):
        p, ny = self.p, self.p.z.ny
        if n == 2:
            for k in range(1, ny):
                self.copy_y(k).wait_recv()
        elif n > 0:
            self.copy(n - 1, False).wait_recv()
        if n == 1:
            for k in range(1, ny):
                self.to_y[k - 1] = self.chip(lax.rem(p.y + k, ny)).astype(BF)
                self.copy_y(k).start()
        elif n == 2:
            def whole(x):
                out = self.chip(p.y, self.x_rows(x))
                for k in range(1, ny):
                    out = out + self.from_y[k - 1, self.x_rows(x), :].astype(F32)
                return out.astype(BF)

            self.to_x[...] = whole(1 - self.x)
            self.summed[...] = whole(self.x)
        elif n == 3:
            self.summed[...] = (self.summed[...].astype(F32) + self.from_x[...].astype(F32)).astype(BF)
        elif n == 4:
            own = self.summed[self.side_rows(self.side), :].astype(F32)
            self.mid[...] = (own + self.near_in[...].astype(F32)).astype(BF)
        elif n == 5:
            out = self.mid[...].astype(F32) + self.mid_in[...].astype(F32)
            self.done[self.done_rows(self.side), :] = out.astype(BF)
        if n != 1 and n < 7:
            self.copy(n).start()

    def finish(self):
        for n in (0, 2, 3, 4, 5, 6):
            self.copy(n).wait_send()
        for k in range(1, self.p.z.ny):
            self.copy_y(k).wait_send()


class SmallReduce:
    def __init__(self, place, part, from_core, to_y, from_y, own, other, sems):
        self.p, self.part, self.from_core = place, part, from_core
        self.to_y, self.from_y, self.own, self.other, self.sems = to_y, from_y, own, other, sems
        zz = lax.div(place.e, 2)
        near = ((zz + 1 - 2 * lax.rem(zz, 2)) * 2 + lax.rem(place.e, 2), place.s)
        self.partners = [(place.expert(0, 1), place.s), near, (place.expert(2, 0), place.s)]

    def copy(self, n):
        p = self.p
        sems = self.sems.at[0, n], self.sems.at[1, n]
        if n == 0:
            return rcopy(self.part.at[1 - p.c], self.from_core, *sems, (p.e, p.shard(0, True)))
        return rcopy(self.own.at[n - 2], self.other.at[n - 2], *sems, self.partners[n - 2])

    def copy_y(self, k):
        p = self.p
        return rcopy(
            self.to_y.at[k - 1], self.from_y.at[k - 1], self.sems.at[0, 4 + k], self.sems.at[1, 4 + k],
            (p.e, p.shard(k, False)),
        )

    def step(self, n):
        p, ny = self.p, self.p.z.ny
        if n == 0:
            self.copy(0).start()
        elif n == 1:
            self.copy(0).wait_recv()
            for k in range(1, ny):
                y = lax.rem(p.y + k, ny)
                self.to_y[k - 1] = (self.part[p.c, y].astype(F32) + self.from_core[y].astype(F32)).astype(BF)
                self.copy_y(k).start()
        elif n == 2:
            out = self.part[p.c, p.y].astype(F32) + self.from_core[p.y].astype(F32)
            for k in range(1, ny):
                self.copy_y(k).wait_recv()
                out = out + self.from_y[k - 1].astype(F32)
            self.own[0] = out.astype(BF)
            self.copy(2).start()
        else:
            self.copy(n - 1).wait_recv()
            out = self.own[n - 3].astype(F32) + self.other[n - 3].astype(F32)
            if n == 5:
                return out
            self.own[n - 2] = out.astype(BF)
            self.copy(n).start()

    def finish(self):
        for n in (0, 2, 3, 4):
            self.copy(n).wait_send()
        for k in range(1, self.p.z.ny):
            self.copy_y(k).wait_send()


GROUPS = ((0, 1), (2, 3), (4,), (5,))


def backward_kernel(
    z,
    dy, counts, routes, dest, place_m, perm, ggrows,
    i_toks, i_hid, i_kk, i_vv, i_qq, i_pp, i_ctx, i_mid, i_nrm, i_sd, i_fk, i_fv, i_fq, i_fo, i_small, i_ret, i_rfin, i_rpart,
    mixed, dtok, done_o, done_0, done_1, done_2, done_3, drouter, dvecs,
    toks, hid, kk, vv, qq, pp, ctx, mid, nrm, sd, fk, fv, fq, fo, smallg, ret, retr,
    fin, rmine, rp, rys, ryr, gctx, gqb, gkb, gvb, gmid, lower, edge_id, edge_ok, tab, gain_rows,
    red_o, red_0, red_1, red_2, red_3,
    gpart, grp, gys, gyr, sbuf, small_refs,
    csem, rr1, rr2, rs1, rs2, rs3, rs4,
    gp1, gp2, gy1, gy2,
):
    p = Place(z)
    t, d, mt = z.t, z.d, z.mt
    half = d // 2
    loads = {}

    def load(src, dst, name):
        loads[name] = pltpu.make_async_copy(src, dst, csem.at[len(loads)])
        loads[name].start()

    load(i_sd, sd, "sd")
    load(i_ret, ret, "ret")
    load(i_small, smallg, "small")
    load(i_mid, mid, "mid")
    load(i_nrm, nrm, "nrm")
    load(i_ctx, ctx, "ctx")
    load(i_fo, fo, "fo")
    for u in range(2):
        load(i_rpart.at[u, p.c], rmine.at[u], ("part", u))
    load(i_qq, qq, "qq")
    load(i_vv, vv, "vv")
    load(i_kk, kk, "kk")
    load(i_pp, pp, "pp")
    load(i_hid, hid, "hid")
    load(i_fk, fk, "fk")
    load(i_fv, fv, "fv")
    load(i_fq, fq, "fq")
    load(i_toks, toks, "toks")
    p.barrier()

    returns, halves = [], []
    for u in range(4):
        h, cols = u // 2, pl.ds((u % 2) * half, half)
        src = i_rfin.at[u] if h == 0 else fin.at[u - 2]
        returns.append(Return(p, src, retr, h, cols, rr1.at[u], rr2.at[u]))
        if h == 0:
            returns[u].start_remote()
            load(i_rfin.at[u, pl.ds(0, z.sp)], retr.at[aligned(p.e * z.sp, z.sp, 16), cols], ("r", u))
    for u in range(2):
        halves.append(
            Scatter(
                p, rmine.at[u], i_rpart.at[u, 1 - p.c], rp.at[u], rys.at[u], ryr.at[u],
                rs1.at[u], rs2.at[u], rs3.at[u], rs4.at[u],
            )
        )
        halves[u].send()

    def result_b(u):
        loads["part", u].wait()
        halves[u].middle()

    def result_c(u):
        fin[u] = tdot(perm[...], halves[u].total().astype(BF)).astype(BF)
        returns[2 + u].start_remote()

    route0, route1 = route_columns(z, routes)
    loads["sd"].wait()
    slot0, slot1 = sd[:, 0:1], sd[:, 1:2]
    gate0, gate1 = sd[:, 2:3], sd[:, 3:4]
    hot0, hot1 = one_hot(z, slot0).astype(BF), one_hot(z, slot1).astype(BF)
    hot = hot0 + hot1

    def toward(hots):
        wide = dot(dot_t(hots, dest[...]).astype(BF), ggrows[...]) * dot(hots, place_m[...])
        return jnp.sum(wide, axis=1, keepdims=True)

    toward0, toward1 = toward(hot0), toward(hot1)
    mean = gate0 * toward0 + gate1 * toward1
    lane = iota((mt, z.small), 1)
    glog = jnp.where(lane == route0, gate0 * (toward0 - mean), 0.0)
    glog = (glog + jnp.where(lane == route1, gate1 * (toward1 - mean), 0.0)).astype(BF)
    result_b(0)
    loads["small"].wait()
    sums = smallg[0].astype(F32)
    for b in range(1, z.ns):
        sums = sums + smallg[b].astype(F32)
    gain_one = sums[z.e : z.e + 1, :]
    gain_two = sums[z.e + 1 : z.e + 2, :]
    router = sums.astype(BF)
    loads["ret"].wait()
    gnorm = dot(glog, router) + dot(hot, ret[...])
    loads["mid"].wait()
    x = mid[...]
    scale = lax.rsqrt(jnp.mean(x * x, axis=1, keepdims=True) + EPS)
    xh = x * scale
    gain_rows[1:2, :] = jnp.sum(gnorm * xh, axis=0, keepdims=True)
    gy = gnorm * gain_two
    gm = dy[...].astype(F32) + scale * (gy - xh * jnp.mean(gy * xh, axis=1, keepdims=True))
    gmid[...] = gm
    gattn = gm.astype(BF)
    loads["nrm"].wait()
    sbuf[...] = tdot(glog, nrm[...])

    reductions = [
        Reduce(p, *refs[:-1], done, refs[-1])
        for refs, done in ((red_0, done_0), (red_1, done_1), (red_2, done_2), (red_3, done_3), (red_o, done_o))
    ]
    parts = [red_0[0], red_1[0], red_2[0], red_3[0], red_o[0]]

    def stage(u, n):
        reductions[u].step(n)

    def put(u, first, value):
        value = value.astype(BF)
        for b in range(z.ns):
            parts[u][b % 2, b // 2, :, first : first + value.shape[1]] = value[b * z.r : (b + 1) * z.r]

    loads["ctx"].wait()
    for i in range(d // 256):
        put(4, i * 256, tdot(ctx[...], gattn[:, i * 256 : (i + 1) * 256]))
    stage(4, 0)
    loads["fo"].wait()
    for i in range(d // 256):
        cols = slice(i * 256, (i + 1) * 256)
        gctx[:, cols] = dot_t(gattn, fo[cols, :]).astype(BF)

    tab[...] = jnp.zeros_like(tab)
    lane = iota((1, LANES), 1)
    starts = jnp.where(lane <= 16, lane, 0)
    for i, edge in enumerate(BUCKET_EDGES):
        starts = jnp.where(lane == 17 + i, edge, starts)
    for m in range(z.m):
        key_pos, _ = key_layout(z, counts, m, (z.g, 1), 0)
        lower[m] = jnp.where(key_pos <= iota((z.g, z.far), 1), 1.0, 0.0).astype(BF)
        at = query_position(z, counts, m, p.s) - starts
        ok = (at >= 0) & (lane < BUCKETS)
        edge_id[m] = jnp.where(ok, at, 0)
        edge_ok[m] = jnp.where(ok, 1.0, 0.0)
    low = iota((t, LANES), 1) < 64

    def attend_back(i, unit):
        m = lax.rem(i, z.m)
        pair = unit
        cols = aligned(pair * LANES, LANES, LANES)
        rows = aligned(m * t, t, 16)
        q, g = qq[rows, cols], gctx[rows, cols]
        zero = jnp.zeros_like(q)
        q_two = jnp.concatenate([jnp.where(low, q, zero), jnp.where(low, zero, q)], 0)
        g_two = jnp.concatenate([jnp.where(low, g, zero), jnp.where(low, zero, g)], 0)
        probs = pp[m * z.pairs + pair]
        pf = probs.astype(F32)
        gp = dot_t(g_two, vv[m, :, cols])
        gs = (pf * (gp - jnp.sum(pf * gp, axis=1, keepdims=True))).astype(BF)
        two = dot(gs, kk[m, :, cols])
        gqb[rows, cols] = (jnp.where(low, two[:t], two[t:]) * 0.125).astype(BF)
        gkb[m, :, cols] = tdot(gs, q_two).astype(BF)
        gvb[m, :, cols] = tdot(probs, g_two).astype(BF)
        total = dot(gs, lower[m])
        for side in range(2):
            found = jnp.zeros((t, LANES), F32)
            for b in range(z.far // LANES):
                at = edge_id[m] - b * LANES
                inside = (at >= 0) & (at < LANES)
                got = jnp.take_along_axis(
                    total[side * t : (side + 1) * t, b * LANES : (b + 1) * LANES], jnp.where(inside, at, 0), axis=1
                )
                found = jnp.where(inside, got, found)
            found = jnp.sum(found * edge_ok[m], axis=0, keepdims=True)
            row = pl.ds(pair * 2 + side, 1)
            tab[row, :] = tab[row, :] + found
        return unit

    def attention(pair):
        lax.fori_loop(0, z.m, attend_back, pair, unroll=2)

    def own_hidden():
        return jnp.concatenate([hid[m, aligned(p.s * t, t, 16), :] for m in range(z.m)], 0)

    def weight_grads(u):
        n = len(GROUPS[u]) * LANES
        cols = slice(GROUPS[u][0] * LANES, GROUPS[u][0] * LANES + n)
        put(u, 0, tdot(own_hidden(), gqb[:, cols]))
        every = hid[...].reshape(z.m * z.g, d)
        put(u, n, tdot(every, gkb[:, :, cols].reshape(z.m * z.g, n)))
        put(u, 2 * n, tdot(every, gvb[:, :, cols].reshape(z.m * z.g, n)))

    grads = [
        Scatter(
            p, gpart.at[m, p.c], gpart.at[m, 1 - p.c], grp.at[m], gys.at[m], gyr.at[m],
            gp1.at[m], gp2.at[m], gy1.at[m], gy2.at[m],
        )
        for m in range(z.m)
    ]

    def hidden_grads(m):
        x = toks[m].astype(F32)
        scale = lax.rsqrt(jnp.mean(x * x, axis=1, keepdims=True) + EPS)
        for i in range(d // 256):
            cols = slice(i * 256, (i + 1) * 256)
            gh = dot_t(gkb[m], fk[cols, :]) + dot_t(gvb[m], fv[cols, :])
            own = dot_t(gqb[m * t : (m + 1) * t, :], fq[cols, :])
            for b in range(z.ns):
                rows = slice(b * t, (b + 1) * t)
                part = gh[rows] + jnp.where(p.s == b, 1.0, 0.0) * own
                gpart[m, b % 2, b // 2, :, cols] = part.astype(BF)
                row = jnp.sum(part * (toks[m, rows, cols].astype(F32) * scale[rows]), axis=0, keepdims=True)
                if m == 0 and b == 0:
                    gain_rows[0:1, cols] = row
                else:
                    gain_rows[0:1, cols] = gain_rows[0:1, cols] + row

    def token_grads(m):
        gh = grads[m].total()
        rows = slice(m * t, (m + 1) * t)
        x = toks[m, aligned(p.s * t, t, 16), :].astype(F32)
        scale = lax.rsqrt(jnp.mean(x * x, axis=1, keepdims=True) + EPS)
        xh = x * scale
        gy = gh * gain_one
        dtok[rows, :] = gmid[rows, :] + scale * (gy - xh * jnp.mean(gy * xh, axis=1, keepdims=True))

    small_sum = SmallReduce(p, *small_refs)

    def small_step(n):
        if n:
            return small_sum.step(n)
        tabs = tab[...]
        tabs = tabs - pltpu.roll(tabs, LANES - 1, 1)
        tabs = jnp.where(iota(tabs.shape, 1) < BUCKETS, tabs, 0.0)
        row = iota(sbuf.shape, 0)
        out = sbuf[...]
        out = jnp.where(row == z.e, gain_rows[0:1, :], out)
        out = jnp.where(row == z.e + 1, gain_rows[1:2, :], out)
        sbuf[...] = out
        per = LANES // BUCKETS
        for c in range(HEADS // per):
            piece = tabs[c * per : c * per + 1, :]
            for j in range(1, per):
                piece = piece + pltpu.roll(tabs[c * per + j : c * per + j + 1, :], j * BUCKETS, 1)
            sbuf[z.e + 2 : z.e + 3, c * LANES : (c + 1) * LANES] = piece
        every = sbuf[...].astype(BF)
        tail = every[z.e : z.small, :]
        for b in range(z.ns):
            block = dot_t(every, spread(z, b, z.r))
            biases = dot_t(tail, spread(z, b, HEADS * BUCKETS // z.ns))
            low_rows = jnp.where(iota(biases.shape, 0) == 2, biases, block[z.e : z.small])
            small_refs[0][b % 2, b // 2, 0 : z.e, :] = block[0 : z.e].astype(BF)
            small_refs[0][b % 2, b // 2, z.e : z.small, :] = low_rows.astype(BF)
        small_sum.step(0)

    def finish_mixed():
        for u in range(4):
            returns[u].arrive()
        for u in range(2):
            loads["r", u].wait()
        for m in range(z.m):
            rows = slice(m * t, (m + 1) * t)
            first, second = dot(hot0[rows], retr[...]), dot(hot1[rows], retr[...])
            mixed[rows, :] = (mid[rows, :] + gate0[rows] * first + gate1[rows] * second).astype(BF)

    for name in ("qq", "vv", "kk", "pp"):
        loads[name].wait()
    attention(0)
    stage(4, 1)
    attention(1)
    loads["hid"].wait()
    weight_grads(0)
    stage(0, 0)
    result_c(0)
    attention(2)
    stage(0, 1)
    attention(3)
    stage(4, 2)
    weight_grads(1)
    stage(1, 0)
    attention(4)
    stage(1, 1)
    weight_grads(2)
    stage(2, 0)
    stage(4, 3)
    attention(5)
    stage(2, 1)
    weight_grads(3)
    stage(3, 0)
    stage(0, 2)
    stage(4, 4)
    for name in ("fk", "fv", "fq", "toks"):
        loads[name].wait()
    hidden_grads(0)
    grads[0].send()
    stage(3, 1)
    stage(4, 5)
    stage(0, 3)
    hidden_grads(1)
    grads[1].send()
    small_step(0)
    stage(1, 2)
    stage(4, 6)
    stage(0, 4)
    small_step(1)
    result_b(1)
    grads[0].middle()
    grads[1].middle()
    stage(2, 2)
    stage(1, 3)
    stage(0, 5)
    stage(3, 2)
    small_step(2)
    stage(2, 3)
    stage(1, 4)
    stage(3, 3)
    stage(0, 6)
    small_step(3)
    stage(2, 4)
    stage(1, 5)
    stage(3, 4)
    result_c(1)
    small_step(4)
    stage(2, 5)
    stage(1, 6)
    stage(3, 5)
    token_grads(0)
    out = small_step(5)
    drouter[...] = out[0 : z.e, :]
    dvecs[...] = out[z.e : z.small, :]
    stage(2, 6)
    stage(3, 6)
    token_grads(1)
    finish_mixed()
    for u in (4, 0, 1, 2, 3):
        stage(u, 7)
    for item in reductions + returns + halves + grads + [small_sum]:
        item.finish()


def backward(z, *inputs):
    def bf(*shape):
        return pltpu.VMEM(shape, BF)

    def f32(*shape):
        return jax.ShapeDtypeStruct(shape, F32)

    dma = pltpu.SemaphoreType.DMA
    d, r, ny, nz, half = z.d, z.r, z.ny, z.nz, z.d // 2
    widths = [d] + [3 * LANES * len(g) for g in GROUPS]
    blocks = [jax.ShapeDtypeStruct((r, w), BF) for w in widths]
    outs = (jax.ShapeDtypeStruct((z.mt, d), BF), f32(z.mt, d), *blocks, f32(z.e, r), f32(z.small - z.e, r))

    def reduction(w):
        half, piece = bf(r // 2, w), bf(r // 4, w)
        return (
            bf(2, ny, r, w), bf(ny, r, w), bf(ny - 1, r, w), bf(ny - 1, r, w), half, half, half, piece, piece, piece,
            dma((2, 5 + ny)),
        )

    small = (
        bf(2, ny, z.small, r), bf(ny, z.small, r), bf(ny - 1, z.small, r), bf(ny - 1, z.small, r),
        bf(3, z.small, r), bf(3, z.small, r), dma((2, 4 + ny)),
    )
    kept = [pltpu.VMEM(x.shape, x.dtype) for x in inputs[7:-2]]
    return pl.pallas_call(
        functools.partial(backward_kernel, z),
        out_shape=outs,
        in_specs=[VMEM, SMEM] + [VMEM] * 5 + [ANY] * 18,
        out_specs=[VMEM] * len(outs),
        scratch_shapes=kept + [
            bf(z.slots, d),
            bf(2, z.hs, half), bf(2, ny, z.cb, half), bf(2, ny, z.cb, half), bf(2, ny - 1, z.cb, half), bf(2, ny - 1, z.cb, half),
            bf(z.mt, d), bf(z.mt, d), bf(z.m, z.g, d), bf(z.m, z.g, d), pltpu.VMEM((z.mt, d), F32),
            bf(z.m, z.g, z.far), pltpu.VMEM((z.m, z.t, LANES), I32), pltpu.VMEM((z.m, z.t, LANES), F32),
            pltpu.VMEM((16, LANES), F32), pltpu.VMEM((8, d), F32),
            *[reduction(w) for w in widths],
            bf(z.m, 2, ny, z.t, d), bf(z.m, ny, z.t, d), bf(z.m, ny - 1, z.t, d), bf(z.m, ny - 1, z.t, d),
            pltpu.VMEM((z.small, d), F32), small,
            dma((20,)), dma((4, z.hn)), dma((4, z.hn)), dma((2,)), dma((2,)), dma((2, ny)), dma((2, ny)),
            dma((z.m,)), dma((z.m,)), dma((z.m, ny)), dma((z.m, ny)),
        ],
        compiler_params=pltpu.CompilerParams(
            collective_id=1, has_side_effects=True, vmem_limit_bytes=63 * 2**20
        ),
        name="backward",
    )(*inputs)


def finish_kernel(
    d_o, d_0, d_1, d_2, d_3, din, dout, mixed, dtok, vecs, o_mixed, o_dtok, o_q, o_k, o_v, o_o, o_in, o_out, o_one, o_two, o_bias
):
    o_in[...] = din[...].astype(F32)
    o_out[...] = dout[...].astype(F32)
    o_mixed[...] = mixed[...]
    o_dtok[...] = dtok[...]
    o_o[...] = d_o[...].astype(F32)
    o_one[...] = vecs[0:1, :]
    o_two[...] = vecs[1:2, :]
    o_bias[...] = vecs[2:3, : o_bias.shape[1]]
    for pairs, block in zip(GROUPS, (d_0, d_1, d_2, d_3)):
        n, first = len(pairs) * LANES, pairs[0] * LANES
        for i, out in enumerate((o_q, o_k, o_v)):
            out[:, first : first + n] = block[:, i * n : (i + 1) * n].astype(F32)


def finish(z, n_bias, blocks, din, dout, mixed, dtok, vecs):
    d, r, n = z.d, z.r, 4
    rows = z.el * d // n

    def f32(*shape):
        return jax.ShapeDtypeStruct(shape, F32)

    def by_row(size, width=d):
        return pl.BlockSpec((size, width), lambda i: (i, 0))

    def once(*shape):
        return pl.BlockSpec(shape, lambda i: (0, 0))

    return pl.pallas_call(
        finish_kernel,
        grid=(n,),
        out_shape=(
            jax.ShapeDtypeStruct((z.mt, d), BF), f32(z.mt, d), *[f32(r, d)] * 4, *[f32(n * rows, d)] * 2,
            f32(1, r), f32(1, r), f32(1, n_bias),
        ),
        in_specs=[by_row(r // n, b.shape[1]) for b in blocks] + [by_row(rows)] * 2 + [by_row(z.mt // n)] * 2
        + [once(*vecs.shape)],
        out_specs=[by_row(z.mt // n)] * 2 + [by_row(r // n)] * 4 + [by_row(rows)] * 2
        + [once(1, r), once(1, r), once(1, n_bias)],
        name="finish",
    )(*blocks, din.reshape(n * rows, d), dout.reshape(n * rows, d), mixed, dtok, vecs)


def fused_device(
    z, tokens, cotangent, routes, prompt_rows, w_query, w_key, w_value, w_output, w_router, gain_attn, gain_ffn,
    pos_table, w_in, w_out,
):
    perm, rows_of, dest, place, gate_of, source, pick = layout_constants(z)
    n = pos_table.shape[0]
    vecs = jnp.concatenate([gain_attn, gain_ffn, pos_table])[None]
    dy = cotangent.reshape(z.mt, z.d)
    routes = routes.transpose(0, 2, 1)
    counts = prompt_rows[:, 0]
    kept = forward(
        z, tokens, dy, routes, counts, w_key, w_value, w_query, w_output, w_router.T, vecs, w_in, w_out,
        perm, rows_of, dest, place, gate_of, source, pick,
    )
    kept, (ggrows, din, dout) = kept[:18], kept[18:]
    mixed, dtok, *blocks, drouter, dvecs = backward(z, dy, counts, routes, dest, place, perm, ggrows, *kept)
    mixed, dtok, dq, dk, dv, do, din, dout, one, two, bias = finish(z, n, blocks, din, dout, mixed, dtok, dvecs)
    return (
        mixed.reshape(tokens.shape),
        dtok.reshape(tokens.shape),
        dq,
        dk,
        dv,
        do,
        drouter.T,
        one.reshape(-1),
        two.reshape(-1),
        bias.reshape(-1),
        din.reshape(w_in.shape),
        dout.reshape(w_out.shape),
    )


HIGHEST = lax.Precision.HIGHEST


def distance_bucket(distance):
    coarse = reduce(
        lambda running, border: running + (distance >= border).astype(jnp.int32),
        BUCKET_EDGES,
        jnp.full(distance.shape, 16, jnp.int32),
    )
    return jnp.where(distance < 16, distance, coarse)


def layout(counts, block_rows):
    shard_count = counts.shape[0]
    offsets = jnp.cumsum(counts, dtype=jnp.int32) - counts
    row_index = jnp.arange(shard_count * block_rows, dtype=jnp.int32)
    device = row_index // block_rows
    local_row = row_index - device * block_rows
    own_count = counts[device]
    is_prompt = local_row < own_count
    prompt_total = jnp.sum(counts, dtype=jnp.int32)
    position = jnp.where(
        is_prompt, offsets[device] + local_row, prompt_total + local_row - own_count
    )
    return (position, is_prompt, device)


def rms_norm(values, gain):
    return values * lax.rsqrt(jnp.mean(values * values, axis=-1, keepdims=True) + EPS) * gain


def matmul(left, right):
    return jnp.dot(left, right, preferred_element_type=jnp.float32)


def matmul_left(left, right):
    return lax.dot_general(
        left, right, (((0,), (0,)), ((), ())), preferred_element_type=jnp.float32
    )


def matmul_right(left, right):
    return lax.dot_general(
        left, right, (((1,), (1,)), ((), ())), preferred_element_type=jnp.float32
    )


def per_device(
    tokens,
    cotangent,
    routes,
    prompt_rows,
    w_query,
    w_key,
    w_value,
    w_output,
    w_router,
    gain_attn,
    gain_ffn,
    pos_table,
    w_in,
    w_out,
):
    shard_count = lax.axis_size("shard")
    expert_ranks = lax.axis_size("expert")
    own_index = lax.axis_index("shard")
    micro_count, tok_rows, model_width = tokens.shape
    local_experts = w_in.shape[0]
    expert_count = w_router.shape[1]
    capacity = (9 * tok_rows + 4 * expert_count - 1) // (4 * expert_count)
    head_count = HEADS
    head_size = model_width // head_count
    bucket_count = BUCKETS
    score_scale = head_size ** (-0.5)
    group_rows = shard_count * tok_rows
    slot_count = expert_ranks * capacity * local_experts
    recv_rows = expert_ranks * capacity
    bucket_ids = jnp.arange(bucket_count, dtype=jnp.int32)
    expert_ids = jnp.arange(expert_count, dtype=jnp.int32)
    gathered = (
        lax.all_gather(w_query, "shard", axis=0, tiled=True),
        lax.all_gather(w_key, "shard", axis=0, tiled=True),
        lax.all_gather(w_value, "shard", axis=0, tiled=True),
        lax.all_gather(w_output, "shard", axis=0, tiled=True),
        lax.all_gather(w_router, "shard", axis=0, tiled=True),
        lax.all_gather(gain_attn, "shard", axis=0, tiled=True),
        lax.all_gather(gain_ffn, "shard", axis=0, tiled=True),
        lax.all_gather(pos_table, "shard", axis=0, tiled=True),
    )
    full_query, full_key, full_value, full_output, full_router, gain_one, gain_two, table_flat = (
        gathered
    )
    gain_first = gain_one.astype(jnp.float32)
    gain_second = gain_two.astype(jnp.float32)
    table = table_flat.astype(jnp.float32).reshape(head_count, bucket_count)
    expert_in, expert_out = (
        lax.all_gather(w_in, "shard", axis=2, tiled=True),
        lax.all_gather(w_out, "shard", axis=1, tiled=True),
    )
    sum_query = jnp.zeros(full_query.shape, jnp.float32)
    sum_key = jnp.zeros(full_key.shape, jnp.float32)
    sum_value = jnp.zeros(full_value.shape, jnp.float32)
    sum_output = jnp.zeros(full_output.shape, jnp.float32)
    sum_router = jnp.zeros(full_router.shape, jnp.float32)
    sum_gain_one = jnp.zeros((model_width,), jnp.float32)
    sum_gain_two = jnp.zeros((model_width,), jnp.float32)
    sum_table = jnp.zeros((head_count, bucket_count), jnp.float32)
    sum_expert_in = jnp.zeros(expert_in.shape, jnp.float32)
    sum_expert_out = jnp.zeros(expert_out.shape, jnp.float32)
    mixed_parts = []
    grad_parts = []
    for micro_index in range(micro_count):
        inputs = tokens[micro_index].astype(jnp.float32)
        counts = prompt_rows[micro_index, 0]
        pos_all, prompt_all, device_all = layout(counts, tok_rows)
        query_pos = lax.dynamic_slice_in_dim(pos_all, own_index * tok_rows, tok_rows)
        hidden = rms_norm(inputs, gain_first).astype(jnp.bfloat16)
        query = matmul(hidden, full_query).astype(jnp.bfloat16)
        key = matmul(hidden, full_key).astype(jnp.bfloat16)
        value = matmul(hidden, full_value).astype(jnp.bfloat16)
        keys_all, values_all = (
            lax.all_gather(key, "shard", axis=0, tiled=True),
            lax.all_gather(value, "shard", axis=0, tiled=True),
        )
        key_index = jnp.arange(group_rows, dtype=jnp.int32)
        key_far = jnp.zeros((group_rows,), jnp.bool_)
        key_total = keys_all.shape[0]
        key_block = math.gcd(key_total, 512)
        block_count = key_total // key_block
        key_pos = pos_all[key_index]
        key_prompt = prompt_all[key_index]
        key_device = device_all[key_index]
        key_mine = key_device == own_index
        distance = query_pos[:, None] - key_pos[None, :]
        visible = (
            (distance >= 0)
            & (key_prompt | key_mine)[None, :]
            & jnp.logical_not(key_far & key_mine)[None, :]
        )
        bucket_all = distance_bucket(jnp.maximum(distance, 0))
        bucket_blocks = bucket_all.reshape(tok_rows, block_count, key_block).transpose(1, 0, 2)
        visible_blocks = visible.reshape(tok_rows, block_count, key_block).transpose(1, 0, 2)
        query_heads = query.reshape(tok_rows, head_count, head_size)
        key_blocks = keys_all.reshape(block_count, key_block, head_count, head_size)
        value_blocks = values_all.reshape(block_count, key_block, head_count, head_size)

        def make_bias(unused, block_item):
            bucket_piece, visible_piece = block_item
            bucket_hits = (bucket_piece[:, :, None] == bucket_ids).astype(jnp.float32)
            bias = jnp.einsum("qkb,hb->hqk", bucket_hits, table, precision=HIGHEST)
            return (unused, jnp.where(visible_piece[None], bias, MASKED))

        _, bias_blocks = lax.scan(
            make_bias, jnp.zeros((), jnp.float32), (bucket_blocks, visible_blocks)
        )

        def score_piece(key_piece, bias_piece):
            raw = jnp.einsum(
                "qhd,khd->hqk", query_heads, key_piece, preferred_element_type=jnp.float32
            )
            return raw * score_scale + bias_piece

        def running(state_pair, block_item):
            running_max, running_sum = state_pair
            key_piece, bias_piece = block_item
            scores = score_piece(key_piece, bias_piece)
            new_max = jnp.maximum(running_max, jnp.max(scores, axis=-1))
            running_sum = running_sum * jnp.exp(running_max - new_max) + jnp.sum(
                jnp.exp(scores - new_max[:, :, None]), axis=-1
            )
            return ((new_max, running_sum), None)

        start_pair = (
            jnp.full((head_count, tok_rows), MASKED, jnp.float32),
            jnp.zeros((head_count, tok_rows), jnp.float32),
        )
        (running_max, running_sum), _ = lax.scan(running, start_pair, (key_blocks, bias_blocks))
        log_total = running_max + jnp.log(running_sum)

        def gather_context(context_sum, block_item):
            key_piece, value_piece, bias_piece = block_item
            weights_low = jnp.exp(
                score_piece(key_piece, bias_piece) - log_total[:, :, None]
            ).astype(jnp.bfloat16)
            return (
                context_sum
                + jnp.einsum(
                    "hqk,khd->qhd", weights_low, value_piece, preferred_element_type=jnp.float32
                ),
                None,
            )

        context, _ = lax.scan(
            gather_context,
            jnp.zeros((tok_rows, head_count, head_size), jnp.float32),
            (key_blocks, value_blocks, bias_blocks),
        )
        context_low = context.reshape(tok_rows, model_width).astype(jnp.bfloat16)
        middle = inputs + matmul(context_low, full_output)
        normed = rms_norm(middle, gain_second).astype(jnp.bfloat16)
        logits = matmul(normed, full_router)
        chosen = routes[micro_index]
        pick_table = (chosen[:, :, None] == expert_ids).astype(jnp.float32)
        picked = jnp.sum(pick_table * logits[:, None, :], axis=-1)
        gate_weights = jax.nn.softmax(picked, axis=-1)
        flat_routes = chosen.reshape(-1)
        expert_hits = (flat_routes[:, None] == expert_ids).astype(jnp.int32)
        expert_rank = (
            jnp.sum(
                jnp.cumsum(expert_hits, axis=0, dtype=jnp.int32) * expert_hits,
                axis=1,
                dtype=jnp.int32,
            )
            - 1
        )
        slot_index = (
            flat_routes // local_experts * (capacity * local_experts)
            + expert_rank * local_experts
            + flat_routes % local_experts
        )
        slot_owner = (
            jnp.full((slot_count,), 2 * tok_rows, jnp.int32)
            .at[slot_index]
            .set(jnp.arange(2 * tok_rows, dtype=jnp.int32))
        )
        padded = jnp.concatenate([normed, jnp.zeros((1, model_width), jnp.bfloat16)], axis=0)
        outgoing = padded[slot_owner // 2].reshape(
            expert_ranks, capacity, local_experts, model_width
        )
        received = lax.all_to_all(
            outgoing, "expert", split_axis=0, concat_axis=0, tiled=True
        ).reshape(recv_rows, local_experts, model_width)
        pre_act = jnp.einsum(
            "red,edf->ref", received, expert_in, preferred_element_type=jnp.float32
        )
        activation = jax.nn.gelu(pre_act).astype(jnp.bfloat16)
        expert_result = jnp.einsum(
            "ref,efd->red", activation, expert_out, preferred_element_type=jnp.float32
        )
        result_low = expert_result.astype(jnp.bfloat16).reshape(
            expert_ranks, capacity, local_experts, model_width
        )
        returned = lax.all_to_all(
            result_low, "expert", split_axis=0, concat_axis=0, tiled=True
        ).reshape(slot_count, model_width)
        picked_rows = returned[slot_index].astype(jnp.float32).reshape(tok_rows, 2, model_width)
        output_rows = middle + jnp.sum(gate_weights[:, :, None] * picked_rows, axis=1)
        mixed_parts.append(output_rows.astype(jnp.bfloat16))
        grad_output = cotangent[micro_index].astype(jnp.float32)
        grad_gate = jnp.sum(grad_output[:, None, :] * picked_rows, axis=-1)
        grad_pick = gate_weights * (
            grad_gate - jnp.sum(gate_weights * grad_gate, axis=-1, keepdims=True)
        )
        grad_logits = jnp.sum(pick_table * grad_pick[:, :, None], axis=1).astype(jnp.bfloat16)
        sum_router = sum_router + matmul_left(normed, grad_logits)
        grad_normed = matmul_right(grad_logits, full_router)
        branch_grad = (gate_weights[:, :, None] * grad_output[:, None, :]).reshape(
            2 * tok_rows, model_width
        )
        padded_grad = jnp.concatenate(
            [branch_grad, jnp.zeros((1, model_width), jnp.float32)], axis=0
        )
        grad_send = (
            padded_grad[slot_owner]
            .astype(jnp.bfloat16)
            .reshape(expert_ranks, capacity, local_experts, model_width)
        )
        grad_recv = lax.all_to_all(
            grad_send, "expert", split_axis=0, concat_axis=0, tiled=True
        ).reshape(recv_rows, local_experts, model_width)
        grad_act = jnp.einsum(
            "red,efd->ref", grad_recv, expert_out, preferred_element_type=jnp.float32
        )
        sum_expert_out = sum_expert_out + jnp.einsum(
            "ref,red->efd", activation, grad_recv, preferred_element_type=jnp.float32
        )
        _, gelu_pull = jax.vjp(jax.nn.gelu, pre_act)
        grad_pre = gelu_pull(grad_act)[0].astype(jnp.bfloat16)
        sum_expert_in = sum_expert_in + jnp.einsum(
            "red,ref->edf", received, grad_pre, preferred_element_type=jnp.float32
        )
        grad_in_rows = jnp.einsum(
            "ref,edf->red", grad_pre, expert_in, preferred_element_type=jnp.float32
        )
        grad_in_low = grad_in_rows.astype(jnp.bfloat16).reshape(
            expert_ranks, capacity, local_experts, model_width
        )
        grad_back = lax.all_to_all(
            grad_in_low, "expert", split_axis=0, concat_axis=0, tiled=True
        ).reshape(slot_count, model_width)
        grad_normed = grad_normed + jnp.sum(
            grad_back[slot_index].astype(jnp.float32).reshape(tok_rows, 2, model_width), axis=1
        )
        _, norm_pull = jax.vjp(rms_norm, middle, gain_second)
        grad_middle, grad_gain_second = norm_pull(grad_normed)
        grad_middle = grad_middle + grad_output
        sum_gain_two = sum_gain_two + grad_gain_second
        grad_attn = grad_middle.astype(jnp.bfloat16)
        sum_output = sum_output + matmul_left(context_low, grad_attn)
        grad_context = (
            matmul_right(grad_attn, full_output)
            .astype(jnp.bfloat16)
            .reshape(tok_rows, head_count, head_size)
        )
        row_delta = jnp.einsum("qhd,qhd->hq", grad_context.astype(jnp.float32), context)

        def attend_back(state_pair, block_item):
            grad_query_sum, grad_table_sum = state_pair
            key_piece, value_piece, bias_piece, bucket_piece = block_item
            probs = jnp.exp(score_piece(key_piece, bias_piece) - log_total[:, :, None])
            grad_probs = jnp.einsum(
                "qhd,khd->hqk", grad_context, value_piece, preferred_element_type=jnp.float32
            )
            grad_scores = probs * (grad_probs - row_delta[:, :, None])
            bucket_hits = (bucket_piece[:, :, None] == bucket_ids).astype(jnp.float32)
            grad_table_sum = grad_table_sum + jnp.einsum(
                "hqk,qkb->hb", grad_scores, bucket_hits, precision=HIGHEST
            )
            grad_raw = (grad_scores * score_scale).astype(jnp.bfloat16)
            grad_query_sum = grad_query_sum + jnp.einsum(
                "hqk,khd->qhd", grad_raw, key_piece, preferred_element_type=jnp.float32
            )
            grad_key_piece = jnp.einsum(
                "hqk,qhd->khd", grad_raw, query_heads, preferred_element_type=jnp.float32
            )
            grad_value_piece = jnp.einsum(
                "hqk,qhd->khd",
                probs.astype(jnp.bfloat16),
                grad_context,
                preferred_element_type=jnp.float32,
            )
            return ((grad_query_sum, grad_table_sum), (grad_key_piece, grad_value_piece))

        back_start = (
            jnp.zeros((tok_rows, head_count, head_size), jnp.float32),
            jnp.zeros((head_count, bucket_count), jnp.float32),
        )
        (grad_query_all, grad_table_all), (grad_key_blocks, grad_value_blocks) = lax.scan(
            attend_back, back_start, (key_blocks, value_blocks, bias_blocks, bucket_blocks)
        )
        sum_table = sum_table + grad_table_all
        key_grad_rows = grad_key_blocks.reshape(key_total, model_width)
        value_grad_rows = grad_value_blocks.reshape(key_total, model_width)
        own_key_grad, own_value_grad = (
            lax.psum_scatter(
                key_grad_rows.astype(jnp.bfloat16), "shard", scatter_dimension=0, tiled=True
            ).astype(jnp.float32),
            lax.psum_scatter(
                value_grad_rows.astype(jnp.bfloat16), "shard", scatter_dimension=0, tiled=True
            ).astype(jnp.float32),
        )
        grad_query_low = grad_query_all.reshape(tok_rows, model_width).astype(jnp.bfloat16)
        grad_key_low = own_key_grad.astype(jnp.bfloat16)
        grad_value_low = own_value_grad.astype(jnp.bfloat16)
        sum_query = sum_query + matmul_left(hidden, grad_query_low)
        sum_key = sum_key + matmul_left(hidden, grad_key_low)
        sum_value = sum_value + matmul_left(hidden, grad_value_low)
        grad_hidden = (
            matmul_right(grad_query_low, full_query)
            + matmul_right(grad_key_low, full_key)
            + matmul_right(grad_value_low, full_value)
        )
        _, first_pull = jax.vjp(rms_norm, inputs, gain_first)
        grad_inputs, grad_gain_first = first_pull(grad_hidden)
        sum_gain_one = sum_gain_one + grad_gain_first
        grad_parts.append(grad_inputs + grad_middle)
    shares = (
        lax.psum_scatter(
            sum_query.astype(jnp.bfloat16), "shard", scatter_dimension=0, tiled=True
        ).astype(jnp.float32),
        lax.psum_scatter(
            sum_key.astype(jnp.bfloat16), "shard", scatter_dimension=0, tiled=True
        ).astype(jnp.float32),
        lax.psum_scatter(
            sum_value.astype(jnp.bfloat16), "shard", scatter_dimension=0, tiled=True
        ).astype(jnp.float32),
        lax.psum_scatter(
            sum_output.astype(jnp.bfloat16), "shard", scatter_dimension=0, tiled=True
        ).astype(jnp.float32),
        lax.psum_scatter(
            sum_router.astype(jnp.bfloat16), "shard", scatter_dimension=0, tiled=True
        ).astype(jnp.float32),
        lax.psum_scatter(
            sum_gain_one.astype(jnp.bfloat16), "shard", scatter_dimension=0, tiled=True
        ).astype(jnp.float32),
        lax.psum_scatter(
            sum_gain_two.astype(jnp.bfloat16), "shard", scatter_dimension=0, tiled=True
        ).astype(jnp.float32),
        lax.psum_scatter(
            sum_table.reshape(-1).astype(jnp.bfloat16), "shard", scatter_dimension=0, tiled=True
        ).astype(jnp.float32),
    )
    own_grads = (
        lax.psum(shares[0].astype(jnp.bfloat16), "expert").astype(jnp.float32),
        lax.psum(shares[1].astype(jnp.bfloat16), "expert").astype(jnp.float32),
        lax.psum(shares[2].astype(jnp.bfloat16), "expert").astype(jnp.float32),
        lax.psum(shares[3].astype(jnp.bfloat16), "expert").astype(jnp.float32),
        lax.psum(shares[4].astype(jnp.bfloat16), "expert").astype(jnp.float32),
        lax.psum(shares[5].astype(jnp.bfloat16), "expert").astype(jnp.float32),
        lax.psum(shares[6].astype(jnp.bfloat16), "expert").astype(jnp.float32),
        lax.psum(shares[7].astype(jnp.bfloat16), "expert").astype(jnp.float32),
    )
    grad_expert_in, grad_expert_out = (
        lax.psum_scatter(
            sum_expert_in.astype(jnp.bfloat16), "shard", scatter_dimension=2, tiled=True
        ).astype(jnp.float32),
        lax.psum_scatter(
            sum_expert_out.astype(jnp.bfloat16), "shard", scatter_dimension=1, tiled=True
        ).astype(jnp.float32),
    )
    return (
        jnp.stack(mixed_parts),
        jnp.stack(grad_parts),
        own_grads[0],
        own_grads[1],
        own_grads[2],
        own_grads[3],
        own_grads[4],
        own_grads[5],
        own_grads[6],
        own_grads[7],
        grad_expert_in,
        grad_expert_out,
    )


def solution(mesh):
    in_specs = (
        P(None, ("expert", "shard"), None),
        P(None, ("expert", "shard"), None),
        P(None, ("expert", "shard"), None),
        P(None, "expert", None),
        P("shard", None),
        P("shard", None),
        P("shard", None),
        P("shard", None),
        P("shard", None),
        P("shard"),
        P("shard"),
        P("shard"),
        P("expert", None, "shard"),
        P("expert", "shard", None),
    )
    out_specs = (
        P(None, ("expert", "shard"), None),
        P(None, ("expert", "shard"), None),
        P("shard", None),
        P("shard", None),
        P("shard", None),
        P("shard", None),
        P("shard", None),
        P("shard"),
        P("shard"),
        P("shard"),
        P("expert", None, "shard"),
        P("expert", "shard", None),
    )
    ne, ns = mesh.shape["expert"], mesh.shape["shard"]

    def device(*args):
        tokens, w_router, w_in = args[0], args[8], args[12]
        z = Sizes(
            ne, ns, tokens.shape[0], tokens.shape[1], tokens.shape[2], w_router.shape[1], w_in.shape[0], w_in.shape[2]
        )
        return fused_device(z, *args) if z.fits() else per_device(*args)

    return jax.shard_map(
        device, mesh=mesh, in_specs=in_specs, out_specs=out_specs, check_vma=False
    )
```

```python
import functools
from functools import reduce
import math

import jax
import jax.numpy as jnp
import numpy as np
from jax import lax
from jax.experimental import pallas as pl
from jax.experimental.pallas import tpu as pltpu
from jax.sharding import PartitionSpec as P

HEADS = 12
BUCKETS = 32
EPS = 1e-06
MASKED = -1e30
BUCKET_EDGES = (24, 32, 48, 64, 96, 128, 192, 256, 384, 512, 768, 1024, 1536, 2048, 3072)
MESH = pl.DeviceIdType.MESH
BF = jnp.bfloat16
F32 = jnp.float32
I32 = jnp.int32
LANES = 128


class Sizes:
    def __init__(self, ne, ns, micro, rows, width, experts, local_experts, ff):
        self.ne, self.ns, self.ny = ne, ns, ns // 2
        self.m, self.t, self.d = micro, rows, width
        self.e, self.el, self.ff = experts, local_experts, ff
        self.g = ns * rows
        self.mt = micro * rows
        self.r = width // ns
        self.cap = (9 * rows + 4 * experts - 1) // (4 * experts)
        self.per = micro * self.cap
        self.sp = -(-(local_experts * self.per + 2) // 16) * 16
        self.slots = ne * self.sp
        self.nz = ne // 2
        self.hn = ne // 2
        self.cr = self.hn * self.per
        self.cb = local_experts * self.cr
        self.blk = 2 * self.cb
        self.hs = self.hn * self.sp
        self.n16 = -(-ne // 16) * 16
        self.pairs = HEADS // 2
        self.small = experts + 16
        self.far = self.g // 2 + rows

    def fits(self):
        return (
            self.ns % 2 == 0
            and self.t == LANES
            and self.d == HEADS * 64
            and self.cr % 16 == 0
            and self.nz == 4
            and self.e % 16 == 0
            and self.r % (16 * self.nz) == 0
            and self.slots % LANES == 0
            and self.el * self.per <= LANES
            and self.d == self.ff
            and self.ns >= 2 * self.m
            and self.blk >= self.g
            and self.d % 256 == 0
        )


def layout_constants(z):
    perm = np.zeros((z.cb, z.hs), np.float32)
    rows_of = np.zeros((2 * z.n16, z.slots), np.float32)
    dest = np.zeros((2 * z.n16, z.slots), np.float32)
    place = np.zeros((z.slots, LANES), np.float32)
    gate_of = np.zeros((2 * z.n16, z.hs), np.float32)
    source = np.zeros((z.cb, 2 * z.n16), np.float32)
    pick = np.zeros((z.cb, LANES), np.float32)
    used = z.el * z.per
    for src in range(z.ne):
        rows_of[src, src * z.sp + used] = 1
        rows_of[z.n16 + src, src * z.sp + used + 1] = 1
        dest[src, src * z.sp : (src + 1) * z.sp] = 1
        dest[z.n16 + src, src * z.sp : (src + 1) * z.sp] = 1
        for q in range(used):
            place[src * z.sp + q, q] = 1
    for src in range(z.hn):
        gate_of[src, src * z.sp + used] = 1
        gate_of[z.n16 + src, src * z.sp + used + 1] = 1
        for q in range(used):
            row = (q // z.per) * z.cr + src * z.per + q % z.per
            perm[row, src * z.sp + q] = 1
            source[row, src] = 1
            source[row, z.n16 + src] = 1
            pick[row, q] = 1
    return [jnp.asarray(a, BF) for a in (perm, rows_of, dest, place, gate_of, source, pick)]


def dot(a, b):
    return jnp.dot(a, b, preferred_element_type=F32)


def dot_t(a, b):
    return lax.dot_general(a, b, (((1,), (1,)), ((), ())), preferred_element_type=F32)


def tdot(a, b):
    return lax.dot_general(a, b, (((0,), (0,)), ((), ())), preferred_element_type=F32)


def iota(shape, dim):
    return lax.broadcasted_iota(I32, shape, dim)


def aligned(start, size, multiple):
    return pl.ds(pl.multiple_of(start, multiple), size)


def offsets(z, chunk=None):
    every = [(kz, kx) for kz in range(z.nz) for kx in range(2)][1:]
    return [k for k in every if chunk is None or k[0] % 2 == chunk]


def position(z, k):
    return (k[0] % 2) * z.hn + (k[0] // 2) * 2 + k[1]


class Place:
    def __init__(self, z):
        self.z = z
        self.e = lax.axis_index("expert")
        self.s = lax.axis_index("shard")
        self.y, self.c = lax.div(self.s, 2), lax.rem(self.s, 2)

    def shard(self, k, other):
        y = lax.rem(self.y + k, self.z.ny)
        return y * 2 + (1 - self.c if other else self.c)

    def expert(self, kz, kx):
        high = lax.rem(lax.div(self.e, 2) + kz, self.z.nz)
        return high * 2 + lax.rem(lax.rem(self.e, 2) + kx, 2)

    def barrier(self, with_experts=True):
        sem = pltpu.get_barrier_semaphore()
        others = [(self.e, self.shard(0, True))]
        others += [(self.e, self.shard(k, False)) for k in range(1, self.z.ny)]
        if with_experts:
            others += [(self.expert(*k), self.s) for k in offsets(self.z)]
        for other in others:
            pl.semaphore_signal(sem, inc=1, device_id=other, device_id_type=MESH)
        pl.semaphore_wait(sem, len(others))


def rcopy(src, dst, send, recv, to):
    return pltpu.make_async_remote_copy(
        src_ref=src, dst_ref=dst, send_sem=send, recv_sem=recv, device_id=to, device_id_type=MESH
    )


class Gather:
    def __init__(self, place, own, full, send, recv, item):
        self.p, self.own, self.full = place, own, full
        self.send, self.recv, self.item = send, recv, item

    def copy(self, origin, src, slot, to):
        return rcopy(src, self.full(origin), self.send.at[self.item, slot], self.recv.at[self.item, slot], to)

    def partner(self):
        return (self.p.e, self.p.shard(0, True))

    def start(self):
        p, ny = self.p, self.p.z.ny
        for k in range(1, ny):
            self.copy(p.s, self.own, k, (p.e, p.shard(k, False))).start()
        self.copy(p.s, self.own, 0, self.partner()).start()

    def forward(self):
        p, ny = self.p, self.p.z.ny
        for k in range(1, ny):
            origin = p.shard(k, False)
            self.copy(origin, self.full(origin), ny - k, self.partner()).wait_recv()
            self.copy(origin, self.full(origin), ny + k - 1, self.partner()).start()

    def arrive(self):
        p, ny = self.p, self.p.z.ny
        for k in range(ny):
            origin = p.shard(k, True)
            self.copy(origin, self.full(origin), ny + k - 1 if k else 0, self.partner()).wait_recv()

    def finish(self):
        p, ny = self.p, self.p.z.ny
        for slot in range(2 * ny - 1):
            self.copy(p.s, self.own, slot, self.partner()).wait_send()


class Exchange:
    def __init__(self, place, src, dst, send, recv, item):
        self.p, self.src, self.dst = place, src, dst
        self.send, self.recv, self.item = send, recv, item

    def copy(self, k):
        z = self.p.z
        back = (-k[0] % z.nz, k[1])
        at = position(z, back)
        to = self.p.expert(*k)
        return rcopy(
            self.src(to),
            self.dst(at),
            self.send.at[self.item, position(z, k) - 1],
            self.recv.at[self.item, at - 1],
            (to, self.p.s),
        )

    def start(self, some=None):
        for k in filter(some, offsets(self.p.z)):
            self.copy(k).start()

    def arrive(self, some=None):
        z = self.p.z
        for k in filter(some, offsets(z)):
            self.copy((-k[0] % z.nz, k[1])).wait_recv()

    def finish(self, some=None):
        for k in filter(some, offsets(self.p.z)):
            self.copy(k).wait_send()


def slot_ids(z, route0, route1):
    lane = iota((z.t, LANES), 1)
    lower = (iota((z.t, z.t), 0) > iota((z.t, z.t), 1)).astype(F32).astype(BF)
    base = lane * z.per
    for d in range(1, z.ne):
        base = base + jnp.where(lane >= d * z.el, z.sp - z.el * z.per, 0)
    firsts, seconds = [], []
    for m in range(z.m):
        rows = slice(m * z.t, (m + 1) * z.t)
        hit0, hit1 = lane == route0[rows], lane == route1[rows]
        hits = jnp.where(hit0 | hit1, 1.0, 0.0).astype(BF)
        spot = dot(lower, hits) + (base + m * z.cap).astype(F32)
        firsts.append(jnp.sum(jnp.where(hit0, spot, 0.0), axis=1, keepdims=True))
        seconds.append(jnp.sum(jnp.where(hit1, spot, 0.0), axis=1, keepdims=True))
    return jnp.concatenate(firsts, 0), jnp.concatenate(seconds, 0)


def one_hot(z, slot):
    return (iota((z.mt, z.slots), 1) == slot.astype(I32)).astype(F32)


def key_layout(z, counts, m, shape, dim):
    row = iota(shape, dim)
    total = counts[m, 0]
    for b in range(1, z.ns):
        total = total + counts[m, b]
    position = jnp.zeros(shape, I32)
    prompt = jnp.zeros(shape, I32)
    offset = 0
    for b in range(z.ns):
        own = counts[m, b]
        local = row - b * z.t
        inside = (local >= 0) & (local < z.t)
        first = local < own
        position = jnp.where(inside, jnp.where(first, offset + local, total + local - own), position)
        prompt = jnp.where(inside & first, 1, prompt)
        offset = offset + own
    return position, prompt


def query_position(z, counts, m, s):
    total, offset, own = 0, 0, 0
    for b in range(z.ns):
        count = counts[m, b]
        total = total + count
        offset = offset + jnp.where(b < s, count, 0)
        own = own + jnp.where(b == s, count, 0)
    local = iota((z.t, 1), 0)
    return jnp.where(local < own, offset + local, total + local - own)


def bucket_of(z, distance):
    coarse = jnp.full(distance.shape, 16, I32)
    for edge in BUCKET_EDGES:
        if edge < z.far:
            coarse = coarse + jnp.where(distance >= edge, 1, 0)
    return jnp.where(distance < 16, distance, coarse)


VMEM = pl.BlockSpec(memory_space=pltpu.VMEM)
SMEM = pl.BlockSpec(memory_space=pltpu.SMEM)


GELU_A = math.sqrt(2.0 / math.pi)
GELU_B = 0.044715


class SharedGather:
    def __init__(self, place, own, full, send, recv, item):
        self.p, self.own, self.full = place, own, full
        self.send, self.recv, self.item = send, recv, item
        self.x = lax.rem(place.e, 2)

    def half(self, ref, x):
        n = ref.shape[1] // 2
        return ref.at[:, aligned(x * n, n, LANES)]

    def copy(self, src, dst, slot, arrival, to):
        return rcopy(src, dst, self.send.at[self.item, slot], self.recv.at[self.item, arrival], to)

    def partner(self):
        return (self.p.e, self.p.shard(0, True))

    def own_copy(self, origin):
        return self.copy(self.own, self.full(origin), 0, 0, self.partner())

    def y_copy(self, k, origin, arrival=None):
        return self.copy(
            self.half(self.own, self.x), self.half(self.full(origin), self.x), k, k if arrival is None else arrival,
            (self.p.e, self.p.shard(k, False)),
        )

    def on_copy(self, k, kind, origin, x, to):
        block = self.half(self.full(origin), x)
        slot = self.p.z.ny + 3 * (k - 1) + kind
        return self.copy(block, block, slot, slot, to)

    def start(self):
        p = self.p
        for k in range(1, p.z.ny):
            self.y_copy(k, p.s).start()
        self.own_copy(p.s).start()

    def forward(self):
        p = self.p
        for k in range(1, p.z.ny):
            origin = p.shard(k, False)
            self.y_copy(k, origin, self.p.z.ny - k).wait_recv()
            self.on_copy(k, 0, origin, self.x, (p.expert(0, 1), p.s)).start()
            self.on_copy(k, 1, origin, self.x, self.partner()).start()

    def forward_rest(self):
        p = self.p
        for k in range(1, p.z.ny):
            origin = p.shard(k, False)
            self.on_copy(k, 0, origin, 1 - self.x, (p.expert(0, 1), p.s)).wait_recv()
            self.on_copy(k, 2, origin, 1 - self.x, self.partner()).start()

    def arrive(self):
        p = self.p
        self.own_copy(p.shard(0, True)).wait_recv()
        for k in range(1, p.z.ny):
            origin = p.shard(k, True)
            self.on_copy(k, 1, origin, self.x, self.partner()).wait_recv()
            self.on_copy(k, 2, origin, 1 - self.x, self.partner()).wait_recv()

    def finish(self):
        p = self.p
        self.own_copy(p.s).wait_send()
        for k in range(1, p.z.ny):
            self.y_copy(k, p.s).wait_send()
            for kind in range(3):
                self.on_copy(k, kind, p.s, 0, self.partner()).wait_send()


class Scatter:
    def __init__(self, place, mine, other, from_core, to_y, from_y, psend, precv, ysend, yrecv):
        self.p, self.mine, self.other, self.from_core = place, mine, other, from_core
        self.to_y, self.from_y = to_y, from_y
        self.psend, self.precv, self.ysend, self.yrecv = psend, precv, ysend, yrecv

    def core_copy(self):
        p = self.p
        return rcopy(self.other, self.from_core, self.psend, self.precv, (p.e, p.shard(0, True)))

    def y_copy(self, k):
        p = self.p
        return rcopy(
            self.to_y.at[k - 1], self.from_y.at[k - 1], self.ysend.at[k - 1], self.yrecv.at[k - 1],
            (p.e, p.shard(k, False)),
        )

    def send(self):
        self.core_copy().start()

    def middle(self):
        p = self.p
        self.core_copy().wait_recv()
        for k in range(1, p.z.ny):
            yy = lax.rem(p.y + k, p.z.ny)
            both = self.mine[yy].astype(F32) + self.from_core[yy].astype(F32)
            self.to_y[k - 1] = both.astype(BF)
            self.y_copy(k).start()

    def total(self):
        p = self.p
        out = self.mine[p.y].astype(F32) + self.from_core[p.y].astype(F32)
        for k in range(1, p.z.ny):
            self.y_copy(k).wait_recv()
            out = out + self.from_y[k - 1].astype(F32)
        return out

    def finish(self):
        self.core_copy().wait_send()
        for k in range(1, self.p.z.ny):
            self.y_copy(k).wait_send()


class Return:
    def __init__(self, place, rows, ret, chunk, cols, send, recv):
        self.p, self.rows, self.ret, self.chunk, self.cols = place, rows, ret, chunk, cols
        self.sems = send, recv

    def copy(self, k, at, away):
        z = self.p.z
        first = self.chunk * z.hn
        return rcopy(
            self.rows.at[pl.ds((position(z, k) - first) * z.sp, z.sp)],
            self.ret.at[aligned(at * z.sp, z.sp, 16), self.cols],
            self.sems[0].at[position(z, k) - first],
            self.sems[1].at[position(z, away) - first],
            (self.p.expert(*k), self.p.s),
        )

    def start_remote(self):
        z = self.p.z
        for k in offsets(z, self.chunk):
            self.copy(k, self.p.e, (-k[0] % z.nz, k[1])).start()

    def arrive(self):
        for k in offsets(self.p.z, self.chunk):
            self.copy(k, self.p.expert(*k), k).wait_recv()

    def finish(self):
        z = self.p.z
        for k in offsets(z, self.chunk):
            self.copy(k, self.p.e, (-k[0] % z.nz, k[1])).wait_send()


def column_of(row):
    n = row.shape[1]
    return jnp.sum(jnp.where(iota((n, n), 0) == iota((n, n), 1), row, 0.0), axis=1, keepdims=True)


def route_columns(z, routes):
    out = []
    for j in range(2):
        parts = [column_of(routes[m, j : j + 1, :].astype(F32)) for m in range(z.m)]
        out.append(jnp.concatenate(parts, 0).astype(I32))
    return out


def spread(z, s, n):
    row, lane = iota((z.r, z.d), 0), iota((z.r, z.d), 1)
    return jnp.where((lane - s * n == row) & (row < n), 1.0, 0.0).astype(BF)


def split_high(x):
    high = x.astype(BF)
    return high, (x - high.astype(F32)).astype(BF)


def forward_kernel(
    z,
    tokens, dy, routes, counts, wk, wv, wq, wo, wr, vecs, w_in_hbm, w_out_hbm,
    perm, rows_of, dest, place_m, gate_of, source, pick,
    o_toks, o_hid, o_kk, o_vv, o_qq, o_pp, o_ctx, o_mid, o_nrm, o_sd, o_fk, o_fv, o_fq, o_fo, o_small,
    o_ret, o_rfin, o_rpart, ggrows, din, dout,
    qq, pp, ctx, mid, nrm, sd, fk, fv, fq, fo, small, smallg,
    xs, dyr, xr, dyg, xg, act, gp, w_in, w_out, table, bias_id, gwg, gwc, ggc,
    part, rp, ys, yr, fin, rpart, rrp, rys, ryr, wstage, gpart, grp, gys, gyr, gout, gret,
    csem, ssem, gsend, grecv, wsend, wrecv, xsend, xrecv, psend, precv, ysend, yrecv, rsend, rrecv, gsem, gsy, gsx,
):
    p = Place(z)
    mt, t, d, r, ff = z.mt, z.t, z.d, z.r, z.ff
    half = d // 2
    tiles = ff // 256
    load_in = pltpu.make_async_copy(w_in_hbm, w_in, csem.at[0])
    load_out = pltpu.make_async_copy(w_out_hbm, w_out, csem.at[1])
    spills, waiting = [], {}

    def spill(src, dst, before=None):
        copy = pltpu.make_async_copy(src, dst, ssem.at[len(spills)])
        copy.start()
        spills.append(copy)
        waiting.setdefault(before, []).append(copy)

    toks, hid = gp.at[pl.ds(0, z.m), pl.ds(0, z.g)], gp.at[pl.ds(z.m, z.m), pl.ds(0, z.g)]
    kk, vv = act.at[pl.ds(0, z.m), pl.ds(0, z.g)], act.at[pl.ds(z.m, z.m), pl.ds(0, z.g)]

    whole = spread(z, p.s, r)
    line = iota((16, d), 0)
    n_bias = HEADS * BUCKETS // z.ns
    row = vecs[...].astype(F32)
    first = jnp.broadcast_to(row[:, 0:r], (16, r))
    gains = jnp.where(iota((16, r), 0) == 0, first, jnp.broadcast_to(row[:, r : 2 * r], (16, r)))
    biases = jnp.broadcast_to(row[:, 2 * r : 2 * r + n_bias], (16, n_bias))
    tail = dot(gains.astype(BF), whole)
    bias_row = dot(biases.astype(BF), spread(z, p.s, n_bias)[0:n_bias, :])
    tail = jnp.where(line < 2, tail, jnp.where(line == 2, bias_row, 0.0))
    small[0 : z.e, :] = dot(wr[...], whole).astype(BF)
    small[z.e : z.small, :] = tail.astype(BF)
    p.barrier()

    def rows(ref, size):
        return lambda origin: ref.at[aligned(origin * size, size, 16)]

    g_small = Gather(p, small, lambda o: smallg.at[o], gsend, grecv, 0)
    g_tok = [
        Gather(p, tokens.at[m], lambda o, m=m: toks.at[m, aligned(o * t, t, 16)], gsend, grecv, 1 + m)
        for m in range(z.m)
    ]
    base = 1 + z.m
    groups = d // 256

    def columns_item(own, full, g, item):
        cols = pl.ds(g * 256, 256)
        return SharedGather(
            p, own.at[:, cols], lambda o: full.at[aligned(o * r, r, 16), cols], wsend, wrecv, item
        )

    g_w = [
        [columns_item(own, full, g, 3 * g + i) for i, (own, full) in enumerate(((wk, fk), (wv, fv), (wq, fq)))]
        for g in range(groups)
    ]
    g_o = SharedGather(p, wo, rows(fo, r), wsend, wrecv, 3 * groups)
    for item in [g_small, g_tok[0]] + g_w[0] + g_tok[1:] + sum(g_w[1:], []) + [g_o]:
        item.start()
    load_out.start()
    load_in.start()
    g_dy = Gather(p, dyg.at[p.s], lambda o: dyg.at[o], gsend, grecv, base)

    def exchange(dst, item):
        return Exchange(
            p,
            lambda to: xs.at[aligned(to * z.sp, z.sp, 16)],
            lambda at: dst.at[pl.ds(at * z.sp, z.sp)],
            xsend,
            xrecv,
            item,
        )

    x_dy, x_move = exchange(dyr, 0), exchange(xr, 1)
    smallg[p.s] = small[...]
    for m in range(z.m):
        toks[m, aligned(p.s * t, t, 16), :] = tokens[m]
    own_weights = []
    for i, (own, full) in enumerate(((wk, fk), (wv, fv), (wq, fq), (wo, fo))):
        own_weights.append(pltpu.make_async_copy(own, full.at[aligned(p.s * r, r, 16)], csem.at[6 + i]))
        own_weights[i].start()

    route0, route1 = route_columns(z, routes)
    slot0, slot1 = slot_ids(z, route0, route1)
    hot = (one_hot(z, slot0) + one_hot(z, slot1)).astype(BF)
    mine = aligned(p.e * z.sp, z.sp, 16)

    def to_slots(ref):
        def step(i, carry):
            cols = aligned(i * 256, 256, 256)
            xs[:, cols] = tdot(hot, ref[:, cols]).astype(BF)
            return carry

        lax.fori_loop(0, d // 256, step, 0)

    across, along = lambda k: k[1] == 1, lambda k: k[1] == 0
    even, odd = lambda k: k[0] % 2 == 0, lambda k: k[0] % 2 == 1
    to_slots(dy)
    x_dy.start(across)
    dyr[0 : z.sp, :] = xs[mine, :]

    for m in range(z.m):
        key_pos, prompt = key_layout(z, counts, m, (1, z.g), 1)
        distance = query_position(z, counts, m, p.s) - key_pos
        lane = iota((1, z.g), 1)
        own_block = (lane >= p.s * t) & (lane < (p.s + 1) * t)
        visible = (distance >= 0) & (own_block | (prompt == 1))
        bias_id[m] = jnp.where(visible, bucket_of(z, distance), 2 * BUCKETS)

    for item in (g_small, g_tok[0]):
        item.forward()
    for item in (g_small, g_tok[0]):
        item.arrive()
    x_dy.start(along)
    spill(smallg, o_small)
    sums = smallg[0].astype(F32)
    for b in range(1, z.ns):
        sums = sums + smallg[b].astype(F32)
    gain_one = sums[z.e : z.e + 1, :]
    gain_two = sums[z.e + 1 : z.e + 2, :]
    router = sums.astype(BF)
    for pair in range(z.pairs):
        lanes = slice(pair // 2 * LANES, (pair // 2 + 1) * LANES)
        row = sums[z.e + 2 : z.e + 3, lanes]
        if pair % 2:
            row = pltpu.roll(row, 2 * BUCKETS, 1)
        table[pair : pair + 1, :] = jnp.where(iota((1, LANES), 1) < 2 * BUCKETS, row, MASKED)

    def normalize(m):
        def step(i, carry):
            at = aligned(i * t, t, 16)
            x = toks[m, at, :].astype(F32)
            scale = lax.rsqrt(jnp.mean(x * x, axis=1, keepdims=True) + EPS)
            hid[m, at, :] = (x * scale * gain_one).astype(BF)
            return carry

        lax.fori_loop(0, z.ns, step, 0)

    for copy in own_weights:
        copy.wait()

    def project(g, m):
        cols = slice(g * 256, (g + 1) * 256)
        for item, full, out in zip(g_w[g][:2], (fk, fv), (kk, vv)):
            if m == 0:
                item.arrive()
            out[m, :, cols] = dot(hid[m], full[:, cols]).astype(BF)
        if m == 0:
            g_w[g][2].arrive()
        own = hid[m, aligned(p.s * t, t, 16), :]
        qq[m * t : (m + 1) * t, cols] = (dot(own, fq[:, cols]).astype(BF).astype(F32) * 0.125).astype(BF)


    def in_order(src, dst, h):
        def step(i, carry):
            cols = aligned(i * 256, 256, 256)
            moved = dot(perm[...], src[h * z.hs : (h + 1) * z.hs, cols])
            dst[p.s, h * z.cb : (h + 1) * z.cb, cols] = moved.astype(BF)
            return carry

        lax.fori_loop(0, d // 256, step, 0)

    def send_dy_rows():
        x_dy.arrive()
        in_order(dyr, dyg, 0)
        in_order(dyr, dyg, 1)
        g_dy.start()

    low = iota((t, LANES), 1) < 64

    def attend(m, pair):
        spot = m * z.pairs + pair
        cols = aligned(pair * LANES, LANES, LANES)
        q = qq[aligned(m * t, t, 16), cols]
        zero = jnp.zeros_like(q)
        q_two = jnp.concatenate([jnp.where(low, q, zero), jnp.where(low, zero, q)], 0)
        scores = dot_t(q_two, kk[m, :, cols])
        biases = jnp.broadcast_to(table[pl.ds(pair, 1), :], (t, LANES))
        for side in range(2):
            pieces = []
            for b in range(z.ns):
                at = slice(b * LANES, (b + 1) * LANES)
                bias = jnp.take_along_axis(biases, bias_id[m, :, at] + BUCKETS * side, axis=1)
                pieces.append(scores[side * t : (side + 1) * t, at] + bias)
            s = jnp.concatenate(pieces, 1)
            top = jnp.max(s, axis=1, keepdims=True)
            e = jnp.exp(s - top)
            total = jnp.sum(e, axis=1, keepdims=True)
            pp[spot, side * t : (side + 1) * t, :] = (e * (1.0 / total)).astype(BF)
        two = dot(pp[spot], vv[m, :, cols])
        ctx[aligned(m * t, t, 16), cols] = jnp.where(low, two[:t], two[t:]).astype(BF)

    chain = g_w + [[g_o]]

    def attention(g, m):
        def step(i, carry):
            attend(m, g * 2 + i)
            return carry

        lax.fori_loop(0, 2, step, 0, unroll=2)

    for item in chain[0]:
        item.forward()
    normalize(0)
    for item in chain[0]:
        item.forward_rest()
    for item in g_tok[1:]:
        item.forward()
    for g in range(groups):
        for m in range(z.m):
            if g == 0 and m > 0:
                g_tok[m].arrive()
                normalize(m)
                spill(toks, o_toks, "gp")
                spill(hid, o_hid, "gp")
            project(g, m)
            if m == 0 and g > 0 or m == 1 and g == 0:
                for item in chain[g + 1]:
                    item.forward()
            if g == 1 and m == 0:
                send_dy_rows()
            attention(g, m)
            if m == z.m - 1:
                for item in chain[g + 1]:
                    item.forward_rest()
    g_o.arrive()

    def output(i, carry):
        cols = aligned(i * 256, 256, 256)
        mid[:, cols] = dot(ctx[...], fo[:, cols])
        return carry

    lax.fori_loop(0, d // 256, output, 0)
    for m in range(z.m):
        at = slice(m * t, (m + 1) * t)
        x = mid[at, :] + tokens[m].astype(F32)
        mid[at, :] = x
        scale = lax.rsqrt(jnp.mean(x * x, axis=1, keepdims=True) + EPS)
        nrm[at, :] = (x * scale * gain_two).astype(BF)
    logits = dot_t(nrm[...], router)
    lane = iota((mt, z.small), 1)
    pick0 = jnp.sum(jnp.where(lane == route0, logits, 0.0), axis=1, keepdims=True)
    pick1 = jnp.sum(jnp.where(lane == route1, logits, 0.0), axis=1, keepdims=True)
    top = jnp.maximum(pick0, pick1)
    e0, e1 = jnp.exp(pick0 - top), jnp.exp(pick1 - top)
    gate0, gate1 = e0 / (e0 + e1), e1 / (e0 + e1)
    lane = iota((mt, LANES), 1)
    sd[...] = jnp.where(
        lane == 0, slot0, jnp.where(lane == 1, slot1, jnp.where(lane == 2, gate0, jnp.where(lane == 3, gate1, 0.0)))
    )
    gate_row = jnp.sum(one_hot(z, slot0) * gate0 + one_hot(z, slot1) * gate1, axis=0, keepdims=True)
    high = gate_row.astype(BF).astype(F32)
    is_high = iota((2 * z.n16, 1), 0) < z.n16
    gates = (dest[...].astype(F32) * jnp.where(is_high, high, gate_row - high)).astype(BF)
    gates = dot(gates, place_m[...]).astype(BF)
    x_dy.finish()
    to_slots(nrm)
    xs[:, :LANES] = (xs[:, :LANES].astype(F32) + tdot(rows_of[...], gates)).astype(BF)
    x_move.start(even)
    xr[0 : z.sp, :] = xs[mine, :]

    load_out.wait()

    def expert_rows(ref, h, l, cols):
        return ref[:, aligned(h * z.cb + l * z.cr, z.cr, 16), cols].reshape(z.ns * z.cr, -1)

    def gradient(h):
        def step(l, carry):
            g = dot_t(expert_rows(dyg, h, l, slice(None)), w_out[l])
            gp[:, aligned(h * z.cb + l * z.cr, z.cr, 16), :] = g.astype(BF).reshape(z.ns, z.cr, ff)
            return carry

        lax.fori_loop(0, z.el, step, 0)

    def gather_of(h):
        item = base + 1 + (1 + z.el) * h
        out = [Gather(p, gwg.at[p.s, h], lambda o: gwg.at[o, h], gsend, grecv, item)]
        for l in range(z.el):
            at = pl.ds(h * z.cb + l * z.cr, z.cr)
            out.append(Gather(p, xg.at[p.s, at], lambda o, at=at: xg.at[o, at], gsend, grecv, item + 1 + l))
        return out

    gathers = [gather_of(h) for h in range(2)]

    def distribute(h):
        x_move.arrive((even, odd)[h])
        if h == 0:
            x_move.start(odd)
        gwg[p.s, h] = dot(gate_of[...], xr[h * z.hs : (h + 1) * z.hs, :LANES]).astype(BF)
        gathers[h][0].start()
        in_order(xr, xg, h)
        for item in gathers[h][1:]:
            item.start()

    def gates_of(h):
        gathers[h][0].arrive()
        for b in range(z.ns):
            wide = dot(source[...], gwg[b, h]) * pick[...].astype(F32)
            gwc[b] = jnp.sum(wide, axis=1, keepdims=True)

    def activate(h, l):
        at_rows = pl.ds(h * z.cb + l * z.cr, z.cr)
        gate = gwc[:, l * z.cr : (l + 1) * z.cr, :]
        gate_column = gate.reshape(z.ns * z.cr, 1)

        def step(tile, carry):
            at = aligned(tile * 256, 256, 256)
            x = dot(expert_rows(xg, h, l, slice(None)), w_in[l, :, at])
            g = expert_rows(gp, h, l, at).astype(F32)
            x2 = x * x
            th = jnp.tanh(x * (GELU_A + (GELU_A * GELU_B) * x2))
            hx = 0.5 * x
            up = 1.0 + th
            a = hx * up
            act[:, at_rows, at] = a.astype(BF).reshape(z.ns, z.cr, 256)
            slope = 0.5 * up + hx * (1.0 - th * th) * (GELU_A + (3.0 * GELU_A * GELU_B) * x2)
            gp[:, at_rows, at] = (g * gate_column * slope).astype(BF).reshape(z.ns, z.cr, 256)
            toward = jnp.sum(a * g, axis=1, keepdims=True).reshape(z.ns, z.cr, 1)
            ggc[:, at_rows, :] = toward + jnp.where(tile == 0, 0.0, ggc[:, at_rows, :])
            return carry

        lax.fori_loop(0, tiles, step, 0, unroll=tiles)
        dyg[:, at_rows, :] = (dyg[:, at_rows, :].astype(F32) * gate).astype(BF)

    def unit(u):
        h, cols = u // 2, pl.ds((u % 2) * half, half)
        return (
            Scatter(
                p, part.at[u, p.c], part.at[u, 1 - p.c], rp.at[u], ys.at[u], yr.at[u],
                psend.at[u], precv.at[u], ysend.at[u], yrecv.at[u],
            ),
            Return(p, fin.at[u], o_ret, h, cols, rsend.at[u], rrecv.at[u]),
        )

    units = [unit(u) for u in range(4)]
    results = [
        Scatter(
            p, rpart.at[u, p.c], rpart.at[u, 1 - p.c], rrp.at[u], rys.at[u], ryr.at[u],
            psend.at[4 + u], precv.at[4 + u], ysend.at[4 + u], yrecv.at[4 + u],
        )
        for u in range(2)
    ]

    def products(ref, weight, transposed, dst, h, l):
        rows = expert_rows(ref, h, l, slice(None))
        out = (dot_t(rows, weight[l]) if transposed else dot(rows, weight[l])).astype(BF)
        for b in range(z.ns):
            for c in range(2):
                block = out[b * z.cr : (b + 1) * z.cr, c * half : (c + 1) * half]
                dst[2 * h + c, b % 2, b // 2, l * z.cr : (l + 1) * z.cr, :] = block

    def stage_a(h, l):
        products(gp, w_in, True, part, h, l)
        if l == z.el - 1:
            units[2 * h][0].send()
            units[2 * h + 1][0].send()

    def stage_b(u):
        units[u][0].middle()

    def stage_c(u):
        fin[u] = tdot(perm[...], units[u][0].total().astype(BF)).astype(BF)
        units[u][1].start_remote()
        if u < 2:
            mine_there = o_ret.at[mine, pl.ds((u % 2) * half, half)]
            spill(fin.at[u, pl.ds(0, z.sp)], mine_there, "fin")

    g_scatter = Scatter(
        p, gpart.at[p.c], gpart.at[1 - p.c], grp, gys, gyr, gsem.at[0], gsem.at[1], gsy.at[0], gsy.at[1]
    )

    def toward_a():
        for b in range(z.ns):
            for h in range(2):
                col = ggc[b, h * z.cb : (h + 1) * z.cb, :]
                high = col.astype(BF).astype(F32)
                put = pick[...].astype(F32)
                top = tdot(source[...], (high * put).astype(BF))
                rest = tdot(source[...], ((col - high) * put).astype(BF))
                both = jnp.where(iota(top.shape, 0) < z.n16, top, rest)
                gpart[b % 2, b // 2, h * 2 * z.n16 : (h + 1) * 2 * z.n16, :] = both.astype(BF)
        g_scatter.send()

    def toward_copy(k):
        back = (-k[0] % z.nz, k[1])
        return rcopy(
            gout.at[k[0] % 2], gret.at[position(z, back)], gsx.at[0, position(z, k) - 1], gsx.at[1, position(z, back) - 1],
            (p.expert(*k), p.s),
        )

    def toward_c():
        total = g_scatter.total()
        for h in range(2):
            first = total[h * 2 * z.n16 : h * 2 * z.n16 + z.n16]
            value = first + total[h * 2 * z.n16 + z.n16 : (h + 1) * 2 * z.n16]
            high, rest = split_high(value)
            gout[h, 0 : z.n16, :] = high
            gout[h, z.n16 : 2 * z.n16, :] = rest
        for k in offsets(z):
            toward_copy(k).start()
        gret[0] = gout[0]

    def toward_d():
        for k in offsets(z):
            toward_copy((-k[0] % z.nz, k[1])).wait_recv()
        line = iota((2 * z.n16, LANES), 0)
        out = jnp.zeros((2 * z.n16, LANES), F32)
        for k in [(0, 0)] + offsets(z):
            back = (-k[0] % z.nz, k[1])
            at = position(z, back) - (k[0] % 2) * z.hn
            got = gret[position(z, k)].astype(F32)
            rank = p.expert(*k)
            out = jnp.where(line == rank, got[at : at + 1, :], out)
            out = jnp.where(line == z.n16 + rank, got[z.n16 + at : z.n16 + at + 1, :], out)
        ggrows[...] = out.astype(BF)
        for k in offsets(z):
            toward_copy(k).wait_send()

    def both(ref, l, cols):
        return jnp.concatenate([expert_rows(ref, h, l, cols) for h in range(2)], 0)

    stores = []

    def weight_grad(n, left, right, out, l):
        if n >= 2:
            stores[n - 2].wait()

        def step(i, carry):
            at = aligned(i * 256, 256, 256)
            wstage[n % 2, :, at] = tdot(both(left, l, slice(None)), both(right, l, at)).astype(BF)
            return carry

        lax.fori_loop(0, d // 256, step, 0)
        copy = pltpu.make_async_copy(wstage.at[n % 2], out.at[l], csem.at[2 + n])
        copy.start()
        stores.append(copy)

    def result_a(h):
        for l in range(z.el):
            products(act, w_out, False, rpart, h, l)
        for u in (2 * h, 2 * h + 1):
            if h == 0:
                results[u].send()
            else:
                spill(rpart.at[u], o_rpart.at[u - 2])

    def result_c(u):
        units[u][1].finish()
        waiting["fin"][u].wait()
        fin[u] = tdot(perm[...], results[u].total().astype(BF)).astype(BF)
        spill(fin.at[u], o_rfin.at[u])

    spill(kk, o_kk, "act")
    spill(vv, o_vv, "act")
    g_dy.forward()
    g_dy.arrive()
    for copy in waiting["gp"]:
        copy.wait()
    for item in g_tok:
        item.finish()
    gradient(0)
    gradient(1)
    distribute(0)
    load_in.wait()
    for copy in waiting["act"]:
        copy.wait()
    g_dy.finish()
    gathers[0][0].forward()
    gathers[0][1].forward()
    gates_of(0)
    gathers[0][1].arrive()
    activate(0, 0)
    stage_a(0, 0)
    for l in range(1, z.el):
        gathers[0][1 + l].forward()
    distribute(1)
    for l in range(1, z.el):
        gathers[0][1 + l].arrive()
        activate(0, l)
        stage_a(0, l)
    gathers[1][0].forward()
    stage_b(0)
    stage_b(1)
    gathers[1][1].forward()
    gates_of(1)
    result_a(0)
    gathers[1][1].arrive()
    activate(1, 0)
    stage_a(1, 0)
    for l in range(1, z.el):
        gathers[1][1 + l].forward()
        gathers[1][1 + l].arrive()
        activate(1, l)
        stage_a(1, l)
    toward_a()
    stage_b(2)
    stage_b(3)
    g_scatter.middle()
    stage_c(0)
    stage_c(1)
    results[0].middle()
    results[1].middle()
    result_a(1)
    for src, dst in (
        (sd, o_sd), (mid, o_mid), (nrm, o_nrm), (ctx, o_ctx), (fo, o_fo), (qq, o_qq), (pp, o_pp), (fk, o_fk), (fv, o_fv),
        (fq, o_fq),
    ):
        spill(src, dst)
    weight_grad(0, act, dyg, dout, 0)
    stage_c(2)
    weight_grad(1, act, dyg, dout, 1)
    stage_c(3)
    toward_c()
    weight_grad(2, xg, gp, din, 0)
    result_c(0)
    weight_grad(3, xg, gp, din, 1)
    result_c(1)
    toward_d()
    for u in range(4):
        units[u][1].arrive()
    for item in [g_small] + sum(g_w, []) + [g_o] + list(gathers[0]) + list(gathers[1]):
        item.finish()
    x_move.finish()
    g_scatter.finish()
    for u in (2, 3):
        units[u][1].finish()
    for scatter, _ in units:
        scatter.finish()
    for scatter in results:
        scatter.finish()
    for copy in waiting[None] + stores[2:]:
        copy.wait()


ANY = pl.BlockSpec(memory_space=pl.ANY)


def forward(z, *inputs):
    def bf(*shape):
        return jax.ShapeDtypeStruct(shape, BF)

    def f32(*shape):
        return jax.ShapeDtypeStruct(shape, F32)

    def vm(x):
        return pltpu.VMEM(x.shape, x.dtype)

    dma = pltpu.SemaphoreType.DMA
    half, ny, nb = z.d // 2, z.ny, 2 * z.n16
    kept = (
        bf(z.m, z.g, z.d), bf(z.m, z.g, z.d), bf(z.m, z.g, z.d), bf(z.m, z.g, z.d), bf(z.mt, z.d),
        bf(z.m * z.pairs, 2 * z.t, z.g), bf(z.mt, z.d), f32(z.mt, z.d), bf(z.mt, z.d), f32(z.mt, LANES),
        bf(z.d, z.d), bf(z.d, z.d), bf(z.d, z.d), bf(z.d, z.d),
    )
    smallg = bf(z.ns, z.small, z.d)
    ret, rpart, rfin = bf(z.slots, z.d), bf(4, 2, ny, z.cb, half), bf(4, z.hs, half)
    outs = kept + (smallg, ret, bf(2, z.hs, half), bf(2, 2, ny, z.cb, half), bf(nb, LANES), bf(z.el, z.d, z.ff), bf(z.el, z.ff, z.d))
    rows = bf(z.ns, z.blk, z.d)
    scratch = [vm(x) for x in kept[4:]]
    scratch += [vm(bf(z.small, z.d)), vm(smallg)]
    scratch += [vm(ret)] * 3 + [vm(rows)] * 2 + [vm(bf(z.ns, z.blk, z.ff))] * 2
    scratch += [vm(bf(z.el, z.d, z.ff)), vm(bf(z.el, z.ff, z.d))]
    scratch += [pltpu.VMEM((8, LANES), F32), pltpu.VMEM((z.m, z.t, z.g), I32)]
    scratch += [vm(bf(z.ns, 2, nb, LANES)), vm(f32(z.ns, z.cb, 1)), vm(f32(z.ns, z.blk, 1))]
    shares = [vm(rpart), vm(bf(4, ny, z.cb, half)), vm(bf(4, ny - 1, z.cb, half)), vm(bf(4, ny - 1, z.cb, half))]
    scratch += shares + [vm(rfin)] + [vm(rpart), vm(bf(2, ny, z.cb, half)), vm(bf(2, ny - 1, z.cb, half)), vm(bf(2, ny - 1, z.cb, half))]
    scratch += [vm(bf(2, z.d, z.d))]
    scratch += [vm(bf(2, ny, 2 * nb, LANES)), vm(bf(ny, 2 * nb, LANES))]
    scratch += [vm(bf(ny - 1, 2 * nb, LANES))] * 2 + [vm(bf(2, nb, LANES)), vm(bf(z.ne, nb, LANES))]
    n_items, n_weights = 1 + z.m + 3 + 2 * z.el, 3 * (z.d // 256) + 1
    scratch += [dma((10,)), dma((21,)), dma((n_items, 2 * ny - 1)), dma((n_items, 2 * ny - 1))]
    scratch += [dma((n_weights, 4 * ny - 3))] * 2 + [dma((2, z.ne - 1))] * 2
    scratch += [dma((6,))] * 2 + [dma((6, ny - 1))] * 2 + [dma((4, z.hn))] * 2
    scratch += [dma((2,)), dma((2, ny - 1)), dma((2, z.ne - 1))]
    return pl.pallas_call(
        functools.partial(forward_kernel, z),
        out_shape=outs,
        in_specs=[VMEM] * 3 + [SMEM] + [ANY] * 4 + [VMEM] * 2 + [ANY] * 2 + [VMEM] * 7,
        out_specs=[ANY] * 18 + [VMEM] + [ANY] * 2,
        scratch_shapes=scratch,
        compiler_params=pltpu.CompilerParams(
            collective_id=0, has_side_effects=True, vmem_limit_bytes=63 * 2**20
        ),
        name="forward",
    )(*inputs)


class Reduce:
    def __init__(self, place, part, from_core, to_y, from_y, to_x, from_x, summed, near_in, mid, mid_in, done, sems):
        self.p, self.part, self.from_core, self.done, self.sems = place, part, from_core, done, sems
        self.to_y, self.from_y, self.to_x, self.from_x = to_y, from_y, to_x, from_x
        self.summed, self.near_in, self.mid, self.mid_in = summed, near_in, mid, mid_in
        self.rows = done.shape[0] // 4
        self.x, zz = lax.rem(place.e, 2), lax.div(place.e, 2)
        self.side = lax.rem(zz, 2)
        self.near_at = ((zz + 1 - 2 * self.side) * 2 + self.x, place.s)

    def x_rows(self, x):
        return aligned(x * (2 * self.rows), 2 * self.rows, 16)

    def side_rows(self, side):
        return aligned(side * self.rows, self.rows, 16)

    def done_rows(self, side):
        return aligned((self.x * 2 + side) * self.rows, self.rows, 16)

    def hop(self, n, src, dst, to):
        return rcopy(src, dst, self.sems.at[0, n], self.sems.at[1, n], to)

    def copy(self, n, out=True):
        p = self.p
        if n == 0:
            return self.hop(0, self.part.at[1 - p.c], self.from_core, (p.e, p.shard(0, True)))
        if n == 2:
            return self.hop(2, self.to_x, self.from_x, (p.expert(0, 1), p.s))
        if n == 3:
            return self.hop(3, self.summed.at[self.side_rows(1 - self.side)], self.near_in, self.near_at)
        if n == 4:
            return self.hop(4, self.mid, self.mid_in, (p.expert(2, 0), p.s))
        if n == 5:
            block = self.done.at[self.done_rows(self.side if out else 1 - self.side)]
            return self.hop(5, block, block, self.near_at)
        block = self.done.at[self.x_rows(self.x if out else 1 - self.x)]
        return self.hop(6, block, block, (p.expert(0, 1), p.s))

    def copy_y(self, k):
        p = self.p
        return self.hop(6 + k if k > 1 else 1, self.to_y.at[k - 1], self.from_y.at[k - 1], (p.e, p.shard(k, False)))

    def chip(self, y, rows=slice(None)):
        return self.part[self.p.c, y, rows, :].astype(F32) + self.from_core[y, rows, :].astype(F32)

    def step(self, n):
        p, ny = self.p, self.p.z.ny
        if n == 2:
            for k in range(1, ny):
                self.copy_y(k).wait_recv()
        elif n > 0:
            self.copy(n - 1, False).wait_recv()
        if n == 1:
            for k in range(1, ny):
                self.to_y[k - 1] = self.chip(lax.rem(p.y + k, ny)).astype(BF)
                self.copy_y(k).start()
        elif n == 2:
            def whole(x):
                out = self.chip(p.y, self.x_rows(x))
                for k in range(1, ny):
                    out = out + self.from_y[k - 1, self.x_rows(x), :].astype(F32)
                return out.astype(BF)

            self.to_x[...] = whole(1 - self.x)
            self.summed[...] = whole(self.x)
        elif n == 3:
            self.summed[...] = (self.summed[...].astype(F32) + self.from_x[...].astype(F32)).astype(BF)
        elif n == 4:
            own = self.summed[self.side_rows(self.side), :].astype(F32)
            self.mid[...] = (own + self.near_in[...].astype(F32)).astype(BF)
        elif n == 5:
            out = self.mid[...].astype(F32) + self.mid_in[...].astype(F32)
            self.done[self.done_rows(self.side), :] = out.astype(BF)
        if n != 1 and n < 7:
            self.copy(n).start()

    def finish(self):
        for n in (0, 2, 3, 4, 5, 6):
            self.copy(n).wait_send()
        for k in range(1, self.p.z.ny):
            self.copy_y(k).wait_send()


class SmallReduce:
    def __init__(self, place, part, from_core, to_y, from_y, own, other, sems):
        self.p, self.part, self.from_core = place, part, from_core
        self.to_y, self.from_y, self.own, self.other, self.sems = to_y, from_y, own, other, sems
        zz = lax.div(place.e, 2)
        near = ((zz + 1 - 2 * lax.rem(zz, 2)) * 2 + lax.rem(place.e, 2), place.s)
        self.partners = [(place.expert(0, 1), place.s), near, (place.expert(2, 0), place.s)]

    def copy(self, n):
        p = self.p
        sems = self.sems.at[0, n], self.sems.at[1, n]
        if n == 0:
            return rcopy(self.part.at[1 - p.c], self.from_core, *sems, (p.e, p.shard(0, True)))
        return rcopy(self.own.at[n - 2], self.other.at[n - 2], *sems, self.partners[n - 2])

    def copy_y(self, k):
        p = self.p
        return rcopy(
            self.to_y.at[k - 1], self.from_y.at[k - 1], self.sems.at[0, 4 + k], self.sems.at[1, 4 + k],
            (p.e, p.shard(k, False)),
        )

    def step(self, n):
        p, ny = self.p, self.p.z.ny
        if n == 0:
            self.copy(0).start()
        elif n == 1:
            self.copy(0).wait_recv()
            for k in range(1, ny):
                y = lax.rem(p.y + k, ny)
                self.to_y[k - 1] = (self.part[p.c, y].astype(F32) + self.from_core[y].astype(F32)).astype(BF)
                self.copy_y(k).start()
        elif n == 2:
            out = self.part[p.c, p.y].astype(F32) + self.from_core[p.y].astype(F32)
            for k in range(1, ny):
                self.copy_y(k).wait_recv()
                out = out + self.from_y[k - 1].astype(F32)
            self.own[0] = out.astype(BF)
            self.copy(2).start()
        else:
            self.copy(n - 1).wait_recv()
            out = self.own[n - 3].astype(F32) + self.other[n - 3].astype(F32)
            if n == 5:
                return out
            self.own[n - 2] = out.astype(BF)
            self.copy(n).start()

    def finish(self):
        for n in (0, 2, 3, 4):
            self.copy(n).wait_send()
        for k in range(1, self.p.z.ny):
            self.copy_y(k).wait_send()


GROUPS = ((0, 1), (2, 3), (4,), (5,))


def backward_kernel(
    z,
    dy, counts, routes, dest, place_m, perm, ggrows,
    i_toks, i_hid, i_kk, i_vv, i_qq, i_pp, i_ctx, i_mid, i_nrm, i_sd, i_fk, i_fv, i_fq, i_fo, i_small, i_ret, i_rfin, i_rpart,
    mixed, dtok, done_o, done_0, done_1, done_2, done_3, drouter, dvecs,
    toks, hid, kk, vv, qq, pp, ctx, mid, nrm, sd, fk, fv, fq, fo, smallg, ret, retr,
    fin, rmine, rp, rys, ryr, gctx, gqb, gkb, gvb, gmid, lower, edge_id, edge_ok, tab, gain_rows,
    red_o, red_0, red_1, red_2, red_3,
    gpart, grp, gys, gyr, sbuf, small_refs,
    csem, rr1, rr2, rs1, rs2, rs3, rs4,
    gp1, gp2, gy1, gy2,
):
    p = Place(z)
    t, d, mt = z.t, z.d, z.mt
    half = d // 2
    loads = {}

    def load(src, dst, name):
        loads[name] = pltpu.make_async_copy(src, dst, csem.at[len(loads)])
        loads[name].start()

    load(i_sd, sd, "sd")
    load(i_ret, ret, "ret")
    load(i_small, smallg, "small")
    load(i_mid, mid, "mid")
    load(i_nrm, nrm, "nrm")
    load(i_ctx, ctx, "ctx")
    load(i_fo, fo, "fo")
    for u in range(2):
        load(i_rpart.at[u, p.c], rmine.at[u], ("part", u))
    load(i_qq, qq, "qq")
    load(i_vv, vv, "vv")
    load(i_kk, kk, "kk")
    load(i_pp, pp, "pp")
    load(i_hid, hid, "hid")
    load(i_fk, fk, "fk")
    load(i_fv, fv, "fv")
    load(i_fq, fq, "fq")
    load(i_toks, toks, "toks")
    p.barrier()

    returns, halves = [], []
    for u in range(4):
        h, cols = u // 2, pl.ds((u % 2) * half, half)
        src = i_rfin.at[u] if h == 0 else fin.at[u - 2]
        returns.append(Return(p, src, retr, h, cols, rr1.at[u], rr2.at[u]))
        if h == 0:
            returns[u].start_remote()
            load(i_rfin.at[u, pl.ds(0, z.sp)], retr.at[aligned(p.e * z.sp, z.sp, 16), cols], ("r", u))
    for u in range(2):
        halves.append(
            Scatter(
                p, rmine.at[u], i_rpart.at[u, 1 - p.c], rp.at[u], rys.at[u], ryr.at[u],
                rs1.at[u], rs2.at[u], rs3.at[u], rs4.at[u],
            )
        )
        halves[u].send()

    def result_b(u):
        loads["part", u].wait()
        halves[u].middle()

    def result_c(u):
        fin[u] = tdot(perm[...], halves[u].total().astype(BF)).astype(BF)
        returns[2 + u].start_remote()

    route0, route1 = route_columns(z, routes)
    loads["sd"].wait()
    slot0, slot1 = sd[:, 0:1], sd[:, 1:2]
    gate0, gate1 = sd[:, 2:3], sd[:, 3:4]
    hot0, hot1 = one_hot(z, slot0).astype(BF), one_hot(z, slot1).astype(BF)
    hot = hot0 + hot1

    def toward(hots):
        wide = dot(dot_t(hots, dest[...]).astype(BF), ggrows[...]) * dot(hots, place_m[...])
        return jnp.sum(wide, axis=1, keepdims=True)

    toward0, toward1 = toward(hot0), toward(hot1)
    mean = gate0 * toward0 + gate1 * toward1
    lane = iota((mt, z.small), 1)
    glog = jnp.where(lane == route0, gate0 * (toward0 - mean), 0.0)
    glog = (glog + jnp.where(lane == route1, gate1 * (toward1 - mean), 0.0)).astype(BF)
    result_b(0)
    loads["small"].wait()
    sums = smallg[0].astype(F32)
    for b in range(1, z.ns):
        sums = sums + smallg[b].astype(F32)
    gain_one = sums[z.e : z.e + 1, :]
    gain_two = sums[z.e + 1 : z.e + 2, :]
    router = sums.astype(BF)
    loads["ret"].wait()
    gnorm = dot(glog, router) + dot(hot, ret[...])
    loads["mid"].wait()
    x = mid[...]
    scale = lax.rsqrt(jnp.mean(x * x, axis=1, keepdims=True) + EPS)
    xh = x * scale
    gain_rows[1:2, :] = jnp.sum(gnorm * xh, axis=0, keepdims=True)
    gy = gnorm * gain_two
    gm = dy[...].astype(F32) + scale * (gy - xh * jnp.mean(gy * xh, axis=1, keepdims=True))
    gmid[...] = gm
    gattn = gm.astype(BF)
    loads["nrm"].wait()
    sbuf[...] = tdot(glog, nrm[...])

    reductions = [
        Reduce(p, *refs[:-1], done, refs[-1])
        for refs, done in ((red_0, done_0), (red_1, done_1), (red_2, done_2), (red_3, done_3), (red_o, done_o))
    ]
    parts = [red_0[0], red_1[0], red_2[0], red_3[0], red_o[0]]

    def stage(u, n):
        reductions[u].step(n)

    def put(u, first, value):
        value = value.astype(BF)
        for b in range(z.ns):
            parts[u][b % 2, b // 2, :, first : first + value.shape[1]] = value[b * z.r : (b + 1) * z.r]

    loads["ctx"].wait()
    for i in range(d // 256):
        put(4, i * 256, tdot(ctx[...], gattn[:, i * 256 : (i + 1) * 256]))
    stage(4, 0)
    loads["fo"].wait()
    for i in range(d // 256):
        cols = slice(i * 256, (i + 1) * 256)
        gctx[:, cols] = dot_t(gattn, fo[cols, :]).astype(BF)

    tab[...] = jnp.zeros_like(tab)
    lane = iota((1, LANES), 1)
    starts = jnp.where(lane <= 16, lane, 0)
    for i, edge in enumerate(BUCKET_EDGES):
        starts = jnp.where(lane == 17 + i, edge, starts)
    for m in range(z.m):
        key_pos, _ = key_layout(z, counts, m, (z.g, 1), 0)
        lower[m] = jnp.where(key_pos <= iota((z.g, z.far), 1), 1.0, 0.0).astype(BF)
        at = query_position(z, counts, m, p.s) - starts
        ok = (at >= 0) & (lane < BUCKETS)
        edge_id[m] = jnp.where(ok, at, 0)
        edge_ok[m] = jnp.where(ok, 1.0, 0.0)
    low = iota((t, LANES), 1) < 64

    def attend_back(i, unit):
        m = lax.rem(i, z.m)
        pair = unit
        cols = aligned(pair * LANES, LANES, LANES)
        rows = aligned(m * t, t, 16)
        q, g = qq[rows, cols], gctx[rows, cols]
        zero = jnp.zeros_like(q)
        q_two = jnp.concatenate([jnp.where(low, q, zero), jnp.where(low, zero, q)], 0)
        g_two = jnp.concatenate([jnp.where(low, g, zero), jnp.where(low, zero, g)], 0)
        probs = pp[m * z.pairs + pair]
        pf = probs.astype(F32)
        gp = dot_t(g_two, vv[m, :, cols])
        gs = (pf * (gp - jnp.sum(pf * gp, axis=1, keepdims=True))).astype(BF)
        two = dot(gs, kk[m, :, cols])
        gqb[rows, cols] = (jnp.where(low, two[:t], two[t:]) * 0.125).astype(BF)
        gkb[m, :, cols] = tdot(gs, q_two).astype(BF)
        gvb[m, :, cols] = tdot(probs, g_two).astype(BF)
        total = dot(gs, lower[m])
        for side in range(2):
            found = jnp.zeros((t, LANES), F32)
            for b in range(z.far // LANES):
                at = edge_id[m] - b * LANES
                inside = (at >= 0) & (at < LANES)
                got = jnp.take_along_axis(
                    total[side * t : (side + 1) * t, b * LANES : (b + 1) * LANES], jnp.where(inside, at, 0), axis=1
                )
                found = jnp.where(inside, got, found)
            found = jnp.sum(found * edge_ok[m], axis=0, keepdims=True)
            row = pl.ds(pair * 2 + side, 1)
            tab[row, :] = tab[row, :] + found
        return unit

    def attention(pair):
        lax.fori_loop(0, z.m, attend_back, pair, unroll=2)

    def own_hidden():
        return jnp.concatenate([hid[m, aligned(p.s * t, t, 16), :] for m in range(z.m)], 0)

    def weight_grads(u):
        n = len(GROUPS[u]) * LANES
        cols = slice(GROUPS[u][0] * LANES, GROUPS[u][0] * LANES + n)
        put(u, 0, tdot(own_hidden(), gqb[:, cols]))
        every = hid[...].reshape(z.m * z.g, d)
        put(u, n, tdot(every, gkb[:, :, cols].reshape(z.m * z.g, n)))
        put(u, 2 * n, tdot(every, gvb[:, :, cols].reshape(z.m * z.g, n)))

    grads = [
        Scatter(
            p, gpart.at[m, p.c], gpart.at[m, 1 - p.c], grp.at[m], gys.at[m], gyr.at[m],
            gp1.at[m], gp2.at[m], gy1.at[m], gy2.at[m],
        )
        for m in range(z.m)
    ]

    def hidden_grads(m):
        x = toks[m].astype(F32)
        scale = lax.rsqrt(jnp.mean(x * x, axis=1, keepdims=True) + EPS)
        for i in range(d // 256):
            cols = slice(i * 256, (i + 1) * 256)
            gh = dot_t(gkb[m], fk[cols, :]) + dot_t(gvb[m], fv[cols, :])
            own = dot_t(gqb[m * t : (m + 1) * t, :], fq[cols, :])
            for b in range(z.ns):
                rows = slice(b * t, (b + 1) * t)
                part = gh[rows] + jnp.where(p.s == b, 1.0, 0.0) * own
                gpart[m, b % 2, b // 2, :, cols] = part.astype(BF)
                row = jnp.sum(part * (toks[m, rows, cols].astype(F32) * scale[rows]), axis=0, keepdims=True)
                if m == 0 and b == 0:
                    gain_rows[0:1, cols] = row
                else:
                    gain_rows[0:1, cols] = gain_rows[0:1, cols] + row

    def token_grads(m):
        gh = grads[m].total()
        rows = slice(m * t, (m + 1) * t)
        x = toks[m, aligned(p.s * t, t, 16), :].astype(F32)
        scale = lax.rsqrt(jnp.mean(x * x, axis=1, keepdims=True) + EPS)
        xh = x * scale
        gy = gh * gain_one
        dtok[rows, :] = gmid[rows, :] + scale * (gy - xh * jnp.mean(gy * xh, axis=1, keepdims=True))

    small_sum = SmallReduce(p, *small_refs)

    def small_step(n):
        if n:
            return small_sum.step(n)
        tabs = tab[...]
        tabs = tabs - pltpu.roll(tabs, LANES - 1, 1)
        tabs = jnp.where(iota(tabs.shape, 1) < BUCKETS, tabs, 0.0)
        row = iota(sbuf.shape, 0)
        out = sbuf[...]
        out = jnp.where(row == z.e, gain_rows[0:1, :], out)
        out = jnp.where(row == z.e + 1, gain_rows[1:2, :], out)
        sbuf[...] = out
        per = LANES // BUCKETS
        for c in range(HEADS // per):
            piece = tabs[c * per : c * per + 1, :]
            for j in range(1, per):
                piece = piece + pltpu.roll(tabs[c * per + j : c * per + j + 1, :], j * BUCKETS, 1)
            sbuf[z.e + 2 : z.e + 3, c * LANES : (c + 1) * LANES] = piece
        every = sbuf[...].astype(BF)
        tail = every[z.e : z.small, :]
        for b in range(z.ns):
            block = dot_t(every, spread(z, b, z.r))
            biases = dot_t(tail, spread(z, b, HEADS * BUCKETS // z.ns))
            low_rows = jnp.where(iota(biases.shape, 0) == 2, biases, block[z.e : z.small])
            small_refs[0][b % 2, b // 2, 0 : z.e, :] = block[0 : z.e].astype(BF)
            small_refs[0][b % 2, b // 2, z.e : z.small, :] = low_rows.astype(BF)
        small_sum.step(0)

    def finish_mixed():
        for u in range(4):
            returns[u].arrive()
        for u in range(2):
            loads["r", u].wait()
        for m in range(z.m):
            rows = slice(m * t, (m + 1) * t)
            first, second = dot(hot0[rows], retr[...]), dot(hot1[rows], retr[...])
            mixed[rows, :] = (mid[rows, :] + gate0[rows] * first + gate1[rows] * second).astype(BF)

    for name in ("qq", "vv", "kk", "pp"):
        loads[name].wait()
    attention(0)
    stage(4, 1)
    attention(1)
    loads["hid"].wait()
    weight_grads(0)
    stage(0, 0)
    result_c(0)
    attention(2)
    stage(0, 1)
    attention(3)
    stage(4, 2)
    weight_grads(1)
    stage(1, 0)
    attention(4)
    stage(1, 1)
    weight_grads(2)
    stage(2, 0)
    stage(4, 3)
    attention(5)
    stage(2, 1)
    weight_grads(3)
    stage(3, 0)
    stage(0, 2)
    stage(4, 4)
    for name in ("fk", "fv", "fq", "toks"):
        loads[name].wait()
    hidden_grads(0)
    grads[0].send()
    stage(3, 1)
    hidden_grads(1)
    grads[1].send()
    small_step(0)
    stage(4, 5)
    stage(0, 3)
    stage(1, 2)
    stage(4, 6)
    stage(0, 4)
    small_step(1)
    result_b(1)
    grads[0].middle()
    grads[1].middle()
    stage(2, 2)
    stage(1, 3)
    stage(0, 5)
    stage(3, 2)
    small_step(2)
    stage(2, 3)
    stage(1, 4)
    stage(3, 3)
    stage(0, 6)
    small_step(3)
    stage(2, 4)
    stage(1, 5)
    stage(3, 4)
    result_c(1)
    small_step(4)
    stage(2, 5)
    stage(1, 6)
    stage(3, 5)
    token_grads(0)
    out = small_step(5)
    drouter[...] = out[0 : z.e, :]
    dvecs[...] = out[z.e : z.small, :]
    stage(2, 6)
    stage(3, 6)
    token_grads(1)
    finish_mixed()
    for u in (4, 0, 1, 2, 3):
        stage(u, 7)
    for item in reductions + returns + halves + grads + [small_sum]:
        item.finish()


def backward(z, *inputs):
    def bf(*shape):
        return pltpu.VMEM(shape, BF)

    def f32(*shape):
        return jax.ShapeDtypeStruct(shape, F32)

    dma = pltpu.SemaphoreType.DMA
    d, r, ny, nz, half = z.d, z.r, z.ny, z.nz, z.d // 2
    widths = [d] + [3 * LANES * len(g) for g in GROUPS]
    blocks = [jax.ShapeDtypeStruct((r, w), BF) for w in widths]
    outs = (jax.ShapeDtypeStruct((z.mt, d), BF), f32(z.mt, d), *blocks, f32(z.e, r), f32(z.small - z.e, r))

    def reduction(w):
        half, piece = bf(r // 2, w), bf(r // 4, w)
        return (
            bf(2, ny, r, w), bf(ny, r, w), bf(ny - 1, r, w), bf(ny - 1, r, w), half, half, half, piece, piece, piece,
            dma((2, 5 + ny)),
        )

    small = (
        bf(2, ny, z.small, r), bf(ny, z.small, r), bf(ny - 1, z.small, r), bf(ny - 1, z.small, r),
        bf(3, z.small, r), bf(3, z.small, r), dma((2, 4 + ny)),
    )
    kept = [pltpu.VMEM(x.shape, x.dtype) for x in inputs[7:-2]]
    return pl.pallas_call(
        functools.partial(backward_kernel, z),
        out_shape=outs,
        in_specs=[VMEM, SMEM] + [VMEM] * 5 + [ANY] * 18,
        out_specs=[VMEM] * len(outs),
        scratch_shapes=kept + [
            bf(z.slots, d),
            bf(2, z.hs, half), bf(2, ny, z.cb, half), bf(2, ny, z.cb, half), bf(2, ny - 1, z.cb, half), bf(2, ny - 1, z.cb, half),
            bf(z.mt, d), bf(z.mt, d), bf(z.m, z.g, d), bf(z.m, z.g, d), pltpu.VMEM((z.mt, d), F32),
            bf(z.m, z.g, z.far), pltpu.VMEM((z.m, z.t, LANES), I32), pltpu.VMEM((z.m, z.t, LANES), F32),
            pltpu.VMEM((16, LANES), F32), pltpu.VMEM((8, d), F32),
            *[reduction(w) for w in widths],
            bf(z.m, 2, ny, z.t, d), bf(z.m, ny, z.t, d), bf(z.m, ny - 1, z.t, d), bf(z.m, ny - 1, z.t, d),
            pltpu.VMEM((z.small, d), F32), small,
            dma((20,)), dma((4, z.hn)), dma((4, z.hn)), dma((2,)), dma((2,)), dma((2, ny)), dma((2, ny)),
            dma((z.m,)), dma((z.m,)), dma((z.m, ny)), dma((z.m, ny)),
        ],
        compiler_params=pltpu.CompilerParams(
            collective_id=1, has_side_effects=True, vmem_limit_bytes=63 * 2**20
        ),
        name="backward",
    )(*inputs)


def finish_kernel(
    d_o, d_0, d_1, d_2, d_3, din, dout, mixed, dtok, vecs, o_mixed, o_dtok, o_q, o_k, o_v, o_o, o_in, o_out, o_one, o_two, o_bias
):
    o_in[...] = din[...].astype(F32)
    o_out[...] = dout[...].astype(F32)
    o_mixed[...] = mixed[...]
    o_dtok[...] = dtok[...]
    o_o[...] = d_o[...].astype(F32)
    o_one[...] = vecs[0:1, :]
    o_two[...] = vecs[1:2, :]
    o_bias[...] = vecs[2:3, : o_bias.shape[1]]
    for pairs, block in zip(GROUPS, (d_0, d_1, d_2, d_3)):
        n, first = len(pairs) * LANES, pairs[0] * LANES
        for i, out in enumerate((o_q, o_k, o_v)):
            out[:, first : first + n] = block[:, i * n : (i + 1) * n].astype(F32)


def finish(z, n_bias, blocks, din, dout, mixed, dtok, vecs):
    d, r, n = z.d, z.r, 4
    rows = z.el * d // n

    def f32(*shape):
        return jax.ShapeDtypeStruct(shape, F32)

    def by_row(size, width=d):
        return pl.BlockSpec((size, width), lambda i: (i, 0))

    def once(*shape):
        return pl.BlockSpec(shape, lambda i: (0, 0))

    return pl.pallas_call(
        finish_kernel,
        grid=(n,),
        out_shape=(
            jax.ShapeDtypeStruct((z.mt, d), BF), f32(z.mt, d), *[f32(r, d)] * 4, *[f32(n * rows, d)] * 2,
            f32(1, r), f32(1, r), f32(1, n_bias),
        ),
        in_specs=[by_row(r // n, b.shape[1]) for b in blocks] + [by_row(rows)] * 2 + [by_row(z.mt // n)] * 2
        + [once(*vecs.shape)],
        out_specs=[by_row(z.mt // n)] * 2 + [by_row(r // n)] * 4 + [by_row(rows)] * 2
        + [once(1, r), once(1, r), once(1, n_bias)],
        name="finish",
    )(*blocks, din.reshape(n * rows, d), dout.reshape(n * rows, d), mixed, dtok, vecs)


def fused_device(
    z, tokens, cotangent, routes, prompt_rows, w_query, w_key, w_value, w_output, w_router, gain_attn, gain_ffn,
    pos_table, w_in, w_out,
):
    perm, rows_of, dest, place, gate_of, source, pick = layout_constants(z)
    n = pos_table.shape[0]
    vecs = jnp.concatenate([gain_attn, gain_ffn, pos_table])[None]
    dy = cotangent.reshape(z.mt, z.d)
    routes = routes.transpose(0, 2, 1)
    counts = prompt_rows[:, 0]
    kept = forward(
        z, tokens, dy, routes, counts, w_key, w_value, w_query, w_output, w_router.T, vecs, w_in, w_out,
        perm, rows_of, dest, place, gate_of, source, pick,
    )
    kept, (ggrows, din, dout) = kept[:18], kept[18:]
    mixed, dtok, *blocks, drouter, dvecs = backward(z, dy, counts, routes, dest, place, perm, ggrows, *kept)
    mixed, dtok, dq, dk, dv, do, din, dout, one, two, bias = finish(z, n, blocks, din, dout, mixed, dtok, dvecs)
    return (
        mixed.reshape(tokens.shape),
        dtok.reshape(tokens.shape),
        dq,
        dk,
        dv,
        do,
        drouter.T,
        one.reshape(-1),
        two.reshape(-1),
        bias.reshape(-1),
        din.reshape(w_in.shape),
        dout.reshape(w_out.shape),
    )


HIGHEST = lax.Precision.HIGHEST


def distance_bucket(distance):
    coarse = reduce(
        lambda running, border: running + (distance >= border).astype(jnp.int32),
        BUCKET_EDGES,
        jnp.full(distance.shape, 16, jnp.int32),
    )
    return jnp.where(distance < 16, distance, coarse)


def layout(counts, block_rows):
    shard_count = counts.shape[0]
    offsets = jnp.cumsum(counts, dtype=jnp.int32) - counts
    row_index = jnp.arange(shard_count * block_rows, dtype=jnp.int32)
    device = row_index // block_rows
    local_row = row_index - device * block_rows
    own_count = counts[device]
    is_prompt = local_row < own_count
    prompt_total = jnp.sum(counts, dtype=jnp.int32)
    position = jnp.where(
        is_prompt, offsets[device] + local_row, prompt_total + local_row - own_count
    )
    return (position, is_prompt, device)


def rms_norm(values, gain):
    return values * lax.rsqrt(jnp.mean(values * values, axis=-1, keepdims=True) + EPS) * gain


def matmul(left, right):
    return jnp.dot(left, right, preferred_element_type=jnp.float32)


def matmul_left(left, right):
    return lax.dot_general(
        left, right, (((0,), (0,)), ((), ())), preferred_element_type=jnp.float32
    )


def matmul_right(left, right):
    return lax.dot_general(
        left, right, (((1,), (1,)), ((), ())), preferred_element_type=jnp.float32
    )


def per_device(
    tokens,
    cotangent,
    routes,
    prompt_rows,
    w_query,
    w_key,
    w_value,
    w_output,
    w_router,
    gain_attn,
    gain_ffn,
    pos_table,
    w_in,
    w_out,
):
    shard_count = lax.axis_size("shard")
    expert_ranks = lax.axis_size("expert")
    own_index = lax.axis_index("shard")
    micro_count, tok_rows, model_width = tokens.shape
    local_experts = w_in.shape[0]
    expert_count = w_router.shape[1]
    capacity = (9 * tok_rows + 4 * expert_count - 1) // (4 * expert_count)
    head_count = HEADS
    head_size = model_width // head_count
    bucket_count = BUCKETS
    score_scale = head_size ** (-0.5)
    group_rows = shard_count * tok_rows
    slot_count = expert_ranks * capacity * local_experts
    recv_rows = expert_ranks * capacity
    bucket_ids = jnp.arange(bucket_count, dtype=jnp.int32)
    expert_ids = jnp.arange(expert_count, dtype=jnp.int32)
    gathered = (
        lax.all_gather(w_query, "shard", axis=0, tiled=True),
        lax.all_gather(w_key, "shard", axis=0, tiled=True),
        lax.all_gather(w_value, "shard", axis=0, tiled=True),
        lax.all_gather(w_output, "shard", axis=0, tiled=True),
        lax.all_gather(w_router, "shard", axis=0, tiled=True),
        lax.all_gather(gain_attn, "shard", axis=0, tiled=True),
        lax.all_gather(gain_ffn, "shard", axis=0, tiled=True),
        lax.all_gather(pos_table, "shard", axis=0, tiled=True),
    )
    full_query, full_key, full_value, full_output, full_router, gain_one, gain_two, table_flat = (
        gathered
    )
    gain_first = gain_one.astype(jnp.float32)
    gain_second = gain_two.astype(jnp.float32)
    table = table_flat.astype(jnp.float32).reshape(head_count, bucket_count)
    expert_in, expert_out = (
        lax.all_gather(w_in, "shard", axis=2, tiled=True),
        lax.all_gather(w_out, "shard", axis=1, tiled=True),
    )
    sum_query = jnp.zeros(full_query.shape, jnp.float32)
    sum_key = jnp.zeros(full_key.shape, jnp.float32)
    sum_value = jnp.zeros(full_value.shape, jnp.float32)
    sum_output = jnp.zeros(full_output.shape, jnp.float32)
    sum_router = jnp.zeros(full_router.shape, jnp.float32)
    sum_gain_one = jnp.zeros((model_width,), jnp.float32)
    sum_gain_two = jnp.zeros((model_width,), jnp.float32)
    sum_table = jnp.zeros((head_count, bucket_count), jnp.float32)
    sum_expert_in = jnp.zeros(expert_in.shape, jnp.float32)
    sum_expert_out = jnp.zeros(expert_out.shape, jnp.float32)
    mixed_parts = []
    grad_parts = []
    for micro_index in range(micro_count):
        inputs = tokens[micro_index].astype(jnp.float32)
        counts = prompt_rows[micro_index, 0]
        pos_all, prompt_all, device_all = layout(counts, tok_rows)
        query_pos = lax.dynamic_slice_in_dim(pos_all, own_index * tok_rows, tok_rows)
        hidden = rms_norm(inputs, gain_first).astype(jnp.bfloat16)
        query = matmul(hidden, full_query).astype(jnp.bfloat16)
        key = matmul(hidden, full_key).astype(jnp.bfloat16)
        value = matmul(hidden, full_value).astype(jnp.bfloat16)
        keys_all, values_all = (
            lax.all_gather(key, "shard", axis=0, tiled=True),
            lax.all_gather(value, "shard", axis=0, tiled=True),
        )
        key_index = jnp.arange(group_rows, dtype=jnp.int32)
        key_far = jnp.zeros((group_rows,), jnp.bool_)
        key_total = keys_all.shape[0]
        key_block = math.gcd(key_total, 512)
        block_count = key_total // key_block
        key_pos = pos_all[key_index]
        key_prompt = prompt_all[key_index]
        key_device = device_all[key_index]
        key_mine = key_device == own_index
        distance = query_pos[:, None] - key_pos[None, :]
        visible = (
            (distance >= 0)
            & (key_prompt | key_mine)[None, :]
            & jnp.logical_not(key_far & key_mine)[None, :]
        )
        bucket_all = distance_bucket(jnp.maximum(distance, 0))
        bucket_blocks = bucket_all.reshape(tok_rows, block_count, key_block).transpose(1, 0, 2)
        visible_blocks = visible.reshape(tok_rows, block_count, key_block).transpose(1, 0, 2)
        query_heads = query.reshape(tok_rows, head_count, head_size)
        key_blocks = keys_all.reshape(block_count, key_block, head_count, head_size)
        value_blocks = values_all.reshape(block_count, key_block, head_count, head_size)

        def make_bias(unused, block_item):
            bucket_piece, visible_piece = block_item
            bucket_hits = (bucket_piece[:, :, None] == bucket_ids).astype(jnp.float32)
            bias = jnp.einsum("qkb,hb->hqk", bucket_hits, table, precision=HIGHEST)
            return (unused, jnp.where(visible_piece[None], bias, MASKED))

        _, bias_blocks = lax.scan(
            make_bias, jnp.zeros((), jnp.float32), (bucket_blocks, visible_blocks)
        )

        def score_piece(key_piece, bias_piece):
            raw = jnp.einsum(
                "qhd,khd->hqk", query_heads, key_piece, preferred_element_type=jnp.float32
            )
            return raw * score_scale + bias_piece

        def running(state_pair, block_item):
            running_max, running_sum = state_pair
            key_piece, bias_piece = block_item
            scores = score_piece(key_piece, bias_piece)
            new_max = jnp.maximum(running_max, jnp.max(scores, axis=-1))
            running_sum = running_sum * jnp.exp(running_max - new_max) + jnp.sum(
                jnp.exp(scores - new_max[:, :, None]), axis=-1
            )
            return ((new_max, running_sum), None)

        start_pair = (
            jnp.full((head_count, tok_rows), MASKED, jnp.float32),
            jnp.zeros((head_count, tok_rows), jnp.float32),
        )
        (running_max, running_sum), _ = lax.scan(running, start_pair, (key_blocks, bias_blocks))
        log_total = running_max + jnp.log(running_sum)

        def gather_context(context_sum, block_item):
            key_piece, value_piece, bias_piece = block_item
            weights_low = jnp.exp(
                score_piece(key_piece, bias_piece) - log_total[:, :, None]
            ).astype(jnp.bfloat16)
            return (
                context_sum
                + jnp.einsum(
                    "hqk,khd->qhd", weights_low, value_piece, preferred_element_type=jnp.float32
                ),
                None,
            )

        context, _ = lax.scan(
            gather_context,
            jnp.zeros((tok_rows, head_count, head_size), jnp.float32),
            (key_blocks, value_blocks, bias_blocks),
        )
        context_low = context.reshape(tok_rows, model_width).astype(jnp.bfloat16)
        middle = inputs + matmul(context_low, full_output)
        normed = rms_norm(middle, gain_second).astype(jnp.bfloat16)
        logits = matmul(normed, full_router)
        chosen = routes[micro_index]
        pick_table = (chosen[:, :, None] == expert_ids).astype(jnp.float32)
        picked = jnp.sum(pick_table * logits[:, None, :], axis=-1)
        gate_weights = jax.nn.softmax(picked, axis=-1)
        flat_routes = chosen.reshape(-1)
        expert_hits = (flat_routes[:, None] == expert_ids).astype(jnp.int32)
        expert_rank = (
            jnp.sum(
                jnp.cumsum(expert_hits, axis=0, dtype=jnp.int32) * expert_hits,
                axis=1,
                dtype=jnp.int32,
            )
            - 1
        )
        slot_index = (
            flat_routes // local_experts * (capacity * local_experts)
            + expert_rank * local_experts
            + flat_routes % local_experts
        )
        slot_owner = (
            jnp.full((slot_count,), 2 * tok_rows, jnp.int32)
            .at[slot_index]
            .set(jnp.arange(2 * tok_rows, dtype=jnp.int32))
        )
        padded = jnp.concatenate([normed, jnp.zeros((1, model_width), jnp.bfloat16)], axis=0)
        outgoing = padded[slot_owner // 2].reshape(
            expert_ranks, capacity, local_experts, model_width
        )
        received = lax.all_to_all(
            outgoing, "expert", split_axis=0, concat_axis=0, tiled=True
        ).reshape(recv_rows, local_experts, model_width)
        pre_act = jnp.einsum(
            "red,edf->ref", received, expert_in, preferred_element_type=jnp.float32
        )
        activation = jax.nn.gelu(pre_act).astype(jnp.bfloat16)
        expert_result = jnp.einsum(
            "ref,efd->red", activation, expert_out, preferred_element_type=jnp.float32
        )
        result_low = expert_result.astype(jnp.bfloat16).reshape(
            expert_ranks, capacity, local_experts, model_width
        )
        returned = lax.all_to_all(
            result_low, "expert", split_axis=0, concat_axis=0, tiled=True
        ).reshape(slot_count, model_width)
        picked_rows = returned[slot_index].astype(jnp.float32).reshape(tok_rows, 2, model_width)
        output_rows = middle + jnp.sum(gate_weights[:, :, None] * picked_rows, axis=1)
        mixed_parts.append(output_rows.astype(jnp.bfloat16))
        grad_output = cotangent[micro_index].astype(jnp.float32)
        grad_gate = jnp.sum(grad_output[:, None, :] * picked_rows, axis=-1)
        grad_pick = gate_weights * (
            grad_gate - jnp.sum(gate_weights * grad_gate, axis=-1, keepdims=True)
        )
        grad_logits = jnp.sum(pick_table * grad_pick[:, :, None], axis=1).astype(jnp.bfloat16)
        sum_router = sum_router + matmul_left(normed, grad_logits)
        grad_normed = matmul_right(grad_logits, full_router)
        branch_grad = (gate_weights[:, :, None] * grad_output[:, None, :]).reshape(
            2 * tok_rows, model_width
        )
        padded_grad = jnp.concatenate(
            [branch_grad, jnp.zeros((1, model_width), jnp.float32)], axis=0
        )
        grad_send = (
            padded_grad[slot_owner]
            .astype(jnp.bfloat16)
            .reshape(expert_ranks, capacity, local_experts, model_width)
        )
        grad_recv = lax.all_to_all(
            grad_send, "expert", split_axis=0, concat_axis=0, tiled=True
        ).reshape(recv_rows, local_experts, model_width)
        grad_act = jnp.einsum(
            "red,efd->ref", grad_recv, expert_out, preferred_element_type=jnp.float32
        )
        sum_expert_out = sum_expert_out + jnp.einsum(
            "ref,red->efd", activation, grad_recv, preferred_element_type=jnp.float32
        )
        _, gelu_pull = jax.vjp(jax.nn.gelu, pre_act)
        grad_pre = gelu_pull(grad_act)[0].astype(jnp.bfloat16)
        sum_expert_in = sum_expert_in + jnp.einsum(
            "red,ref->edf", received, grad_pre, preferred_element_type=jnp.float32
        )
        grad_in_rows = jnp.einsum(
            "ref,edf->red", grad_pre, expert_in, preferred_element_type=jnp.float32
        )
        grad_in_low = grad_in_rows.astype(jnp.bfloat16).reshape(
            expert_ranks, capacity, local_experts, model_width
        )
        grad_back = lax.all_to_all(
            grad_in_low, "expert", split_axis=0, concat_axis=0, tiled=True
        ).reshape(slot_count, model_width)
        grad_normed = grad_normed + jnp.sum(
            grad_back[slot_index].astype(jnp.float32).reshape(tok_rows, 2, model_width), axis=1
        )
        _, norm_pull = jax.vjp(rms_norm, middle, gain_second)
        grad_middle, grad_gain_second = norm_pull(grad_normed)
        grad_middle = grad_middle + grad_output
        sum_gain_two = sum_gain_two + grad_gain_second
        grad_attn = grad_middle.astype(jnp.bfloat16)
        sum_output = sum_output + matmul_left(context_low, grad_attn)
        grad_context = (
            matmul_right(grad_attn, full_output)
            .astype(jnp.bfloat16)
            .reshape(tok_rows, head_count, head_size)
        )
        row_delta = jnp.einsum("qhd,qhd->hq", grad_context.astype(jnp.float32), context)

        def attend_back(state_pair, block_item):
            grad_query_sum, grad_table_sum = state_pair
            key_piece, value_piece, bias_piece, bucket_piece = block_item
            probs = jnp.exp(score_piece(key_piece, bias_piece) - log_total[:, :, None])
            grad_probs = jnp.einsum(
                "qhd,khd->hqk", grad_context, value_piece, preferred_element_type=jnp.float32
            )
            grad_scores = probs * (grad_probs - row_delta[:, :, None])
            bucket_hits = (bucket_piece[:, :, None] == bucket_ids).astype(jnp.float32)
            grad_table_sum = grad_table_sum + jnp.einsum(
                "hqk,qkb->hb", grad_scores, bucket_hits, precision=HIGHEST
            )
            grad_raw = (grad_scores * score_scale).astype(jnp.bfloat16)
            grad_query_sum = grad_query_sum + jnp.einsum(
                "hqk,khd->qhd", grad_raw, key_piece, preferred_element_type=jnp.float32
            )
            grad_key_piece = jnp.einsum(
                "hqk,qhd->khd", grad_raw, query_heads, preferred_element_type=jnp.float32
            )
            grad_value_piece = jnp.einsum(
                "hqk,qhd->khd",
                probs.astype(jnp.bfloat16),
                grad_context,
                preferred_element_type=jnp.float32,
            )
            return ((grad_query_sum, grad_table_sum), (grad_key_piece, grad_value_piece))

        back_start = (
            jnp.zeros((tok_rows, head_count, head_size), jnp.float32),
            jnp.zeros((head_count, bucket_count), jnp.float32),
        )
        (grad_query_all, grad_table_all), (grad_key_blocks, grad_value_blocks) = lax.scan(
            attend_back, back_start, (key_blocks, value_blocks, bias_blocks, bucket_blocks)
        )
        sum_table = sum_table + grad_table_all
        key_grad_rows = grad_key_blocks.reshape(key_total, model_width)
        value_grad_rows = grad_value_blocks.reshape(key_total, model_width)
        own_key_grad, own_value_grad = (
            lax.psum_scatter(
                key_grad_rows.astype(jnp.bfloat16), "shard", scatter_dimension=0, tiled=True
            ).astype(jnp.float32),
            lax.psum_scatter(
                value_grad_rows.astype(jnp.bfloat16), "shard", scatter_dimension=0, tiled=True
            ).astype(jnp.float32),
        )
        grad_query_low = grad_query_all.reshape(tok_rows, model_width).astype(jnp.bfloat16)
        grad_key_low = own_key_grad.astype(jnp.bfloat16)
        grad_value_low = own_value_grad.astype(jnp.bfloat16)
        sum_query = sum_query + matmul_left(hidden, grad_query_low)
        sum_key = sum_key + matmul_left(hidden, grad_key_low)
        sum_value = sum_value + matmul_left(hidden, grad_value_low)
        grad_hidden = (
            matmul_right(grad_query_low, full_query)
            + matmul_right(grad_key_low, full_key)
            + matmul_right(grad_value_low, full_value)
        )
        _, first_pull = jax.vjp(rms_norm, inputs, gain_first)
        grad_inputs, grad_gain_first = first_pull(grad_hidden)
        sum_gain_one = sum_gain_one + grad_gain_first
        grad_parts.append(grad_inputs + grad_middle)
    shares = (
        lax.psum_scatter(
            sum_query.astype(jnp.bfloat16), "shard", scatter_dimension=0, tiled=True
        ).astype(jnp.float32),
        lax.psum_scatter(
            sum_key.astype(jnp.bfloat16), "shard", scatter_dimension=0, tiled=True
        ).astype(jnp.float32),
        lax.psum_scatter(
            sum_value.astype(jnp.bfloat16), "shard", scatter_dimension=0, tiled=True
        ).astype(jnp.float32),
        lax.psum_scatter(
            sum_output.astype(jnp.bfloat16), "shard", scatter_dimension=0, tiled=True
        ).astype(jnp.float32),
        lax.psum_scatter(
            sum_router.astype(jnp.bfloat16), "shard", scatter_dimension=0, tiled=True
        ).astype(jnp.float32),
        lax.psum_scatter(
            sum_gain_one.astype(jnp.bfloat16), "shard", scatter_dimension=0, tiled=True
        ).astype(jnp.float32),
        lax.psum_scatter(
            sum_gain_two.astype(jnp.bfloat16), "shard", scatter_dimension=0, tiled=True
        ).astype(jnp.float32),
        lax.psum_scatter(
            sum_table.reshape(-1).astype(jnp.bfloat16), "shard", scatter_dimension=0, tiled=True
        ).astype(jnp.float32),
    )
    own_grads = (
        lax.psum(shares[0].astype(jnp.bfloat16), "expert").astype(jnp.float32),
        lax.psum(shares[1].astype(jnp.bfloat16), "expert").astype(jnp.float32),
        lax.psum(shares[2].astype(jnp.bfloat16), "expert").astype(jnp.float32),
        lax.psum(shares[3].astype(jnp.bfloat16), "expert").astype(jnp.float32),
        lax.psum(shares[4].astype(jnp.bfloat16), "expert").astype(jnp.float32),
        lax.psum(shares[5].astype(jnp.bfloat16), "expert").astype(jnp.float32),
        lax.psum(shares[6].astype(jnp.bfloat16), "expert").astype(jnp.float32),
        lax.psum(shares[7].astype(jnp.bfloat16), "expert").astype(jnp.float32),
    )
    grad_expert_in, grad_expert_out = (
        lax.psum_scatter(
            sum_expert_in.astype(jnp.bfloat16), "shard", scatter_dimension=2, tiled=True
        ).astype(jnp.float32),
        lax.psum_scatter(
            sum_expert_out.astype(jnp.bfloat16), "shard", scatter_dimension=1, tiled=True
        ).astype(jnp.float32),
    )
    return (
        jnp.stack(mixed_parts),
        jnp.stack(grad_parts),
        own_grads[0],
        own_grads[1],
        own_grads[2],
        own_grads[3],
        own_grads[4],
        own_grads[5],
        own_grads[6],
        own_grads[7],
        grad_expert_in,
        grad_expert_out,
    )


def solution(mesh):
    in_specs = (
        P(None, ("expert", "shard"), None),
        P(None, ("expert", "shard"), None),
        P(None, ("expert", "shard"), None),
        P(None, "expert", None),
        P("shard", None),
        P("shard", None),
        P("shard", None),
        P("shard", None),
        P("shard", None),
        P("shard"),
        P("shard"),
        P("shard"),
        P("expert", None, "shard"),
        P("expert", "shard", None),
    )
    out_specs = (
        P(None, ("expert", "shard"), None),
        P(None, ("expert", "shard"), None),
        P("shard", None),
        P("shard", None),
        P("shard", None),
        P("shard", None),
        P("shard", None),
        P("shard"),
        P("shard"),
        P("shard"),
        P("expert", None, "shard"),
        P("expert", "shard", None),
    )
    ne, ns = mesh.shape["expert"], mesh.shape["shard"]

    def device(*args):
        tokens, w_router, w_in = args[0], args[8], args[12]
        z = Sizes(
            ne, ns, tokens.shape[0], tokens.shape[1], tokens.shape[2], w_router.shape[1], w_in.shape[0], w_in.shape[2]
        )
        return fused_device(z, *args) if z.fits() else per_device(*args)

    return jax.shard_map(
        device, mesh=mesh, in_specs=in_specs, out_specs=out_specs, check_vma=False
    )
```

```python
import functools
from functools import reduce
import math

import jax
import jax.numpy as jnp
import numpy as np
from jax import lax
from jax.experimental import pallas as pl
from jax.experimental.pallas import tpu as pltpu
from jax.sharding import PartitionSpec as P

HEADS = 12
BUCKETS = 32
EPS = 1e-06
MASKED = -1e30
BUCKET_EDGES = (24, 32, 48, 64, 96, 128, 192, 256, 384, 512, 768, 1024, 1536, 2048, 3072)
MESH = pl.DeviceIdType.MESH
BF = jnp.bfloat16
F32 = jnp.float32
I32 = jnp.int32
LANES = 128


class Sizes:
    def __init__(self, ne, ns, micro, rows, width, experts, local_experts, ff):
        self.ne, self.ns, self.ny = ne, ns, ns // 2
        self.m, self.t, self.d = micro, rows, width
        self.e, self.el, self.ff = experts, local_experts, ff
        self.g = ns * rows
        self.mt = micro * rows
        self.r = width // ns
        self.cap = (9 * rows + 4 * experts - 1) // (4 * experts)
        self.per = micro * self.cap
        self.sp = -(-(local_experts * self.per + 2) // 16) * 16
        self.slots = ne * self.sp
        self.nz = ne // 2
        self.hn = ne // 2
        self.cr = self.hn * self.per
        self.cb = local_experts * self.cr
        self.blk = 2 * self.cb
        self.hs = self.hn * self.sp
        self.n16 = -(-ne // 16) * 16
        self.pairs = HEADS // 2
        self.small = experts + 16
        self.far = self.g // 2 + rows

    def fits(self):
        return (
            self.ns % 2 == 0
            and self.t == LANES
            and self.d == HEADS * 64
            and self.cr % 16 == 0
            and self.nz == 4
            and self.e % 16 == 0
            and self.r % (16 * self.nz) == 0
            and self.slots % LANES == 0
            and self.el * self.per <= LANES
            and self.d == self.ff
            and self.ns >= 2 * self.m
            and self.blk >= self.g
            and self.d % 256 == 0
        )


def layout_constants(z):
    perm = np.zeros((z.cb, z.hs), np.float32)
    rows_of = np.zeros((2 * z.n16, z.slots), np.float32)
    dest = np.zeros((2 * z.n16, z.slots), np.float32)
    place = np.zeros((z.slots, LANES), np.float32)
    gate_of = np.zeros((2 * z.n16, z.hs), np.float32)
    source = np.zeros((z.cb, 2 * z.n16), np.float32)
    pick = np.zeros((z.cb, LANES), np.float32)
    used = z.el * z.per
    for src in range(z.ne):
        rows_of[src, src * z.sp + used] = 1
        rows_of[z.n16 + src, src * z.sp + used + 1] = 1
        dest[src, src * z.sp : (src + 1) * z.sp] = 1
        dest[z.n16 + src, src * z.sp : (src + 1) * z.sp] = 1
        for q in range(used):
            place[src * z.sp + q, q] = 1
    for src in range(z.hn):
        gate_of[src, src * z.sp + used] = 1
        gate_of[z.n16 + src, src * z.sp + used + 1] = 1
        for q in range(used):
            row = (q // z.per) * z.cr + src * z.per + q % z.per
            perm[row, src * z.sp + q] = 1
            source[row, src] = 1
            source[row, z.n16 + src] = 1
            pick[row, q] = 1
    return [jnp.asarray(a, BF) for a in (perm, rows_of, dest, place, gate_of, source, pick)]


def dot(a, b):
    return jnp.dot(a, b, preferred_element_type=F32)


def dot_t(a, b):
    return lax.dot_general(a, b, (((1,), (1,)), ((), ())), preferred_element_type=F32)


def tdot(a, b):
    return lax.dot_general(a, b, (((0,), (0,)), ((), ())), preferred_element_type=F32)


def iota(shape, dim):
    return lax.broadcasted_iota(I32, shape, dim)


def aligned(start, size, multiple):
    return pl.ds(pl.multiple_of(start, multiple), size)


def offsets(z, chunk=None):
    every = [(kz, kx) for kz in range(z.nz) for kx in range(2)][1:]
    return [k for k in every if chunk is None or k[0] % 2 == chunk]


def position(z, k):
    return (k[0] % 2) * z.hn + (k[0] // 2) * 2 + k[1]


class Place:
    def __init__(self, z):
        self.z = z
        self.e = lax.axis_index("expert")
        self.s = lax.axis_index("shard")
        self.y, self.c = lax.div(self.s, 2), lax.rem(self.s, 2)

    def shard(self, k, other):
        y = lax.rem(self.y + k, self.z.ny)
        return y * 2 + (1 - self.c if other else self.c)

    def expert(self, kz, kx):
        high = lax.rem(lax.div(self.e, 2) + kz, self.z.nz)
        return high * 2 + lax.rem(lax.rem(self.e, 2) + kx, 2)

    def barrier(self, with_experts=True):
        sem = pltpu.get_barrier_semaphore()
        others = [(self.e, self.shard(0, True))]
        others += [(self.e, self.shard(k, False)) for k in range(1, self.z.ny)]
        if with_experts:
            others += [(self.expert(*k), self.s) for k in offsets(self.z)]
        for other in others:
            pl.semaphore_signal(sem, inc=1, device_id=other, device_id_type=MESH)
        pl.semaphore_wait(sem, len(others))


def rcopy(src, dst, send, recv, to):
    return pltpu.make_async_remote_copy(
        src_ref=src, dst_ref=dst, send_sem=send, recv_sem=recv, device_id=to, device_id_type=MESH
    )


class Gather:
    def __init__(self, place, own, full, send, recv, item):
        self.p, self.own, self.full = place, own, full
        self.send, self.recv, self.item = send, recv, item

    def copy(self, origin, src, slot, to):
        return rcopy(src, self.full(origin), self.send.at[self.item, slot], self.recv.at[self.item, slot], to)

    def partner(self):
        return (self.p.e, self.p.shard(0, True))

    def start(self):
        p, ny = self.p, self.p.z.ny
        for k in range(1, ny):
            self.copy(p.s, self.own, k, (p.e, p.shard(k, False))).start()
        self.copy(p.s, self.own, 0, self.partner()).start()

    def forward(self):
        p, ny = self.p, self.p.z.ny
        for k in range(1, ny):
            origin = p.shard(k, False)
            self.copy(origin, self.full(origin), ny - k, self.partner()).wait_recv()
            self.copy(origin, self.full(origin), ny + k - 1, self.partner()).start()

    def arrive(self):
        p, ny = self.p, self.p.z.ny
        for k in range(ny):
            origin = p.shard(k, True)
            self.copy(origin, self.full(origin), ny + k - 1 if k else 0, self.partner()).wait_recv()

    def finish(self):
        p, ny = self.p, self.p.z.ny
        for slot in range(2 * ny - 1):
            self.copy(p.s, self.own, slot, self.partner()).wait_send()


class Exchange:
    def __init__(self, place, src, dst, send, recv, item):
        self.p, self.src, self.dst = place, src, dst
        self.send, self.recv, self.item = send, recv, item

    def copy(self, k):
        z = self.p.z
        back = (-k[0] % z.nz, k[1])
        at = position(z, back)
        to = self.p.expert(*k)
        return rcopy(
            self.src(to),
            self.dst(at),
            self.send.at[self.item, position(z, k) - 1],
            self.recv.at[self.item, at - 1],
            (to, self.p.s),
        )

    def start(self, some=None):
        for k in filter(some, offsets(self.p.z)):
            self.copy(k).start()

    def arrive(self, some=None):
        z = self.p.z
        for k in filter(some, offsets(z)):
            self.copy((-k[0] % z.nz, k[1])).wait_recv()

    def finish(self, some=None):
        for k in filter(some, offsets(self.p.z)):
            self.copy(k).wait_send()


def slot_ids(z, route0, route1):
    lane = iota((z.t, LANES), 1)
    lower = (iota((z.t, z.t), 0) > iota((z.t, z.t), 1)).astype(F32).astype(BF)
    base = lane * z.per
    for d in range(1, z.ne):
        base = base + jnp.where(lane >= d * z.el, z.sp - z.el * z.per, 0)
    firsts, seconds = [], []
    for m in range(z.m):
        rows = slice(m * z.t, (m + 1) * z.t)
        hit0, hit1 = lane == route0[rows], lane == route1[rows]
        hits = jnp.where(hit0 | hit1, 1.0, 0.0).astype(BF)
        spot = dot(lower, hits) + (base + m * z.cap).astype(F32)
        firsts.append(jnp.sum(jnp.where(hit0, spot, 0.0), axis=1, keepdims=True))
        seconds.append(jnp.sum(jnp.where(hit1, spot, 0.0), axis=1, keepdims=True))
    return jnp.concatenate(firsts, 0), jnp.concatenate(seconds, 0)


def one_hot(z, slot):
    return (iota((z.mt, z.slots), 1) == slot.astype(I32)).astype(F32)


def key_layout(z, counts, m, shape, dim):
    row = iota(shape, dim)
    total = counts[m, 0]
    for b in range(1, z.ns):
        total = total + counts[m, b]
    position = jnp.zeros(shape, I32)
    prompt = jnp.zeros(shape, I32)
    offset = 0
    for b in range(z.ns):
        own = counts[m, b]
        local = row - b * z.t
        inside = (local >= 0) & (local < z.t)
        first = local < own
        position = jnp.where(inside, jnp.where(first, offset + local, total + local - own), position)
        prompt = jnp.where(inside & first, 1, prompt)
        offset = offset + own
    return position, prompt


def query_position(z, counts, m, s):
    total, offset, own = 0, 0, 0
    for b in range(z.ns):
        count = counts[m, b]
        total = total + count
        offset = offset + jnp.where(b < s, count, 0)
        own = own + jnp.where(b == s, count, 0)
    local = iota((z.t, 1), 0)
    return jnp.where(local < own, offset + local, total + local - own)


def bucket_of(z, distance):
    coarse = jnp.full(distance.shape, 16, I32)
    for edge in BUCKET_EDGES:
        if edge < z.far:
            coarse = coarse + jnp.where(distance >= edge, 1, 0)
    return jnp.where(distance < 16, distance, coarse)


VMEM = pl.BlockSpec(memory_space=pltpu.VMEM)
SMEM = pl.BlockSpec(memory_space=pltpu.SMEM)


GELU_A = math.sqrt(2.0 / math.pi)
GELU_B = 0.044715


class SharedGather:
    def __init__(self, place, own, full, send, recv, item):
        self.p, self.own, self.full = place, own, full
        self.send, self.recv, self.item = send, recv, item
        self.x = lax.rem(place.e, 2)

    def half(self, ref, x):
        n = ref.shape[1] // 2
        return ref.at[:, aligned(x * n, n, LANES)]

    def copy(self, src, dst, slot, arrival, to):
        return rcopy(src, dst, self.send.at[self.item, slot], self.recv.at[self.item, arrival], to)

    def partner(self):
        return (self.p.e, self.p.shard(0, True))

    def own_copy(self, origin):
        return self.copy(self.own, self.full(origin), 0, 0, self.partner())

    def y_copy(self, k, origin, arrival=None):
        return self.copy(
            self.half(self.own, self.x), self.half(self.full(origin), self.x), k, k if arrival is None else arrival,
            (self.p.e, self.p.shard(k, False)),
        )

    def on_copy(self, k, kind, origin, x, to):
        block = self.half(self.full(origin), x)
        slot = self.p.z.ny + 3 * (k - 1) + kind
        return self.copy(block, block, slot, slot, to)

    def start(self):
        p = self.p
        for k in range(1, p.z.ny):
            self.y_copy(k, p.s).start()
        self.own_copy(p.s).start()

    def forward(self):
        p = self.p
        for k in range(1, p.z.ny):
            origin = p.shard(k, False)
            self.y_copy(k, origin, self.p.z.ny - k).wait_recv()
            self.on_copy(k, 0, origin, self.x, (p.expert(0, 1), p.s)).start()
            self.on_copy(k, 1, origin, self.x, self.partner()).start()

    def forward_rest(self):
        p = self.p
        for k in range(1, p.z.ny):
            origin = p.shard(k, False)
            self.on_copy(k, 0, origin, 1 - self.x, (p.expert(0, 1), p.s)).wait_recv()
            self.on_copy(k, 2, origin, 1 - self.x, self.partner()).start()

    def arrive(self):
        p = self.p
        self.own_copy(p.shard(0, True)).wait_recv()
        for k in range(1, p.z.ny):
            origin = p.shard(k, True)
            self.on_copy(k, 1, origin, self.x, self.partner()).wait_recv()
            self.on_copy(k, 2, origin, 1 - self.x, self.partner()).wait_recv()

    def finish(self):
        p = self.p
        self.own_copy(p.s).wait_send()
        for k in range(1, p.z.ny):
            self.y_copy(k, p.s).wait_send()
            for kind in range(3):
                self.on_copy(k, kind, p.s, 0, self.partner()).wait_send()


class Scatter:
    def __init__(self, place, mine, other, from_core, to_y, from_y, psend, precv, ysend, yrecv):
        self.p, self.mine, self.other, self.from_core = place, mine, other, from_core
        self.to_y, self.from_y = to_y, from_y
        self.psend, self.precv, self.ysend, self.yrecv = psend, precv, ysend, yrecv

    def core_copy(self):
        p = self.p
        return rcopy(self.other, self.from_core, self.psend, self.precv, (p.e, p.shard(0, True)))

    def y_copy(self, k):
        p = self.p
        return rcopy(
            self.to_y.at[k - 1], self.from_y.at[k - 1], self.ysend.at[k - 1], self.yrecv.at[k - 1],
            (p.e, p.shard(k, False)),
        )

    def send(self):
        self.core_copy().start()

    def middle(self):
        p = self.p
        self.core_copy().wait_recv()
        for k in range(1, p.z.ny):
            yy = lax.rem(p.y + k, p.z.ny)
            both = self.mine[yy].astype(F32) + self.from_core[yy].astype(F32)
            self.to_y[k - 1] = both.astype(BF)
            self.y_copy(k).start()

    def total(self):
        p = self.p
        out = self.mine[p.y].astype(F32) + self.from_core[p.y].astype(F32)
        for k in range(1, p.z.ny):
            self.y_copy(k).wait_recv()
            out = out + self.from_y[k - 1].astype(F32)
        return out

    def finish(self):
        self.core_copy().wait_send()
        for k in range(1, self.p.z.ny):
            self.y_copy(k).wait_send()


class Return:
    def __init__(self, place, rows, ret, chunk, cols, send, recv):
        self.p, self.rows, self.ret, self.chunk, self.cols = place, rows, ret, chunk, cols
        self.sems = send, recv

    def copy(self, k, at, away):
        z = self.p.z
        first = self.chunk * z.hn
        return rcopy(
            self.rows.at[pl.ds((position(z, k) - first) * z.sp, z.sp)],
            self.ret.at[aligned(at * z.sp, z.sp, 16), self.cols],
            self.sems[0].at[position(z, k) - first],
            self.sems[1].at[position(z, away) - first],
            (self.p.expert(*k), self.p.s),
        )

    def start_remote(self):
        z = self.p.z
        for k in offsets(z, self.chunk):
            self.copy(k, self.p.e, (-k[0] % z.nz, k[1])).start()

    def arrive(self):
        for k in offsets(self.p.z, self.chunk):
            self.copy(k, self.p.expert(*k), k).wait_recv()

    def finish(self):
        z = self.p.z
        for k in offsets(z, self.chunk):
            self.copy(k, self.p.e, (-k[0] % z.nz, k[1])).wait_send()


def column_of(row):
    n = row.shape[1]
    return jnp.sum(jnp.where(iota((n, n), 0) == iota((n, n), 1), row, 0.0), axis=1, keepdims=True)


def route_columns(z, routes):
    out = []
    for j in range(2):
        parts = [column_of(routes[m, j : j + 1, :].astype(F32)) for m in range(z.m)]
        out.append(jnp.concatenate(parts, 0).astype(I32))
    return out


def spread(z, s, n):
    row, lane = iota((z.r, z.d), 0), iota((z.r, z.d), 1)
    return jnp.where((lane - s * n == row) & (row < n), 1.0, 0.0).astype(BF)


def split_high(x):
    high = x.astype(BF)
    return high, (x - high.astype(F32)).astype(BF)


def forward_kernel(
    z,
    tokens, dy, routes, counts, wk, wv, wq, wo, wr, vecs, w_in_hbm, w_out_hbm,
    perm, rows_of, dest, place_m, gate_of, source, pick,
    o_toks, o_hid, o_kk, o_vv, o_qq, o_pp, o_ctx, o_mid, o_nrm, o_sd, o_fk, o_fv, o_fq, o_fo, o_small,
    o_ret, o_rfin, o_rpart, ggrows, din, dout,
    qq, pp, ctx, mid, nrm, sd, fk, fv, fq, fo, small, smallg,
    xs, dyr, xr, dyg, xg, act, gp, w_in, w_out, table, bias_id, gwg, gwc, ggc,
    part, rp, ys, yr, fin, rpart, rrp, rys, ryr, wstage, gpart, grp, gys, gyr, gout, gret,
    csem, ssem, gsend, grecv, wsend, wrecv, xsend, xrecv, psend, precv, ysend, yrecv, rsend, rrecv, gsem, gsy, gsx,
):
    p = Place(z)
    mt, t, d, r, ff = z.mt, z.t, z.d, z.r, z.ff
    half = d // 2
    tiles = ff // 256
    load_in = pltpu.make_async_copy(w_in_hbm, w_in, csem.at[0])
    load_out = pltpu.make_async_copy(w_out_hbm, w_out, csem.at[1])
    spills, waiting = [], {}

    def spill(src, dst, before=None):
        copy = pltpu.make_async_copy(src, dst, ssem.at[len(spills)])
        copy.start()
        spills.append(copy)
        waiting.setdefault(before, []).append(copy)

    toks, hid = gp.at[pl.ds(0, z.m), pl.ds(0, z.g)], gp.at[pl.ds(z.m, z.m), pl.ds(0, z.g)]
    kk, vv = act.at[pl.ds(0, z.m), pl.ds(0, z.g)], act.at[pl.ds(z.m, z.m), pl.ds(0, z.g)]

    whole = spread(z, p.s, r)
    line = iota((16, d), 0)
    n_bias = HEADS * BUCKETS // z.ns
    row = vecs[...].astype(F32)
    first = jnp.broadcast_to(row[:, 0:r], (16, r))
    gains = jnp.where(iota((16, r), 0) == 0, first, jnp.broadcast_to(row[:, r : 2 * r], (16, r)))
    biases = jnp.broadcast_to(row[:, 2 * r : 2 * r + n_bias], (16, n_bias))
    tail = dot(gains.astype(BF), whole)
    bias_row = dot(biases.astype(BF), spread(z, p.s, n_bias)[0:n_bias, :])
    tail = jnp.where(line < 2, tail, jnp.where(line == 2, bias_row, 0.0))
    small[0 : z.e, :] = dot(wr[...], whole).astype(BF)
    small[z.e : z.small, :] = tail.astype(BF)
    p.barrier()

    def rows(ref, size):
        return lambda origin: ref.at[aligned(origin * size, size, 16)]

    g_small = Gather(p, small, lambda o: smallg.at[o], gsend, grecv, 0)
    g_tok = [
        Gather(p, tokens.at[m], lambda o, m=m: toks.at[m, aligned(o * t, t, 16)], gsend, grecv, 1 + m)
        for m in range(z.m)
    ]
    base = 1 + z.m
    groups = d // 256

    def columns_item(own, full, g, item):
        cols = pl.ds(g * 256, 256)
        return SharedGather(
            p, own.at[:, cols], lambda o: full.at[aligned(o * r, r, 16), cols], wsend, wrecv, item
        )

    g_w = [
        [columns_item(own, full, g, 3 * g + i) for i, (own, full) in enumerate(((wk, fk), (wv, fv), (wq, fq)))]
        for g in range(groups)
    ]
    g_o = SharedGather(p, wo, rows(fo, r), wsend, wrecv, 3 * groups)
    for item in [g_small, g_tok[0]] + g_w[0] + g_tok[1:] + sum(g_w[1:], []) + [g_o]:
        item.start()
    load_out.start()
    load_in.start()
    g_dy = Gather(p, dyg.at[p.s], lambda o: dyg.at[o], gsend, grecv, base)

    def exchange(dst, item):
        return Exchange(
            p,
            lambda to: xs.at[aligned(to * z.sp, z.sp, 16)],
            lambda at: dst.at[pl.ds(at * z.sp, z.sp)],
            xsend,
            xrecv,
            item,
        )

    x_dy, x_move = exchange(dyr, 0), exchange(xr, 1)
    smallg[p.s] = small[...]
    for m in range(z.m):
        toks[m, aligned(p.s * t, t, 16), :] = tokens[m]
    own_weights = []
    for i, (own, full) in enumerate(((wk, fk), (wv, fv), (wq, fq), (wo, fo))):
        own_weights.append(pltpu.make_async_copy(own, full.at[aligned(p.s * r, r, 16)], csem.at[6 + i]))
        own_weights[i].start()

    route0, route1 = route_columns(z, routes)
    slot0, slot1 = slot_ids(z, route0, route1)
    hot = (one_hot(z, slot0) + one_hot(z, slot1)).astype(BF)
    mine = aligned(p.e * z.sp, z.sp, 16)

    def to_slots(ref):
        def step(i, carry):
            cols = aligned(i * 256, 256, 256)
            xs[:, cols] = tdot(hot, ref[:, cols]).astype(BF)
            return carry

        lax.fori_loop(0, d // 256, step, 0)

    across, along = lambda k: k[1] == 1, lambda k: k[1] == 0
    even, odd = lambda k: k[0] % 2 == 0, lambda k: k[0] % 2 == 1
    to_slots(dy)
    x_dy.start(across)
    dyr[0 : z.sp, :] = xs[mine, :]

    for m in range(z.m):
        key_pos, prompt = key_layout(z, counts, m, (1, z.g), 1)
        distance = query_position(z, counts, m, p.s) - key_pos
        lane = iota((1, z.g), 1)
        own_block = (lane >= p.s * t) & (lane < (p.s + 1) * t)
        visible = (distance >= 0) & (own_block | (prompt == 1))
        bias_id[m] = jnp.where(visible, bucket_of(z, distance), 2 * BUCKETS)

    for item in (g_small, g_tok[0]):
        item.forward()
    for item in (g_small, g_tok[0]):
        item.arrive()
    x_dy.start(along)
    spill(smallg, o_small)
    sums = smallg[0].astype(F32)
    for b in range(1, z.ns):
        sums = sums + smallg[b].astype(F32)
    gain_one = sums[z.e : z.e + 1, :]
    gain_two = sums[z.e + 1 : z.e + 2, :]
    router = sums.astype(BF)
    for pair in range(z.pairs):
        lanes = slice(pair // 2 * LANES, (pair // 2 + 1) * LANES)
        row = sums[z.e + 2 : z.e + 3, lanes]
        if pair % 2:
            row = pltpu.roll(row, 2 * BUCKETS, 1)
        table[pair : pair + 1, :] = jnp.where(iota((1, LANES), 1) < 2 * BUCKETS, row, MASKED)

    def normalize(m):
        def step(i, carry):
            at = aligned(i * t, t, 16)
            x = toks[m, at, :].astype(F32)
            scale = lax.rsqrt(jnp.mean(x * x, axis=1, keepdims=True) + EPS)
            hid[m, at, :] = (x * scale * gain_one).astype(BF)
            return carry

        lax.fori_loop(0, z.ns, step, 0)

    for copy in own_weights:
        copy.wait()

    def project(g, m):
        cols = slice(g * 256, (g + 1) * 256)
        for item, full, out in zip(g_w[g][:2], (fk, fv), (kk, vv)):
            if m == 0:
                item.arrive()
            out[m, :, cols] = dot(hid[m], full[:, cols]).astype(BF)
        if m == 0:
            g_w[g][2].arrive()
        own = hid[m, aligned(p.s * t, t, 16), :]
        qq[m * t : (m + 1) * t, cols] = (dot(own, fq[:, cols]).astype(BF).astype(F32) * 0.125).astype(BF)


    def in_order(src, dst, h):
        def step(i, carry):
            cols = aligned(i * 256, 256, 256)
            moved = dot(perm[...], src[h * z.hs : (h + 1) * z.hs, cols])
            dst[p.s, h * z.cb : (h + 1) * z.cb, cols] = moved.astype(BF)
            return carry

        lax.fori_loop(0, d // 256, step, 0)

    def send_dy_rows():
        x_dy.arrive()
        in_order(dyr, dyg, 0)
        in_order(dyr, dyg, 1)
        g_dy.start()

    low = iota((t, LANES), 1) < 64

    def attend(m, pair):
        spot = m * z.pairs + pair
        cols = aligned(pair * LANES, LANES, LANES)
        q = qq[aligned(m * t, t, 16), cols]
        zero = jnp.zeros_like(q)
        q_two = jnp.concatenate([jnp.where(low, q, zero), jnp.where(low, zero, q)], 0)
        scores = dot_t(q_two, kk[m, :, cols])
        biases = jnp.broadcast_to(table[pl.ds(pair, 1), :], (t, LANES))
        for side in range(2):
            pieces = []
            for b in range(z.ns):
                at = slice(b * LANES, (b + 1) * LANES)
                bias = jnp.take_along_axis(biases, bias_id[m, :, at] + BUCKETS * side, axis=1)
                pieces.append(scores[side * t : (side + 1) * t, at] + bias)
            s = jnp.concatenate(pieces, 1)
            top = jnp.max(s, axis=1, keepdims=True)
            e = jnp.exp(s - top)
            total = jnp.sum(e, axis=1, keepdims=True)
            pp[spot, side * t : (side + 1) * t, :] = (e * (1.0 / total)).astype(BF)
        two = dot(pp[spot], vv[m, :, cols])
        ctx[aligned(m * t, t, 16), cols] = jnp.where(low, two[:t], two[t:]).astype(BF)

    chain = g_w + [[g_o]]

    def attention(g, m):
        def step(i, carry):
            attend(m, g * 2 + i)
            return carry

        lax.fori_loop(0, 2, step, 0, unroll=2)

    for item in chain[0]:
        item.forward()
    normalize(0)
    for item in chain[0]:
        item.forward_rest()
    for item in g_tok[1:]:
        item.forward()
    for g in range(groups):
        for m in range(z.m):
            if g == 0 and m > 0:
                g_tok[m].arrive()
                normalize(m)
                spill(toks, o_toks, "gp")
                spill(hid, o_hid, "gp")
            project(g, m)
            if m == 0 and g > 0 or m == 1 and g == 0:
                for item in chain[g + 1]:
                    item.forward()
            if g == 1 and m == 0:
                send_dy_rows()
            attention(g, m)
            if m == z.m - 1:
                for item in chain[g + 1]:
                    item.forward_rest()
    g_o.arrive()

    def output(i, carry):
        cols = aligned(i * 256, 256, 256)
        mid[:, cols] = dot(ctx[...], fo[:, cols])
        return carry

    lax.fori_loop(0, d // 256, output, 0)
    for m in range(z.m):
        at = slice(m * t, (m + 1) * t)
        x = mid[at, :] + tokens[m].astype(F32)
        mid[at, :] = x
        scale = lax.rsqrt(jnp.mean(x * x, axis=1, keepdims=True) + EPS)
        nrm[at, :] = (x * scale * gain_two).astype(BF)
    logits = dot_t(nrm[...], router)
    lane = iota((mt, z.small), 1)
    pick0 = jnp.sum(jnp.where(lane == route0, logits, 0.0), axis=1, keepdims=True)
    pick1 = jnp.sum(jnp.where(lane == route1, logits, 0.0), axis=1, keepdims=True)
    top = jnp.maximum(pick0, pick1)
    e0, e1 = jnp.exp(pick0 - top), jnp.exp(pick1 - top)
    gate0, gate1 = e0 / (e0 + e1), e1 / (e0 + e1)
    lane = iota((mt, LANES), 1)
    sd[...] = jnp.where(
        lane == 0, slot0, jnp.where(lane == 1, slot1, jnp.where(lane == 2, gate0, jnp.where(lane == 3, gate1, 0.0)))
    )
    gate_row = jnp.sum(one_hot(z, slot0) * gate0 + one_hot(z, slot1) * gate1, axis=0, keepdims=True)
    high = gate_row.astype(BF).astype(F32)
    is_high = iota((2 * z.n16, 1), 0) < z.n16
    gates = (dest[...].astype(F32) * jnp.where(is_high, high, gate_row - high)).astype(BF)
    gates = dot(gates, place_m[...]).astype(BF)
    x_dy.finish()
    to_slots(nrm)
    xs[:, :LANES] = (xs[:, :LANES].astype(F32) + tdot(rows_of[...], gates)).astype(BF)
    x_move.start(even)
    xr[0 : z.sp, :] = xs[mine, :]

    load_out.wait()

    def expert_rows(ref, h, l, cols):
        return ref[:, aligned(h * z.cb + l * z.cr, z.cr, 16), cols].reshape(z.ns * z.cr, -1)

    def gradient(h):
        def step(l, carry):
            g = dot_t(expert_rows(dyg, h, l, slice(None)), w_out[l])
            gp[:, aligned(h * z.cb + l * z.cr, z.cr, 16), :] = g.astype(BF).reshape(z.ns, z.cr, ff)
            return carry

        lax.fori_loop(0, z.el, step, 0)

    def gather_of(h):
        item = base + 1 + (1 + z.el) * h
        out = [Gather(p, gwg.at[p.s, h], lambda o: gwg.at[o, h], gsend, grecv, item)]
        for l in range(z.el):
            at = pl.ds(h * z.cb + l * z.cr, z.cr)
            out.append(Gather(p, xg.at[p.s, at], lambda o, at=at: xg.at[o, at], gsend, grecv, item + 1 + l))
        return out

    gathers = [gather_of(h) for h in range(2)]

    def distribute(h):
        x_move.arrive((even, odd)[h])
        if h == 0:
            x_move.start(odd)
        gwg[p.s, h] = dot(gate_of[...], xr[h * z.hs : (h + 1) * z.hs, :LANES]).astype(BF)
        gathers[h][0].start()
        in_order(xr, xg, h)
        for item in gathers[h][1:]:
            item.start()

    def gates_of(h):
        gathers[h][0].arrive()
        for b in range(z.ns):
            wide = dot(source[...], gwg[b, h]) * pick[...].astype(F32)
            gwc[b] = jnp.sum(wide, axis=1, keepdims=True)

    def activate(h, l):
        at_rows = pl.ds(h * z.cb + l * z.cr, z.cr)
        gate = gwc[:, l * z.cr : (l + 1) * z.cr, :]
        gate_column = gate.reshape(z.ns * z.cr, 1)

        def step(tile, carry):
            at = aligned(tile * 256, 256, 256)
            x = dot(expert_rows(xg, h, l, slice(None)), w_in[l, :, at])
            g = expert_rows(gp, h, l, at).astype(F32)
            x2 = x * x
            th = jnp.tanh(x * (GELU_A + (GELU_A * GELU_B) * x2))
            hx = 0.5 * x
            up = 1.0 + th
            a = hx * up
            act[:, at_rows, at] = a.astype(BF).reshape(z.ns, z.cr, 256)
            slope = 0.5 * up + hx * (1.0 - th * th) * (GELU_A + (3.0 * GELU_A * GELU_B) * x2)
            gp[:, at_rows, at] = (g * gate_column * slope).astype(BF).reshape(z.ns, z.cr, 256)
            toward = jnp.sum(a * g, axis=1, keepdims=True).reshape(z.ns, z.cr, 1)
            ggc[:, at_rows, :] = toward + jnp.where(tile == 0, 0.0, ggc[:, at_rows, :])
            return carry

        lax.fori_loop(0, tiles, step, 0, unroll=tiles)
        dyg[:, at_rows, :] = (dyg[:, at_rows, :].astype(F32) * gate).astype(BF)

    def unit(u):
        h, cols = u // 2, pl.ds((u % 2) * half, half)
        return (
            Scatter(
                p, part.at[u, p.c], part.at[u, 1 - p.c], rp.at[u], ys.at[u], yr.at[u],
                psend.at[u], precv.at[u], ysend.at[u], yrecv.at[u],
            ),
            Return(p, fin.at[u], o_ret, h, cols, rsend.at[u], rrecv.at[u]),
        )

    units = [unit(u) for u in range(4)]
    results = [
        Scatter(
            p, rpart.at[u, p.c], rpart.at[u, 1 - p.c], rrp.at[u], rys.at[u], ryr.at[u],
            psend.at[4 + u], precv.at[4 + u], ysend.at[4 + u], yrecv.at[4 + u],
        )
        for u in range(2)
    ]

    def products(ref, weight, transposed, dst, h, l):
        rows = expert_rows(ref, h, l, slice(None))
        out = (dot_t(rows, weight[l]) if transposed else dot(rows, weight[l])).astype(BF)
        for b in range(z.ns):
            for c in range(2):
                block = out[b * z.cr : (b + 1) * z.cr, c * half : (c + 1) * half]
                dst[2 * h + c, b % 2, b // 2, l * z.cr : (l + 1) * z.cr, :] = block

    def stage_a(h, l):
        products(gp, w_in, True, part, h, l)
        if l == z.el - 1:
            units[2 * h][0].send()
            units[2 * h + 1][0].send()

    def stage_b(u):
        units[u][0].middle()

    def stage_c(u):
        fin[u] = tdot(perm[...], units[u][0].total().astype(BF)).astype(BF)
        units[u][1].start_remote()
        if u < 2:
            mine_there = o_ret.at[mine, pl.ds((u % 2) * half, half)]
            spill(fin.at[u, pl.ds(0, z.sp)], mine_there, "fin")

    g_scatter = Scatter(
        p, gpart.at[p.c], gpart.at[1 - p.c], grp, gys, gyr, gsem.at[0], gsem.at[1], gsy.at[0], gsy.at[1]
    )

    def toward_a():
        for b in range(z.ns):
            for h in range(2):
                col = ggc[b, h * z.cb : (h + 1) * z.cb, :]
                high = col.astype(BF).astype(F32)
                put = pick[...].astype(F32)
                top = tdot(source[...], (high * put).astype(BF))
                rest = tdot(source[...], ((col - high) * put).astype(BF))
                both = jnp.where(iota(top.shape, 0) < z.n16, top, rest)
                gpart[b % 2, b // 2, h * 2 * z.n16 : (h + 1) * 2 * z.n16, :] = both.astype(BF)
        g_scatter.send()

    def toward_copy(k):
        back = (-k[0] % z.nz, k[1])
        return rcopy(
            gout.at[k[0] % 2], gret.at[position(z, back)], gsx.at[0, position(z, k) - 1], gsx.at[1, position(z, back) - 1],
            (p.expert(*k), p.s),
        )

    def toward_c():
        total = g_scatter.total()
        for h in range(2):
            first = total[h * 2 * z.n16 : h * 2 * z.n16 + z.n16]
            value = first + total[h * 2 * z.n16 + z.n16 : (h + 1) * 2 * z.n16]
            high, rest = split_high(value)
            gout[h, 0 : z.n16, :] = high
            gout[h, z.n16 : 2 * z.n16, :] = rest
        for k in offsets(z):
            toward_copy(k).start()
        gret[0] = gout[0]

    def toward_d():
        for k in offsets(z):
            toward_copy((-k[0] % z.nz, k[1])).wait_recv()
        line = iota((2 * z.n16, LANES), 0)
        out = jnp.zeros((2 * z.n16, LANES), F32)
        for k in [(0, 0)] + offsets(z):
            back = (-k[0] % z.nz, k[1])
            at = position(z, back) - (k[0] % 2) * z.hn
            got = gret[position(z, k)].astype(F32)
            rank = p.expert(*k)
            out = jnp.where(line == rank, got[at : at + 1, :], out)
            out = jnp.where(line == z.n16 + rank, got[z.n16 + at : z.n16 + at + 1, :], out)
        ggrows[...] = out.astype(BF)
        for k in offsets(z):
            toward_copy(k).wait_send()

    def both(ref, l, cols):
        return jnp.concatenate([expert_rows(ref, h, l, cols) for h in range(2)], 0)

    stores = []

    def weight_grad(n, left, right, out, l):
        if n >= 2:
            stores[n - 2].wait()

        def step(i, carry):
            at = aligned(i * 256, 256, 256)
            wstage[n % 2, :, at] = tdot(both(left, l, slice(None)), both(right, l, at)).astype(BF)
            return carry

        lax.fori_loop(0, d // 256, step, 0)
        copy = pltpu.make_async_copy(wstage.at[n % 2], out.at[l], csem.at[2 + n])
        copy.start()
        stores.append(copy)

    def result_a(h):
        for l in range(z.el):
            products(act, w_out, False, rpart, h, l)
        for u in (2 * h, 2 * h + 1):
            if h == 0:
                results[u].send()
            else:
                spill(rpart.at[u], o_rpart.at[u - 2])

    def result_c(u):
        units[u][1].finish()
        waiting["fin"][u].wait()
        fin[u] = tdot(perm[...], results[u].total().astype(BF)).astype(BF)
        spill(fin.at[u], o_rfin.at[u])

    spill(kk, o_kk, "act")
    spill(vv, o_vv, "act")
    g_dy.forward()
    g_dy.arrive()
    for copy in waiting["gp"]:
        copy.wait()
    for item in g_tok:
        item.finish()
    gradient(0)
    gradient(1)
    distribute(0)
    load_in.wait()
    for copy in waiting["act"]:
        copy.wait()
    g_dy.finish()
    gathers[0][0].forward()
    gathers[0][1].forward()
    gates_of(0)
    gathers[0][1].arrive()
    activate(0, 0)
    stage_a(0, 0)
    for l in range(1, z.el):
        gathers[0][1 + l].forward()
    distribute(1)
    for l in range(1, z.el):
        gathers[0][1 + l].arrive()
        activate(0, l)
        stage_a(0, l)
    gathers[1][0].forward()
    stage_b(0)
    stage_b(1)
    gathers[1][1].forward()
    gates_of(1)
    result_a(0)
    gathers[1][1].arrive()
    activate(1, 0)
    stage_a(1, 0)
    for l in range(1, z.el):
        gathers[1][1 + l].forward()
        gathers[1][1 + l].arrive()
        activate(1, l)
        stage_a(1, l)
    toward_a()
    stage_b(2)
    stage_b(3)
    g_scatter.middle()
    stage_c(0)
    stage_c(1)
    results[0].middle()
    results[1].middle()
    result_a(1)
    for src, dst in (
        (sd, o_sd), (mid, o_mid), (nrm, o_nrm), (ctx, o_ctx), (fo, o_fo), (qq, o_qq), (pp, o_pp), (fk, o_fk), (fv, o_fv),
        (fq, o_fq),
    ):
        spill(src, dst)
    weight_grad(0, act, dyg, dout, 0)
    stage_c(2)
    weight_grad(1, act, dyg, dout, 1)
    stage_c(3)
    toward_c()
    weight_grad(2, xg, gp, din, 0)
    result_c(0)
    weight_grad(3, xg, gp, din, 1)
    result_c(1)
    toward_d()
    for u in range(4):
        units[u][1].arrive()
    for item in [g_small] + sum(g_w, []) + [g_o] + list(gathers[0]) + list(gathers[1]):
        item.finish()
    x_move.finish()
    g_scatter.finish()
    for u in (2, 3):
        units[u][1].finish()
    for scatter, _ in units:
        scatter.finish()
    for scatter in results:
        scatter.finish()
    for copy in waiting[None] + stores[2:]:
        copy.wait()


ANY = pl.BlockSpec(memory_space=pl.ANY)


def forward(z, *inputs):
    def bf(*shape):
        return jax.ShapeDtypeStruct(shape, BF)

    def f32(*shape):
        return jax.ShapeDtypeStruct(shape, F32)

    def vm(x):
        return pltpu.VMEM(x.shape, x.dtype)

    dma = pltpu.SemaphoreType.DMA
    half, ny, nb = z.d // 2, z.ny, 2 * z.n16
    kept = (
        bf(z.m, z.g, z.d), bf(z.m, z.g, z.d), bf(z.m, z.g, z.d), bf(z.m, z.g, z.d), bf(z.mt, z.d),
        bf(z.m * z.pairs, 2 * z.t, z.g), bf(z.mt, z.d), f32(z.mt, z.d), bf(z.mt, z.d), f32(z.mt, LANES),
        bf(z.d, z.d), bf(z.d, z.d), bf(z.d, z.d), bf(z.d, z.d),
    )
    smallg = bf(z.ns, z.small, z.d)
    ret, rpart, rfin = bf(z.slots, z.d), bf(4, 2, ny, z.cb, half), bf(4, z.hs, half)
    outs = kept + (smallg, ret, bf(2, z.hs, half), bf(2, 2, ny, z.cb, half), bf(nb, LANES), bf(z.el, z.d, z.ff), bf(z.el, z.ff, z.d))
    rows = bf(z.ns, z.blk, z.d)
    scratch = [vm(x) for x in kept[4:]]
    scratch += [vm(bf(z.small, z.d)), vm(smallg)]
    scratch += [vm(ret)] * 3 + [vm(rows)] * 2 + [vm(bf(z.ns, z.blk, z.ff))] * 2
    scratch += [vm(bf(z.el, z.d, z.ff)), vm(bf(z.el, z.ff, z.d))]
    scratch += [pltpu.VMEM((8, LANES), F32), pltpu.VMEM((z.m, z.t, z.g), I32)]
    scratch += [vm(bf(z.ns, 2, nb, LANES)), vm(f32(z.ns, z.cb, 1)), vm(f32(z.ns, z.blk, 1))]
    shares = [vm(rpart), vm(bf(4, ny, z.cb, half)), vm(bf(4, ny - 1, z.cb, half)), vm(bf(4, ny - 1, z.cb, half))]
    scratch += shares + [vm(rfin)] + [vm(rpart), vm(bf(2, ny, z.cb, half)), vm(bf(2, ny - 1, z.cb, half)), vm(bf(2, ny - 1, z.cb, half))]
    scratch += [vm(bf(2, z.d, z.d))]
    scratch += [vm(bf(2, ny, 2 * nb, LANES)), vm(bf(ny, 2 * nb, LANES))]
    scratch += [vm(bf(ny - 1, 2 * nb, LANES))] * 2 + [vm(bf(2, nb, LANES)), vm(bf(z.ne, nb, LANES))]
    n_items, n_weights = 1 + z.m + 3 + 2 * z.el, 3 * (z.d // 256) + 1
    scratch += [dma((10,)), dma((21,)), dma((n_items, 2 * ny - 1)), dma((n_items, 2 * ny - 1))]
    scratch += [dma((n_weights, 4 * ny - 3))] * 2 + [dma((2, z.ne - 1))] * 2
    scratch += [dma((6,))] * 2 + [dma((6, ny - 1))] * 2 + [dma((4, z.hn))] * 2
    scratch += [dma((2,)), dma((2, ny - 1)), dma((2, z.ne - 1))]
    return pl.pallas_call(
        functools.partial(forward_kernel, z),
        out_shape=outs,
        in_specs=[VMEM] * 3 + [SMEM] + [ANY] * 4 + [VMEM] * 2 + [ANY] * 2 + [VMEM] * 7,
        out_specs=[ANY] * 18 + [VMEM] + [ANY] * 2,
        scratch_shapes=scratch,
        compiler_params=pltpu.CompilerParams(
            collective_id=0, has_side_effects=True, vmem_limit_bytes=63 * 2**20
        ),
        name="forward",
    )(*inputs)


class Reduce:
    def __init__(self, place, part, from_core, to_y, from_y, to_x, from_x, summed, near_in, mid, mid_in, done, sems):
        self.p, self.part, self.from_core, self.done, self.sems = place, part, from_core, done, sems
        self.to_y, self.from_y, self.to_x, self.from_x = to_y, from_y, to_x, from_x
        self.summed, self.near_in, self.mid, self.mid_in = summed, near_in, mid, mid_in
        self.rows = done.shape[0] // 4
        self.x, zz = lax.rem(place.e, 2), lax.div(place.e, 2)
        self.side = lax.rem(zz, 2)
        self.near_at = ((zz + 1 - 2 * self.side) * 2 + self.x, place.s)

    def x_rows(self, x):
        return aligned(x * (2 * self.rows), 2 * self.rows, 16)

    def side_rows(self, side):
        return aligned(side * self.rows, self.rows, 16)

    def done_rows(self, side):
        return aligned((self.x * 2 + side) * self.rows, self.rows, 16)

    def hop(self, n, src, dst, to):
        return rcopy(src, dst, self.sems.at[0, n], self.sems.at[1, n], to)

    def copy(self, n, out=True):
        p = self.p
        if n == 0:
            return self.hop(0, self.part.at[1 - p.c], self.from_core, (p.e, p.shard(0, True)))
        if n == 2:
            return self.hop(2, self.to_x, self.from_x, (p.expert(0, 1), p.s))
        if n == 3:
            return self.hop(3, self.summed.at[self.side_rows(1 - self.side)], self.near_in, self.near_at)
        if n == 4:
            return self.hop(4, self.mid, self.mid_in, (p.expert(2, 0), p.s))
        if n == 5:
            block = self.done.at[self.done_rows(self.side if out else 1 - self.side)]
            return self.hop(5, block, block, self.near_at)
        block = self.done.at[self.x_rows(self.x if out else 1 - self.x)]
        return self.hop(6, block, block, (p.expert(0, 1), p.s))

    def copy_y(self, k):
        p = self.p
        return self.hop(6 + k if k > 1 else 1, self.to_y.at[k - 1], self.from_y.at[k - 1], (p.e, p.shard(k, False)))

    def chip(self, y, rows=slice(None)):
        return self.part[self.p.c, y, rows, :].astype(F32) + self.from_core[y, rows, :].astype(F32)

    def step(self, n):
        p, ny = self.p, self.p.z.ny
        if n == 2:
            for k in range(1, ny):
                self.copy_y(k).wait_recv()
        elif n > 0:
            self.copy(n - 1, False).wait_recv()
        if n == 1:
            for k in range(1, ny):
                self.to_y[k - 1] = self.chip(lax.rem(p.y + k, ny)).astype(BF)
                self.copy_y(k).start()
        elif n == 2:
            def whole(x):
                out = self.chip(p.y, self.x_rows(x))
                for k in range(1, ny):
                    out = out + self.from_y[k - 1, self.x_rows(x), :].astype(F32)
                return out.astype(BF)

            self.to_x[...] = whole(1 - self.x)
            self.summed[...] = whole(self.x)
        elif n == 3:
            self.summed[...] = (self.summed[...].astype(F32) + self.from_x[...].astype(F32)).astype(BF)
        elif n == 4:
            own = self.summed[self.side_rows(self.side), :].astype(F32)
            self.mid[...] = (own + self.near_in[...].astype(F32)).astype(BF)
        elif n == 5:
            out = self.mid[...].astype(F32) + self.mid_in[...].astype(F32)
            self.done[self.done_rows(self.side), :] = out.astype(BF)
        if n != 1 and n < 7:
            self.copy(n).start()

    def finish(self):
        for n in (0, 2, 3, 4, 5, 6):
            self.copy(n).wait_send()
        for k in range(1, self.p.z.ny):
            self.copy_y(k).wait_send()


class SmallReduce:
    def __init__(self, place, part, from_core, to_y, from_y, own, other, sems):
        self.p, self.part, self.from_core = place, part, from_core
        self.to_y, self.from_y, self.own, self.other, self.sems = to_y, from_y, own, other, sems
        zz = lax.div(place.e, 2)
        near = ((zz + 1 - 2 * lax.rem(zz, 2)) * 2 + lax.rem(place.e, 2), place.s)
        self.partners = [(place.expert(0, 1), place.s), near, (place.expert(2, 0), place.s)]

    def copy(self, n):
        p = self.p
        sems = self.sems.at[0, n], self.sems.at[1, n]
        if n == 0:
            return rcopy(self.part.at[1 - p.c], self.from_core, *sems, (p.e, p.shard(0, True)))
        return rcopy(self.own.at[n - 2], self.other.at[n - 2], *sems, self.partners[n - 2])

    def copy_y(self, k):
        p = self.p
        return rcopy(
            self.to_y.at[k - 1], self.from_y.at[k - 1], self.sems.at[0, 4 + k], self.sems.at[1, 4 + k],
            (p.e, p.shard(k, False)),
        )

    def step(self, n):
        p, ny = self.p, self.p.z.ny
        if n == 0:
            self.copy(0).start()
        elif n == 1:
            self.copy(0).wait_recv()
            for k in range(1, ny):
                y = lax.rem(p.y + k, ny)
                self.to_y[k - 1] = (self.part[p.c, y].astype(F32) + self.from_core[y].astype(F32)).astype(BF)
                self.copy_y(k).start()
        elif n == 2:
            out = self.part[p.c, p.y].astype(F32) + self.from_core[p.y].astype(F32)
            for k in range(1, ny):
                self.copy_y(k).wait_recv()
                out = out + self.from_y[k - 1].astype(F32)
            self.own[0] = out.astype(BF)
            self.copy(2).start()
        else:
            self.copy(n - 1).wait_recv()
            out = self.own[n - 3].astype(F32) + self.other[n - 3].astype(F32)
            if n == 5:
                return out
            self.own[n - 2] = out.astype(BF)
            self.copy(n).start()

    def finish(self):
        for n in (0, 2, 3, 4):
            self.copy(n).wait_send()
        for k in range(1, self.p.z.ny):
            self.copy_y(k).wait_send()


GROUPS = ((0, 1), (2, 3), (4,), (5,))


def backward_kernel(
    z,
    dy, counts, routes, dest, place_m, perm, ggrows,
    i_toks, i_hid, i_kk, i_vv, i_qq, i_pp, i_ctx, i_mid, i_nrm, i_sd, i_fk, i_fv, i_fq, i_fo, i_small, i_ret, i_rfin, i_rpart,
    mixed, dtok, done_o, done_0, done_1, done_2, done_3, drouter, dvecs,
    toks, hid, kk, vv, qq, pp, ctx, mid, nrm, sd, fk, fv, fq, fo, smallg, ret, retr,
    fin, rmine, rp, rys, ryr, gctx, gqb, gkb, gvb, gmid, lower, edge_id, edge_ok, tab, gain_rows,
    red_o, red_0, red_1, red_2, red_3,
    gpart, grp, gys, gyr, sbuf, small_refs,
    csem, rr1, rr2, rs1, rs2, rs3, rs4,
    gp1, gp2, gy1, gy2,
):
    p = Place(z)
    t, d, mt = z.t, z.d, z.mt
    half = d // 2
    loads = {}

    def load(src, dst, name):
        loads[name] = pltpu.make_async_copy(src, dst, csem.at[len(loads)])
        loads[name].start()

    load(i_sd, sd, "sd")
    load(i_ret, ret, "ret")
    load(i_small, smallg, "small")
    load(i_mid, mid, "mid")
    load(i_nrm, nrm, "nrm")
    load(i_ctx, ctx, "ctx")
    load(i_fo, fo, "fo")
    for u in range(2):
        load(i_rpart.at[u, p.c], rmine.at[u], ("part", u))
    load(i_qq, qq, "qq")
    load(i_vv, vv, "vv")
    load(i_kk, kk, "kk")
    load(i_pp, pp, "pp")
    load(i_hid, hid, "hid")
    load(i_fk, fk, "fk")
    load(i_fv, fv, "fv")
    load(i_fq, fq, "fq")
    load(i_toks, toks, "toks")
    p.barrier()

    returns, halves = [], []
    for u in range(4):
        h, cols = u // 2, pl.ds((u % 2) * half, half)
        src = i_rfin.at[u] if h == 0 else fin.at[u - 2]
        returns.append(Return(p, src, retr, h, cols, rr1.at[u], rr2.at[u]))
        if h == 0:
            returns[u].start_remote()
            load(i_rfin.at[u, pl.ds(0, z.sp)], retr.at[aligned(p.e * z.sp, z.sp, 16), cols], ("r", u))
    for u in range(2):
        halves.append(
            Scatter(
                p, rmine.at[u], i_rpart.at[u, 1 - p.c], rp.at[u], rys.at[u], ryr.at[u],
                rs1.at[u], rs2.at[u], rs3.at[u], rs4.at[u],
            )
        )
        halves[u].send()

    def result_b(u):
        loads["part", u].wait()
        halves[u].middle()

    def result_c(u):
        fin[u] = tdot(perm[...], halves[u].total().astype(BF)).astype(BF)
        returns[2 + u].start_remote()

    route0, route1 = route_columns(z, routes)
    loads["sd"].wait()
    slot0, slot1 = sd[:, 0:1], sd[:, 1:2]
    gate0, gate1 = sd[:, 2:3], sd[:, 3:4]
    hot0, hot1 = one_hot(z, slot0).astype(BF), one_hot(z, slot1).astype(BF)
    hot = hot0 + hot1

    def toward(hots):
        wide = dot(dot_t(hots, dest[...]).astype(BF), ggrows[...]) * dot(hots, place_m[...])
        return jnp.sum(wide, axis=1, keepdims=True)

    toward0, toward1 = toward(hot0), toward(hot1)
    mean = gate0 * toward0 + gate1 * toward1
    lane = iota((mt, z.small), 1)
    glog = jnp.where(lane == route0, gate0 * (toward0 - mean), 0.0)
    glog = (glog + jnp.where(lane == route1, gate1 * (toward1 - mean), 0.0)).astype(BF)
    result_b(0)
    loads["small"].wait()
    sums = smallg[0].astype(F32)
    for b in range(1, z.ns):
        sums = sums + smallg[b].astype(F32)
    gain_one = sums[z.e : z.e + 1, :]
    gain_two = sums[z.e + 1 : z.e + 2, :]
    router = sums.astype(BF)
    loads["ret"].wait()
    gnorm = dot(glog, router) + dot(hot, ret[...])
    loads["mid"].wait()
    x = mid[...]
    scale = lax.rsqrt(jnp.mean(x * x, axis=1, keepdims=True) + EPS)
    xh = x * scale
    gain_rows[1:2, :] = jnp.sum(gnorm * xh, axis=0, keepdims=True)
    gy = gnorm * gain_two
    gm = dy[...].astype(F32) + scale * (gy - xh * jnp.mean(gy * xh, axis=1, keepdims=True))
    gmid[...] = gm
    gattn = gm.astype(BF)
    loads["nrm"].wait()
    sbuf[...] = tdot(glog, nrm[...])

    reductions = [
        Reduce(p, *refs[:-1], done, refs[-1])
        for refs, done in ((red_0, done_0), (red_1, done_1), (red_2, done_2), (red_3, done_3), (red_o, done_o))
    ]
    parts = [red_0[0], red_1[0], red_2[0], red_3[0], red_o[0]]

    def stage(u, n):
        reductions[u].step(n)

    def put(u, first, value):
        value = value.astype(BF)
        for b in range(z.ns):
            parts[u][b % 2, b // 2, :, first : first + value.shape[1]] = value[b * z.r : (b + 1) * z.r]

    loads["ctx"].wait()
    for i in range(d // 256):
        put(4, i * 256, tdot(ctx[...], gattn[:, i * 256 : (i + 1) * 256]))
    stage(4, 0)
    loads["fo"].wait()
    for i in range(d // 256):
        cols = slice(i * 256, (i + 1) * 256)
        gctx[:, cols] = dot_t(gattn, fo[cols, :]).astype(BF)

    tab[...] = jnp.zeros_like(tab)
    lane = iota((1, LANES), 1)
    starts = jnp.where(lane <= 16, lane, 0)
    for i, edge in enumerate(BUCKET_EDGES):
        starts = jnp.where(lane == 17 + i, edge, starts)
    for m in range(z.m):
        key_pos, _ = key_layout(z, counts, m, (z.g, 1), 0)
        lower[m] = jnp.where(key_pos <= iota((z.g, z.far), 1), 1.0, 0.0).astype(BF)
        at = query_position(z, counts, m, p.s) - starts
        ok = (at >= 0) & (lane < BUCKETS)
        edge_id[m] = jnp.where(ok, at, 0)
        edge_ok[m] = jnp.where(ok, 1.0, 0.0)
    low = iota((t, LANES), 1) < 64

    def attend_back(i, unit):
        m = lax.rem(i, z.m)
        pair = unit
        cols = aligned(pair * LANES, LANES, LANES)
        rows = aligned(m * t, t, 16)
        q, g = qq[rows, cols], gctx[rows, cols]
        zero = jnp.zeros_like(q)
        q_two = jnp.concatenate([jnp.where(low, q, zero), jnp.where(low, zero, q)], 0)
        g_two = jnp.concatenate([jnp.where(low, g, zero), jnp.where(low, zero, g)], 0)
        probs = pp[m * z.pairs + pair]
        pf = probs.astype(F32)
        gp = dot_t(g_two, vv[m, :, cols])
        gs = (pf * (gp - jnp.sum(pf * gp, axis=1, keepdims=True))).astype(BF)
        two = dot(gs, kk[m, :, cols])
        gqb[rows, cols] = (jnp.where(low, two[:t], two[t:]) * 0.125).astype(BF)
        gkb[m, :, cols] = tdot(gs, q_two).astype(BF)
        gvb[m, :, cols] = tdot(probs, g_two).astype(BF)
        total = dot(gs, lower[m])
        for side in range(2):
            found = jnp.zeros((t, LANES), F32)
            for b in range(z.far // LANES):
                at = edge_id[m] - b * LANES
                inside = (at >= 0) & (at < LANES)
                got = jnp.take_along_axis(
                    total[side * t : (side + 1) * t, b * LANES : (b + 1) * LANES], jnp.where(inside, at, 0), axis=1
                )
                found = jnp.where(inside, got, found)
            found = jnp.sum(found * edge_ok[m], axis=0, keepdims=True)
            row = pl.ds(pair * 2 + side, 1)
            tab[row, :] = tab[row, :] + found
        return unit

    def attention(pair):
        lax.fori_loop(0, z.m, attend_back, pair, unroll=2)

    def own_hidden():
        return jnp.concatenate([hid[m, aligned(p.s * t, t, 16), :] for m in range(z.m)], 0)

    def weight_grads(u):
        n = len(GROUPS[u]) * LANES
        cols = slice(GROUPS[u][0] * LANES, GROUPS[u][0] * LANES + n)
        put(u, 0, tdot(own_hidden(), gqb[:, cols]))
        every = hid[...].reshape(z.m * z.g, d)
        put(u, n, tdot(every, gkb[:, :, cols].reshape(z.m * z.g, n)))
        put(u, 2 * n, tdot(every, gvb[:, :, cols].reshape(z.m * z.g, n)))

    grads = [
        Scatter(
            p, gpart.at[m, p.c], gpart.at[m, 1 - p.c], grp.at[m], gys.at[m], gyr.at[m],
            gp1.at[m], gp2.at[m], gy1.at[m], gy2.at[m],
        )
        for m in range(z.m)
    ]

    def hidden_grads(m):
        x = toks[m].astype(F32)
        scale = lax.rsqrt(jnp.mean(x * x, axis=1, keepdims=True) + EPS)
        for i in range(d // 256):
            cols = slice(i * 256, (i + 1) * 256)
            gh = dot_t(gkb[m], fk[cols, :]) + dot_t(gvb[m], fv[cols, :])
            own = dot_t(gqb[m * t : (m + 1) * t, :], fq[cols, :])
            for b in range(z.ns):
                rows = slice(b * t, (b + 1) * t)
                part = gh[rows] + jnp.where(p.s == b, 1.0, 0.0) * own
                gpart[m, b % 2, b // 2, :, cols] = part.astype(BF)
                row = jnp.sum(part * (toks[m, rows, cols].astype(F32) * scale[rows]), axis=0, keepdims=True)
                if m == 0 and b == 0:
                    gain_rows[0:1, cols] = row
                else:
                    gain_rows[0:1, cols] = gain_rows[0:1, cols] + row

    def token_grads(m):
        gh = grads[m].total()
        rows = slice(m * t, (m + 1) * t)
        x = toks[m, aligned(p.s * t, t, 16), :].astype(F32)
        scale = lax.rsqrt(jnp.mean(x * x, axis=1, keepdims=True) + EPS)
        xh = x * scale
        gy = gh * gain_one
        dtok[rows, :] = gmid[rows, :] + scale * (gy - xh * jnp.mean(gy * xh, axis=1, keepdims=True))

    small_sum = SmallReduce(p, *small_refs)

    def small_step(n):
        if n:
            return small_sum.step(n)
        tabs = tab[...]
        tabs = tabs - pltpu.roll(tabs, LANES - 1, 1)
        tabs = jnp.where(iota(tabs.shape, 1) < BUCKETS, tabs, 0.0)
        row = iota(sbuf.shape, 0)
        out = sbuf[...]
        out = jnp.where(row == z.e, gain_rows[0:1, :], out)
        out = jnp.where(row == z.e + 1, gain_rows[1:2, :], out)
        sbuf[...] = out
        per = LANES // BUCKETS
        for c in range(HEADS // per):
            piece = tabs[c * per : c * per + 1, :]
            for j in range(1, per):
                piece = piece + pltpu.roll(tabs[c * per + j : c * per + j + 1, :], j * BUCKETS, 1)
            sbuf[z.e + 2 : z.e + 3, c * LANES : (c + 1) * LANES] = piece
        every = sbuf[...].astype(BF)
        tail = every[z.e : z.small, :]
        for b in range(z.ns):
            block = dot_t(every, spread(z, b, z.r))
            biases = dot_t(tail, spread(z, b, HEADS * BUCKETS // z.ns))
            low_rows = jnp.where(iota(biases.shape, 0) == 2, biases, block[z.e : z.small])
            small_refs[0][b % 2, b // 2, 0 : z.e, :] = block[0 : z.e].astype(BF)
            small_refs[0][b % 2, b // 2, z.e : z.small, :] = low_rows.astype(BF)
        small_sum.step(0)

    def finish_mixed():
        for u in range(4):
            returns[u].arrive()
        for u in range(2):
            loads["r", u].wait()
        for m in range(z.m):
            rows = slice(m * t, (m + 1) * t)
            first, second = dot(hot0[rows], retr[...]), dot(hot1[rows], retr[...])
            mixed[rows, :] = (mid[rows, :] + gate0[rows] * first + gate1[rows] * second).astype(BF)

    for name in ("qq", "vv", "kk", "pp"):
        loads[name].wait()
    attention(0)
    stage(4, 1)
    attention(1)
    loads["hid"].wait()
    weight_grads(0)
    stage(0, 0)
    result_c(0)
    attention(2)
    stage(0, 1)
    attention(3)
    stage(4, 2)
    weight_grads(1)
    stage(1, 0)
    attention(4)
    stage(1, 1)
    weight_grads(2)
    stage(2, 0)
    stage(4, 3)
    attention(5)
    stage(2, 1)
    weight_grads(3)
    stage(3, 0)
    stage(0, 2)
    stage(4, 4)
    for name in ("fk", "fv", "fq", "toks"):
        loads[name].wait()
    hidden_grads(0)
    grads[0].send()
    stage(3, 1)
    hidden_grads(1)
    grads[1].send()
    small_step(0)
    stage(4, 5)
    stage(0, 3)
    stage(1, 2)
    stage(4, 6)
    stage(0, 4)
    small_step(1)
    result_b(1)
    grads[0].middle()
    grads[1].middle()
    stage(2, 2)
    stage(1, 3)
    stage(0, 5)
    stage(3, 2)
    small_step(2)
    stage(2, 3)
    stage(1, 4)
    stage(3, 3)
    stage(0, 6)
    small_step(3)
    stage(2, 4)
    stage(1, 5)
    stage(3, 4)
    result_c(1)
    small_step(4)
    stage(2, 5)
    stage(1, 6)
    stage(3, 5)
    token_grads(0)
    out = small_step(5)
    drouter[...] = out[0 : z.e, :]
    dvecs[...] = out[z.e : z.small, :]
    stage(2, 6)
    stage(3, 6)
    token_grads(1)
    finish_mixed()
    for u in (4, 0, 1, 2, 3):
        stage(u, 7)
    for item in reductions + returns + halves + grads + [small_sum]:
        item.finish()


def backward(z, *inputs):
    def bf(*shape):
        return pltpu.VMEM(shape, BF)

    def f32(*shape):
        return jax.ShapeDtypeStruct(shape, F32)

    dma = pltpu.SemaphoreType.DMA
    d, r, ny, nz, half = z.d, z.r, z.ny, z.nz, z.d // 2
    widths = [d] + [3 * LANES * len(g) for g in GROUPS]
    blocks = [jax.ShapeDtypeStruct((r, w), BF) for w in widths]
    outs = (jax.ShapeDtypeStruct((z.mt, d), BF), f32(z.mt, d), *blocks, f32(z.e, r), f32(z.small - z.e, r))

    def reduction(w):
        half, piece = bf(r // 2, w), bf(r // 4, w)
        return (
            bf(2, ny, r, w), bf(ny, r, w), bf(ny - 1, r, w), bf(ny - 1, r, w), half, half, half, piece, piece, piece,
            dma((2, 5 + ny)),
        )

    small = (
        bf(2, ny, z.small, r), bf(ny, z.small, r), bf(ny - 1, z.small, r), bf(ny - 1, z.small, r),
        bf(3, z.small, r), bf(3, z.small, r), dma((2, 4 + ny)),
    )
    kept = [pltpu.VMEM(x.shape, x.dtype) for x in inputs[7:-2]]
    return pl.pallas_call(
        functools.partial(backward_kernel, z),
        out_shape=outs,
        in_specs=[VMEM, SMEM] + [VMEM] * 5 + [ANY] * 18,
        out_specs=[VMEM] * len(outs),
        scratch_shapes=kept + [
            bf(z.slots, d),
            bf(2, z.hs, half), bf(2, ny, z.cb, half), bf(2, ny, z.cb, half), bf(2, ny - 1, z.cb, half), bf(2, ny - 1, z.cb, half),
            bf(z.mt, d), bf(z.mt, d), bf(z.m, z.g, d), bf(z.m, z.g, d), pltpu.VMEM((z.mt, d), F32),
            bf(z.m, z.g, z.far), pltpu.VMEM((z.m, z.t, LANES), I32), pltpu.VMEM((z.m, z.t, LANES), F32),
            pltpu.VMEM((16, LANES), F32), pltpu.VMEM((8, d), F32),
            *[reduction(w) for w in widths],
            bf(z.m, 2, ny, z.t, d), bf(z.m, ny, z.t, d), bf(z.m, ny - 1, z.t, d), bf(z.m, ny - 1, z.t, d),
            pltpu.VMEM((z.small, d), F32), small,
            dma((20,)), dma((4, z.hn)), dma((4, z.hn)), dma((2,)), dma((2,)), dma((2, ny)), dma((2, ny)),
            dma((z.m,)), dma((z.m,)), dma((z.m, ny)), dma((z.m, ny)),
        ],
        compiler_params=pltpu.CompilerParams(
            collective_id=1, has_side_effects=True, vmem_limit_bytes=63 * 2**20
        ),
        name="backward",
    )(*inputs)


def finish_kernel(
    d_o, d_0, d_1, d_2, d_3, din, dout, mixed, dtok, router, vecs, o_mixed, o_dtok, o_q, o_k, o_v, o_o, o_in, o_out, o_router, o_one,
    o_two, o_bias,
):
    o_in[...] = din[...].astype(F32)
    o_out[...] = dout[...].astype(F32)
    o_mixed[...] = mixed[...]
    o_dtok[...] = dtok[...]
    o_o[...] = d_o[...].astype(F32)
    o_router[...] = router[...]
    o_one[...] = vecs[0:1, :]
    o_two[...] = vecs[1:2, :]
    o_bias[...] = vecs[2:3, : o_bias.shape[1]]
    for pairs, block in zip(GROUPS, (d_0, d_1, d_2, d_3)):
        n, first = len(pairs) * LANES, pairs[0] * LANES
        for i, out in enumerate((o_q, o_k, o_v)):
            out[:, first : first + n] = block[:, i * n : (i + 1) * n].astype(F32)


def finish(z, n_bias, blocks, din, dout, mixed, dtok, router, vecs):
    d, r, n = z.d, z.r, 4
    rows = z.el * d // n

    def f32(*shape):
        return jax.ShapeDtypeStruct(shape, F32)

    def by_row(size, width=d):
        return pl.BlockSpec((size, width), lambda i: (i, 0))

    def once(*shape):
        return pl.BlockSpec(shape, lambda i: (0, 0))

    return pl.pallas_call(
        finish_kernel,
        grid=(n,),
        out_shape=(
            jax.ShapeDtypeStruct((z.mt, d), BF), f32(z.mt, d), *[f32(r, d)] * 4, *[f32(n * rows, d)] * 2,
            f32(*router.shape), f32(1, r), f32(1, r), f32(1, n_bias),
        ),
        in_specs=[by_row(r // n, b.shape[1]) for b in blocks] + [by_row(rows)] * 2 + [by_row(z.mt // n)] * 2
        + [once(*router.shape), once(*vecs.shape)],
        out_specs=[by_row(z.mt // n)] * 2 + [by_row(r // n)] * 4 + [by_row(rows)] * 2
        + [once(*router.shape), once(1, r), once(1, r), once(1, n_bias)],
        name="finish",
    )(*blocks, din.reshape(n * rows, d), dout.reshape(n * rows, d), mixed, dtok, router, vecs)


def fused_device(
    z, tokens, cotangent, routes, prompt_rows, w_query, w_key, w_value, w_output, w_router, gain_attn, gain_ffn,
    pos_table, w_in, w_out,
):
    perm, rows_of, dest, place, gate_of, source, pick = layout_constants(z)
    n = pos_table.shape[0]
    vecs = jnp.concatenate([gain_attn, gain_ffn, pos_table])[None]
    dy = cotangent.reshape(z.mt, z.d)
    routes = routes.transpose(0, 2, 1)
    counts = prompt_rows[:, 0]
    kept = forward(
        z, tokens, dy, routes, counts, w_key, w_value, w_query, w_output, w_router.T, vecs, w_in, w_out,
        perm, rows_of, dest, place, gate_of, source, pick,
    )
    kept, (ggrows, din, dout) = kept[:18], kept[18:]
    mixed, dtok, *blocks, drouter, dvecs = backward(z, dy, counts, routes, dest, place, perm, ggrows, *kept)
    mixed, dtok, dq, dk, dv, do, din, dout, drouter, one, two, bias = finish(
        z, n, blocks, din, dout, mixed, dtok, drouter, dvecs
    )
    return (
        mixed.reshape(tokens.shape),
        dtok.reshape(tokens.shape),
        dq,
        dk,
        dv,
        do,
        drouter.T,
        one.reshape(-1),
        two.reshape(-1),
        bias.reshape(-1),
        din.reshape(w_in.shape),
        dout.reshape(w_out.shape),
    )


HIGHEST = lax.Precision.HIGHEST


def distance_bucket(distance):
    coarse = reduce(
        lambda running, border: running + (distance >= border).astype(jnp.int32),
        BUCKET_EDGES,
        jnp.full(distance.shape, 16, jnp.int32),
    )
    return jnp.where(distance < 16, distance, coarse)


def layout(counts, block_rows):
    shard_count = counts.shape[0]
    offsets = jnp.cumsum(counts, dtype=jnp.int32) - counts
    row_index = jnp.arange(shard_count * block_rows, dtype=jnp.int32)
    device = row_index // block_rows
    local_row = row_index - device * block_rows
    own_count = counts[device]
    is_prompt = local_row < own_count
    prompt_total = jnp.sum(counts, dtype=jnp.int32)
    position = jnp.where(
        is_prompt, offsets[device] + local_row, prompt_total + local_row - own_count
    )
    return (position, is_prompt, device)


def rms_norm(values, gain):
    return values * lax.rsqrt(jnp.mean(values * values, axis=-1, keepdims=True) + EPS) * gain


def matmul(left, right):
    return jnp.dot(left, right, preferred_element_type=jnp.float32)


def matmul_left(left, right):
    return lax.dot_general(
        left, right, (((0,), (0,)), ((), ())), preferred_element_type=jnp.float32
    )


def matmul_right(left, right):
    return lax.dot_general(
        left, right, (((1,), (1,)), ((), ())), preferred_element_type=jnp.float32
    )


def per_device(
    tokens,
    cotangent,
    routes,
    prompt_rows,
    w_query,
    w_key,
    w_value,
    w_output,
    w_router,
    gain_attn,
    gain_ffn,
    pos_table,
    w_in,
    w_out,
):
    shard_count = lax.axis_size("shard")
    expert_ranks = lax.axis_size("expert")
    own_index = lax.axis_index("shard")
    micro_count, tok_rows, model_width = tokens.shape
    local_experts = w_in.shape[0]
    expert_count = w_router.shape[1]
    capacity = (9 * tok_rows + 4 * expert_count - 1) // (4 * expert_count)
    head_count = HEADS
    head_size = model_width // head_count
    bucket_count = BUCKETS
    score_scale = head_size ** (-0.5)
    group_rows = shard_count * tok_rows
    slot_count = expert_ranks * capacity * local_experts
    recv_rows = expert_ranks * capacity
    bucket_ids = jnp.arange(bucket_count, dtype=jnp.int32)
    expert_ids = jnp.arange(expert_count, dtype=jnp.int32)
    gathered = (
        lax.all_gather(w_query, "shard", axis=0, tiled=True),
        lax.all_gather(w_key, "shard", axis=0, tiled=True),
        lax.all_gather(w_value, "shard", axis=0, tiled=True),
        lax.all_gather(w_output, "shard", axis=0, tiled=True),
        lax.all_gather(w_router, "shard", axis=0, tiled=True),
        lax.all_gather(gain_attn, "shard", axis=0, tiled=True),
        lax.all_gather(gain_ffn, "shard", axis=0, tiled=True),
        lax.all_gather(pos_table, "shard", axis=0, tiled=True),
    )
    full_query, full_key, full_value, full_output, full_router, gain_one, gain_two, table_flat = (
        gathered
    )
    gain_first = gain_one.astype(jnp.float32)
    gain_second = gain_two.astype(jnp.float32)
    table = table_flat.astype(jnp.float32).reshape(head_count, bucket_count)
    expert_in, expert_out = (
        lax.all_gather(w_in, "shard", axis=2, tiled=True),
        lax.all_gather(w_out, "shard", axis=1, tiled=True),
    )
    sum_query = jnp.zeros(full_query.shape, jnp.float32)
    sum_key = jnp.zeros(full_key.shape, jnp.float32)
    sum_value = jnp.zeros(full_value.shape, jnp.float32)
    sum_output = jnp.zeros(full_output.shape, jnp.float32)
    sum_router = jnp.zeros(full_router.shape, jnp.float32)
    sum_gain_one = jnp.zeros((model_width,), jnp.float32)
    sum_gain_two = jnp.zeros((model_width,), jnp.float32)
    sum_table = jnp.zeros((head_count, bucket_count), jnp.float32)
    sum_expert_in = jnp.zeros(expert_in.shape, jnp.float32)
    sum_expert_out = jnp.zeros(expert_out.shape, jnp.float32)
    mixed_parts = []
    grad_parts = []
    for micro_index in range(micro_count):
        inputs = tokens[micro_index].astype(jnp.float32)
        counts = prompt_rows[micro_index, 0]
        pos_all, prompt_all, device_all = layout(counts, tok_rows)
        query_pos = lax.dynamic_slice_in_dim(pos_all, own_index * tok_rows, tok_rows)
        hidden = rms_norm(inputs, gain_first).astype(jnp.bfloat16)
        query = matmul(hidden, full_query).astype(jnp.bfloat16)
        key = matmul(hidden, full_key).astype(jnp.bfloat16)
        value = matmul(hidden, full_value).astype(jnp.bfloat16)
        keys_all, values_all = (
            lax.all_gather(key, "shard", axis=0, tiled=True),
            lax.all_gather(value, "shard", axis=0, tiled=True),
        )
        key_index = jnp.arange(group_rows, dtype=jnp.int32)
        key_far = jnp.zeros((group_rows,), jnp.bool_)
        key_total = keys_all.shape[0]
        key_block = math.gcd(key_total, 512)
        block_count = key_total // key_block
        key_pos = pos_all[key_index]
        key_prompt = prompt_all[key_index]
        key_device = device_all[key_index]
        key_mine = key_device == own_index
        distance = query_pos[:, None] - key_pos[None, :]
        visible = (
            (distance >= 0)
            & (key_prompt | key_mine)[None, :]
            & jnp.logical_not(key_far & key_mine)[None, :]
        )
        bucket_all = distance_bucket(jnp.maximum(distance, 0))
        bucket_blocks = bucket_all.reshape(tok_rows, block_count, key_block).transpose(1, 0, 2)
        visible_blocks = visible.reshape(tok_rows, block_count, key_block).transpose(1, 0, 2)
        query_heads = query.reshape(tok_rows, head_count, head_size)
        key_blocks = keys_all.reshape(block_count, key_block, head_count, head_size)
        value_blocks = values_all.reshape(block_count, key_block, head_count, head_size)

        def make_bias(unused, block_item):
            bucket_piece, visible_piece = block_item
            bucket_hits = (bucket_piece[:, :, None] == bucket_ids).astype(jnp.float32)
            bias = jnp.einsum("qkb,hb->hqk", bucket_hits, table, precision=HIGHEST)
            return (unused, jnp.where(visible_piece[None], bias, MASKED))

        _, bias_blocks = lax.scan(
            make_bias, jnp.zeros((), jnp.float32), (bucket_blocks, visible_blocks)
        )

        def score_piece(key_piece, bias_piece):
            raw = jnp.einsum(
                "qhd,khd->hqk", query_heads, key_piece, preferred_element_type=jnp.float32
            )
            return raw * score_scale + bias_piece

        def running(state_pair, block_item):
            running_max, running_sum = state_pair
            key_piece, bias_piece = block_item
            scores = score_piece(key_piece, bias_piece)
            new_max = jnp.maximum(running_max, jnp.max(scores, axis=-1))
            running_sum = running_sum * jnp.exp(running_max - new_max) + jnp.sum(
                jnp.exp(scores - new_max[:, :, None]), axis=-1
            )
            return ((new_max, running_sum), None)

        start_pair = (
            jnp.full((head_count, tok_rows), MASKED, jnp.float32),
            jnp.zeros((head_count, tok_rows), jnp.float32),
        )
        (running_max, running_sum), _ = lax.scan(running, start_pair, (key_blocks, bias_blocks))
        log_total = running_max + jnp.log(running_sum)

        def gather_context(context_sum, block_item):
            key_piece, value_piece, bias_piece = block_item
            weights_low = jnp.exp(
                score_piece(key_piece, bias_piece) - log_total[:, :, None]
            ).astype(jnp.bfloat16)
            return (
                context_sum
                + jnp.einsum(
                    "hqk,khd->qhd", weights_low, value_piece, preferred_element_type=jnp.float32
                ),
                None,
            )

        context, _ = lax.scan(
            gather_context,
            jnp.zeros((tok_rows, head_count, head_size), jnp.float32),
            (key_blocks, value_blocks, bias_blocks),
        )
        context_low = context.reshape(tok_rows, model_width).astype(jnp.bfloat16)
        middle = inputs + matmul(context_low, full_output)
        normed = rms_norm(middle, gain_second).astype(jnp.bfloat16)
        logits = matmul(normed, full_router)
        chosen = routes[micro_index]
        pick_table = (chosen[:, :, None] == expert_ids).astype(jnp.float32)
        picked = jnp.sum(pick_table * logits[:, None, :], axis=-1)
        gate_weights = jax.nn.softmax(picked, axis=-1)
        flat_routes = chosen.reshape(-1)
        expert_hits = (flat_routes[:, None] == expert_ids).astype(jnp.int32)
        expert_rank = (
            jnp.sum(
                jnp.cumsum(expert_hits, axis=0, dtype=jnp.int32) * expert_hits,
                axis=1,
                dtype=jnp.int32,
            )
            - 1
        )
        slot_index = (
            flat_routes // local_experts * (capacity * local_experts)
            + expert_rank * local_experts
            + flat_routes % local_experts
        )
        slot_owner = (
            jnp.full((slot_count,), 2 * tok_rows, jnp.int32)
            .at[slot_index]
            .set(jnp.arange(2 * tok_rows, dtype=jnp.int32))
        )
        padded = jnp.concatenate([normed, jnp.zeros((1, model_width), jnp.bfloat16)], axis=0)
        outgoing = padded[slot_owner // 2].reshape(
            expert_ranks, capacity, local_experts, model_width
        )
        received = lax.all_to_all(
            outgoing, "expert", split_axis=0, concat_axis=0, tiled=True
        ).reshape(recv_rows, local_experts, model_width)
        pre_act = jnp.einsum(
            "red,edf->ref", received, expert_in, preferred_element_type=jnp.float32
        )
        activation = jax.nn.gelu(pre_act).astype(jnp.bfloat16)
        expert_result = jnp.einsum(
            "ref,efd->red", activation, expert_out, preferred_element_type=jnp.float32
        )
        result_low = expert_result.astype(jnp.bfloat16).reshape(
            expert_ranks, capacity, local_experts, model_width
        )
        returned = lax.all_to_all(
            result_low, "expert", split_axis=0, concat_axis=0, tiled=True
        ).reshape(slot_count, model_width)
        picked_rows = returned[slot_index].astype(jnp.float32).reshape(tok_rows, 2, model_width)
        output_rows = middle + jnp.sum(gate_weights[:, :, None] * picked_rows, axis=1)
        mixed_parts.append(output_rows.astype(jnp.bfloat16))
        grad_output = cotangent[micro_index].astype(jnp.float32)
        grad_gate = jnp.sum(grad_output[:, None, :] * picked_rows, axis=-1)
        grad_pick = gate_weights * (
            grad_gate - jnp.sum(gate_weights * grad_gate, axis=-1, keepdims=True)
        )
        grad_logits = jnp.sum(pick_table * grad_pick[:, :, None], axis=1).astype(jnp.bfloat16)
        sum_router = sum_router + matmul_left(normed, grad_logits)
        grad_normed = matmul_right(grad_logits, full_router)
        branch_grad = (gate_weights[:, :, None] * grad_output[:, None, :]).reshape(
            2 * tok_rows, model_width
        )
        padded_grad = jnp.concatenate(
            [branch_grad, jnp.zeros((1, model_width), jnp.float32)], axis=0
        )
        grad_send = (
            padded_grad[slot_owner]
            .astype(jnp.bfloat16)
            .reshape(expert_ranks, capacity, local_experts, model_width)
        )
        grad_recv = lax.all_to_all(
            grad_send, "expert", split_axis=0, concat_axis=0, tiled=True
        ).reshape(recv_rows, local_experts, model_width)
        grad_act = jnp.einsum(
            "red,efd->ref", grad_recv, expert_out, preferred_element_type=jnp.float32
        )
        sum_expert_out = sum_expert_out + jnp.einsum(
            "ref,red->efd", activation, grad_recv, preferred_element_type=jnp.float32
        )
        _, gelu_pull = jax.vjp(jax.nn.gelu, pre_act)
        grad_pre = gelu_pull(grad_act)[0].astype(jnp.bfloat16)
        sum_expert_in = sum_expert_in + jnp.einsum(
            "red,ref->edf", received, grad_pre, preferred_element_type=jnp.float32
        )
        grad_in_rows = jnp.einsum(
            "ref,edf->red", grad_pre, expert_in, preferred_element_type=jnp.float32
        )
        grad_in_low = grad_in_rows.astype(jnp.bfloat16).reshape(
            expert_ranks, capacity, local_experts, model_width
        )
        grad_back = lax.all_to_all(
            grad_in_low, "expert", split_axis=0, concat_axis=0, tiled=True
        ).reshape(slot_count, model_width)
        grad_normed = grad_normed + jnp.sum(
            grad_back[slot_index].astype(jnp.float32).reshape(tok_rows, 2, model_width), axis=1
        )
        _, norm_pull = jax.vjp(rms_norm, middle, gain_second)
        grad_middle, grad_gain_second = norm_pull(grad_normed)
        grad_middle = grad_middle + grad_output
        sum_gain_two = sum_gain_two + grad_gain_second
        grad_attn = grad_middle.astype(jnp.bfloat16)
        sum_output = sum_output + matmul_left(context_low, grad_attn)
        grad_context = (
            matmul_right(grad_attn, full_output)
            .astype(jnp.bfloat16)
            .reshape(tok_rows, head_count, head_size)
        )
        row_delta = jnp.einsum("qhd,qhd->hq", grad_context.astype(jnp.float32), context)

        def attend_back(state_pair, block_item):
            grad_query_sum, grad_table_sum = state_pair
            key_piece, value_piece, bias_piece, bucket_piece = block_item
            probs = jnp.exp(score_piece(key_piece, bias_piece) - log_total[:, :, None])
            grad_probs = jnp.einsum(
                "qhd,khd->hqk", grad_context, value_piece, preferred_element_type=jnp.float32
            )
            grad_scores = probs * (grad_probs - row_delta[:, :, None])
            bucket_hits = (bucket_piece[:, :, None] == bucket_ids).astype(jnp.float32)
            grad_table_sum = grad_table_sum + jnp.einsum(
                "hqk,qkb->hb", grad_scores, bucket_hits, precision=HIGHEST
            )
            grad_raw = (grad_scores * score_scale).astype(jnp.bfloat16)
            grad_query_sum = grad_query_sum + jnp.einsum(
                "hqk,khd->qhd", grad_raw, key_piece, preferred_element_type=jnp.float32
            )
            grad_key_piece = jnp.einsum(
                "hqk,qhd->khd", grad_raw, query_heads, preferred_element_type=jnp.float32
            )
            grad_value_piece = jnp.einsum(
                "hqk,qhd->khd",
                probs.astype(jnp.bfloat16),
                grad_context,
                preferred_element_type=jnp.float32,
            )
            return ((grad_query_sum, grad_table_sum), (grad_key_piece, grad_value_piece))

        back_start = (
            jnp.zeros((tok_rows, head_count, head_size), jnp.float32),
            jnp.zeros((head_count, bucket_count), jnp.float32),
        )
        (grad_query_all, grad_table_all), (grad_key_blocks, grad_value_blocks) = lax.scan(
            attend_back, back_start, (key_blocks, value_blocks, bias_blocks, bucket_blocks)
        )
        sum_table = sum_table + grad_table_all
        key_grad_rows = grad_key_blocks.reshape(key_total, model_width)
        value_grad_rows = grad_value_blocks.reshape(key_total, model_width)
        own_key_grad, own_value_grad = (
            lax.psum_scatter(
                key_grad_rows.astype(jnp.bfloat16), "shard", scatter_dimension=0, tiled=True
            ).astype(jnp.float32),
            lax.psum_scatter(
                value_grad_rows.astype(jnp.bfloat16), "shard", scatter_dimension=0, tiled=True
            ).astype(jnp.float32),
        )
        grad_query_low = grad_query_all.reshape(tok_rows, model_width).astype(jnp.bfloat16)
        grad_key_low = own_key_grad.astype(jnp.bfloat16)
        grad_value_low = own_value_grad.astype(jnp.bfloat16)
        sum_query = sum_query + matmul_left(hidden, grad_query_low)
        sum_key = sum_key + matmul_left(hidden, grad_key_low)
        sum_value = sum_value + matmul_left(hidden, grad_value_low)
        grad_hidden = (
            matmul_right(grad_query_low, full_query)
            + matmul_right(grad_key_low, full_key)
            + matmul_right(grad_value_low, full_value)
        )
        _, first_pull = jax.vjp(rms_norm, inputs, gain_first)
        grad_inputs, grad_gain_first = first_pull(grad_hidden)
        sum_gain_one = sum_gain_one + grad_gain_first
        grad_parts.append(grad_inputs + grad_middle)
    shares = (
        lax.psum_scatter(
            sum_query.astype(jnp.bfloat16), "shard", scatter_dimension=0, tiled=True
        ).astype(jnp.float32),
        lax.psum_scatter(
            sum_key.astype(jnp.bfloat16), "shard", scatter_dimension=0, tiled=True
        ).astype(jnp.float32),
        lax.psum_scatter(
            sum_value.astype(jnp.bfloat16), "shard", scatter_dimension=0, tiled=True
        ).astype(jnp.float32),
        lax.psum_scatter(
            sum_output.astype(jnp.bfloat16), "shard", scatter_dimension=0, tiled=True
        ).astype(jnp.float32),
        lax.psum_scatter(
            sum_router.astype(jnp.bfloat16), "shard", scatter_dimension=0, tiled=True
        ).astype(jnp.float32),
        lax.psum_scatter(
            sum_gain_one.astype(jnp.bfloat16), "shard", scatter_dimension=0, tiled=True
        ).astype(jnp.float32),
        lax.psum_scatter(
            sum_gain_two.astype(jnp.bfloat16), "shard", scatter_dimension=0, tiled=True
        ).astype(jnp.float32),
        lax.psum_scatter(
            sum_table.reshape(-1).astype(jnp.bfloat16), "shard", scatter_dimension=0, tiled=True
        ).astype(jnp.float32),
    )
    own_grads = (
        lax.psum(shares[0].astype(jnp.bfloat16), "expert").astype(jnp.float32),
        lax.psum(shares[1].astype(jnp.bfloat16), "expert").astype(jnp.float32),
        lax.psum(shares[2].astype(jnp.bfloat16), "expert").astype(jnp.float32),
        lax.psum(shares[3].astype(jnp.bfloat16), "expert").astype(jnp.float32),
        lax.psum(shares[4].astype(jnp.bfloat16), "expert").astype(jnp.float32),
        lax.psum(shares[5].astype(jnp.bfloat16), "expert").astype(jnp.float32),
        lax.psum(shares[6].astype(jnp.bfloat16), "expert").astype(jnp.float32),
        lax.psum(shares[7].astype(jnp.bfloat16), "expert").astype(jnp.float32),
    )
    grad_expert_in, grad_expert_out = (
        lax.psum_scatter(
            sum_expert_in.astype(jnp.bfloat16), "shard", scatter_dimension=2, tiled=True
        ).astype(jnp.float32),
        lax.psum_scatter(
            sum_expert_out.astype(jnp.bfloat16), "shard", scatter_dimension=1, tiled=True
        ).astype(jnp.float32),
    )
    return (
        jnp.stack(mixed_parts),
        jnp.stack(grad_parts),
        own_grads[0],
        own_grads[1],
        own_grads[2],
        own_grads[3],
        own_grads[4],
        own_grads[5],
        own_grads[6],
        own_grads[7],
        grad_expert_in,
        grad_expert_out,
    )


def solution(mesh):
    in_specs = (
        P(None, ("expert", "shard"), None),
        P(None, ("expert", "shard"), None),
        P(None, ("expert", "shard"), None),
        P(None, "expert", None),
        P("shard", None),
        P("shard", None),
        P("shard", None),
        P("shard", None),
        P("shard", None),
        P("shard"),
        P("shard"),
        P("shard"),
        P("expert", None, "shard"),
        P("expert", "shard", None),
    )
    out_specs = (
        P(None, ("expert", "shard"), None),
        P(None, ("expert", "shard"), None),
        P("shard", None),
        P("shard", None),
        P("shard", None),
        P("shard", None),
        P("shard", None),
        P("shard"),
        P("shard"),
        P("shard"),
        P("expert", None, "shard"),
        P("expert", "shard", None),
    )
    ne, ns = mesh.shape["expert"], mesh.shape["shard"]

    def device(*args):
        tokens, w_router, w_in = args[0], args[8], args[12]
        z = Sizes(
            ne, ns, tokens.shape[0], tokens.shape[1], tokens.shape[2], w_router.shape[1], w_in.shape[0], w_in.shape[2]
        )
        return fused_device(z, *args) if z.fits() else per_device(*args)

    return jax.shard_map(
        device, mesh=mesh, in_specs=in_specs, out_specs=out_specs, check_vma=False
    )
```
